32 devices in a mesh: region: 16 (over z, x, core), member: 2 (over y).
Axes of the slice: x: 2, y: 2, z: 4, core: 2. Of those that a mesh axis runs over, the one named last changes fastest.
Arguments:
- state: float32 [1024, 32, 256], P('member', 'region'), may hold values from -8 to 8
- neighbours: int32 [32, 5], replicated, may hold values from 0 to 31, as said below
- obs_cell: int32 [32, 2, 64], replicated, may hold values from 0 to 255
- obs_values: float32 [32, 2, 64], replicated, may hold values from -6 to 6
- obs_var: float32 [32, 2, 64], replicated, may hold values from 0.25 to 1
Outputs:
- analysis: float32 [1024, 32, 256], P('member', 'region')
The draws below stay inside these ranges and needn't reach their ends.
Inputs may be any that keep to these rules, and one draw needn't show every extreme that they name: `neighbours`: patch g lies in region g // 2. Each patch lists 5 different patches in some order: two of the region before its own and two of the region after it (regions wrap around), and one other patch of its own region.
All inputs are finite; a program needn't handle non-finite values.
Results may differ from the reference program's by a relative error of at most 0.0003.
Values sent between devices are 32-bit elements; how exact they have to be, the bound alone decides.
No kernel may reach another device: no remote copies, remote signals or barrier semaphores. Data moves between devices by JAX's collectives and lax.ppermute only.
A program may use at most 128 MiB of HBM per device.

```python
import math
import jax
import jax.numpy as jnp
from jax import lax

K = 1024
CELLS = 256
OBS = 64
NBR = 5
NBATCH = 2
P_REG = 2
NPATCH = 32


def neighbour_table(key):
    base = jax.random.fold_in(key, 101)
    keys = jax.random.split(base, 6)
    patch = jnp.arange(NPATCH, dtype=jnp.int32)
    regions = NPATCH // P_REG
    region = patch // P_REG
    within = patch % P_REG
    first_prev = jax.random.randint(keys[0], (NPATCH,), 0, P_REG)
    second_prev = (first_prev + 1 + jax.random.randint(keys[1], (NPATCH,), 0, P_REG - 1)) % P_REG
    first_next = jax.random.randint(keys[2], (NPATCH,), 0, P_REG)
    second_next = (first_next + 1 + jax.random.randint(keys[3], (NPATCH,), 0, P_REG - 1)) % P_REG
    same_region = (within + 1 + jax.random.randint(keys[4], (NPATCH,), 0, P_REG - 1)) % P_REG
    before = (region - 1) % regions * P_REG
    after = (region + 1) % regions * P_REG
    own_base = region * P_REG
    columns = jnp.stack([before + first_prev, before + second_prev, after + first_next, after + second_next, own_base + same_region], axis=1)
    orders = jax.vmap(lambda single: jax.random.permutation(single, NBR))(jax.random.split(keys[5], NPATCH))
    return jnp.take_along_axis(columns, orders, axis=1).astype(jnp.int32)


def draw_neighbours(key, part):
    return neighbour_table(key)


def draw_state(key, part):
    table = neighbour_table(key)
    white_key = jax.random.fold_in(key, 23)
    walk_key = jax.random.fold_in(key, 31)
    shared_key = jax.random.fold_in(key, 37)
    norm = jnp.sqrt(jnp.float32(CELLS))
    white = 0.5 * jax.random.normal(white_key, (K, NPATCH, CELLS), jnp.float32)
    steps = jax.random.normal(walk_key, (K, NPATCH, CELLS), jnp.float32)
    shared_steps = jax.random.normal(shared_key, (K, CELLS), jnp.float32)
    walk = jnp.cumsum(steps, axis=2) / norm
    local = walk
    for column in range(NBR):
        local = local + jnp.take(walk, table[:, column], axis=1)
    shared = jnp.cumsum(shared_steps, axis=1) / norm
    field = 2.0 * shared[:, None, :] + 0.5 * local + white
    return jnp.clip(field, -8.0, 8.0)


def set_ends(result, stream_key, low, top_value):
    longest = result.shape.index(max(result.shape))
    spots = []
    for shift in (0, 1):
        where = [jax.random.randint(jax.random.fold_in(stream_key, axis), (), 0, length) for axis, length in enumerate(result.shape)]
        where[longest] = (where[longest] + shift) % result.shape[longest]
        spots.append(tuple(where))
    return result.at[spots[0]].set(low).at[spots[1]].set(top_value)


def scatter_about(own_key, shape, width, bound, kind=jnp.bfloat16):
    result = width * jax.random.normal(own_key, shape, jnp.float32)
    return jnp.clip(result, min=-bound, max=bound).astype(kind)


def setup_inputs(seed: int = 0) -> dict:
    streams_of = jax.random.split(jax.random.key(seed), 6)
    return {
        "state": draw_state(jax.random.fold_in(streams_of[5], 71), 0),
        "neighbours": draw_neighbours(jax.random.fold_in(streams_of[5], 71), 0),
        "obs_cell": set_ends(jax.random.randint(streams_of[2], (NPATCH, NBATCH, OBS), 0, CELLS), jax.random.fold_in(streams_of[2], 1), 0, CELLS - 1).astype(jnp.int32),
        "obs_values": scatter_about(streams_of[3], (NPATCH, NBATCH, OBS), 1.0, 6.0, jnp.float32),
        "obs_var": jnp.clip(jnp.exp(jax.random.uniform(streams_of[4], (NPATCH, NBATCH, OBS), jnp.float32, math.log(0.25), math.log(1.0))), 0.25, 1.0),
    }


HIGHEST = lax.Precision.HIGHEST

def analyse(stacked, values, variances, patch_state):
    members = stacked.shape[1]
    obs_mean = jnp.mean(stacked, axis=1)
    spread = stacked - obs_mean[:, None]
    innovation = values - obs_mean
    covariance = jnp.dot(spread, spread.T, precision=HIGHEST) / (members - 1.0) + jnp.diag(variances)
    state_mean = jnp.mean(patch_state, axis=0)
    anomaly = patch_state - state_mean[None, :]
    cross_cov = jnp.dot(spread, anomaly, precision=HIGHEST)
    factor = jnp.linalg.cholesky(covariance)
    kalman_gain = jax.scipy.linalg.cho_solve((factor, True), cross_cov) / (members - 1.0)
    combined = innovation[:, None] - 0.5 * spread
    update = lax.dot_general(combined, kalman_gain, (((0,), (0,)), ((), ())), precision=HIGHEST)
    return patch_state + update

def reference(state, neighbours, obs_cell, obs_values, obs_var):
    ensemble = jnp.transpose(state, (1, 0, 2))
    widening = jnp.arange(NBR, dtype=jnp.float32) + 2.0
    for batch in range(NBATCH):
        picks = obs_cell[:, batch, :]
        obs_rows = jax.vmap(lambda field, index: field[:, index].T)(ensemble, picks)
        values = obs_values[:, batch, :]
        variances = obs_var[:, batch, :]

        def per_patch(inputs):
            patch, field = inputs
            links = neighbours[patch]
            stacked = jnp.concatenate([obs_rows[patch], obs_rows[links].reshape(NBR * OBS, K)], axis=0)
            wanted = jnp.concatenate([values[patch], values[links].reshape(-1)])
            noise = jnp.concatenate([variances[patch], (variances[links] * widening[:, None]).reshape(-1)])
            return analyse(stacked, wanted, noise, field)
        ensemble = lax.map(per_patch, (jnp.arange(NPATCH, dtype=jnp.int32), ensemble))
    return jnp.transpose(ensemble, (1, 0, 2))
```

```python
import functools
import math

import jax
import jax.numpy as jnp
from jax import lax
from jax.experimental import pallas as pl
from jax.experimental.pallas import tpu as pltpu
from jax.sharding import PartitionSpec as P

NBATCH = 2
HIGHEST = lax.Precision.HIGHEST
F32 = jnp.float32
BF16 = jnp.bfloat16
VMEM = pl.BlockSpec(memory_space=pltpu.VMEM)
SMEM = pl.BlockSpec(memory_space=pltpu.SMEM)
NN = (((1,), (0,)), ((), ()))
NT = (((1,), (1,)), ((), ()))
TN = (((0,), (0,)), ((), ()))
RESIDUAL = 1e-3
MOST_STEPS = 15


def call(kernel, outs, ins, args, scratch=(), flops=0):
    shapes = [jax.ShapeDtypeStruct(shape, dtype) for shape, dtype, _ in outs]
    moved = sum(math.prod(s.shape) * s.dtype.itemsize for s in shapes)
    moved += sum(a.size * a.dtype.itemsize for a in args)
    return pl.pallas_call(
        kernel,
        out_shape=shapes,
        in_specs=ins,
        out_specs=[space for _, _, space in outs],
        scratch_shapes=list(scratch),
        compiler_params=pltpu.CompilerParams(vmem_limit_bytes=48 * 1024 * 1024),
        cost_estimate=pl.CostEstimate(flops=flops, bytes_accessed=moved, transcendentals=0),
    )(*args)


def split(x):
    high = x.astype(BF16)
    return high, (x - high.astype(F32)).astype(BF16)


def dot(a, b, dims=NN):
    return lax.dot_general(a, b, dims, preferred_element_type=F32)


def dot3(a, b, dims=NN):
    return dot(a[0], b[0], dims) + (dot(a[0], b[1], dims) + dot(a[1], b[0], dims))


def step_limits():
    limits = []
    for steps in range(MOST_STEPS):
        rho = RESIDUAL
        for _ in range(steps):
            rho = math.sqrt(2.0 * rho / (1.0 + rho))
        limits.append(2.0 * rho / (1.0 - rho) if rho < 1.0 else math.inf)
    return limits


def diagonal(n, columns, first):
    row = lax.broadcasted_iota(jnp.int32, (n, columns), 0)
    column = lax.broadcasted_iota(jnp.int32, (n, columns), 1)
    return row + first == column


def selector(cells_ref, patch, batch, cells, scratch):
    per_patch = cells_ref.shape[2]
    scratch[...] = jnp.full_like(scratch, -1)
    scratch[0:1, 0:per_patch] = cells_ref[pl.ds(patch, 1), batch, :]
    picks = scratch[0:1, :]
    grid = lax.broadcasted_iota(jnp.int32, (cells, picks.shape[1]), 0)
    hot = (grid == picks).astype(F32)
    return jnp.transpose(hot)[0:per_patch, :]


def pick_kernel(place_ref, cells_ref, state_ref, rows_ref, keep_ref, send_ref, scratch):
    first, column = place_ref[0], place_ref[1]
    patches, cells = state_ref.shape[1:]
    fields = [state_ref[:, p, :] for p in range(patches)]
    for p in range(patches):
        hot = selector(cells_ref, first + p, 0, cells, scratch)
        rows_ref[p] = lax.dot_general(hot, fields[p], NT, precision=HIGHEST, preferred_element_type=F32)
    keep_ref[...] = jnp.where(column == 0, fields[0], fields[1])
    send_ref[...] = jnp.where(column == 0, fields[1], fields[0])


def factor_kernel(pieces, batch, members, ids_ref, mult_ref, values_ref, var_ref, *refs):
    count = len(refs) - 9
    sources = refs[:count]
    sh_ref, sl_ref, d_ref, g_ref, x_ref, n_ref, flat, wh, wl = refs[count:]
    per_patch = values_ref.shape[2]
    flat[...] = jnp.ones_like(flat)
    blocks = len(pieces)
    for i in range(blocks):
        patch = ids_ref[i]
        flat[i : i + 1, 0:per_patch] = values_ref[pl.ds(patch, 1), batch, :]
        noise = var_ref[pl.ds(patch, 1), batch, :] * mult_ref[i]
        flat[blocks + i : blocks + i + 1, 0:per_patch] = noise
    upright = jnp.transpose(flat[...])
    for i, halves in enumerate(pieces):
        rows = [sources[which][index] for which, index in halves]
        total = sum(jnp.sum(part, axis=1, keepdims=True) for part in rows)
        mean = total * (1.0 / members)
        noise = upright[0:per_patch, blocks + i : blocks + i + 1]
        scale = lax.rsqrt(noise * (members - 1.0))
        at = slice(i * per_patch, (i + 1) * per_patch)
        start = 0
        for part in rows:
            high, low = split((part - mean) * scale)
            sh_ref[at, start : start + part.shape[1]] = high
            sl_ref[at, start : start + part.shape[1]] = low
            start += part.shape[1]
        shift = (upright[0:per_patch, i : i + 1] - mean) * scale
        d_ref[at, :] = jnp.broadcast_to(shift, (per_patch, d_ref.shape[1]))
    sh, sl = sh_ref[...], sl_ref[...]
    g = dot3((sh, sl), (sh, sl), NT)
    g_ref[...] = g
    n = g.shape[0]
    square = jnp.sum(jnp.sum(g * g, axis=0, keepdims=True), axis=1, keepdims=True)
    norm = jnp.sqrt(square) * (1.0 + 1e-5)
    size = square[0, 0]
    limits = step_limits()
    steps = jnp.int32(4)
    for k in range(4, MOST_STEPS - 1):
        limit = min(limits[k] * (1.0 - 1e-4), 1e18)
        steps = steps + (size > limit * limit).astype(jnp.int32)
    extra = (size > 1.6e7).astype(jnp.int32) + (size > 1e8).astype(jnp.int32)
    n_ref[0] = 1 + extra
    eye = diagonal(n, n, 0).astype(F32)
    first = 2.0 / (2.0 + norm)
    rho = norm * (0.5 * first)
    rho2 = rho * rho
    weight = 2.0 / (2.0 - rho2)
    r = (1.0 - first) * eye - first * g
    x = (weight * first) * (eye + r)
    parts = split(r)
    r = weight * dot3(parts, parts) - (0.5 * rho2 * weight) * eye
    rho2 = (0.5 * rho2 * weight) * (0.5 * rho2 * weight)
    x_ref[...] = x
    for ref, part in zip((wh, wl), split(r)):
        ref[0, :, 0:n] = part
    for ref, part in zip((wh, wl), split(x)):
        ref[0, :, n : 2 * n] = part

    def step(k, rho2):
        now, then = lax.rem(k, 2), lax.rem(k + 1, 2)
        weight = 2.0 / (2.0 - rho2)
        keep = 0.5 * rho2 * weight
        rh, rl = wh[now, :, 0:n], wl[now, :, 0:n]
        product = dot3((rh, rl), (wh[now, :, 0:n], wl[now, :, 0:n]))
        high, low = split(weight * product - keep * eye)
        wh[then, :, 0:n] = high
        wl[then, :, 0:n] = low
        product = dot3((rh, rl), (wh[now, :, n : 2 * n], wl[now, :, n : 2 * n]))
        x = weight * (x_ref[...] + product)
        x_ref[...] = x
        high, low = split(x)
        wh[then, :, n : 2 * n] = high
        wl[then, :, n : 2 * n] = low
        return keep * keep

    rho2 = lax.fori_loop(0, steps - 2, step, rho2)
    now = lax.rem(steps - 2, 2)
    weight = 2.0 / (2.0 - rho2)
    parts = (wh[now, :, 0:n], wl[now, :, 0:n])
    product = dot3(parts, (wh[now, :, n : 2 * n], wl[now, :, n : 2 * n]))
    x_ref[...] = weight * (x_ref[...] + product)


def solve(n_ref, s, g_ref, x_ref, fields, z_ref):
    members = sum(field.shape[0] for field in fields)
    mean = sum(jnp.sum(field, axis=0, keepdims=True) for field in fields) * (1.0 / members)
    cross, start = None, 0
    for field in fields:
        size = field.shape[0]
        part = dot3([h[:, start : start + size] for h in s], split(field - mean))
        cross = part if cross is None else cross + part
        start += size
    x = split(x_ref[...])
    z_ref[...] = dot3(x, split(cross))

    def refine(_, carry):
        z = z_ref[...]
        gz = lax.dot_general(g_ref[...], z, NN, precision=HIGHEST, preferred_element_type=F32)
        z_ref[...] = z + dot3(x, split(cross - z - gz))
        return carry

    lax.fori_loop(0, n_ref[0], refine, 0)


def gain_kernel(batch, parts, place_ref, n_ref, cells_ref, sh_ref, sl_ref, d_ref, g_ref, x_ref, *refs):
    states = refs[:parts]
    z_ref, rows_ref, scratch = refs[parts:]
    fields = [state[...] for state in states]
    s = (sh_ref[...], sl_ref[...])
    solve(n_ref, s, g_ref, x_ref, fields, z_ref)
    z = z_ref[...]
    hot = selector(cells_ref, place_ref[2], batch, z.shape[1], scratch)
    zt = lax.dot_general(hot, z, NT, precision=HIGHEST, preferred_element_type=F32)
    shift = lax.dot_general(zt, d_ref[...], NN, precision=HIGHEST, preferred_element_type=F32)
    moved = shift[:, 0:1] - 0.5 * dot3(split(zt), s)
    start = 0
    for field in fields:
        size = field.shape[0]
        picked = lax.dot_general(hot, field, NT, precision=HIGHEST, preferred_element_type=F32)
        rows_ref[:, start : start + size] = picked + moved[:, start : start + size]
        start += size


def updated(field, start, s, shift, z):
    size = field.shape[0]
    return field + shift - 0.5 * dot3([h[:, start : start + size] for h in s], z, TN)


def shift_of(z, d_ref):
    return jnp.sum(z * d_ref[:, 0:1], axis=0, keepdims=True)


def update_kernel(parts, sh_ref, sl_ref, d_ref, z_ref, *refs):
    states, outs = refs[:parts], refs[parts:]
    z = z_ref[...]
    shift = shift_of(z, d_ref)
    s, zs = (sh_ref[...], sl_ref[...]), split(z)
    start = 0
    for state, out in zip(states, outs):
        out[...] = updated(state[...], start, s, shift, zs)
        start += state.shape[0]


def last_kernel(parts, n_ref, sh_ref, sl_ref, d_ref, g_ref, x_ref, *refs):
    states, outs, z_ref = refs[:parts], refs[parts : 2 * parts], refs[2 * parts]
    fields = [state[...] for state in states]
    s = (sh_ref[...], sl_ref[...])
    solve(n_ref, s, g_ref, x_ref, fields, z_ref)
    z = z_ref[...]
    shift = shift_of(z, d_ref)
    zs = split(z)
    start = 0
    for field, out in zip(fields, outs):
        out[...] = updated(field, start, s, shift, zs)
        start += field.shape[0]


def join_kernel(place_ref, own_ref, other_ref, out_ref):
    own, other = own_ref[...], other_ref[...]
    column = place_ref[1]
    out_ref[:, 0, :] = jnp.where(column == 0, own, other)
    out_ref[:, 1, :] = jnp.where(column == 0, other, own)


def factor(pieces, batch, members, ids, mult, values, var, sources):
    per_patch = values.shape[2]
    n = len(pieces) * per_patch
    outs = [
        ((n, members), BF16, VMEM),
        ((n, members), BF16, VMEM),
        ((n, 128), F32, VMEM),
        ((n, n), F32, VMEM),
        ((n, n), F32, VMEM),
        ((1,), jnp.int32, SMEM),
    ]
    scratch = [
        pltpu.VMEM((128, 128), F32),
        pltpu.VMEM((2, n, 2 * n), BF16),
        pltpu.VMEM((2, n, 2 * n), BF16),
    ]
    kernel = functools.partial(factor_kernel, pieces, batch, members)
    args = [ids, mult, values, var, *sources]
    flops = 6 * n * n * members + 60 * n * n * n
    return call(kernel, outs, [SMEM, SMEM] + [VMEM] * (2 + len(sources)), args, scratch, flops)


def gain(batch, place, cells, factored, states):
    sh, sl, d, g, x, steps = factored
    n, members = sh.shape
    kernel = functools.partial(gain_kernel, batch, len(states))
    outs = [((n, states[0].shape[1]), F32, VMEM), ((cells.shape[2], members), F32, VMEM)]
    ins = [SMEM, SMEM] + [VMEM] * (6 + len(states))
    args = [place, steps, cells, sh, sl, d, g, x, *states]
    flops = 8 * n * members * states[0].shape[1]
    return call(kernel, outs, ins, args, [pltpu.VMEM((8, 128), jnp.int32)], flops)


def update(factored, z, states):
    sh, sl, d = factored[:3]
    kernel = functools.partial(update_kernel, len(states))
    outs = [(state.shape, F32, VMEM) for state in states]
    flops = 6 * sh.shape[0] * sh.shape[1] * z.shape[1]
    return call(kernel, outs, [VMEM] * (4 + len(states)), [sh, sl, d, z, *states], (), flops)


def last(factored, states):
    sh, sl, d, g, x, steps = factored
    kernel = functools.partial(last_kernel, len(states))
    n, width = sh.shape[0], states[0].shape[1]
    outs = [(state.shape, F32, VMEM) for state in states]
    args = [steps, sh, sl, d, g, x, *states]
    flops = 12 * sh.shape[0] * sh.shape[1] * width
    ins = [SMEM] + [VMEM] * (5 + len(states))
    return call(kernel, outs, ins, args, [pltpu.VMEM((n, width), F32)], flops)


def rings(size):
    up = [(i, (i + 1) % size) for i in range(size)]
    return up, [(j, i) for i, j in up]


def multipliers(ids, own, links):
    order = jnp.arange(links.shape[0], dtype=F32) + 2.0
    listed = jnp.sum(jnp.where(ids[:, None] == links[None, :], order[None, :], 0.0), axis=1)
    return jnp.where(ids == own, 1.0, listed)


def paired(state, neighbours, obs_cell, obs_values, obs_var):
    half, _, cells = state.shape
    members = 2 * half
    regions = lax.axis_size("region")
    region, column = lax.axis_index("region"), lax.axis_index("member")
    up, down = rings(regions)
    swap = [(0, 1), (1, 0)]
    own = region * 2 + column
    place = jnp.stack([region * 2, column, own]).astype(jnp.int32)
    links = lax.dynamic_index_in_dim(neighbours, own, 0, keepdims=False)
    before, after = (region + regions - 1) % regions, (region + 1) % regions
    around = jnp.stack([region, before, after])
    ids_first = (around[:, None] * 2 + jnp.arange(2)[None, :]).reshape(-1).astype(jnp.int32)
    within = jnp.stack([column, 1 - column])
    ids_next = (around[:, None] * 2 + within[None, :]).reshape(-1).astype(jnp.int32)

    outs = [
        ((2, obs_cell.shape[2], half), F32, VMEM),
        ((half, cells), F32, VMEM),
        ((half, cells), F32, VMEM),
    ]
    rows, keep, send = call(
        pick_kernel,
        outs,
        [SMEM, VMEM, VMEM],
        [place, obs_cell, state],
        [pltpu.VMEM((8, 128), jnp.int32)],
    )
    other = lax.ppermute(rows, "member", swap)
    sources = [rows, lax.ppermute(rows, "region", up), lax.ppermute(rows, "region", down)]
    sources += [other, lax.ppermute(other, "region", up), lax.ppermute(other, "region", down)]
    states = [keep, lax.ppermute(send, "member", swap)]
    pieces = [[(i, (p,)), (3 + i, (p,))] for i in range(3) for p in range(2)]
    mult = multipliers(ids_first, own, links)
    factored = factor(pieces, 0, members, ids_first, mult, obs_values, obs_var, sources)
    everything = slice(None)
    low, high = (everything, slice(0, half)), (everything, slice(half, members))
    for batch in range(1, NBATCH):
        z, rows = gain(batch, place, obs_cell, factored, states)
        other = lax.ppermute(rows, "member", swap)
        sources = [rows, lax.ppermute(rows, "region", up), lax.ppermute(rows, "region", down)]
        sources += [other, lax.ppermute(other, "region", up), lax.ppermute(other, "region", down)]
        states = update(factored, z, states)
        pieces = []
        for i in range(3):
            pieces += [[(i, low), (i, high)], [(3 + i, high), (3 + i, low)]]
        mult = multipliers(ids_next, own, links)
        factored = factor(pieces, batch, members, ids_next, mult, obs_values, obs_var, sources)
    mine, theirs = last(factored, states)
    back = lax.ppermute(theirs, "member", swap)
    (joined,) = call(join_kernel, [(state.shape, F32, VMEM)], [SMEM, VMEM, VMEM], [place, mine, back])
    return joined


def general(state, neighbours, obs_cell, obs_values, obs_var):
    ensemble = lax.all_to_all(state, "member", split_axis=1, concat_axis=0, tiled=True)
    members, owned, cells = ensemble.shape
    regions = lax.axis_size("region")
    region_patches = owned * lax.axis_size("member")
    region = lax.axis_index("region")
    first = region * region_patches + lax.axis_index("member") * owned
    up, down = rings(regions)
    fields = [ensemble[:, p, :] for p in range(owned)]
    grid = jnp.arange(cells, dtype=jnp.int32)
    for batch in range(NBATCH):
        picks = lax.dynamic_slice_in_dim(obs_cell, first, owned, 0)[:, batch, :]
        hot = (picks[:, :, None] == grid[None, None, :]).astype(F32)
        own_rows = jnp.einsum("poc,pkc->pok", hot, jnp.stack(fields), precision=HIGHEST)
        region_rows = lax.all_gather(own_rows, "member", axis=0, tiled=True)
        before = lax.ppermute(region_rows, "region", up)
        after = lax.ppermute(region_rows, "region", down)
        beside = jnp.concatenate([before, region_rows, after], axis=0)
        new = []
        for p in range(owned):
            own = first + p
            links = lax.dynamic_index_in_dim(neighbours, own, 0, keepdims=False)
            ids = jnp.concatenate([own[None], links]).astype(jnp.int32)
            home = (ids // region_patches - region + 1) % regions
            rows = jnp.take(beside, home * region_patches + ids % region_patches, axis=0)
            mult = multipliers(ids, own, links)
            pieces = [[(0, (i,))] for i in range(ids.shape[0])]
            factored = factor(pieces, batch, members, ids, mult, obs_values, obs_var, [rows])
            new += last(factored, [fields[p]])
        fields = new
    ensemble = jnp.stack(fields, axis=1)
    return lax.all_to_all(ensemble, "member", split_axis=0, concat_axis=1, tiled=True)


def on_device(state, neighbours, obs_cell, obs_values, obs_var):
    patches, links = state.shape[1], neighbours.shape[1]
    if patches == 2 and lax.axis_size("member") == 2 and links + 1 == 3 * patches:
        return paired(state, neighbours, obs_cell, obs_values, obs_var)
    return general(state, neighbours, obs_cell, obs_values, obs_var)


def solution(mesh):
    in_specs = (P("member", "region", None), P(), P(), P(), P())
    out_specs = P("member", "region", None)
    return jax.shard_map(
        on_device, mesh=mesh, in_specs=in_specs, out_specs=out_specs, check_vma=False
    )
```

```python
import functools
import math

import jax
import jax.numpy as jnp
from jax import lax
from jax.experimental import pallas as pl
from jax.experimental.pallas import tpu as pltpu
from jax.sharding import PartitionSpec as P

NBATCH = 2
HIGHEST = lax.Precision.HIGHEST
F32 = jnp.float32
BF16 = jnp.bfloat16
VMEM = pl.BlockSpec(memory_space=pltpu.VMEM)
SMEM = pl.BlockSpec(memory_space=pltpu.SMEM)
NN = (((1,), (0,)), ((), ()))
NT = (((1,), (1,)), ((), ()))
TN = (((0,), (0,)), ((), ()))
RESIDUAL = 1e-3
MOST_STEPS = 15


def call(kernel, outs, ins, args, scratch=(), flops=0):
    shapes = [jax.ShapeDtypeStruct(shape, dtype) for shape, dtype, _ in outs]
    moved = sum(math.prod(s.shape) * s.dtype.itemsize for s in shapes)
    moved += sum(a.size * a.dtype.itemsize for a in args)
    return pl.pallas_call(
        kernel,
        out_shape=shapes,
        in_specs=ins,
        out_specs=[space for _, _, space in outs],
        scratch_shapes=list(scratch),
        compiler_params=pltpu.CompilerParams(vmem_limit_bytes=48 * 1024 * 1024),
        cost_estimate=pl.CostEstimate(flops=flops, bytes_accessed=moved, transcendentals=0),
    )(*args)


def split(x):
    high = x.astype(BF16)
    return high, (x - high.astype(F32)).astype(BF16)


def dot(a, b, dims=NN):
    return lax.dot_general(a, b, dims, preferred_element_type=F32)


def dot3(a, b, dims=NN):
    (left,), (right,) = dims[0]
    lhs = jnp.concatenate([a[0], a[0], a[1]], axis=left)
    rhs = jnp.concatenate([b[0], b[1], b[0]], axis=right)
    return dot(lhs, rhs, dims)


def select(hot, parts, dims):
    (left,), (right,) = dims[0]
    hot = hot.astype(BF16)
    lhs = jnp.concatenate([hot] * len(parts), axis=left)
    return dot(lhs, jnp.concatenate(parts, axis=right), dims)


def split_all(x):
    high, middle = split(x)
    low = x - high.astype(F32) - middle.astype(F32)
    return high, middle, low.astype(BF16)


def step_limits():
    limits = []
    for steps in range(MOST_STEPS):
        rho = RESIDUAL
        for _ in range(steps):
            rho = math.sqrt(2.0 * rho / (1.0 + rho))
        limits.append(2.0 * rho / (1.0 - rho) if rho < 1.0 else math.inf)
    return limits


def diagonal(n, columns, first):
    row = lax.broadcasted_iota(jnp.int32, (n, columns), 0)
    column = lax.broadcasted_iota(jnp.int32, (n, columns), 1)
    return row + first == column


def selector(cells_ref, patch, batch, cells, scratch):
    per_patch = cells_ref.shape[2]
    scratch[...] = jnp.full_like(scratch, -1)
    scratch[0:1, 0:per_patch] = cells_ref[pl.ds(patch, 1), batch, :]
    picks = scratch[0:1, :]
    grid = lax.broadcasted_iota(jnp.int32, (cells, picks.shape[1]), 0)
    hot = (grid == picks).astype(F32)
    return jnp.transpose(hot)[0:per_patch, :]


def pick_kernel(place_ref, cells_ref, state_ref, rows_ref, scratch):
    patches, cells = state_ref.shape[1:]
    for p in range(patches):
        hot = selector(cells_ref, place_ref[0] + p, 0, cells, scratch)
        rows_ref[p] = select(hot, split_all(state_ref[:, p, :]), NT)


def sort_kernel(place_ref, state_ref, *refs):
    same_ref, cross_ref = refs[-2:]
    column = place_ref[1]
    first, second = state_ref[:, 0, :], state_ref[:, 1, :]
    same_ref[...] = jnp.where(column == 0, first, second)
    cross_ref[...] = jnp.where(column == 0, second, first)


def factor_kernel(pieces, batch, members, ids_ref, near_ref, values_ref, var_ref, *refs):
    count = len(refs) - 10
    sources = refs[:count]
    sh_ref, sl_ref, d_ref, g_ref, xh_ref, xl_ref, n_ref, flat, wide, w = refs[count:]
    per_patch = values_ref.shape[2]
    flat[...] = jnp.ones_like(flat)
    blocks = len(pieces)
    own = ids_ref[blocks]
    turn = ids_ref[blocks + 1]
    for i in range(blocks):
        patch = ids_ref[i]
        widening = (patch == own).astype(jnp.int32)
        for j in range(near_ref.shape[1]):
            widening = widening + (near_ref[own, j] == patch).astype(jnp.int32) * (j + 2)
        flat[i : i + 1, 0:per_patch] = values_ref[pl.ds(patch, 1), batch, :]
        noise = var_ref[pl.ds(patch, 1), batch, :] * widening.astype(F32)
        flat[blocks + i : blocks + i + 1, 0:per_patch] = noise
    upright = jnp.transpose(flat[...])
    for i, halves in enumerate(pieces):
        rows = [sources[which][index] for which, index, _ in halves]
        total = sum(jnp.sum(part, axis=1, keepdims=True) for part in rows)
        mean = total * (1.0 / members)
        noise = upright[0:per_patch, blocks + i : blocks + i + 1]
        scale = lax.rsqrt(noise * (members - 1.0))
        at = slice(i * per_patch, (i + 1) * per_patch)
        for part, (_, _, start) in zip(rows, halves):
            size = part.shape[1]
            high, low = split((part - mean) * scale)
            if start is None:
                lanes = slice(0, size)
            elif start < 2:
                lanes = slice(start * size, (start + 1) * size)
            else:
                offset = (turn if start == 2 else 1 - turn) * size
                lanes = pl.ds(pl.multiple_of(offset, size), size)
            sh_ref[at, lanes] = high
            sl_ref[at, lanes] = low
        shift = (upright[0:per_patch, i : i + 1] - mean) * scale
        d_ref[at, :] = jnp.broadcast_to(shift, (per_patch, d_ref.shape[1]))
    s = (sh_ref[...], sl_ref[...])
    g = dot3(s, s, NT)
    g_ref[...] = g
    n = g.shape[0]
    square = jnp.sum(jnp.sum(g * g, axis=0, keepdims=True), axis=1, keepdims=True)
    norm = jnp.sqrt(square) * (1.0 + 1e-5)
    size = square[0, 0]
    limits = step_limits()
    steps = jnp.int32(4)
    for k in range(4, MOST_STEPS - 1):
        limit = min(limits[k] * (1.0 - 1e-4), 1e18)
        steps = steps + (size > limit * limit).astype(jnp.int32)
    n_ref[0] = (size > 1.6e7).astype(jnp.int32) + (size > 1e8).astype(jnp.int32)
    eye = diagonal(n, n, 0).astype(F32)
    first = 2.0 / (2.0 + norm)
    rho = norm * (0.5 * first)
    rho2 = rho * rho
    weight = 2.0 / (2.0 - rho2)
    r = (1.0 - first) * eye - first * g
    parts = split(r)
    wide[:, n : 2 * n] = (weight * first) * (eye + r)
    wide[:, 0:n] = weight * dot3(parts, parts) - (0.5 * rho2 * weight) * eye
    for i, part in enumerate(split(wide[...])):
        w[0, i] = part

    def step(k, rho2):
        now, then = lax.rem(k, 2), lax.rem(k + 1, 2)
        weight = 2.0 / (2.0 - rho2)
        keep = 0.5 * rho2 * weight
        parts = (w[now, 0, :, 0:n], w[now, 1, :, 0:n])
        product = weight * dot3(parts, (w[now, 0], w[now, 1]))
        high, low = split(product[:, 0:n] - keep * eye)
        w[then, 0, :, 0:n] = high
        w[then, 1, :, 0:n] = low
        x = weight * wide[:, n : 2 * n] + product[:, n : 2 * n]
        wide[:, n : 2 * n] = x
        high, low = split(x)
        w[then, 0, :, n : 2 * n] = high
        w[then, 1, :, n : 2 * n] = low
        return keep * keep

    rho2 = lax.fori_loop(0, steps - 2, step, rho2 * rho2 * (0.25 * weight * weight))
    now = lax.rem(steps - 2, 2)
    weight = 2.0 / (2.0 - rho2)
    parts = (w[now, 0, :, 0:n], w[now, 1, :, 0:n])
    product = dot3(parts, (w[now, 0, :, n : 2 * n], w[now, 1, :, n : 2 * n]))
    high, low = split(weight * (wide[:, n : 2 * n] + product))
    xh_ref[...] = high
    xl_ref[...] = low


def solve(n_ref, s, g_ref, x, fields, z_ref):
    members = sum(field.shape[0] for field in fields)
    mean = sum(jnp.sum(field, axis=0, keepdims=True) for field in fields) * (1.0 / members)
    pairs = [split(field - mean) for field in fields]
    anomaly = [jnp.concatenate(parts, axis=0) for parts in zip(*pairs)]
    cross = dot3(s, anomaly)
    z = dot3(x, split(cross))
    g = g_ref[...]
    left = cross - z - dot3(split(g), split(z))
    z_ref[...] = z + dot3(x, split(left))

    def refine(_, carry):
        z = z_ref[...]
        gz = lax.dot_general(g_ref[...], z, NN, precision=HIGHEST, preferred_element_type=F32)
        z_ref[...] = z + dot3(x, split(cross - z - gz))
        return carry

    lax.fori_loop(0, n_ref[0], refine, 0)
    return anomaly, mean


def gain_kernel(batch, parts, ids_ref, n_ref, cells_ref, sh_ref, sl_ref, d_ref, g_ref, xh_ref, xl_ref, *refs):
    states = refs[:parts]
    z_ref, rows_ref, scratch = refs[parts:]
    fields = [state[...] for state in states]
    s = (sh_ref[...], sl_ref[...])
    anomaly, mean = solve(n_ref, s, g_ref, (xh_ref[...], xl_ref[...]), fields, z_ref)
    hot = selector(cells_ref, ids_ref[ids_ref.shape[0] - 2], batch, mean.shape[1], scratch)
    zt = split(select(hot, split_all(z_ref[...]), NT))
    base = jnp.sum(hot * mean, axis=1, keepdims=True) + dot3(zt, split(d_ref[...]))[:, 0:1]
    rows_ref[...] = base + select(hot, anomaly, NT) - 0.5 * dot3(zt, s)


def updated(field, start, s, shift, z):
    size = field.shape[0]
    return field + shift - 0.5 * dot3([h[:, start : start + size] for h in s], z, TN)


def shift_of(z, d_ref):
    return jnp.sum(z * d_ref[:, 0:1], axis=0, keepdims=True)


def update_kernel(starts, sh_ref, sl_ref, d_ref, z_ref, *refs):
    states, outs = refs[: len(starts)], refs[len(starts) :]
    z = z_ref[...]
    shift = shift_of(z, d_ref)
    s, zs = (sh_ref[...], sl_ref[...]), split(z)
    for start, state, out in zip(starts, states, outs):
        out[...] = updated(state[...], start, s, shift, zs)


def last_kernel(parts, n_ref, sh_ref, sl_ref, d_ref, g_ref, xh_ref, xl_ref, *refs):
    states, (z_ref, out_ref) = refs[:parts], refs[parts:]
    fields = [state[...] for state in states]
    s = (sh_ref[...], sl_ref[...])
    solve(n_ref, s, g_ref, (xh_ref[...], xl_ref[...]), fields, z_ref)
    z = z_ref[...]
    start = sum(field.shape[0] for field in fields[:-1])
    out_ref[...] = updated(fields[-1], start, s, shift_of(z, d_ref), split(z))


def join_kernel(place_ref, same_ref, cross_ref, out_ref):
    same, cross = same_ref[...], cross_ref[...]
    column = place_ref[1]
    out_ref[:, 0, :] = jnp.where(column == 0, same, cross)
    out_ref[:, 1, :] = jnp.where(column == 0, cross, same)


def factor(pieces, batch, members, ids, neighbours, values, var, sources):
    per_patch = values.shape[2]
    n = len(pieces) * per_patch
    outs = [
        ((n, members), BF16, VMEM),
        ((n, members), BF16, VMEM),
        ((n, 128), F32, VMEM),
        ((n, n), F32, VMEM),
        ((n, n), BF16, VMEM),
        ((n, n), BF16, VMEM),
        ((1,), jnp.int32, SMEM),
    ]
    scratch = [
        pltpu.VMEM((128, 128), F32),
        pltpu.VMEM((n, 2 * n), F32),
        pltpu.VMEM((2, 2, n, 2 * n), BF16),
    ]
    kernel = functools.partial(factor_kernel, pieces, batch, members)
    args = [ids, neighbours, values, var, *sources]
    flops = 6 * n * n * members + 60 * n * n * n
    return call(kernel, outs, [SMEM, SMEM] + [VMEM] * (2 + len(sources)), args, scratch, flops)


def gain(batch, ids, cells, factored, states):
    sh, sl, d, g, xh, xl, more = factored
    n, members = sh.shape
    kernel = functools.partial(gain_kernel, batch, len(states))
    outs = [((n, states[0].shape[1]), F32, VMEM), ((cells.shape[2], members), F32, VMEM)]
    ins = [SMEM, SMEM] + [VMEM] * (7 + len(states))
    args = [ids, more, cells, sh, sl, d, g, xh, xl, *states]
    flops = 8 * n * members * states[0].shape[1]
    return call(kernel, outs, ins, args, [pltpu.VMEM((8, 128), jnp.int32)], flops)


def update(factored, z, states, starts):
    sh, sl, d = factored[:3]
    kernel = functools.partial(update_kernel, starts)
    outs = [(state.shape, F32, VMEM) for state in states]
    flops = 6 * sh.shape[0] * sh.shape[1] * z.shape[1]
    return call(kernel, outs, [VMEM] * (4 + len(states)), [sh, sl, d, z, *states], (), flops)


def last(factored, states):
    sh, sl, d, g, xh, xl, more = factored
    kernel = functools.partial(last_kernel, len(states))
    n, width = sh.shape[0], states[0].shape[1]
    outs = [((n, width), F32, VMEM), (states[-1].shape, F32, VMEM)]
    args = [more, sh, sl, d, g, xh, xl, *states]
    flops = 12 * sh.shape[0] * sh.shape[1] * width
    return call(kernel, outs, [SMEM] + [VMEM] * (6 + len(states)), args, (), flops)


def rings(size):
    up = [(i, (i + 1) % size) for i in range(size)]
    return up, [(j, i) for i, j in up]


BOTH = ("region", "member")


def permute(x, moves, regions):
    table = []
    for region in range(regions):
        for column in range(2):
            pair, parity, to = moves(region // 2, region % 2, column)
            pair %= regions // 2
            table.append((region * 2 + column, (pair * 2 + parity) * 2 + to))
    return lax.ppermute(x, BOTH, table)


def paired(state, neighbours, obs_cell, obs_values, obs_var):
    half, _, cells = state.shape
    members = 2 * half
    regions = lax.axis_size("region")
    region, column = lax.axis_index("region"), lax.axis_index("member")
    pair, parity = region // 2, region % 2
    side = (column + pair) % 2
    home, aside = 2 * pair + side, 2 * pair + 1 - side
    outer = (home + regions + 2 * side - 1) % regions
    own = home * 2 + parity
    turn = (column + parity) % 2
    place = jnp.stack([region * 2, column]).astype(jnp.int32)
    mate = 2 * pair + 1 - parity
    ids_first = [region * 2, region * 2 + 1, mate * 2, mate * 2 + 1, outer * 2, outer * 2 + 1]
    ids_next = [home * 2 + parity, home * 2 + 1 - parity, aside * 2 + parity]
    ids_next += [aside * 2 + 1 - parity, outer * 2 + parity, outer * 2 + 1 - parity]
    ids_first = jnp.stack(ids_first + [own, turn]).astype(jnp.int32)
    ids_next = jnp.stack(ids_next + [own, turn]).astype(jnp.int32)

    def across(x):
        return permute(x, lambda c, q, m: (c, q, 1 - m), regions)

    def beside(x):
        return permute(x, lambda c, q, m: (c, 1 - q, m), regions)

    (rows,) = call(
        pick_kernel,
        [((2, obs_cell.shape[2], half), F32, VMEM)],
        [SMEM, VMEM, VMEM],
        [place, obs_cell, state],
        [pltpu.VMEM((8, 128), jnp.int32)],
    )
    other = across(rows)
    out = permute(rows, lambda c, q, m: (c + 2 * q - 1, m, (q + c) % 2), regions)
    sources = [rows, other, beside(rows), beside(other), out, beside(out)]
    pieces = []
    for i, starts in enumerate([(2, 3), (2, 3), (0, 1)]):
        for p in range(2):
            pieces.append([(2 * i, (p,), starts[0]), (2 * i + 1, (p,), starts[1])])
    anywhere = pl.BlockSpec(memory_space=pl.ANY)
    same, cross = call(
        sort_kernel,
        [((half, cells), F32, VMEM)] * 2,
        [SMEM, VMEM, anywhere, anywhere],
        [place, state, other, out],
    )
    states = [
        permute(same, lambda c, q, m: (c, m, (q + c) % 2), regions),
        permute(cross, lambda c, q, m: (c, 1 - m, (q + c) % 2), regions),
    ]
    factored = factor(pieces, 0, members, ids_first, neighbours, obs_values, obs_var, sources)
    everything = slice(None)
    low, high = (everything, slice(0, half)), (everything, slice(half, members))
    straight = [[(i, low, 0), (i, high, 1)] for i in range(6)]
    turned = [[(i, high, 0), (i, low, 1)] for i in range(6)]
    pieces = [(turned if i % 2 else straight)[i] for i in range(6)]
    for batch in range(1, NBATCH):
        z, rows = gain(batch, ids_next, obs_cell, factored, states)
        other = across(rows)
        out = permute(rows, lambda c, q, m: (c + 2 * ((m + c) % 2) - 1, q, m), regions)
        sources = [rows, beside(rows), other, beside(other), out, beside(out)]
        states = update(factored, z, states, (0, half))
        factored = factor(pieces, batch, members, ids_next, neighbours, obs_values, obs_var, sources)
    z, cross = last(factored, states)
    cross = permute(cross, lambda c, q, m: (c, (m + c) % 2, 1 - q), regions)
    (same,) = update(factored, z, states[:1], (0,))
    same = permute(same, lambda c, q, m: (c, (m + c) % 2, q), regions)
    (joined,) = call(join_kernel, [(state.shape, F32, VMEM)], [SMEM, VMEM, VMEM], [place, same, cross])
    return joined


def general(state, neighbours, obs_cell, obs_values, obs_var):
    ensemble = lax.all_to_all(state, "member", split_axis=1, concat_axis=0, tiled=True)
    members, owned, cells = ensemble.shape
    regions = lax.axis_size("region")
    region_patches = owned * lax.axis_size("member")
    region = lax.axis_index("region")
    first = region * region_patches + lax.axis_index("member") * owned
    up, down = rings(regions)
    fields = [ensemble[:, p, :] for p in range(owned)]
    grid = jnp.arange(cells, dtype=jnp.int32)
    for batch in range(NBATCH):
        picks = lax.dynamic_slice_in_dim(obs_cell, first, owned, 0)[:, batch, :]
        hot = (picks[:, :, None] == grid[None, None, :]).astype(F32)
        own_rows = jnp.einsum("poc,pkc->pok", hot, jnp.stack(fields), precision=HIGHEST)
        region_rows = lax.all_gather(own_rows, "member", axis=0, tiled=True)
        before = lax.ppermute(region_rows, "region", up)
        after = lax.ppermute(region_rows, "region", down)
        beside = jnp.concatenate([before, region_rows, after], axis=0)
        new = []
        for p in range(owned):
            own = first + p
            links = lax.dynamic_index_in_dim(neighbours, own, 0, keepdims=False)
            ids = jnp.concatenate([own[None], links]).astype(jnp.int32)
            table = jnp.concatenate([ids, own[None], jnp.zeros_like(own)[None]]).astype(jnp.int32)
            home = (ids // region_patches - region + 1) % regions
            rows = jnp.take(beside, home * region_patches + ids % region_patches, axis=0)
            pieces = [[(0, (i,), None)] for i in range(ids.shape[0])]
            factored = factor(pieces, batch, members, table, neighbours, obs_values, obs_var, [rows])
            new.append(last(factored, [fields[p]])[1])
        fields = new
    ensemble = jnp.stack(fields, axis=1)
    return lax.all_to_all(ensemble, "member", split_axis=0, concat_axis=1, tiled=True)


def on_device(state, neighbours, obs_cell, obs_values, obs_var):
    patches, links = state.shape[1], neighbours.shape[1]
    even = lax.axis_size("region") % 4 == 0
    if even and patches == 2 and lax.axis_size("member") == 2 and links + 1 == 3 * patches:
        return paired(state, neighbours, obs_cell, obs_values, obs_var)
    return general(state, neighbours, obs_cell, obs_values, obs_var)


def solution(mesh):
    in_specs = (P("member", "region", None), P(), P(), P(), P())
    out_specs = P("member", "region", None)
    return jax.shard_map(
        on_device, mesh=mesh, in_specs=in_specs, out_specs=out_specs, check_vma=False
    )
```

```python
import functools
import math

import jax
import jax.numpy as jnp
from jax import lax
from jax.experimental import pallas as pl
from jax.experimental.pallas import tpu as pltpu
from jax.sharding import PartitionSpec as P

NBATCH = 2
HIGHEST = lax.Precision.HIGHEST
F32 = jnp.float32
BF16 = jnp.bfloat16
VMEM = pl.BlockSpec(memory_space=pltpu.VMEM)
SMEM = pl.BlockSpec(memory_space=pltpu.SMEM)
NN = (((1,), (0,)), ((), ()))
NT = (((1,), (1,)), ((), ()))
TN = (((0,), (0,)), ((), ()))
RESIDUAL = 1e-3
MOST_STEPS = 15


def call(kernel, outs, ins, args, scratch=(), flops=0):
    shapes = [jax.ShapeDtypeStruct(shape, dtype) for shape, dtype, _ in outs]
    moved = sum(math.prod(s.shape) * s.dtype.itemsize for s in shapes)
    moved += sum(a.size * a.dtype.itemsize for a in args)
    return pl.pallas_call(
        kernel,
        out_shape=shapes,
        in_specs=ins,
        out_specs=[space for _, _, space in outs],
        scratch_shapes=list(scratch),
        compiler_params=pltpu.CompilerParams(vmem_limit_bytes=48 * 1024 * 1024),
        cost_estimate=pl.CostEstimate(flops=flops, bytes_accessed=moved, transcendentals=0),
    )(*args)


def split(x):
    high = x.astype(BF16)
    return high, (x - high.astype(F32)).astype(BF16)


def dot(a, b, dims=NN):
    return lax.dot_general(a, b, dims, preferred_element_type=F32)


def dot3(a, b, dims=NN):
    (left,), (right,) = dims[0]
    lhs = jnp.concatenate([a[0], a[0], a[1]], axis=left)
    rhs = jnp.concatenate([b[0], b[1], b[0]], axis=right)
    return dot(lhs, rhs, dims)


def select(hot, parts, dims):
    (left,), (right,) = dims[0]
    hot = hot.astype(BF16)
    lhs = jnp.concatenate([hot] * len(parts), axis=left)
    return dot(lhs, jnp.concatenate(parts, axis=right), dims)


def split_all(x):
    high, middle = split(x)
    low = x - high.astype(F32) - middle.astype(F32)
    return high, middle, low.astype(BF16)


def step_limits():
    limits = []
    for steps in range(MOST_STEPS):
        rho = RESIDUAL
        for _ in range(steps):
            rho = math.sqrt(2.0 * rho / (1.0 + rho))
        limits.append(2.0 * rho / (1.0 - rho) if rho < 1.0 else math.inf)
    return limits


def diagonal(n, columns, first):
    row = lax.broadcasted_iota(jnp.int32, (n, columns), 0)
    column = lax.broadcasted_iota(jnp.int32, (n, columns), 1)
    return row + first == column


def selector(cells_ref, patch, batch, cells, scratch):
    per_patch = cells_ref.shape[2]
    scratch[...] = jnp.full_like(scratch, -1)
    scratch[0:1, 0:per_patch] = cells_ref[pl.ds(patch, 1), batch, :]
    picks = scratch[0:1, :]
    grid = lax.broadcasted_iota(jnp.int32, (cells, picks.shape[1]), 0)
    hot = (grid == picks).astype(F32)
    return jnp.transpose(hot)[0:per_patch, :]


def pick_kernel(place_ref, cells_ref, state_ref, rows_ref, scratch, field_ref):
    patches, cells = state_ref.shape[1:]
    for p in range(patches):
        field_ref[p] = state_ref[:, p, :]
        hot = selector(cells_ref, place_ref[0] + p, 0, cells, scratch)
        rows_ref[p] = select(hot, split_all(field_ref[p]), NT)


def sort_kernel(place_ref, state_ref, *refs):
    own_ref, mate_ref = refs[-2:]
    parity = place_ref[1]
    first, second = state_ref[:, 0, :], state_ref[:, 1, :]
    own_ref[...] = jnp.where(parity == 0, first, second)
    mate_ref[...] = jnp.where(parity == 0, second, first)


def choose_kernel(place_ref, own_ref, mate_ref, *refs):
    keep_ref, send_ref = refs[-2:]
    here = place_ref[2]
    keep_ref[...] = jnp.where(here == 1, own_ref[...], mate_ref[...])
    send_ref[...] = jnp.where(here == 1, mate_ref[...], own_ref[...])


def factor_kernel(pieces, batch, members, ids_ref, values_ref, var_ref, *refs):
    count = len(refs) - 12
    sources = refs[:count]
    sh_ref, sl_ref, d_ref, g_ref, xh_ref, xl_ref, n_ref, flat, eye_ref, x_ref, wa, wb = refs[count:]
    per_patch = values_ref.shape[2]
    flat[...] = jnp.ones_like(flat)
    blocks = len(pieces)
    own = ids_ref[blocks]
    turn = ids_ref[blocks + 1]
    for i in range(blocks):
        patch = ids_ref[i]
        widening = (patch == own).astype(jnp.int32)
        for j in range(ids_ref.shape[0] - blocks - 2):
            widening = widening + (ids_ref[blocks + 2 + j] == patch).astype(jnp.int32) * (j + 2)
        flat[i : i + 1, 0:per_patch] = values_ref[pl.ds(patch, 1), batch, :]
        noise = var_ref[pl.ds(patch, 1), batch, :] * widening.astype(F32)
        flat[blocks + i : blocks + i + 1, 0:per_patch] = noise
    upright = jnp.transpose(flat[...])
    for i, halves in enumerate(pieces):
        rows = [sources[which][index] for which, index, _ in halves]
        total = sum(jnp.sum(part, axis=1, keepdims=True) for part in rows)
        mean = total * (1.0 / members)
        noise = upright[0:per_patch, blocks + i : blocks + i + 1]
        scale = lax.rsqrt(noise * (members - 1.0))
        at = slice(i * per_patch, (i + 1) * per_patch)
        for part, (_, _, start) in zip(rows, halves):
            size = part.shape[1]
            high, low = split((part - mean) * scale)
            if start is None:
                lanes = slice(0, size)
            elif start < 2:
                lanes = slice(start * size, (start + 1) * size)
            else:
                offset = (turn if start == 2 else 1 - turn) * size
                lanes = pl.ds(pl.multiple_of(offset, size), size)
            sh_ref[at, lanes] = high
            sl_ref[at, lanes] = low
        shift = (upright[0:per_patch, i : i + 1] - mean) * scale
        d_ref[at, :] = jnp.broadcast_to(shift, (per_patch, d_ref.shape[1]))
    s = (sh_ref[...], sl_ref[...])
    g = dot3(s, s, NT)
    g_ref[...] = g
    n = g.shape[0]
    square = jnp.sum(jnp.sum(g * g, axis=0, keepdims=True), axis=1, keepdims=True)
    norm = jnp.sqrt(square) * (1.0 + 1e-5)
    size = square[0, 0]
    limits = step_limits()
    pairs = jnp.int32(0)
    for k in range(3, MOST_STEPS - 2, 2):
        limit = limits[k] * (1.0 - 1e-4)
        pairs = pairs + (size > limit * limit).astype(jnp.int32)
    n_ref[0] = (size > 1.6e7).astype(jnp.int32) + (size > 1e8).astype(jnp.int32)
    eye_ref[...] = diagonal(n, n, 0).astype(F32)
    eye = eye_ref[...]
    first = 2.0 / (2.0 + norm)
    rho = norm * (0.5 * first)
    rho2 = rho * rho
    weight = 2.0 / (2.0 - rho2)
    keep = 0.5 * rho2 * weight
    r = (1.0 - first) * eye - first * g
    parts = split(r)
    x = (weight * first) * (eye + r)
    x_ref[...] = x
    for i, part in enumerate(split(x)):
        wa[i, :, n : 2 * n] = part
    for i, part in enumerate(split(weight * dot3(parts, parts) - keep * eye)):
        wa[i, :, 0:n] = part

    def advance(source, target, rho2):
        weight = 2.0 / (2.0 - rho2)
        keep = 0.5 * rho2 * weight
        parts = (source[0, :, 0:n], source[1, :, 0:n])
        product = dot3(parts, (source[0], source[1]))
        for i, part in enumerate(split(weight * product[:, 0:n] - keep * eye_ref[...])):
            target[i, :, 0:n] = part
        x = weight * (x_ref[...] + product[:, n : 2 * n])
        x_ref[...] = x
        for i, part in enumerate(split(x)):
            target[i, :, n : 2 * n] = part
        return keep * keep

    rho2 = advance(wa, wb, keep * keep)

    def twice(_, rho2):
        return advance(wa, wb, advance(wb, wa, rho2))

    rho2 = lax.fori_loop(0, pairs, twice, rho2)
    weight = 2.0 / (2.0 - rho2)
    parts = (wb[0, :, 0:n], wb[1, :, 0:n])
    product = dot3(parts, (wb[0, :, n : 2 * n], wb[1, :, n : 2 * n]))
    high, low = split(weight * (x_ref[...] + product))
    xh_ref[...] = high
    xl_ref[...] = low


def solve(n_ref, s, g_ref, x, fields, z_ref):
    members = sum(field.shape[0] for field in fields)
    mean = sum(jnp.sum(field, axis=0, keepdims=True) for field in fields) * (1.0 / members)
    pairs = [split(field - mean) for field in fields]
    anomaly = [jnp.concatenate(parts, axis=0) for parts in zip(*pairs)]
    cross = dot3(s, anomaly)
    z = dot3(x, split(cross))
    g = g_ref[...]
    left = cross - z - dot3(split(g), split(z))
    z_ref[...] = z + dot3(x, split(left))

    def refine(_, carry):
        z = z_ref[...]
        gz = lax.dot_general(g_ref[...], z, NN, precision=HIGHEST, preferred_element_type=F32)
        z_ref[...] = z + dot3(x, split(cross - z - gz))
        return carry

    lax.fori_loop(0, n_ref[0], refine, 0)
    return anomaly, mean


def gain_kernel(batch, parts, ids_ref, n_ref, cells_ref, sh_ref, sl_ref, d_ref, g_ref, xh_ref, xl_ref, *refs):
    states = refs[:parts]
    z_ref, rows_ref, scratch = refs[parts:]
    fields = [state[...] for state in states]
    s = (sh_ref[...], sl_ref[...])
    anomaly, mean = solve(n_ref, s, g_ref, (xh_ref[...], xl_ref[...]), fields, z_ref)
    blocks = s[0].shape[0] // cells_ref.shape[2]
    hot = selector(cells_ref, ids_ref[blocks], batch, mean.shape[1], scratch)
    zt = split(select(hot, split(z_ref[...]), NT))
    base = jnp.sum(hot * mean, axis=1, keepdims=True) + dot3(zt, split(d_ref[...]))[:, 0:1]
    rows_ref[...] = base + select(hot, anomaly, NT) - 0.5 * dot3(zt, s)


def updated(field, start, s, shift, z):
    size = field.shape[0]
    return field + shift - 0.5 * dot3([h[:, start : start + size] for h in s], z, TN)


def shift_of(z, d_ref):
    return jnp.sum(z * d_ref[:, 0:1], axis=0, keepdims=True)


def update_kernel(starts, sh_ref, sl_ref, d_ref, z_ref, *refs):
    states, outs = refs[: len(starts)], refs[len(starts) :]
    z = z_ref[...]
    shift = shift_of(z, d_ref)
    s, zs = (sh_ref[...], sl_ref[...]), split(z)
    for start, state, out in zip(starts, states, outs):
        out[...] = updated(state[...], start, s, shift, zs)


def last_kernel(parts, first, n_ref, sh_ref, sl_ref, d_ref, g_ref, xh_ref, xl_ref, *refs):
    states, (z_ref, out_ref) = refs[:parts], refs[parts:]
    fields = [state[...] for state in states]
    s = (sh_ref[...], sl_ref[...])
    solve(n_ref, s, g_ref, (xh_ref[...], xl_ref[...]), fields, z_ref)
    z = z_ref[...]
    start = sum(field.shape[0] for field in fields[:-1])
    out_ref[...] = updated(states[-1][0:first, :], start, s, shift_of(z, d_ref), split(z))


def rest_kernel(at, sh_ref, sl_ref, d_ref, z_ref, mine_ref, other_ref, out_ref, rest_ref):
    z = z_ref[...]
    shift = shift_of(z, d_ref)
    s, zs = (sh_ref[...], sl_ref[...]), split(z)
    half = mine_ref.shape[0]
    rest_ref[...] = updated(other_ref[at:, :], half + at, s, shift, zs)
    out_ref[...] = updated(mine_ref[...], 0, s, shift, zs)


def join_kernel(at, place_ref, mine_ref, theirs_ref, mate_ref, *refs):
    out_ref, both, sem = refs[-3:]
    count = both.shape[0]
    own = jnp.where(place_ref[2] == 1, mine_ref[at : at + count, :], theirs_ref[...])
    mate = mate_ref[...]
    parity = place_ref[1]
    both[:, 0, :] = jnp.where(parity == 0, own, mate)
    both[:, 1, :] = jnp.where(parity == 0, mate, own)
    copy = pltpu.make_async_copy(both, out_ref.at[pl.ds(at, count)], sem)
    copy.start()
    copy.wait()


def factor(pieces, batch, members, ids, values, var, sources):
    per_patch = values.shape[2]
    n = len(pieces) * per_patch
    outs = [
        ((n, members), BF16, VMEM),
        ((n, members), BF16, VMEM),
        ((n, 128), F32, VMEM),
        ((n, n), F32, VMEM),
        ((n, n), BF16, VMEM),
        ((n, n), BF16, VMEM),
        ((1,), jnp.int32, SMEM),
    ]
    scratch = [
        pltpu.VMEM((128, 128), F32),
        pltpu.VMEM((n, n), F32),
        pltpu.VMEM((n, n), F32),
        pltpu.VMEM((2, n, 2 * n), BF16),
        pltpu.VMEM((2, n, 2 * n), BF16),
    ]
    kernel = functools.partial(factor_kernel, pieces, batch, members)
    args = [ids, values, var, *sources]
    flops = 6 * n * n * members + 60 * n * n * n
    return call(kernel, outs, [SMEM] + [VMEM] * (2 + len(sources)), args, scratch, flops)


def gain(batch, ids, cells, factored, states):
    sh, sl, d, g, xh, xl, more = factored
    n, members = sh.shape
    kernel = functools.partial(gain_kernel, batch, len(states))
    outs = [((n, states[0].shape[1]), F32, VMEM), ((cells.shape[2], members), F32, VMEM)]
    ins = [SMEM, SMEM] + [VMEM] * (7 + len(states))
    args = [ids, more, cells, sh, sl, d, g, xh, xl, *states]
    flops = 8 * n * members * states[0].shape[1]
    return call(kernel, outs, ins, args, [pltpu.VMEM((8, 128), jnp.int32)], flops)


def update(factored, z, states, starts):
    sh, sl, d = factored[:3]
    kernel = functools.partial(update_kernel, starts)
    outs = [(state.shape, F32, VMEM) for state in states]
    flops = 6 * sh.shape[0] * sh.shape[1] * z.shape[1]
    return call(kernel, outs, [VMEM] * (4 + len(states)), [sh, sl, d, z, *states], (), flops)


def last(factored, states, first):
    sh, sl, d, g, xh, xl, more = factored
    kernel = functools.partial(last_kernel, len(states), first)
    n, width = sh.shape[0], states[0].shape[1]
    outs = [((n, width), F32, VMEM), ((first, width), F32, VMEM)]
    args = [more, sh, sl, d, g, xh, xl, *states]
    flops = 12 * sh.shape[0] * sh.shape[1] * width
    return call(kernel, outs, [SMEM] + [VMEM] * (6 + len(states)), args, (), flops)


def rings(size):
    up = [(i, (i + 1) % size) for i in range(size)]
    return up, [(j, i) for i, j in up]


BOTH = ("region", "member")


def permute(x, moves, regions):
    table = []
    for region in range(regions):
        for column in range(2):
            pair, parity, to = moves(region // 2, region % 2, column)
            pair %= regions // 2
            table.append((region * 2 + column, (pair * 2 + parity) * 2 + to))
    return lax.ppermute(x, BOTH, table)


def paired(state, neighbours, obs_cell, obs_values, obs_var):
    half, _, cells = state.shape
    members = 2 * half
    regions = lax.axis_size("region")
    region, column = lax.axis_index("region"), lax.axis_index("member")
    pair, parity = region // 2, region % 2
    side = (column + pair) % 2
    home, aside = 2 * pair + side, 2 * pair + 1 - side
    outer = (home + regions + 2 * side - 1) % regions
    own = home * 2 + parity
    turn = (column + parity) % 2
    here = (side + parity + 1) % 2
    place = jnp.stack([region * 2, parity, here]).astype(jnp.int32)
    mate = 2 * pair + 1 - parity
    links = lax.dynamic_index_in_dim(neighbours, own, 0, keepdims=False)
    ids_first = [region * 2, region * 2 + 1, mate * 2, mate * 2 + 1, outer * 2, outer * 2 + 1]
    ids_next = [home * 2 + parity, home * 2 + 1 - parity, aside * 2 + parity]
    ids_next += [aside * 2 + 1 - parity, outer * 2 + parity, outer * 2 + 1 - parity]
    ids_first = jnp.concatenate([jnp.stack(ids_first + [own, turn]).astype(jnp.int32), links])
    ids_next = jnp.concatenate([jnp.stack(ids_next + [own, turn]).astype(jnp.int32), links])

    def across(x):
        return permute(x, lambda c, q, m: (c, q, 1 - m), regions)

    def beside(x):
        return permute(x, lambda c, q, m: (c, 1 - q, m), regions)

    (rows,) = call(
        pick_kernel,
        [((2, obs_cell.shape[2], half), F32, VMEM)],
        [SMEM, VMEM, VMEM],
        [place, obs_cell, state],
        [pltpu.VMEM((8, 128), jnp.int32), pltpu.VMEM((2, half, cells), F32)],
    )
    other = across(rows)
    out = permute(rows, lambda c, q, m: (c + 2 * q - 1, m, (q + c) % 2), regions)
    sources = [rows, other, beside(rows), beside(other), out, beside(out)]
    pieces = []
    for i, starts in enumerate([(0, 1), (0, 1), (2, 3)]):
        for p in range(2):
            pieces.append([(2 * i, (p,), starts[0]), (2 * i + 1, (p,), starts[1])])
    anywhere = pl.BlockSpec(memory_space=pl.ANY)
    shape = ((half, cells), F32, VMEM)
    first, second = call(sort_kernel, [shape] * 2, [SMEM, VMEM, anywhere], [place, state, rows])
    second = beside(second)
    ins = [SMEM, VMEM, VMEM, anywhere, anywhere]
    mine, theirs = call(choose_kernel, [shape] * 2, ins, [place, first, second, other, out])
    states = [mine, across(theirs)]
    factored = factor(pieces, 0, members, ids_first, obs_values, obs_var, sources)
    everything = slice(None)
    low, high = (everything, slice(0, half)), (everything, slice(half, members))
    straight = [[(i, low, 0), (i, high, 1)] for i in range(6)]
    turned = [[(i, high, 0), (i, low, 1)] for i in range(6)]
    pieces = straight[0:2] + turned[2:4] + straight[4:6]
    for batch in range(1, NBATCH):
        z, rows = gain(batch, ids_next, obs_cell, factored, states)
        other = across(rows)
        out = permute(rows, lambda c, q, m: (c + 2 * ((m + c) % 2) - 1, q, m), regions)
        sources = [rows, beside(rows), other, beside(other), out, beside(out)]
        states = update(factored, z, states, (0, half))
        factored = factor(pieces, batch, members, ids_next, obs_values, obs_var, sources)
    size = half // 2
    z, lead = last(factored, states, size)
    lead = across(lead)
    outs = [shape, ((half - size, cells), F32, VMEM)]
    sh, sl, d = factored[:3]
    flops = 9 * sh.shape[0] * half * cells
    mine, rest = call(
        functools.partial(rest_kernel, size), outs, [VMEM] * 6, [sh, sl, d, z, *states], (), flops
    )
    rest = across(rest)
    joined = None
    for at, theirs in ((0, lead), (size, rest)):
        count = theirs.shape[0]
        mate = beside(jnp.where(here == 1, theirs, lax.slice_in_dim(mine, at, at + count)))
        args = [place, mine, theirs, mate] + ([] if joined is None else [joined])
        (joined,) = pl.pallas_call(
            functools.partial(join_kernel, at),
            out_shape=[jax.ShapeDtypeStruct(state.shape, F32)],
            in_specs=[SMEM, VMEM, VMEM, VMEM] + [anywhere] * (len(args) - 4),
            out_specs=[anywhere],
            scratch_shapes=[pltpu.VMEM((count, 2, cells), F32), pltpu.SemaphoreType.DMA],
            input_output_aliases={4: 0} if len(args) > 4 else {},
            compiler_params=pltpu.CompilerParams(vmem_limit_bytes=48 * 1024 * 1024),
        )(*args)
    return joined


def general(state, neighbours, obs_cell, obs_values, obs_var):
    ensemble = lax.all_to_all(state, "member", split_axis=1, concat_axis=0, tiled=True)
    members, owned, cells = ensemble.shape
    regions = lax.axis_size("region")
    region_patches = owned * lax.axis_size("member")
    region = lax.axis_index("region")
    first = region * region_patches + lax.axis_index("member") * owned
    up, down = rings(regions)
    fields = [ensemble[:, p, :] for p in range(owned)]
    grid = jnp.arange(cells, dtype=jnp.int32)
    for batch in range(NBATCH):
        picks = lax.dynamic_slice_in_dim(obs_cell, first, owned, 0)[:, batch, :]
        hot = (picks[:, :, None] == grid[None, None, :]).astype(F32)
        own_rows = jnp.einsum("poc,pkc->pok", hot, jnp.stack(fields), precision=HIGHEST)
        region_rows = lax.all_gather(own_rows, "member", axis=0, tiled=True)
        before = lax.ppermute(region_rows, "region", up)
        after = lax.ppermute(region_rows, "region", down)
        beside = jnp.concatenate([before, region_rows, after], axis=0)
        new = []
        for p in range(owned):
            own = first + p
            links = lax.dynamic_index_in_dim(neighbours, own, 0, keepdims=False)
            ids = jnp.concatenate([own[None], links]).astype(jnp.int32)
            table = jnp.concatenate([ids, jnp.stack([own, jnp.zeros_like(own)]), links])
            table = table.astype(jnp.int32)
            home = (ids // region_patches - region + 1) % regions
            rows = jnp.take(beside, home * region_patches + ids % region_patches, axis=0)
            pieces = [[(0, (i,), None)] for i in range(ids.shape[0])]
            factored = factor(pieces, batch, members, table, obs_values, obs_var, [rows])
            new.append(last(factored, [fields[p]], members)[1])
        fields = new
    ensemble = jnp.stack(fields, axis=1)
    return lax.all_to_all(ensemble, "member", split_axis=0, concat_axis=1, tiled=True)


def on_device(state, neighbours, obs_cell, obs_values, obs_var):
    patches, links = state.shape[1], neighbours.shape[1]
    even = lax.axis_size("region") % 4 == 0
    if even and patches == 2 and lax.axis_size("member") == 2 and links + 1 == 3 * patches:
        return paired(state, neighbours, obs_cell, obs_values, obs_var)
    return general(state, neighbours, obs_cell, obs_values, obs_var)


def solution(mesh):
    in_specs = (P("member", "region", None), P(), P(), P(), P())
    out_specs = P("member", "region", None)
    return jax.shard_map(
        on_device, mesh=mesh, in_specs=in_specs, out_specs=out_specs, check_vma=False
    )
```

```python
import functools
import math

import jax
import jax.numpy as jnp
from jax import lax
from jax.experimental import pallas as pl
from jax.experimental.pallas import tpu as pltpu
from jax.sharding import PartitionSpec as P

NBATCH = 2
HIGHEST = lax.Precision.HIGHEST
F32 = jnp.float32
BF16 = jnp.bfloat16
VMEM = pl.BlockSpec(memory_space=pltpu.VMEM)
SMEM = pl.BlockSpec(memory_space=pltpu.SMEM)
NN = (((1,), (0,)), ((), ()))
NT = (((1,), (1,)), ((), ()))
TN = (((0,), (0,)), ((), ()))
RESIDUAL = 1e-3
MOST_STEPS = 15
TILE = 256


def call(kernel, outs, ins, args, scratch=(), flops=0):
    shapes = [jax.ShapeDtypeStruct(shape, dtype) for shape, dtype, _ in outs]
    moved = sum(math.prod(s.shape) * s.dtype.itemsize for s in shapes)
    moved += sum(a.size * a.dtype.itemsize for a in args)
    return pl.pallas_call(
        kernel,
        out_shape=shapes,
        in_specs=ins,
        out_specs=[space for _, _, space in outs],
        scratch_shapes=list(scratch),
        compiler_params=pltpu.CompilerParams(vmem_limit_bytes=48 * 1024 * 1024),
        cost_estimate=pl.CostEstimate(flops=flops, bytes_accessed=moved, transcendentals=0),
    )(*args)


def split(x):
    high = x.astype(BF16)
    return high, (x - high.astype(F32)).astype(BF16)


def dot(a, b, dims=NN):
    return lax.dot_general(a, b, dims, preferred_element_type=F32)


def dot3(a, b, dims=NN):
    (left,), (right,) = dims[0]
    lhs = jnp.concatenate([a[0], a[0], a[1]], axis=left)
    rhs = jnp.concatenate([b[0], b[1], b[0]], axis=right)
    return dot(lhs, rhs, dims)


def select(hot, parts, dims):
    (left,), (right,) = dims[0]
    hot = hot.astype(BF16)
    lhs = jnp.concatenate([hot] * len(parts), axis=left)
    return dot(lhs, jnp.concatenate(parts, axis=right), dims)


def split_all(x):
    high, middle = split(x)
    low = x - high.astype(F32) - middle.astype(F32)
    return high, middle, low.astype(BF16)


def step_limits():
    limits = []
    for steps in range(MOST_STEPS):
        rho = RESIDUAL
        for _ in range(steps):
            rho = math.sqrt(2.0 * rho / (1.0 + rho))
        limits.append(2.0 * rho / (1.0 - rho) if rho < 1.0 else math.inf)
    return limits


def diagonal(n, columns, first):
    row = lax.broadcasted_iota(jnp.int32, (n, columns), 0)
    column = lax.broadcasted_iota(jnp.int32, (n, columns), 1)
    return row + first == column


def selector(picks, cells, scratch):
    per_patch = picks.shape[1]
    scratch[...] = jnp.full_like(scratch, -1)
    scratch[0:1, 0:per_patch] = picks
    grid = lax.broadcasted_iota(jnp.int32, (cells, scratch.shape[1]), 0)
    hot = (grid == scratch[0:1, :]).astype(F32)
    return jnp.transpose(hot)[0:per_patch, :]


def pick_kernel(picks_ref, state_ref, rows_ref, scratch, field_ref):
    patches, cells = state_ref.shape[1:]
    for p in range(patches):
        field_ref[p] = state_ref[:, p, :]
        hot = selector(picks_ref[p : p + 1, :], cells, scratch)
        rows_ref[p] = select(hot, split_all(field_ref[p]), NT)


def sort_kernel(place_ref, state_ref, *refs):
    keep_ref, send_ref = refs[-2:]
    column = place_ref[0]
    first, second = state_ref[:, 0, :], state_ref[:, 1, :]
    keep_ref[...] = jnp.where(column == 0, first, second)
    send_ref[...] = jnp.where(column == 0, second, first)


def factor_kernel(pieces, batch, members, ids_ref, values_ref, var_ref, *refs):
    count = len(refs) - 12
    sources = refs[:count]
    sh_ref, sl_ref, d_ref, g_ref, xh_ref, xl_ref, n_ref, flat, eye_ref, x_ref, wa, wb = refs[count:]
    per_patch = values_ref.shape[2]
    flat[...] = jnp.ones_like(flat)
    blocks = len(pieces)
    own = ids_ref[blocks]
    for i in range(blocks):
        patch = ids_ref[i]
        widening = (patch == own).astype(jnp.int32)
        for j in range(ids_ref.shape[0] - blocks - 1):
            widening = widening + (ids_ref[blocks + 1 + j] == patch).astype(jnp.int32) * (j + 2)
        flat[i : i + 1, 0:per_patch] = values_ref[pl.ds(patch, 1), batch, :]
        noise = var_ref[pl.ds(patch, 1), batch, :] * widening.astype(F32)
        flat[blocks + i : blocks + i + 1, 0:per_patch] = noise
    upright = jnp.transpose(flat[...])
    for i, halves in enumerate(pieces):
        rows = [sources[which][index] for which, index, _ in halves]
        total = sum(jnp.sum(part, axis=1, keepdims=True) for part in rows)
        mean = total * (1.0 / members)
        noise = upright[0:per_patch, blocks + i : blocks + i + 1]
        scale = lax.rsqrt(noise * (members - 1.0))
        at = slice(i * per_patch, (i + 1) * per_patch)
        for part, (_, _, start) in zip(rows, halves):
            size = part.shape[1]
            high, low = split((part - mean) * scale)
            lanes = slice(start * size, (start + 1) * size)
            sh_ref[at, lanes] = high
            sl_ref[at, lanes] = low
        shift = (upright[0:per_patch, i : i + 1] - mean) * scale
        d_ref[at, :] = jnp.broadcast_to(shift, (per_patch, d_ref.shape[1]))
    n = sh_ref.shape[0]
    head = min(TILE, n)
    s = (sh_ref[...], sl_ref[...])
    left = dot3(s, [part[0:head] for part in s], NT)
    g_ref[:, 0:head] = left
    if head < n:
        g_ref[0:head, head:n] = jnp.transpose(left[head:n])
        low = [part[head:n] for part in s]
        g_ref[head:n, head:n] = dot3(low, low, NT)
    g = g_ref[...]
    square = jnp.sum(jnp.sum(g * g, axis=0, keepdims=True), axis=1, keepdims=True)
    norm = jnp.sqrt(square) * (1.0 + 1e-5)
    size = square[0, 0]
    limits = step_limits()
    pairs = jnp.int32(0)
    for k in range(3, MOST_STEPS - 2, 2):
        limit = limits[k] * (1.0 - 1e-4)
        pairs = pairs + (size > limit * limit).astype(jnp.int32)
    n_ref[0] = (size > 1.6e7).astype(jnp.int32) + (size > 1e8).astype(jnp.int32)
    eye_ref[...] = diagonal(n, n, 0).astype(F32)
    eye = eye_ref[...]
    first = 2.0 / (2.0 + norm)
    rho = norm * (0.5 * first)
    rho2 = rho * rho
    weight = 2.0 / (2.0 - rho2)
    keep = 0.5 * rho2 * weight
    r = (1.0 - first) * eye - first * g
    parts = split(r)
    x = (weight * first) * (eye + r)
    x_ref[...] = x
    for i, part in enumerate(split(x)):
        wa[i, :, n : 2 * n] = part
    for i, part in enumerate(split(weight * dot3(parts, parts) - keep * eye)):
        wa[i, :, 0:n] = part

    def advance(source, target, rho2):
        weight = 2.0 / (2.0 - rho2)
        keep = 0.5 * rho2 * weight
        parts = (source[0, :, 0:n], source[1, :, 0:n])
        for start in range(0, 2 * n, TILE):
            stop = min(start + TILE, 2 * n)
            product = dot3(parts, (source[0, :, start:stop], source[1, :, start:stop]))
            cut = min(max(n - start, 0), stop - start)
            if cut > 0:
                r = weight * product[:, 0:cut] - keep * eye_ref[:, start : start + cut]
                for i, part in enumerate(split(r)):
                    target[i, :, start : start + cut] = part
            if cut < stop - start:
                at = slice(start + cut - n, stop - n)
                x = weight * (x_ref[:, at] + product[:, cut:])
                x_ref[:, at] = x
                for i, part in enumerate(split(x)):
                    target[i, :, start + cut : stop] = part
        return keep * keep

    rho2 = advance(wa, wb, keep * keep)

    def twice(_, rho2):
        return advance(wa, wb, advance(wb, wa, rho2))

    rho2 = lax.fori_loop(0, pairs, twice, rho2)
    weight = 2.0 / (2.0 - rho2)
    parts = (wb[0, :, 0:n], wb[1, :, 0:n])
    product = dot3(parts, (wb[0, :, n : 2 * n], wb[1, :, n : 2 * n]))
    high, low = split(weight * (x_ref[...] + product))
    xh_ref[...] = high
    xl_ref[...] = low


def solve(n_ref, s, g_ref, x, fields, z_ref):
    members = sum(field.shape[0] for field in fields)
    mean = sum(jnp.sum(field, axis=0, keepdims=True) for field in fields) * (1.0 / members)
    pairs = [split(field - mean) for field in fields]
    anomaly = [jnp.concatenate(parts, axis=0) for parts in zip(*pairs)]
    cross = dot3(s, anomaly)
    z = dot3(x, split(cross))
    g = g_ref[...]
    left = cross - z - dot3(split(g), split(z))
    z_ref[...] = z + dot3(x, split(left))

    def refine(_, carry):
        z = z_ref[...]
        gz = lax.dot_general(g_ref[...], z, NN, precision=HIGHEST, preferred_element_type=F32)
        z_ref[...] = z + dot3(x, split(cross - z - gz))
        return carry

    lax.fori_loop(0, n_ref[0], refine, 0)
    return anomaly, mean


def gain_kernel(parts, n_ref, picks_ref, sh_ref, sl_ref, d_ref, g_ref, xh_ref, xl_ref, *refs):
    states = refs[:parts]
    z_ref, rows_ref, scratch = refs[parts:]
    fields = [state[...] for state in states]
    s = (sh_ref[...], sl_ref[...])
    anomaly, mean = solve(n_ref, s, g_ref, (xh_ref[...], xl_ref[...]), fields, z_ref)
    hot = selector(picks_ref[...], mean.shape[1], scratch)
    zt = split(select(hot, split(z_ref[...]), NT))
    base = jnp.sum(hot * mean, axis=1, keepdims=True) + dot3(zt, split(d_ref[...]))[:, 0:1]
    rows_ref[...] = base + select(hot, anomaly, NT) - 0.5 * dot3(zt, s)


def updated(field, start, s, shift, z):
    size = field.shape[0]
    return field + shift - 0.5 * dot3([h[:, start : start + size] for h in s], z, TN)


def shift_of(z, d_ref):
    return jnp.sum(z * d_ref[:, 0:1], axis=0, keepdims=True)


def update_kernel(starts, sh_ref, sl_ref, d_ref, z_ref, *refs):
    states, outs = refs[: len(starts)], refs[len(starts) :]
    z = z_ref[...]
    shift = shift_of(z, d_ref)
    s, zs = (sh_ref[...], sl_ref[...]), split(z)
    for start, state, out in zip(starts, states, outs):
        out[...] = updated(state[...], start, s, shift, zs)


def last_kernel(parts, n_ref, sh_ref, sl_ref, d_ref, g_ref, xh_ref, xl_ref, *refs):
    states, (z_ref, out_ref) = refs[:parts], refs[parts:]
    fields = [state[...] for state in states]
    s = (sh_ref[...], sl_ref[...])
    solve(n_ref, s, g_ref, (xh_ref[...], xl_ref[...]), fields, z_ref)
    z = z_ref[...]
    start = sum(field.shape[0] for field in fields[:-1])
    out_ref[...] = updated(states[-1][...], start, s, shift_of(z, d_ref), split(z))


def join_kernel(place_ref, mine_ref, theirs_ref, out_ref, both, sems):
    chunks = sems.shape[0]
    size = both.shape[0] // chunks
    column = place_ref[0]
    copies = []
    for i in range(chunks):
        at = slice(i * size, (i + 1) * size)
        mine, theirs = mine_ref[at, :], theirs_ref[at, :]
        both[at, 0, :] = jnp.where(column == 0, mine, theirs)
        both[at, 1, :] = jnp.where(column == 0, theirs, mine)
        span = pl.ds(i * size, size)
        copies.append(pltpu.make_async_copy(both.at[span], out_ref.at[span], sems.at[i]))
        copies[-1].start()
    for copy in copies:
        copy.wait()


def factor(pieces, batch, members, ids, values, var, sources):
    per_patch = values.shape[2]
    n = len(pieces) * per_patch
    outs = [
        ((n, members), BF16, VMEM),
        ((n, members), BF16, VMEM),
        ((n, 128), F32, VMEM),
        ((n, n), F32, VMEM),
        ((n, n), BF16, VMEM),
        ((n, n), BF16, VMEM),
        ((1,), jnp.int32, SMEM),
    ]
    scratch = [
        pltpu.VMEM((128, 128), F32),
        pltpu.VMEM((n, n), F32),
        pltpu.VMEM((n, n), F32),
        pltpu.VMEM((2, n, 2 * n), BF16),
        pltpu.VMEM((2, n, 2 * n), BF16),
    ]
    kernel = functools.partial(factor_kernel, pieces, batch, members)
    args = [ids, values, var, *sources]
    flops = 6 * n * n * members + 60 * n * n * n
    return call(kernel, outs, [SMEM] + [VMEM] * (2 + len(sources)), args, scratch, flops)


def gain(picks, factored, states):
    sh, sl, d, g, xh, xl, more = factored
    n, members = sh.shape
    kernel = functools.partial(gain_kernel, len(states))
    outs = [((n, states[0].shape[1]), F32, VMEM), ((picks.shape[1], members), F32, VMEM)]
    ins = [SMEM] + [VMEM] * (7 + len(states))
    args = [more, picks, sh, sl, d, g, xh, xl, *states]
    flops = 8 * n * members * states[0].shape[1]
    return call(kernel, outs, ins, args, [pltpu.VMEM((8, 128), jnp.int32)], flops)


def update(factored, z, states, starts):
    sh, sl, d = factored[:3]
    kernel = functools.partial(update_kernel, starts)
    outs = [(state.shape, F32, VMEM) for state in states]
    flops = 6 * sh.shape[0] * sh.shape[1] * z.shape[1]
    return call(kernel, outs, [VMEM] * (4 + len(states)), [sh, sl, d, z, *states], (), flops)


def last(factored, states):
    sh, sl, d, g, xh, xl, more = factored
    kernel = functools.partial(last_kernel, len(states))
    n, width = sh.shape[0], states[0].shape[1]
    outs = [((n, width), F32, VMEM), (states[-1].shape, F32, VMEM)]
    args = [more, sh, sl, d, g, xh, xl, *states]
    flops = 12 * sh.shape[0] * sh.shape[1] * width
    return call(kernel, outs, [SMEM] + [VMEM] * (6 + len(states)), args, (), flops)


def rings(size):
    up = [(i, (i + 1) % size) for i in range(size)]
    return up, [(j, i) for i, j in up]


BOTH = ("region", "member")


def permute(x, moves, regions):
    table = []
    for region in range(regions):
        for column in range(2):
            pair, parity, to = moves(region // 2, region % 2, column)
            pair %= regions // 2
            table.append((region * 2 + column, (pair * 2 + parity) * 2 + to))
    return lax.ppermute(x, BOTH, table)


def paired(state, neighbours, obs_cell, obs_values, obs_var):
    half, _, cells = state.shape
    members = 2 * half
    regions = lax.axis_size("region")
    region, column = lax.axis_index("region"), lax.axis_index("member")
    parity = region % 2
    mate = region + 1 - 2 * parity
    outer = (region + regions + 2 * parity - 1) % regions
    own = region * 2 + column
    place = column.astype(jnp.int32)[None]
    links = lax.dynamic_index_in_dim(neighbours, own, 0, keepdims=False)
    around = (region, mate, outer)
    ids_first = [r * 2 + p for r in around for p in (0, 1)]
    ids_next = [r * 2 + p for r in around for p in (column, 1 - column)]
    ids_first = jnp.concatenate([jnp.stack(ids_first + [own]).astype(jnp.int32), links])
    ids_next = jnp.concatenate([jnp.stack(ids_next + [own]).astype(jnp.int32), links])

    def across(x):
        return permute(x, lambda c, q, m: (c, q, 1 - m), regions)

    def beside(x):
        return permute(x, lambda c, q, m: (c, 1 - q, m), regions)

    def outside(x):
        return permute(x, lambda c, q, m: (c + 2 * q - 1, 1 - q, m), regions)

    picks = lax.dynamic_slice_in_dim(obs_cell[:, 0, :], region * 2, 2, 0)
    (rows,) = call(
        pick_kernel,
        [((2, obs_cell.shape[2], half), F32, VMEM)],
        [VMEM, VMEM],
        [picks, state],
        [pltpu.VMEM((8, 128), jnp.int32), pltpu.VMEM((2, half, cells), F32)],
    )
    other = across(rows)
    sources = [rows, beside(rows), outside(rows), other, beside(other), outside(other)]
    pieces = [[(i, (p,), 0), (3 + i, (p,), 1)] for i in range(3) for p in range(2)]
    anywhere = pl.BlockSpec(memory_space=pl.ANY)
    shape = ((half, cells), F32, VMEM)
    keep, send = call(sort_kernel, [shape] * 2, [SMEM, VMEM, anywhere], [place, state, other])
    states = [keep, across(send)]
    factored = factor(pieces, 0, members, ids_first, obs_values, obs_var, sources)
    everything = slice(None)
    low, high = (everything, slice(0, half)), (everything, slice(half, members))
    pieces = []
    for i in range(3):
        pieces += [[(i, low, 0), (i, high, 1)], [(3 + i, high, 0), (3 + i, low, 1)]]
    for batch in range(1, NBATCH):
        picks = lax.dynamic_slice_in_dim(obs_cell[:, batch, :], own, 1, 0)
        z, rows = gain(picks, factored, states)
        other = across(rows)
        sources = [rows, beside(rows), outside(rows), other, beside(other), outside(other)]
        states = update(factored, z, states, (0, half))
        factored = factor(pieces, batch, members, ids_next, obs_values, obs_var, sources)
    z, theirs = last(factored, states)
    theirs = across(theirs)
    (mine,) = update(factored, z, states[:1], (0,))
    return pl.pallas_call(
        join_kernel,
        out_shape=jax.ShapeDtypeStruct(state.shape, F32),
        in_specs=[SMEM, VMEM, VMEM],
        out_specs=anywhere,
        scratch_shapes=[pltpu.VMEM(state.shape, F32), pltpu.SemaphoreType.DMA((4,))],
        compiler_params=pltpu.CompilerParams(vmem_limit_bytes=48 * 1024 * 1024),
    )(place, mine, theirs)


def general(state, neighbours, obs_cell, obs_values, obs_var):
    ensemble = lax.all_to_all(state, "member", split_axis=1, concat_axis=0, tiled=True)
    members, owned, cells = ensemble.shape
    regions = lax.axis_size("region")
    region_patches = owned * lax.axis_size("member")
    region = lax.axis_index("region")
    first = region * region_patches + lax.axis_index("member") * owned
    up, down = rings(regions)
    fields = [ensemble[:, p, :] for p in range(owned)]
    grid = jnp.arange(cells, dtype=jnp.int32)
    for batch in range(NBATCH):
        picks = lax.dynamic_slice_in_dim(obs_cell, first, owned, 0)[:, batch, :]
        hot = (picks[:, :, None] == grid[None, None, :]).astype(F32)
        own_rows = jnp.einsum("poc,pkc->pok", hot, jnp.stack(fields), precision=HIGHEST)
        region_rows = lax.all_gather(own_rows, "member", axis=0, tiled=True)
        before = lax.ppermute(region_rows, "region", up)
        after = lax.ppermute(region_rows, "region", down)
        beside = jnp.concatenate([before, region_rows, after], axis=0)
        new = []
        for p in range(owned):
            own = first + p
            links = lax.dynamic_index_in_dim(neighbours, own, 0, keepdims=False)
            ids = jnp.concatenate([own[None], links]).astype(jnp.int32)
            table = jnp.concatenate([ids, own[None], links]).astype(jnp.int32)
            home = (ids // region_patches - region + 1) % regions
            rows = jnp.take(beside, home * region_patches + ids % region_patches, axis=0)
            pieces = [[(0, (i,), 0)] for i in range(ids.shape[0])]
            factored = factor(pieces, batch, members, table, obs_values, obs_var, [rows])
            new.append(last(factored, [fields[p]])[1])
        fields = new
    ensemble = jnp.stack(fields, axis=1)
    return lax.all_to_all(ensemble, "member", split_axis=0, concat_axis=1, tiled=True)


def on_device(state, neighbours, obs_cell, obs_values, obs_var):
    patches, links = state.shape[1], neighbours.shape[1]
    even = lax.axis_size("region") % 2 == 0
    if even and patches == 2 and lax.axis_size("member") == 2 and links + 1 == 3 * patches:
        return paired(state, neighbours, obs_cell, obs_values, obs_var)
    return general(state, neighbours, obs_cell, obs_values, obs_var)


def solution(mesh):
    in_specs = (P("member", "region", None), P(), P(), P(), P())
    out_specs = P("member", "region", None)
    return jax.shard_map(
        on_device, mesh=mesh, in_specs=in_specs, out_specs=out_specs, check_vma=False
    )
```

```python
import functools
import math

import jax
import jax.numpy as jnp
from jax import lax
from jax.experimental import pallas as pl
from jax.experimental.pallas import tpu as pltpu
from jax.sharding import PartitionSpec as P

NBATCH = 2
HIGHEST = lax.Precision.HIGHEST
F32 = jnp.float32
BF16 = jnp.bfloat16
VMEM = pl.BlockSpec(memory_space=pltpu.VMEM)
SMEM = pl.BlockSpec(memory_space=pltpu.SMEM)
NN = (((1,), (0,)), ((), ()))
NT = (((1,), (1,)), ((), ()))
TN = (((0,), (0,)), ((), ()))
RESIDUAL = 1e-3
MOST_STEPS = 15
TILE = 256


def call(kernel, outs, ins, args, scratch=(), flops=0, limit=48):
    shapes = [jax.ShapeDtypeStruct(shape, dtype) for shape, dtype, _ in outs]
    moved = sum(math.prod(s.shape) * s.dtype.itemsize for s in shapes)
    moved += sum(a.size * a.dtype.itemsize for a in args)
    return pl.pallas_call(
        kernel,
        out_shape=shapes,
        in_specs=ins,
        out_specs=[space for _, _, space in outs],
        scratch_shapes=list(scratch),
        compiler_params=pltpu.CompilerParams(vmem_limit_bytes=limit * 1024 * 1024),
        cost_estimate=pl.CostEstimate(flops=flops, bytes_accessed=moved, transcendentals=0),
    )(*args)


def split(x):
    high = x.astype(BF16)
    return high, (x - high.astype(F32)).astype(BF16)


def dot(a, b, dims=NN):
    return lax.dot_general(a, b, dims, preferred_element_type=F32)


def dot3(a, b, dims=NN):
    (left,), (right,) = dims[0]
    lhs = jnp.concatenate([a[0], a[0], a[1]], axis=left)
    rhs = jnp.concatenate([b[0], b[1], b[0]], axis=right)
    return dot(lhs, rhs, dims)


def dot2(a, b, dims=NN):
    (left,), (right,) = dims[0]
    return dot(jnp.concatenate([a[0], a[0]], axis=left), jnp.concatenate(b, axis=right), dims)


def select(hot, parts, dims):
    (left,), (right,) = dims[0]
    hot = hot.astype(BF16)
    lhs = jnp.concatenate([hot] * len(parts), axis=left)
    return dot(lhs, jnp.concatenate(parts, axis=right), dims)


def split_all(x):
    high, middle = split(x)
    low = x - high.astype(F32) - middle.astype(F32)
    return high, middle, low.astype(BF16)


def step_limits():
    limits = []
    for steps in range(MOST_STEPS):
        rho = RESIDUAL
        for _ in range(steps):
            rho = math.sqrt(2.0 * rho / (1.0 + rho))
        limits.append(2.0 * rho / (1.0 - rho) if rho < 1.0 else math.inf)
    return limits


def diagonal(n, columns, first):
    row = lax.broadcasted_iota(jnp.int32, (n, columns), 0)
    column = lax.broadcasted_iota(jnp.int32, (n, columns), 1)
    return row + first == column


def selector(picks, cells, scratch):
    per_patch = picks.shape[1]
    scratch[...] = jnp.full_like(scratch, -1)
    scratch[0:1, 0:per_patch] = picks
    grid = lax.broadcasted_iota(jnp.int32, (cells, scratch.shape[1]), 0)
    hot = (grid == scratch[0:1, :]).astype(F32)
    return jnp.transpose(hot)[0:per_patch, :]


def pick_kernel(first_ref, cells_hbm, state_hbm, rows_ref, cells_ref, state_ref, scratch, field_ref, sems):
    members, patches, cells = state_ref.shape
    chunks = sems.shape[0] - 1
    size = members // chunks
    spans = [pl.ds(i * size, size) for i in range(chunks)]
    first = pltpu.make_async_copy(cells_hbm, cells_ref, sems.at[chunks])
    first.start()
    copies = []
    for i, span in enumerate(spans):
        copies.append(pltpu.make_async_copy(state_hbm.at[span], state_ref.at[span], sems.at[i]))
        copies[-1].start()
    first.wait()
    hots = [selector(cells_ref[pl.ds(first_ref[0] + p, 1), 0, :], cells, scratch) for p in range(patches)]
    for i, span in enumerate(spans):
        copies[i].wait()
        for p in range(patches):
            field_ref[p, span] = state_ref[span, p, :]
            rows_ref[p, :, i * size : (i + 1) * size] = select(hots[p], split_all(field_ref[p, span]), NT)


def sort_kernel(place_ref, values_hbm, var_hbm, state_ref, *refs):
    keep_ref, send_ref, values_ref, var_ref, sems = refs[-5:]
    copies = [
        pltpu.make_async_copy(values_hbm, values_ref, sems.at[0]),
        pltpu.make_async_copy(var_hbm, var_ref, sems.at[1]),
    ]
    for copy in copies:
        copy.start()
    column = place_ref[0]
    first, second = state_ref[:, 0, :], state_ref[:, 1, :]
    keep_ref[...] = jnp.where(column == 0, first, second)
    send_ref[...] = jnp.where(column == 0, second, first)
    for copy in copies:
        copy.wait()


def factor_kernel(pieces, batch, members, ids_ref, values_ref, var_ref, *refs):
    count = len(refs) - 12
    sources = refs[:count]
    sh_ref, sl_ref, d_ref, g_ref, xh_ref, xl_ref, n_ref, flat, eye_ref, x_ref, wa, wb = refs[count:]
    per_patch = values_ref.shape[2]
    flat[...] = jnp.ones_like(flat)
    blocks = len(pieces)
    own = ids_ref[blocks]
    for i in range(blocks):
        patch = ids_ref[i]
        widening = (patch == own).astype(jnp.int32)
        for j in range(ids_ref.shape[0] - blocks - 1):
            widening = widening + (ids_ref[blocks + 1 + j] == patch).astype(jnp.int32) * (j + 2)
        flat[i : i + 1, 0:per_patch] = values_ref[pl.ds(patch, 1), batch, :]
        noise = var_ref[pl.ds(patch, 1), batch, :] * widening.astype(F32)
        flat[blocks + i : blocks + i + 1, 0:per_patch] = noise
    upright = jnp.transpose(flat[...])
    for i, halves in enumerate(pieces):
        rows = [sources[which][index] for which, index, _ in halves]
        total = sum(jnp.sum(part, axis=1, keepdims=True) for part in rows)
        mean = total * (1.0 / members)
        noise = upright[0:per_patch, blocks + i : blocks + i + 1]
        scale = lax.rsqrt(noise * (members - 1.0))
        at = slice(i * per_patch, (i + 1) * per_patch)
        for part, (_, _, start) in zip(rows, halves):
            size = part.shape[1]
            high, low = split((part - mean) * scale)
            lanes = slice(start * size, (start + 1) * size)
            sh_ref[at, lanes] = high
            sl_ref[at, lanes] = low
        shift = (upright[0:per_patch, i : i + 1] - mean) * scale
        d_ref[at, :] = jnp.broadcast_to(shift, (per_patch, d_ref.shape[1]))
    n = sh_ref.shape[0]
    head = min(TILE, n)
    tail = n - head
    s = (sh_ref[...], sl_ref[...])
    left = dot3(s, [part[0:head] for part in s], NT)
    g_ref[:, 0:head] = left
    g_ref[0:head, head:n] = jnp.transpose(left[head:n])
    low = [part[head:n] for part in s]
    g_ref[head:n, head:n] = dot3(low, low, NT)
    g = g_ref[...]
    square = jnp.sum(jnp.sum(g * g, axis=0, keepdims=True), axis=1, keepdims=True)
    norm = jnp.sqrt(square) * (1.0 + 1e-5)
    size = square[0, 0]
    limits = step_limits()
    pairs = jnp.int32(0)
    for k in range(5, MOST_STEPS - 2, 2):
        limit = limits[k] * (1.0 - 1e-4)
        pairs = pairs + (size > limit * limit).astype(jnp.int32)
    n_ref[0] = (size > 1.6e7).astype(jnp.int32) + (size > 1e8).astype(jnp.int32)
    eye_ref[...] = diagonal(n, n, 0).astype(F32)
    eye = eye_ref[...]
    first = 2.0 / (2.0 + norm)
    rho = norm * (0.5 * first)
    rho2 = rho * rho
    weight = 2.0 / (2.0 - rho2)
    keep = 0.5 * rho2 * weight
    r = (1.0 - first) * eye - first * g
    parts = split(r)
    x = (weight * first) * (eye + r)
    x_ref[...] = x
    for i, part in enumerate(split(x)):
        wa[i, :, n : 2 * n] = part

    def store(targets, start, left, corner):
        blocks = [(slice(0, n), slice(start, start + head), left)]
        blocks.append((slice(head, n), slice(start + head, start + n), corner))
        blocks.append((slice(0, head), slice(start + head, start + n), jnp.transpose(left[head:n])))
        for rows, columns, block in blocks:
            for target, part in zip(targets, split(block)):
                target[rows, columns] = part

    def corner_of(weight, keep, left, corner):
        left = weight * left - keep * eye_ref[:, 0:head]
        return left, weight * corner - keep * eye_ref[head:n, head:n]

    left = dot3(parts, [part[:, 0:head] for part in parts])
    corner = dot3([part[head:n] for part in parts], [part[:, head:n] for part in parts])
    store((wa.at[0], wa.at[1]), 0, *corner_of(weight, keep, left, corner))

    def advance(source, target, rho2, exact):
        weight = 2.0 / (2.0 - rho2)
        keep = 0.5 * rho2 * weight
        parts = (source[0, :, 0:n], source[1, :, 0:n])
        ends = [jnp.concatenate([source[i, :, head:n], source[i, :, n + head : 2 * n]], axis=1) for i in (0, 1)]
        times = dot3 if exact else dot2
        left = times(parts, (source[0, :, 0:head], source[1, :, 0:head]))
        corners = times([part[head:n] for part in parts], ends)
        both = (target.at[0], target.at[1])
        store(both, 0, *corner_of(weight, keep, left, corners[:, 0:tail]))
        left = dot2(parts, (source[0, :, n : n + head], source[1, :, n : n + head]))
        left = weight * (x_ref[:, 0:head] + left)
        corner = weight * (x_ref[head:n, head:n] + corners[:, tail : 2 * tail])
        x_ref[:, 0:head] = left
        x_ref[head:n, head:n] = corner
        store(both, n, left, corner)
        return keep * keep

    rho2 = advance(wa, wb, keep * keep, True)

    def twice(_, rho2):
        return advance(wa, wb, advance(wb, wa, rho2, True), True)

    rho2 = lax.fori_loop(0, pairs, twice, rho2)
    rho2 = advance(wa, wb, advance(wb, wa, rho2, False), False)
    weight = 2.0 / (2.0 - rho2)
    parts = (wb[0, :, 0:n], wb[1, :, 0:n])
    left = dot2(parts, (wb[0, :, n : n + head], wb[1, :, n : n + head]))
    corner = dot2([part[head:n] for part in parts], (wb[0, :, n + head : 2 * n], wb[1, :, n + head : 2 * n]))
    left = weight * (x_ref[:, 0:head] + left)
    corner = weight * (x_ref[head:n, head:n] + corner)
    store((xh_ref, xl_ref), 0, left, corner)


def solve(n_ref, s, g_ref, x, fields, z_ref):
    members = sum(field.shape[0] for field in fields)
    mean = sum(jnp.sum(field, axis=0, keepdims=True) for field in fields) * (1.0 / members)
    pairs = [split(field - mean) for field in fields]
    anomaly = [jnp.concatenate(parts, axis=0) for parts in zip(*pairs)]
    cross = dot3(s, anomaly)
    z = dot3(x, split(cross))
    g = g_ref[...]
    left = cross - z - dot3(split(g), split(z))
    z_ref[...] = z + dot3(x, split(left))

    def refine(_, carry):
        z = z_ref[...]
        gz = lax.dot_general(g_ref[...], z, NN, precision=HIGHEST, preferred_element_type=F32)
        z_ref[...] = z + dot3(x, split(cross - z - gz))
        return carry

    lax.fori_loop(0, n_ref[0], refine, 0)
    return anomaly, mean


def gain_kernel(parts, n_ref, picks_ref, sh_ref, sl_ref, d_ref, g_ref, xh_ref, xl_ref, *refs):
    states = refs[:parts]
    z_ref, rows_ref, scratch = refs[parts:]
    fields = [state[...] for state in states]
    s = (sh_ref[...], sl_ref[...])
    anomaly, mean = solve(n_ref, s, g_ref, (xh_ref[...], xl_ref[...]), fields, z_ref)
    hot = selector(picks_ref[...], mean.shape[1], scratch)
    zt = split(select(hot, split(z_ref[...]), NT))
    base = jnp.sum(hot * mean, axis=1, keepdims=True) + dot3(zt, split(d_ref[...]))[:, 0:1]
    rows_ref[...] = base + select(hot, anomaly, NT) - 0.5 * dot3(zt, s)


def updated(field, start, s, shift, z):
    size = field.shape[0]
    return field + shift - 0.5 * dot3([h[:, start : start + size] for h in s], z, TN)


def shift_of(z, d_ref):
    return jnp.sum(z * d_ref[:, 0:1], axis=0, keepdims=True)


def update_kernel(starts, sh_ref, sl_ref, d_ref, z_ref, *refs):
    states, outs = refs[: len(starts)], refs[len(starts) :]
    z = z_ref[...]
    shift = shift_of(z, d_ref)
    s, zs = (sh_ref[...], sl_ref[...]), split(z)
    for start, state, out in zip(starts, states, outs):
        out[...] = updated(state[...], start, s, shift, zs)


def last_kernel(parts, n_ref, sh_ref, sl_ref, d_ref, g_ref, xh_ref, xl_ref, *refs):
    states, (z_ref, out_ref) = refs[:parts], refs[parts:]
    fields = [state[...] for state in states]
    s = (sh_ref[...], sl_ref[...])
    solve(n_ref, s, g_ref, (xh_ref[...], xl_ref[...]), fields, z_ref)
    z = z_ref[...]
    start = sum(field.shape[0] for field in fields[:-1])
    out_ref[...] = updated(states[-1][...], start, s, shift_of(z, d_ref), split(z))


def join_kernel(place_ref, mine_ref, theirs_ref, out_ref, both, sems):
    chunks = sems.shape[0]
    size = both.shape[0] // chunks
    column = place_ref[0]
    copies = []
    for i in range(chunks):
        at = slice(i * size, (i + 1) * size)
        mine, theirs = mine_ref[at, :], theirs_ref[at, :]
        both[at, 0, :] = jnp.where(column == 0, mine, theirs)
        both[at, 1, :] = jnp.where(column == 0, theirs, mine)
        span = pl.ds(i * size, size)
        copies.append(pltpu.make_async_copy(both.at[span], out_ref.at[span], sems.at[i]))
        copies[-1].start()
    for copy in copies:
        copy.wait()


def factor(pieces, batch, members, ids, values, var, sources):
    per_patch = values.shape[2]
    n = len(pieces) * per_patch
    outs = [
        ((n, members), BF16, VMEM),
        ((n, members), BF16, VMEM),
        ((n, 128), F32, VMEM),
        ((n, n), F32, VMEM),
        ((n, n), BF16, VMEM),
        ((n, n), BF16, VMEM),
        ((1,), jnp.int32, SMEM),
    ]
    scratch = [
        pltpu.VMEM((128, 128), F32),
        pltpu.VMEM((n, n), F32),
        pltpu.VMEM((n, n), F32),
        pltpu.VMEM((2, n, 2 * n), BF16),
        pltpu.VMEM((2, n, 2 * n), BF16),
    ]
    kernel = functools.partial(factor_kernel, pieces, batch, members)
    args = [ids, values, var, *sources]
    flops = 6 * n * n * members + 60 * n * n * n
    return call(kernel, outs, [SMEM] + [VMEM] * (2 + len(sources)), args, scratch, flops)


def gain(picks, factored, states):
    sh, sl, d, g, xh, xl, more = factored
    n, members = sh.shape
    kernel = functools.partial(gain_kernel, len(states))
    outs = [((n, states[0].shape[1]), F32, VMEM), ((picks.shape[1], members), F32, VMEM)]
    ins = [SMEM] + [VMEM] * (7 + len(states))
    args = [more, picks, sh, sl, d, g, xh, xl, *states]
    flops = 8 * n * members * states[0].shape[1]
    return call(kernel, outs, ins, args, [pltpu.VMEM((8, 128), jnp.int32)], flops)


def update(factored, z, states, starts):
    sh, sl, d = factored[:3]
    kernel = functools.partial(update_kernel, starts)
    outs = [(state.shape, F32, VMEM) for state in states]
    flops = 6 * sh.shape[0] * sh.shape[1] * z.shape[1]
    return call(kernel, outs, [VMEM] * (4 + len(states)), [sh, sl, d, z, *states], (), flops)


def last(factored, states):
    sh, sl, d, g, xh, xl, more = factored
    kernel = functools.partial(last_kernel, len(states))
    n, width = sh.shape[0], states[0].shape[1]
    outs = [((n, width), F32, VMEM), (states[-1].shape, F32, VMEM)]
    args = [more, sh, sl, d, g, xh, xl, *states]
    flops = 12 * sh.shape[0] * sh.shape[1] * width
    return call(kernel, outs, [SMEM] + [VMEM] * (6 + len(states)), args, (), flops)


def rings(size):
    up = [(i, (i + 1) % size) for i in range(size)]
    return up, [(j, i) for i, j in up]


BOTH = ("region", "member")


def permute(x, moves, regions):
    table = []
    for region in range(regions):
        for column in range(2):
            pair, parity, to = moves(region // 2, region % 2, column)
            pair %= regions // 2
            table.append((region * 2 + column, (pair * 2 + parity) * 2 + to))
    return lax.ppermute(x, BOTH, table)


def paired(state, neighbours, obs_cell, obs_values, obs_var):
    half, _, cells = state.shape
    members = 2 * half
    regions = lax.axis_size("region")
    region, column = lax.axis_index("region"), lax.axis_index("member")
    parity = region % 2
    mate = region + 1 - 2 * parity
    outer = (region + regions + 2 * parity - 1) % regions
    own = region * 2 + column
    place = column.astype(jnp.int32)[None]
    links = lax.dynamic_index_in_dim(neighbours, own, 0, keepdims=False)
    around = (region, mate, outer)
    ids_first = [r * 2 + p for r in around for p in (0, 1)]
    ids_next = [r * 2 + p for r in around for p in (column, 1 - column)]
    ids_first = jnp.concatenate([jnp.stack(ids_first + [own]).astype(jnp.int32), links])
    ids_next = jnp.concatenate([jnp.stack(ids_next + [own]).astype(jnp.int32), links])

    def across(x):
        return permute(x, lambda c, q, m: (c, q, 1 - m), regions)

    def beside(x):
        return permute(x, lambda c, q, m: (c, 1 - q, m), regions)

    def outside(x):
        return permute(x, lambda c, q, m: (c + 2 * q - 1, 1 - q, m), regions)

    anywhere = pl.BlockSpec(memory_space=pl.ANY)
    (rows,) = call(
        pick_kernel,
        [((2, obs_cell.shape[2], half), F32, VMEM)],
        [SMEM, anywhere, anywhere],
        [(region * 2).astype(jnp.int32)[None], obs_cell, state],
        [
            pltpu.VMEM(obs_cell.shape, jnp.int32),
            pltpu.VMEM(state.shape, F32),
            pltpu.VMEM((8, 128), jnp.int32),
            pltpu.VMEM((2, half, cells), F32),
            pltpu.SemaphoreType.DMA((3,)),
        ],
        limit=56,
    )
    other = across(rows)
    sources = [rows, beside(rows), outside(rows), other, beside(other), outside(other)]
    pieces = [[(i, (p,), 0), (3 + i, (p,), 1)] for i in range(3) for p in range(2)]
    shape = ((half, cells), F32, VMEM)
    keep, send, values, var = call(
        sort_kernel,
        [shape, shape, (obs_values.shape, F32, VMEM), (obs_var.shape, F32, VMEM)],
        [SMEM, anywhere, anywhere, VMEM, anywhere],
        [place, obs_values, obs_var, state, other],
        [pltpu.SemaphoreType.DMA((2,))],
    )
    states = [keep, across(send)]
    factored = factor(pieces, 0, members, ids_first, values, var, sources)
    everything = slice(None)
    low, high = (everything, slice(0, half)), (everything, slice(half, members))
    pieces = []
    for i in range(3):
        pieces += [[(i, low, 0), (i, high, 1)], [(3 + i, high, 0), (3 + i, low, 1)]]
    for batch in range(1, NBATCH):
        picks = lax.dynamic_slice_in_dim(obs_cell[:, batch, :], own, 1, 0)
        z, rows = gain(picks, factored, states)
        other = across(rows)
        out = outside(rows)
        sources = [rows, beside(rows), out, other, beside(other), across(out)]
        states = update(factored, z, states, (0, half))
        factored = factor(pieces, batch, members, ids_next, values, var, sources)
    z, theirs = last(factored, states)
    theirs = across(theirs)
    (mine,) = update(factored, z, states[:1], (0,))
    return pl.pallas_call(
        join_kernel,
        out_shape=jax.ShapeDtypeStruct(state.shape, F32),
        in_specs=[SMEM, VMEM, VMEM],
        out_specs=anywhere,
        scratch_shapes=[pltpu.VMEM(state.shape, F32), pltpu.SemaphoreType.DMA((4,))],
        compiler_params=pltpu.CompilerParams(vmem_limit_bytes=48 * 1024 * 1024),
    )(place, mine, theirs)


def general(state, neighbours, obs_cell, obs_values, obs_var):
    ensemble = lax.all_to_all(state, "member", split_axis=1, concat_axis=0, tiled=True)
    members, owned, cells = ensemble.shape
    regions = lax.axis_size("region")
    region_patches = owned * lax.axis_size("member")
    region = lax.axis_index("region")
    first = region * region_patches + lax.axis_index("member") * owned
    up, down = rings(regions)
    fields = [ensemble[:, p, :] for p in range(owned)]
    grid = jnp.arange(cells, dtype=jnp.int32)
    for batch in range(NBATCH):
        picks = lax.dynamic_slice_in_dim(obs_cell, first, owned, 0)[:, batch, :]
        hot = (picks[:, :, None] == grid[None, None, :]).astype(F32)
        own_rows = jnp.einsum("poc,pkc->pok", hot, jnp.stack(fields), precision=HIGHEST)
        region_rows = lax.all_gather(own_rows, "member", axis=0, tiled=True)
        before = lax.ppermute(region_rows, "region", up)
        after = lax.ppermute(region_rows, "region", down)
        beside = jnp.concatenate([before, region_rows, after], axis=0)
        new = []
        for p in range(owned):
            own = first + p
            links = lax.dynamic_index_in_dim(neighbours, own, 0, keepdims=False)
            ids = jnp.concatenate([own[None], links]).astype(jnp.int32)
            table = jnp.concatenate([ids, own[None], links]).astype(jnp.int32)
            home = (ids // region_patches - region + 1) % regions
            rows = jnp.take(beside, home * region_patches + ids % region_patches, axis=0)
            pieces = [[(0, (i,), 0)] for i in range(ids.shape[0])]
            factored = factor(pieces, batch, members, table, obs_values, obs_var, [rows])
            new.append(last(factored, [fields[p]])[1])
        fields = new
    ensemble = jnp.stack(fields, axis=1)
    return lax.all_to_all(ensemble, "member", split_axis=0, concat_axis=1, tiled=True)


def on_device(state, neighbours, obs_cell, obs_values, obs_var):
    patches, links = state.shape[1], neighbours.shape[1]
    even = lax.axis_size("region") % 2 == 0
    if even and patches == 2 and lax.axis_size("member") == 2 and links + 1 == 3 * patches:
        return paired(state, neighbours, obs_cell, obs_values, obs_var)
    return general(state, neighbours, obs_cell, obs_values, obs_var)


def solution(mesh):
    in_specs = (P("member", "region", None), P(), P(), P(), P())
    out_specs = P("member", "region", None)
    return jax.shard_map(
        on_device, mesh=mesh, in_specs=in_specs, out_specs=out_specs, check_vma=False
    )
```

```python
import functools
import math

import jax
import jax.numpy as jnp
from jax import lax
from jax.experimental import pallas as pl
from jax.experimental.pallas import tpu as pltpu
from jax.sharding import PartitionSpec as P

NBATCH = 2
HIGHEST = lax.Precision.HIGHEST
F32 = jnp.float32
BF16 = jnp.bfloat16
VMEM = pl.BlockSpec(memory_space=pltpu.VMEM)
SMEM = pl.BlockSpec(memory_space=pltpu.SMEM)
NN = (((1,), (0,)), ((), ()))
NT = (((1,), (1,)), ((), ()))
TN = (((0,), (0,)), ((), ()))
RESIDUAL = 1e-3
FACTOR_LIMIT = 24
MOST_STEPS = 15
TILE = 256


def call(kernel, outs, ins, args, scratch=(), flops=0, limit=16):
    shapes = [jax.ShapeDtypeStruct(shape, dtype) for shape, dtype, _ in outs]
    moved = sum(math.prod(s.shape) * s.dtype.itemsize for s in shapes)
    moved += sum(a.size * a.dtype.itemsize for a in args)
    return pl.pallas_call(
        kernel,
        out_shape=shapes,
        in_specs=ins,
        out_specs=[space for _, _, space in outs],
        scratch_shapes=list(scratch),
        compiler_params=pltpu.CompilerParams(vmem_limit_bytes=limit * 1024 * 1024),
        cost_estimate=pl.CostEstimate(flops=flops, bytes_accessed=moved, transcendentals=0),
    )(*args)


def split(x):
    high = x.astype(BF16)
    return high, (x - high.astype(F32)).astype(BF16)


def dot(a, b, dims=NN):
    return lax.dot_general(a, b, dims, preferred_element_type=F32)


def dot3(a, b, dims=NN):
    (left,), (right,) = dims[0]
    lhs = jnp.concatenate([a[0], a[0], a[1]], axis=left)
    rhs = jnp.concatenate([b[0], b[1], b[0]], axis=right)
    return dot(lhs, rhs, dims)


def select(hot, parts, dims):
    (left,), (right,) = dims[0]
    hot = hot.astype(BF16)
    lhs = jnp.concatenate([hot] * len(parts), axis=left)
    return dot(lhs, jnp.concatenate(parts, axis=right), dims)


def split_all(x):
    high, middle = split(x)
    low = x - high.astype(F32) - middle.astype(F32)
    return high, middle, low.astype(BF16)


def step_limits():
    limits = []
    for steps in range(MOST_STEPS):
        rho = RESIDUAL
        for _ in range(steps):
            rho = math.sqrt(2.0 * rho / (1.0 + rho))
        limits.append(2.0 * rho / (1.0 - rho) if rho < 1.0 else math.inf)
    return limits


def diagonal(n, columns, first):
    row = lax.broadcasted_iota(jnp.int32, (n, columns), 0)
    column = lax.broadcasted_iota(jnp.int32, (n, columns), 1)
    return row + first == column


def selector(picks, cells, scratch):
    per_patch = picks.shape[1]
    scratch[...] = jnp.full_like(scratch, -1)
    scratch[0:1, 0:per_patch] = picks
    grid = lax.broadcasted_iota(jnp.int32, (cells, scratch.shape[1]), 0)
    hot = (grid == scratch[0:1, :]).astype(F32)
    return jnp.transpose(hot)[0:per_patch, :]


def pick_kernel(picks_ref, state_ref, rows_ref, scratch, field_ref):
    patches, cells = state_ref.shape[1:]
    for p in range(patches):
        field_ref[p] = state_ref[:, p, :]
        hot = selector(picks_ref[p : p + 1, :], cells, scratch)
        rows_ref[p] = select(hot, split_all(field_ref[p]), NT)


def sort_kernel(place_ref, values_hbm, var_hbm, state_ref, *refs):
    keep_ref, send_ref, values_ref, var_ref, sems = refs[-5:]
    copies = [
        pltpu.make_async_copy(values_hbm, values_ref, sems.at[0]),
        pltpu.make_async_copy(var_hbm, var_ref, sems.at[1]),
    ]
    for copy in copies:
        copy.start()
    column = place_ref[0]
    first, second = state_ref[:, 0, :], state_ref[:, 1, :]
    keep_ref[...] = jnp.where(column == 0, first, second)
    send_ref[...] = jnp.where(column == 0, second, first)
    for copy in copies:
        copy.wait()


def factor_kernel(pieces, batch, members, ids_ref, values_ref, var_ref, *refs):
    count = len(refs) - 12
    sources = refs[:count]
    sh_ref, sl_ref, d_ref, g_ref, xh_ref, xl_ref, n_ref, flat, eye_ref, x_ref, wa, wb = refs[count:]
    per_patch = values_ref.shape[2]
    flat[...] = jnp.ones_like(flat)
    blocks = len(pieces)
    own = ids_ref[blocks]
    for i in range(blocks):
        patch = ids_ref[i]
        widening = (patch == own).astype(jnp.int32)
        for j in range(ids_ref.shape[0] - blocks - 1):
            widening = widening + (ids_ref[blocks + 1 + j] == patch).astype(jnp.int32) * (j + 2)
        flat[i : i + 1, 0:per_patch] = values_ref[pl.ds(patch, 1), batch, :]
        noise = var_ref[pl.ds(patch, 1), batch, :] * widening.astype(F32)
        flat[blocks + i : blocks + i + 1, 0:per_patch] = noise
    upright = jnp.transpose(flat[...])
    for i, halves in enumerate(pieces):
        rows = [sources[which][index] for which, index, _ in halves]
        total = sum(jnp.sum(part, axis=1, keepdims=True) for part in rows)
        mean = total * (1.0 / members)
        noise = upright[0:per_patch, blocks + i : blocks + i + 1]
        scale = lax.rsqrt(noise * (members - 1.0))
        at = slice(i * per_patch, (i + 1) * per_patch)
        for part, (_, _, start) in zip(rows, halves):
            size = part.shape[1]
            high, low = split((part - mean) * scale)
            lanes = slice(start * size, (start + 1) * size)
            sh_ref[at, lanes] = high
            sl_ref[at, lanes] = low
        shift = (upright[0:per_patch, i : i + 1] - mean) * scale
        d_ref[at, :] = jnp.broadcast_to(shift, (per_patch, d_ref.shape[1]))
    n = sh_ref.shape[0]
    head = min(TILE, n)
    tail = n - head
    s = (sh_ref[...], sl_ref[...])
    left = dot3(s, [part[0:head] for part in s], NT)
    g_ref[:, 0:head] = left
    g_ref[0:head, head:n] = jnp.transpose(left[head:n])
    low = [part[head:n] for part in s]
    g_ref[head:n, head:n] = dot3(low, low, NT)
    g = g_ref[...]
    square = jnp.sum(jnp.sum(g * g, axis=0, keepdims=True), axis=1, keepdims=True)
    norm = jnp.sqrt(square) * (1.0 + 1e-5)
    size = square[0, 0]
    limits = step_limits()
    pairs = jnp.int32(0)
    for k in range(7, MOST_STEPS - 2, 2):
        limit = limits[k] * (1.0 - 1e-4)
        pairs = pairs + (size > limit * limit).astype(jnp.int32)
    n_ref[0] = (size > 1.6e7).astype(jnp.int32) + (size > 1e8).astype(jnp.int32)
    eye_ref[...] = diagonal(n, n, 0).astype(F32)
    eye = eye_ref[...]
    first = 2.0 / (2.0 + norm)
    rho = norm * (0.5 * first)
    rho2 = rho * rho
    weight = 2.0 / (2.0 - rho2)
    keep = 0.5 * rho2 * weight
    r = (1.0 - first) * eye - first * g
    parts = split(r)
    x = (weight * first) * (eye + r)
    x_ref[...] = x
    for i, part in enumerate(split(x)):
        wa[i, :, n : 2 * n] = part

    def store(targets, start, left, corner):
        blocks = [(slice(0, n), slice(start, start + head), left)]
        blocks.append((slice(head, n), slice(start + head, start + n), corner))
        blocks.append((slice(0, head), slice(start + head, start + n), jnp.transpose(left[head:n])))
        for rows, columns, block in blocks:
            for target, part in zip(targets, split(block)):
                target[rows, columns] = part

    def corner_of(weight, keep, left, corner):
        left = weight * left - keep * eye_ref[:, 0:head]
        return left, weight * corner - keep * eye_ref[head:n, head:n]

    left = dot3(parts, [part[:, 0:head] for part in parts])
    corner = dot3([part[head:n] for part in parts], [part[:, head:n] for part in parts])
    store((wa.at[0], wa.at[1]), 0, *corner_of(weight, keep, left, corner))

    def advance(source, target, rho2):
        weight = 2.0 / (2.0 - rho2)
        keep = 0.5 * rho2 * weight
        parts = (source[0, :, 0:n], source[1, :, 0:n])
        ends = [jnp.concatenate([source[i, :, head:n], source[i, :, n + head : 2 * n]], axis=1) for i in (0, 1)]
        left = dot3(parts, (source[0, :, 0:head], source[1, :, 0:head]))
        corners = dot3([part[head:n] for part in parts], ends)
        both = (target.at[0], target.at[1])
        store(both, 0, *corner_of(weight, keep, left, corners[:, 0:tail]))
        left = dot3(parts, (source[0, :, n : n + head], source[1, :, n : n + head]))
        left = weight * (x_ref[:, 0:head] + left)
        corner = weight * (x_ref[head:n, head:n] + corners[:, tail : 2 * tail])
        x_ref[:, 0:head] = left
        x_ref[head:n, head:n] = corner
        store(both, n, left, corner)
        return keep * keep

    def twice(_, rho2):
        return advance(wb, wa, advance(wa, wb, rho2))

    rho2 = lax.fori_loop(0, pairs, twice, keep * keep)
    for source, target in ((wa, wb), (wb, wa)) * 2 + ((wa, wb),):
        rho2 = advance(source, target, rho2)
    weight = 2.0 / (2.0 - rho2)
    parts = (wb[0, :, 0:n], wb[1, :, 0:n])
    left = dot3(parts, (wb[0, :, n : n + head], wb[1, :, n : n + head]))
    ends = [wb[i, :, n + head : 2 * n] for i in (0, 1)]
    corner = dot3([part[head:n] for part in parts], ends)
    left = weight * (x_ref[:, 0:head] + left)
    corner = weight * (x_ref[head:n, head:n] + corner)
    store((xh_ref, xl_ref), 0, left, corner)


def solve(n_ref, s, g_ref, x, fields, z_ref):
    members = sum(field.shape[0] for field in fields)
    mean = sum(jnp.sum(field, axis=0, keepdims=True) for field in fields) * (1.0 / members)
    pairs = [split(field - mean) for field in fields]
    anomaly = [jnp.concatenate(parts, axis=0) for parts in zip(*pairs)]
    cross = dot3(s, anomaly)
    z = dot3(x, split(cross))
    g = g_ref[...]
    left = cross - z - dot3(split(g), split(z))
    z_ref[...] = z + dot3(x, split(left))

    def refine(_, carry):
        z = z_ref[...]
        gz = lax.dot_general(g_ref[...], z, NN, precision=HIGHEST, preferred_element_type=F32)
        z_ref[...] = z + dot3(x, split(cross - z - gz))
        return carry

    lax.fori_loop(0, n_ref[0], refine, 0)
    return anomaly, mean


def gain_kernel(parts, n_ref, picks_ref, sh_ref, sl_ref, d_ref, g_ref, xh_ref, xl_ref, *refs):
    states = refs[:parts]
    z_ref, rows_ref, scratch = refs[parts:]
    fields = [state[...] for state in states]
    s = (sh_ref[...], sl_ref[...])
    anomaly, mean = solve(n_ref, s, g_ref, (xh_ref[...], xl_ref[...]), fields, z_ref)
    hot = selector(picks_ref[...], mean.shape[1], scratch)
    zt = split(select(hot, split(z_ref[...]), NT))
    base = jnp.sum(hot * mean, axis=1, keepdims=True) + dot3(zt, split(d_ref[...]))[:, 0:1]
    rows_ref[...] = base + select(hot, anomaly, NT) - 0.5 * dot3(zt, s)


def updated(field, start, s, shift, z):
    size = field.shape[0]
    return field + shift - 0.5 * dot3([h[:, start : start + size] for h in s], z, TN)


def shift_of(z, d_ref):
    return jnp.sum(z * d_ref[:, 0:1], axis=0, keepdims=True)


def update_kernel(starts, sh_ref, sl_ref, d_ref, z_ref, *refs):
    states, outs = refs[: len(starts)], refs[len(starts) :]
    z = z_ref[...]
    shift = shift_of(z, d_ref)
    s, zs = (sh_ref[...], sl_ref[...]), split(z)
    for start, state, out in zip(starts, states, outs):
        out[...] = updated(state[...], start, s, shift, zs)


def last_kernel(parts, n_ref, sh_ref, sl_ref, d_ref, g_ref, xh_ref, xl_ref, *refs):
    states, (z_ref, out_ref) = refs[:parts], refs[parts:]
    fields = [state[...] for state in states]
    s = (sh_ref[...], sl_ref[...])
    solve(n_ref, s, g_ref, (xh_ref[...], xl_ref[...]), fields, z_ref)
    z = z_ref[...]
    start = sum(field.shape[0] for field in fields[:-1])
    out_ref[...] = updated(states[-1][...], start, s, shift_of(z, d_ref), split(z))


def join_kernel(place_ref, mine_ref, theirs_ref, out_ref, both, sems):
    chunks = sems.shape[0]
    size = both.shape[0] // chunks
    column = place_ref[0]
    copies = []
    for i in range(chunks):
        at = slice(i * size, (i + 1) * size)
        mine, theirs = mine_ref[at, :], theirs_ref[at, :]
        both[at, 0, :] = jnp.where(column == 0, mine, theirs)
        both[at, 1, :] = jnp.where(column == 0, theirs, mine)
        span = pl.ds(i * size, size)
        copies.append(pltpu.make_async_copy(both.at[span], out_ref.at[span], sems.at[i]))
        copies[-1].start()
    for copy in copies:
        copy.wait()


def factor(pieces, batch, members, ids, values, var, sources):
    per_patch = values.shape[2]
    n = len(pieces) * per_patch
    outs = [
        ((n, members), BF16, VMEM),
        ((n, members), BF16, VMEM),
        ((n, 128), F32, VMEM),
        ((n, n), F32, VMEM),
        ((n, n), BF16, VMEM),
        ((n, n), BF16, VMEM),
        ((1,), jnp.int32, SMEM),
    ]
    scratch = [
        pltpu.VMEM((128, 128), F32),
        pltpu.VMEM((n, n), F32),
        pltpu.VMEM((n, n), F32),
        pltpu.VMEM((2, n, 2 * n), BF16),
        pltpu.VMEM((2, n, 2 * n), BF16),
    ]
    kernel = functools.partial(factor_kernel, pieces, batch, members)
    args = [ids, values, var, *sources]
    flops = 6 * n * n * members + 60 * n * n * n
    return call(kernel, outs, [SMEM] + [VMEM] * (2 + len(sources)), args, scratch, flops, FACTOR_LIMIT)


def gain(picks, factored, states):
    sh, sl, d, g, xh, xl, more = factored
    n, members = sh.shape
    kernel = functools.partial(gain_kernel, len(states))
    outs = [((n, states[0].shape[1]), F32, VMEM), ((picks.shape[1], members), F32, VMEM)]
    ins = [SMEM] + [VMEM] * (7 + len(states))
    args = [more, picks, sh, sl, d, g, xh, xl, *states]
    flops = 8 * n * members * states[0].shape[1]
    return call(kernel, outs, ins, args, [pltpu.VMEM((8, 128), jnp.int32)], flops)


def update(factored, z, states, starts):
    sh, sl, d = factored[:3]
    kernel = functools.partial(update_kernel, starts)
    outs = [(state.shape, F32, VMEM) for state in states]
    flops = 6 * sh.shape[0] * sh.shape[1] * z.shape[1]
    return call(kernel, outs, [VMEM] * (4 + len(states)), [sh, sl, d, z, *states], (), flops)


def last(factored, states):
    sh, sl, d, g, xh, xl, more = factored
    kernel = functools.partial(last_kernel, len(states))
    n, width = sh.shape[0], states[0].shape[1]
    outs = [((n, width), F32, VMEM), (states[-1].shape, F32, VMEM)]
    args = [more, sh, sl, d, g, xh, xl, *states]
    flops = 12 * sh.shape[0] * sh.shape[1] * width
    return call(kernel, outs, [SMEM] + [VMEM] * (6 + len(states)), args, (), flops)


def rings(size):
    up = [(i, (i + 1) % size) for i in range(size)]
    return up, [(j, i) for i, j in up]


BOTH = ("region", "member")


def permute(x, moves, regions):
    table = []
    for region in range(regions):
        for column in range(2):
            pair, parity, to = moves(region // 2, region % 2, column)
            pair %= regions // 2
            table.append((region * 2 + column, (pair * 2 + parity) * 2 + to))
    return lax.ppermute(x, BOTH, table)


def paired(state, neighbours, obs_cell, obs_values, obs_var):
    half, _, cells = state.shape
    members = 2 * half
    regions = lax.axis_size("region")
    region, column = lax.axis_index("region"), lax.axis_index("member")
    parity = region % 2
    mate = region + 1 - 2 * parity
    outer = (region + regions + 2 * parity - 1) % regions
    own = region * 2 + column
    place = column.astype(jnp.int32)[None]
    links = lax.dynamic_index_in_dim(neighbours, own, 0, keepdims=False)
    around = (region, mate, outer)
    ids_first = [r * 2 + p for r in around for p in (0, 1)]
    ids_next = [r * 2 + p for r in around for p in (column, 1 - column)]
    ids_first = jnp.concatenate([jnp.stack(ids_first + [own]).astype(jnp.int32), links])
    ids_next = jnp.concatenate([jnp.stack(ids_next + [own]).astype(jnp.int32), links])

    def across(x):
        return permute(x, lambda c, q, m: (c, q, 1 - m), regions)

    def beside(x):
        return permute(x, lambda c, q, m: (c, 1 - q, m), regions)

    def outside(x):
        return permute(x, lambda c, q, m: (c + 2 * q - 1, 1 - q, m), regions)

    anywhere = pl.BlockSpec(memory_space=pl.ANY)
    per_patch = obs_cell.shape[2]
    picks = lax.dynamic_slice(obs_cell, (region * 2, 0, 0), (2, 1, per_patch)).reshape(2, per_patch)
    (rows,) = call(
        pick_kernel,
        [((2, per_patch, half), F32, VMEM)],
        [VMEM, VMEM],
        [picks, state],
        [pltpu.VMEM((8, 128), jnp.int32), pltpu.VMEM((2, half, cells), F32)],
    )
    other = across(rows)
    sources = [rows, beside(rows), outside(rows), other, beside(other), outside(other)]
    pieces = [[(i, (p,), 0), (3 + i, (p,), 1)] for i in range(3) for p in range(2)]
    shape = ((half, cells), F32, VMEM)
    keep, send, values, var = call(
        sort_kernel,
        [shape, shape, (obs_values.shape, F32, VMEM), (obs_var.shape, F32, VMEM)],
        [SMEM, anywhere, anywhere, VMEM, anywhere],
        [place, obs_values, obs_var, state, other],
        [pltpu.SemaphoreType.DMA((2,))],
    )
    states = [keep, across(send)]
    factored = factor(pieces, 0, members, ids_first, values, var, sources)
    everything = slice(None)
    low, high = (everything, slice(0, half)), (everything, slice(half, members))
    pieces = []
    for i in range(3):
        pieces += [[(i, low, 0), (i, high, 1)], [(3 + i, high, 0), (3 + i, low, 1)]]
    for batch in range(1, NBATCH):
        picks = lax.dynamic_slice(obs_cell, (own, batch, 0), (1, 1, per_patch)).reshape(1, per_patch)
        z, rows = gain(picks, factored, states)
        other = across(rows)
        sources = [rows, beside(rows), outside(rows), other, beside(other), outside(other)]
        states = update(factored, z, states, (0, half))
        factored = factor(pieces, batch, members, ids_next, values, var, sources)
    z, theirs = last(factored, states)
    theirs = across(theirs)
    (mine,) = update(factored, z, states[:1], (0,))
    return pl.pallas_call(
        join_kernel,
        out_shape=jax.ShapeDtypeStruct(state.shape, F32),
        in_specs=[SMEM, VMEM, VMEM],
        out_specs=anywhere,
        scratch_shapes=[pltpu.VMEM(state.shape, F32), pltpu.SemaphoreType.DMA((4,))],
        compiler_params=pltpu.CompilerParams(vmem_limit_bytes=16 * 1024 * 1024),
    )(place, mine, theirs)


def general(state, neighbours, obs_cell, obs_values, obs_var):
    ensemble = lax.all_to_all(state, "member", split_axis=1, concat_axis=0, tiled=True)
    members, owned, cells = ensemble.shape
    regions = lax.axis_size("region")
    region_patches = owned * lax.axis_size("member")
    region = lax.axis_index("region")
    first = region * region_patches + lax.axis_index("member") * owned
    up, down = rings(regions)
    fields = [ensemble[:, p, :] for p in range(owned)]
    grid = jnp.arange(cells, dtype=jnp.int32)
    for batch in range(NBATCH):
        picks = lax.dynamic_slice_in_dim(obs_cell, first, owned, 0)[:, batch, :]
        hot = (picks[:, :, None] == grid[None, None, :]).astype(F32)
        own_rows = jnp.einsum("poc,pkc->pok", hot, jnp.stack(fields), precision=HIGHEST)
        region_rows = lax.all_gather(own_rows, "member", axis=0, tiled=True)
        before = lax.ppermute(region_rows, "region", up)
        after = lax.ppermute(region_rows, "region", down)
        beside = jnp.concatenate([before, region_rows, after], axis=0)
        new = []
        for p in range(owned):
            own = first + p
            links = lax.dynamic_index_in_dim(neighbours, own, 0, keepdims=False)
            ids = jnp.concatenate([own[None], links]).astype(jnp.int32)
            table = jnp.concatenate([ids, own[None], links]).astype(jnp.int32)
            home = (ids // region_patches - region + 1) % regions
            rows = jnp.take(beside, home * region_patches + ids % region_patches, axis=0)
            pieces = [[(0, (i,), 0)] for i in range(ids.shape[0])]
            factored = factor(pieces, batch, members, table, obs_values, obs_var, [rows])
            new.append(last(factored, [fields[p]])[1])
        fields = new
    ensemble = jnp.stack(fields, axis=1)
    return lax.all_to_all(ensemble, "member", split_axis=0, concat_axis=1, tiled=True)


def on_device(state, neighbours, obs_cell, obs_values, obs_var):
    patches, links = state.shape[1], neighbours.shape[1]
    even = lax.axis_size("region") % 2 == 0
    if even and patches == 2 and lax.axis_size("member") == 2 and links + 1 == 3 * patches:
        return paired(state, neighbours, obs_cell, obs_values, obs_var)
    return general(state, neighbours, obs_cell, obs_values, obs_var)


def solution(mesh):
    in_specs = (P("member", "region", None), P(), P(), P(), P())
    out_specs = P("member", "region", None)
    return jax.shard_map(
        on_device, mesh=mesh, in_specs=in_specs, out_specs=out_specs, check_vma=False
    )
```

```python
import functools
import math

import jax
import jax.numpy as jnp
from jax import lax
from jax.experimental import pallas as pl
from jax.experimental.pallas import tpu as pltpu
from jax.sharding import PartitionSpec as P

NBATCH = 2
HIGHEST = lax.Precision.HIGHEST
F32 = jnp.float32
BF16 = jnp.bfloat16
VMEM = pl.BlockSpec(memory_space=pltpu.VMEM)
SMEM = pl.BlockSpec(memory_space=pltpu.SMEM)
NN = (((1,), (0,)), ((), ()))
NT = (((1,), (1,)), ((), ()))
TN = (((0,), (0,)), ((), ()))
RESIDUAL = 1e-3
FACTOR_LIMIT = 24
MOST_STEPS = 15
TILE = 256
CHUNK = 128


def call(kernel, outs, ins, args, scratch=(), flops=0, limit=16):
    shapes = [jax.ShapeDtypeStruct(shape, dtype) for shape, dtype, _ in outs]
    moved = sum(math.prod(s.shape) * s.dtype.itemsize for s in shapes)
    moved += sum(a.size * a.dtype.itemsize for a in args)
    return pl.pallas_call(
        kernel,
        out_shape=shapes,
        in_specs=ins,
        out_specs=[space for _, _, space in outs],
        scratch_shapes=list(scratch),
        compiler_params=pltpu.CompilerParams(vmem_limit_bytes=limit * 1024 * 1024),
        cost_estimate=pl.CostEstimate(flops=flops, bytes_accessed=moved, transcendentals=0),
    )(*args)


def split(x):
    high = x.astype(BF16)
    return high, (x - high.astype(F32)).astype(BF16)


def dot(a, b, dims=NN):
    return lax.dot_general(a, b, dims, preferred_element_type=F32)


def dot3(a, b, dims=NN):
    (left,), (right,) = dims[0]
    lhs = jnp.concatenate([a[0], a[0], a[1]], axis=left)
    rhs = jnp.concatenate([b[0], b[1], b[0]], axis=right)
    return dot(lhs, rhs, dims)


def select(hot, parts, dims):
    (left,), (right,) = dims[0]
    hot = hot.astype(BF16)
    lhs = jnp.concatenate([hot] * len(parts), axis=left)
    return dot(lhs, jnp.concatenate(parts, axis=right), dims)


def split_all(x):
    high, middle = split(x)
    low = x - high.astype(F32) - middle.astype(F32)
    return high, middle, low.astype(BF16)


def step_limits():
    limits = []
    for steps in range(MOST_STEPS):
        rho = RESIDUAL
        for _ in range(steps):
            rho = math.sqrt(2.0 * rho / (1.0 + rho))
        limits.append(2.0 * rho / (1.0 - rho) if rho < 1.0 else math.inf)
    return limits


def diagonal(n, columns, first):
    row = lax.broadcasted_iota(jnp.int32, (n, columns), 0)
    column = lax.broadcasted_iota(jnp.int32, (n, columns), 1)
    return row + first == column


def selector(picks, cells, scratch):
    per_patch = picks.shape[1]
    scratch[...] = jnp.full_like(scratch, -1)
    scratch[0:1, 0:per_patch] = picks
    grid = lax.broadcasted_iota(jnp.int32, (cells, scratch.shape[1]), 0)
    hot = (grid == scratch[0:1, :]).astype(F32)
    return jnp.transpose(hot)[0:per_patch, :]


def pick_kernel(picks_ref, state_ref, rows_ref, scratch, field_ref):
    patches, cells = state_ref.shape[1:]
    for p in range(patches):
        field_ref[p] = state_ref[:, p, :]
        hot = selector(picks_ref[p : p + 1, :], cells, scratch)
        rows_ref[p] = select(hot, split_all(field_ref[p]), NT)


def sort_kernel(place_ref, values_hbm, var_hbm, state_ref, *refs):
    first_ref, second_ref, keep_ref, send_ref, values_ref, var_ref, near_ref, sems = refs[-8:]
    near_ref[0] = first_ref[...]
    near_ref[1] = second_ref[...]
    copies = [
        pltpu.make_async_copy(values_hbm, values_ref, sems.at[0]),
        pltpu.make_async_copy(var_hbm, var_ref, sems.at[1]),
    ]
    for copy in copies:
        copy.start()
    column = place_ref[0]
    first, second = state_ref[:, 0, :], state_ref[:, 1, :]
    keep_ref[...] = jnp.where(column == 0, first, second)
    send_ref[...] = jnp.where(column == 0, second, first)
    for copy in copies:
        copy.wait()


def factor_kernel(pieces, batch, members, chunk, ids_ref, values_ref, var_ref, *refs):
    count = len(refs) - 12
    sources = refs[:count]
    sh_ref, sl_ref, d_ref, g_ref, xh_ref, xl_ref, n_ref, flat, eye_ref, x_ref, wa, wb = refs[count:]
    per_patch = values_ref.shape[2]
    flat[...] = jnp.ones_like(flat)
    blocks = len(pieces)
    own = ids_ref[blocks]
    for i in range(blocks):
        patch = ids_ref[i]
        widening = (patch == own).astype(jnp.int32)
        for j in range(ids_ref.shape[0] - blocks - 1):
            widening = widening + (ids_ref[blocks + 1 + j] == patch).astype(jnp.int32) * (j + 2)
        flat[i : i + 1, 0:per_patch] = values_ref[pl.ds(patch, 1), batch, :]
        noise = var_ref[pl.ds(patch, 1), batch, :] * widening.astype(F32)
        flat[blocks + i : blocks + i + 1, 0:per_patch] = noise
    upright = jnp.transpose(flat[...])
    for i, halves in enumerate(pieces):
        rows = [sources[which][index] for which, index, _ in halves]
        total = sum(jnp.sum(part, axis=1, keepdims=True) for part in rows)
        mean = total * (1.0 / members)
        noise = upright[0:per_patch, blocks + i : blocks + i + 1]
        scale = lax.rsqrt(noise * (members - 1.0))
        at = slice(i * per_patch, (i + 1) * per_patch)
        for part, (_, _, start) in zip(rows, halves):
            size = part.shape[1]
            high, low = split((part - mean) * scale)
            lanes = slice(start * size, (start + 1) * size)
            sh_ref[at, lanes] = high
            sl_ref[at, lanes] = low
        shift = (upright[0:per_patch, i : i + 1] - mean) * scale
        d_ref[at, :] = jnp.broadcast_to(shift, (per_patch, d_ref.shape[1]))
    n = sh_ref.shape[0]
    head = min(TILE, n)
    tail = n - head
    s = (sh_ref[...], sl_ref[...])
    left = dot3(s, [part[0:head] for part in s], NT)
    g_ref[:, 0:head] = left
    g_ref[0:head, head:n] = jnp.transpose(left[head:n])
    low = [part[head:n] for part in s]
    g_ref[head:n, head:n] = dot3(low, low, NT)
    g = g_ref[...]
    square = jnp.sum(jnp.sum(g * g, axis=0, keepdims=True), axis=1, keepdims=True)
    norm = jnp.sqrt(square) * (1.0 + 1e-5)
    size = square[0, 0]
    limits = step_limits()
    pairs = jnp.int32(0)
    for k in range(7, MOST_STEPS - 2, 2):
        limit = limits[k] * (1.0 - 1e-4)
        pairs = pairs + (size > limit * limit).astype(jnp.int32)
    n_ref[0] = (size > 1.6e7).astype(jnp.int32) + (size > 1e8).astype(jnp.int32)
    eye_ref[...] = diagonal(n, n, 0).astype(F32)
    eye = eye_ref[...]
    first = 2.0 / (2.0 + norm)
    rho = norm * (0.5 * first)
    rho2 = rho * rho
    weight = 2.0 / (2.0 - rho2)
    keep = 0.5 * rho2 * weight
    r = (1.0 - first) * eye - first * g
    parts = split(r)
    x = (weight * first) * (eye + r)
    x_ref[...] = x
    for i, part in enumerate(split(x)):
        wa[i, :, n : 2 * n] = part

    def store(targets, start, left, corner):
        blocks = [(slice(0, n), slice(start, start + head), left)]
        blocks.append((slice(head, n), slice(start + head, start + n), corner))
        blocks.append((slice(0, head), slice(start + head, start + n), jnp.transpose(left[head:n])))
        for rows, columns, block in blocks:
            for target, part in zip(targets, split(block)):
                target[rows, columns] = part

    def corner_of(weight, keep, left, corner):
        left = weight * left - keep * eye_ref[:, 0:head]
        return left, weight * corner - keep * eye_ref[head:n, head:n]

    left = dot3(parts, [part[:, 0:head] for part in parts])
    corner = dot3([part[head:n] for part in parts], [part[:, head:n] for part in parts])
    store((wa.at[0], wa.at[1]), 0, *corner_of(weight, keep, left, corner))

    def advance(source, target, rho2):
        weight = 2.0 / (2.0 - rho2)
        keep = 0.5 * rho2 * weight
        parts = (source[0, :, 0:n], source[1, :, 0:n])
        ends = [jnp.concatenate([source[i, :, head:n], source[i, :, n + head : 2 * n]], axis=1) for i in (0, 1)]
        left = dot3(parts, (source[0, :, 0:head], source[1, :, 0:head]))
        corners = dot3([part[head:n] for part in parts], ends)
        both = (target.at[0], target.at[1])
        store(both, 0, *corner_of(weight, keep, left, corners[:, 0:tail]))
        left = dot3(parts, (source[0, :, n : n + head], source[1, :, n : n + head]))
        left = weight * (x_ref[:, 0:head] + left)
        corner = weight * (x_ref[head:n, head:n] + corners[:, tail : 2 * tail])
        x_ref[:, 0:head] = left
        x_ref[head:n, head:n] = corner
        store(both, n, left, corner)
        return keep * keep

    def twice(_, rho2):
        return advance(wb, wa, advance(wa, wb, rho2))

    rho2 = lax.fori_loop(0, pairs, twice, keep * keep)
    chunks = [(i, min(i + chunk, n)) for i in range(0, n, chunk)]

    def sides(source, span):
        return [source[i, span[0] : span[1], 0:n] for i in (0, 1)]

    def put(targets, start, span, block):
        for target, part in zip(targets, split(block)):
            target[span[0] : span[1], start : start + head] = part
        low = max(span[0], head)
        if low < span[1]:
            for target, part in zip(targets, split(jnp.transpose(block[low - span[0] :]))):
                target[0:head, start + low : start + span[1]] = part

    def put_corner(targets, start, block):
        for target, part in zip(targets, split(block)):
            target[head:n, start + head : start + n] = part

    def put_x(targets, start, weight, span, product):
        x = weight * (x_ref[span[0] : span[1], 0:head] + product)
        x_ref[span[0] : span[1], 0:head] = x
        put(targets, start, span, x)

    def put_x_corner(targets, start, weight, product):
        x = weight * (x_ref[head:n, head:n] + product)
        x_ref[head:n, head:n] = x
        put_corner(targets, start, x)

    waiting = None
    source, target = wa, wb
    for _ in range(5):
        weight = 2.0 / (2.0 - rho2)
        keep = 0.5 * rho2 * weight
        first = (source[0, :, 0:head], source[1, :, 0:head])
        r = []
        for k, span in enumerate(chunks):
            r.append(dot3(sides(source, span), first))
            if waiting is not None:
                put_x((source.at[0], source.at[1]), n, waiting[0], span, waiting[1][k])
        if waiting is not None:
            put_x_corner((source.at[0], source.at[1]), n, waiting[0], waiting[2])
        ends = [jnp.concatenate([source[i, :, head:n], source[i, :, n + head : 2 * n]], axis=1) for i in (0, 1)]
        corners = dot3(sides(source, (head, n)), ends)
        first = (source[0, :, n : n + head], source[1, :, n : n + head])
        both = (target.at[0], target.at[1])
        x = []
        for k, span in enumerate(chunks):
            x.append(dot3(sides(source, span), first))
            put(both, 0, span, weight * r[k] - keep * eye_ref[span[0] : span[1], 0:head])
        put_corner(both, 0, weight * corners[:, 0:tail] - keep * eye_ref[head:n, head:n])
        waiting = (weight, x, corners[:, tail : 2 * tail])
        rho2 = keep * keep
        source, target = target, source
    for k, span in enumerate(chunks):
        put_x((source.at[0], source.at[1]), n, waiting[0], span, waiting[1][k])
    put_x_corner((source.at[0], source.at[1]), n, waiting[0], waiting[2])
    weight = 2.0 / (2.0 - rho2)
    first = (source[0, :, n : n + head], source[1, :, n : n + head])
    done = (xh_ref, xl_ref)
    ends = [source[i, :, n + head : 2 * n] for i in (0, 1)]
    put_x_corner(done, 0, weight, dot3(sides(source, (head, n)), ends))
    x = [dot3(sides(source, span), first) for span in chunks]
    for k, span in enumerate(chunks):
        put_x(done, 0, weight, span, x[k])


def centred(fields):
    members = sum(field.shape[0] for field in fields)
    mean = sum(jnp.sum(field, axis=0, keepdims=True) for field in fields) * (1.0 / members)
    pairs = [split(field - mean) for field in fields]
    return [jnp.concatenate(parts, axis=0) for parts in zip(*pairs)], mean


def solve(n_ref, s, g_ref, x, anomaly, z_ref):
    cross = dot3(s, anomaly)
    z = dot3(x, split(cross))
    g = g_ref[...]
    left = cross - z - dot3(split(g), split(z))
    z_ref[...] = z + dot3(x, split(left))

    def refine(_, carry):
        z = z_ref[...]
        gz = lax.dot_general(g_ref[...], z, NN, precision=HIGHEST, preferred_element_type=F32)
        z_ref[...] = z + dot3(x, split(cross - z - gz))
        return carry

    lax.fori_loop(0, n_ref[0], refine, 0)


def gain_kernel(parts, n_ref, picks_ref, sh_ref, sl_ref, d_ref, g_ref, xh_ref, xl_ref, *refs):
    states = refs[:parts]
    z_ref, rows_ref, scratch = refs[parts:]
    fields = [state[...] for state in states]
    s = (sh_ref[...], sl_ref[...])
    anomaly, mean = centred(fields)
    solve(n_ref, s, g_ref, (xh_ref[...], xl_ref[...]), anomaly, z_ref)
    hot = selector(picks_ref[...], mean.shape[1], scratch)
    zt = split(select(hot, split(z_ref[...]), NT))
    base = jnp.sum(hot * mean, axis=1, keepdims=True) + dot3(zt, split(d_ref[...]))[:, 0:1]
    rows_ref[...] = base + select(hot, anomaly, NT) - 0.5 * dot3(zt, s)


def updated(field, start, s, shift, z):
    size = field.shape[0]
    return field + shift - 0.5 * dot3([h[:, start : start + size] for h in s], z, TN)


def shift_of(z, d_ref):
    return jnp.sum(z * d_ref[:, 0:1], axis=0, keepdims=True)


def update_kernel(starts, sh_ref, sl_ref, d_ref, z_ref, *refs):
    count = len(starts)
    states, outs, parts = refs[:count], refs[count : 2 * count], refs[2 * count :]
    z = z_ref[...]
    shift = shift_of(z, d_ref)
    s, zs = (sh_ref[...], sl_ref[...]), split(z)
    for start, state, out in zip(starts, states, outs):
        out[...] = updated(state[...], start, s, shift, zs)
    if parts:
        anomaly, _ = centred([out[...] for out in outs])
        for ref, part in zip(parts, anomaly):
            ref[...] = part


def last_kernel(n_ref, sh_ref, sl_ref, d_ref, g_ref, xh_ref, xl_ref, *refs):
    (state_ref, *parts), (z_ref, out_ref) = refs[:-2], refs[-2:]
    s = (sh_ref[...], sl_ref[...])
    anomaly = [part[...] for part in parts] if parts else centred([state_ref[...]])[0]
    solve(n_ref, s, g_ref, (xh_ref[...], xl_ref[...]), anomaly, z_ref)
    z = z_ref[...]
    start = sh_ref.shape[1] - state_ref.shape[0]
    out_ref[...] = updated(state_ref[...], start, s, shift_of(z, d_ref), split(z))


def join_kernel(place_ref, mine_ref, theirs_ref, out_ref, both, sems):
    chunks = sems.shape[0]
    size = both.shape[0] // chunks
    column = place_ref[0]
    copies = []
    for i in range(chunks):
        at = slice(i * size, (i + 1) * size)
        mine, theirs = mine_ref[at, :], theirs_ref[at, :]
        both[at, 0, :] = jnp.where(column == 0, mine, theirs)
        both[at, 1, :] = jnp.where(column == 0, theirs, mine)
        span = pl.ds(i * size, size)
        copies.append(pltpu.make_async_copy(both.at[span], out_ref.at[span], sems.at[i]))
        copies[-1].start()
    for copy in copies:
        copy.wait()


def factor(pieces, batch, members, chunk, ids, values, var, sources):
    per_patch = values.shape[2]
    n = len(pieces) * per_patch
    outs = [
        ((n, members), BF16, VMEM),
        ((n, members), BF16, VMEM),
        ((n, 128), F32, VMEM),
        ((n, n), F32, VMEM),
        ((n, n), BF16, VMEM),
        ((n, n), BF16, VMEM),
        ((1,), jnp.int32, SMEM),
    ]
    scratch = [
        pltpu.VMEM((128, 128), F32),
        pltpu.VMEM((n, n), F32),
        pltpu.VMEM((n, n), F32),
        pltpu.VMEM((2, n, 2 * n), BF16),
        pltpu.VMEM((2, n, 2 * n), BF16),
    ]
    kernel = functools.partial(factor_kernel, pieces, batch, members, chunk)
    args = [ids, values, var, *sources]
    flops = 6 * n * n * members + 60 * n * n * n
    return call(kernel, outs, [SMEM] + [VMEM] * (2 + len(sources)), args, scratch, flops, FACTOR_LIMIT)


def gain(picks, factored, states):
    sh, sl, d, g, xh, xl, more = factored
    n, members = sh.shape
    kernel = functools.partial(gain_kernel, len(states))
    outs = [((n, states[0].shape[1]), F32, VMEM), ((picks.shape[1], members), F32, VMEM)]
    ins = [SMEM] + [VMEM] * (7 + len(states))
    args = [more, picks, sh, sl, d, g, xh, xl, *states]
    flops = 8 * n * members * states[0].shape[1]
    return call(kernel, outs, ins, args, [pltpu.VMEM((8, 128), jnp.int32)], flops)


def update(factored, z, states, starts, more=False):
    sh, sl, d = factored[:3]
    kernel = functools.partial(update_kernel, starts)
    outs = [(state.shape, F32, VMEM) for state in states]
    if more:
        outs += [((sh.shape[1], z.shape[1]), BF16, VMEM)] * 2
    flops = 6 * sh.shape[0] * sh.shape[1] * z.shape[1]
    return call(kernel, outs, [VMEM] * (4 + len(states)), [sh, sl, d, z, *states], (), flops)


def last(factored, state, anomaly=()):
    sh, sl, d, g, xh, xl, more = factored
    n, width = sh.shape[0], state.shape[1]
    outs = [((n, width), F32, VMEM), (state.shape, F32, VMEM)]
    args = [more, sh, sl, d, g, xh, xl, state, *anomaly]
    flops = 12 * sh.shape[0] * sh.shape[1] * width
    return call(last_kernel, outs, [SMEM] + [VMEM] * (len(args) - 1), args, (), flops)


def rings(size):
    up = [(i, (i + 1) % size) for i in range(size)]
    return up, [(j, i) for i, j in up]


BOTH = ("region", "member")


def permute(x, moves, regions):
    table = []
    for region in range(regions):
        for column in range(2):
            pair, parity, to = moves(region // 2, region % 2, column)
            pair %= regions // 2
            table.append((region * 2 + column, (pair * 2 + parity) * 2 + to))
    return lax.ppermute(x, BOTH, table)


def paired(state, neighbours, obs_cell, obs_values, obs_var):
    half, _, cells = state.shape
    members = 2 * half
    regions = lax.axis_size("region")
    region, column = lax.axis_index("region"), lax.axis_index("member")
    parity = region % 2
    mate = region + 1 - 2 * parity
    outer = (region + regions + 2 * parity - 1) % regions
    own = region * 2 + column
    place = column.astype(jnp.int32)[None]
    links = lax.dynamic_index_in_dim(neighbours, own, 0, keepdims=False)
    around = (region, mate, outer)
    ids_first = [r * 2 + p for r in around for p in (0, 1)]
    ids_next = [r * 2 + p for r in around for p in (column, 1 - column)]
    ids_first = jnp.concatenate([jnp.stack(ids_first + [own]).astype(jnp.int32), links])
    ids_next = jnp.concatenate([jnp.stack(ids_next + [own]).astype(jnp.int32), links])

    def across(x):
        return permute(x, lambda c, q, m: (c, q, 1 - m), regions)

    def beside(x):
        return permute(x, lambda c, q, m: (c, 1 - q, m), regions)

    def outside(x):
        return permute(x, lambda c, q, m: (c + 2 * q - 1, 1 - q, m), regions)

    anywhere = pl.BlockSpec(memory_space=pl.ANY)
    per_patch = obs_cell.shape[2]
    picks = lax.dynamic_slice(obs_cell, (region * 2, 0, 0), (2, 1, per_patch)).reshape(2, per_patch)
    (rows,) = call(
        pick_kernel,
        [((2, per_patch, half), F32, VMEM)],
        [VMEM, VMEM],
        [picks, state],
        [pltpu.VMEM((8, 128), jnp.int32), pltpu.VMEM((2, half, cells), F32)],
    )
    other = across(rows)
    sources = [rows, beside(rows), outside(rows), other, beside(other), outside(other)]
    shape = ((half, cells), F32, VMEM)
    outs = [shape, shape, (obs_values.shape, F32, VMEM), (obs_var.shape, F32, VMEM)]
    keep, send, values, var, near = call(
        sort_kernel,
        outs + [((2, *rows.shape), F32, VMEM)],
        [SMEM, anywhere, anywhere, VMEM, anywhere, VMEM, VMEM],
        [place, obs_values, obs_var, state, other, sources[1], sources[2]],
        [pltpu.SemaphoreType.DMA((2,))],
    )
    sources[1:3] = [near]
    pieces = []
    for p in range(2):
        pieces.append([(0, (p,), 0), (2, (p,), 1)])
    for i in range(2):
        for p in range(2):
            pieces.append([(1, (i, p), 0), (3 + i, (p,), 1)])
    states = [keep, across(send)]
    factored = factor(pieces, 0, members, CHUNK, ids_first, values, var, sources)
    everything = slice(None)
    low, high = (everything, slice(0, half)), (everything, slice(half, members))
    pieces = []
    for i in range(3):
        pieces += [[(i, low, 0), (i, high, 1)], [(3 + i, high, 0), (3 + i, low, 1)]]
    for batch in range(1, NBATCH):
        picks = lax.dynamic_slice(obs_cell, (own, batch, 0), (1, 1, per_patch)).reshape(1, per_patch)
        z, rows = gain(picks, factored, states)
        other = across(rows)
        sources = [rows, beside(rows), outside(rows), other, beside(other), outside(other)]
        mine, theirs, *anomaly = update(factored, z, states, (0, half), True)
        states = [mine, theirs]
        factored = factor(pieces, batch, members, 3 * CHUNK, ids_next, values, var, sources)
    z, theirs = last(factored, states[1], anomaly)
    theirs = across(theirs)
    (mine,) = update(factored, z, states[:1], (0,))
    return pl.pallas_call(
        join_kernel,
        out_shape=jax.ShapeDtypeStruct(state.shape, F32),
        in_specs=[SMEM, VMEM, VMEM],
        out_specs=anywhere,
        scratch_shapes=[pltpu.VMEM(state.shape, F32), pltpu.SemaphoreType.DMA((4,))],
        compiler_params=pltpu.CompilerParams(vmem_limit_bytes=16 * 1024 * 1024),
    )(place, mine, theirs)


def general(state, neighbours, obs_cell, obs_values, obs_var):
    ensemble = lax.all_to_all(state, "member", split_axis=1, concat_axis=0, tiled=True)
    members, owned, cells = ensemble.shape
    regions = lax.axis_size("region")
    region_patches = owned * lax.axis_size("member")
    region = lax.axis_index("region")
    first = region * region_patches + lax.axis_index("member") * owned
    up, down = rings(regions)
    fields = [ensemble[:, p, :] for p in range(owned)]
    grid = jnp.arange(cells, dtype=jnp.int32)
    for batch in range(NBATCH):
        picks = lax.dynamic_slice_in_dim(obs_cell, first, owned, 0)[:, batch, :]
        hot = (picks[:, :, None] == grid[None, None, :]).astype(F32)
        own_rows = jnp.einsum("poc,pkc->pok", hot, jnp.stack(fields), precision=HIGHEST)
        region_rows = lax.all_gather(own_rows, "member", axis=0, tiled=True)
        before = lax.ppermute(region_rows, "region", up)
        after = lax.ppermute(region_rows, "region", down)
        beside = jnp.concatenate([before, region_rows, after], axis=0)
        new = []
        for p in range(owned):
            own = first + p
            links = lax.dynamic_index_in_dim(neighbours, own, 0, keepdims=False)
            ids = jnp.concatenate([own[None], links]).astype(jnp.int32)
            table = jnp.concatenate([ids, own[None], links]).astype(jnp.int32)
            home = (ids // region_patches - region + 1) % regions
            rows = jnp.take(beside, home * region_patches + ids % region_patches, axis=0)
            pieces = [[(0, (i,), 0)] for i in range(ids.shape[0])]
            factored = factor(pieces, batch, members, CHUNK, table, obs_values, obs_var, [rows])
            new.append(last(factored, fields[p])[1])
        fields = new
    ensemble = jnp.stack(fields, axis=1)
    return lax.all_to_all(ensemble, "member", split_axis=0, concat_axis=1, tiled=True)


def on_device(state, neighbours, obs_cell, obs_values, obs_var):
    patches, links = state.shape[1], neighbours.shape[1]
    even = lax.axis_size("region") % 2 == 0
    if even and patches == 2 and lax.axis_size("member") == 2 and links + 1 == 3 * patches:
        return paired(state, neighbours, obs_cell, obs_values, obs_var)
    return general(state, neighbours, obs_cell, obs_values, obs_var)


def solution(mesh):
    in_specs = (P("member", "region", None), P(), P(), P(), P())
    out_specs = P("member", "region", None)
    return jax.shard_map(
        on_device, mesh=mesh, in_specs=in_specs, out_specs=out_specs, check_vma=False
    )
```

```python
import functools
import math

import jax
import jax.numpy as jnp
from jax import lax
from jax.experimental import pallas as pl
from jax.experimental.pallas import tpu as pltpu
from jax.sharding import PartitionSpec as P

NBATCH = 2
HIGHEST = lax.Precision.HIGHEST
F32 = jnp.float32
BF16 = jnp.bfloat16
VMEM = pl.BlockSpec(memory_space=pltpu.VMEM)
SMEM = pl.BlockSpec(memory_space=pltpu.SMEM)
NN = (((1,), (0,)), ((), ()))
NT = (((1,), (1,)), ((), ()))
TN = (((0,), (0,)), ((), ()))
RESIDUAL = 1e-3
FACTOR_LIMIT = 24
MOST_STEPS = 15
TILE = 256
CHUNK = 128


def call(kernel, outs, ins, args, scratch=(), flops=0, limit=16):
    shapes = [jax.ShapeDtypeStruct(shape, dtype) for shape, dtype, _ in outs]
    moved = sum(math.prod(s.shape) * s.dtype.itemsize for s in shapes)
    moved += sum(a.size * a.dtype.itemsize for a in args)
    return pl.pallas_call(
        kernel,
        out_shape=shapes,
        in_specs=ins,
        out_specs=[space for _, _, space in outs],
        scratch_shapes=list(scratch),
        compiler_params=pltpu.CompilerParams(vmem_limit_bytes=limit * 1024 * 1024),
        cost_estimate=pl.CostEstimate(flops=flops, bytes_accessed=moved, transcendentals=0),
    )(*args)


def split(x):
    high = x.astype(BF16)
    return high, (x - high.astype(F32)).astype(BF16)


def dot(a, b, dims=NN):
    return lax.dot_general(a, b, dims, preferred_element_type=F32)


def dot3(a, b, dims=NN):
    (left,), (right,) = dims[0]
    lhs = jnp.concatenate([a[0], a[0], a[1]], axis=left)
    rhs = jnp.concatenate([b[0], b[1], b[0]], axis=right)
    return dot(lhs, rhs, dims)


def select(hot, parts, dims):
    (left,), (right,) = dims[0]
    hot = hot.astype(BF16)
    lhs = jnp.concatenate([hot] * len(parts), axis=left)
    return dot(lhs, jnp.concatenate(parts, axis=right), dims)


def split_all(x):
    high, middle = split(x)
    low = x - high.astype(F32) - middle.astype(F32)
    return high, middle, low.astype(BF16)


def step_limits():
    limits = []
    for steps in range(MOST_STEPS):
        rho = RESIDUAL
        for _ in range(steps):
            rho = math.sqrt(2.0 * rho / (1.0 + rho))
        limits.append(2.0 * rho / (1.0 - rho) if rho < 1.0 else math.inf)
    return limits


def diagonal(n, columns, first):
    row = lax.broadcasted_iota(jnp.int32, (n, columns), 0)
    column = lax.broadcasted_iota(jnp.int32, (n, columns), 1)
    return row + first == column


def selector(picks, cells, scratch):
    per_patch = picks.shape[1]
    scratch[...] = jnp.full_like(scratch, -1)
    scratch[0:1, 0:per_patch] = picks
    grid = lax.broadcasted_iota(jnp.int32, (cells, scratch.shape[1]), 0)
    hot = (grid == scratch[0:1, :]).astype(F32)
    return jnp.transpose(hot)[0:per_patch, :]


def pick_kernel(place_ref, cells_ref, state_ref, rows_ref, scratch, field_ref):
    patches, cells = state_ref.shape[1:]
    for p in range(patches):
        field_ref[p] = state_ref[:, p, :]
        hot = selector(cells_ref[pl.ds(place_ref[0] * patches + p, 1), 0, :], cells, scratch)
        rows_ref[p] = select(hot, split_all(field_ref[p]), NT)


def sort_kernel(place_ref, values_hbm, var_hbm, state_ref, *refs):
    keep_ref, send_ref, values_ref, var_ref, sems = refs[-5:]
    copies = [
        pltpu.make_async_copy(values_hbm, values_ref, sems.at[0]),
        pltpu.make_async_copy(var_hbm, var_ref, sems.at[1]),
    ]
    for copy in copies:
        copy.start()
    column = place_ref[1]
    first, second = state_ref[:, 0, :], state_ref[:, 1, :]
    keep_ref[...] = jnp.where(column == 0, first, second)
    send_ref[...] = jnp.where(column == 0, second, first)
    for copy in copies:
        copy.wait()


def factor_kernel(pieces, batch, members, chunk, patches_of, place_ref, near_ref, values_ref, var_ref, *refs):
    count = len(refs) - 12
    sources = refs[:count]
    sh_ref, sl_ref, d_ref, g_ref, xh_ref, xl_ref, n_ref, flat, eye_ref, x_ref, wa, wb = refs[count:]
    per_patch = values_ref.shape[2]
    flat[...] = jnp.ones_like(flat)
    blocks = len(pieces)
    ids, own = patches_of(place_ref)
    for i in range(blocks):
        patch = ids[i]
        widening = (patch == own).astype(jnp.int32)
        for j in range(near_ref.shape[0]):
            widening = widening + (near_ref[j, own] == patch).astype(jnp.int32) * (j + 2)
        flat[i : i + 1, 0:per_patch] = values_ref[pl.ds(patch, 1), batch, :]
        noise = var_ref[pl.ds(patch, 1), batch, :] * widening.astype(F32)
        flat[blocks + i : blocks + i + 1, 0:per_patch] = noise
    upright = jnp.transpose(flat[...])

    def scaled(i):
        rows = [sources[which][index] for which, index, _ in pieces[i]]
        total = sum(jnp.sum(part, axis=1, keepdims=True) for part in rows)
        mean = total * (1.0 / members)
        noise = upright[0:per_patch, blocks + i : blocks + i + 1]
        scale = lax.rsqrt(noise * (members - 1.0))
        at = slice(i * per_patch, (i + 1) * per_patch)
        for part, (_, _, start) in zip(rows, pieces[i]):
            size = part.shape[1]
            lanes = slice(start * size, (start + 1) * size)
            sh_ref[at, lanes], sl_ref[at, lanes] = split((part - mean) * scale)
        shift = (upright[0:per_patch, i : i + 1] - mean) * scale
        d_ref[at, :] = jnp.broadcast_to(shift, (per_patch, d_ref.shape[1]))

    n = sh_ref.shape[0]
    head = min(TILE, n)
    tail = n - head
    chunks = [(i, min(i + chunk, n)) for i in range(0, n, chunk)]
    first = head // per_patch
    for i in range(first):
        scaled(i)
    left = (sh_ref[0:head], sl_ref[0:head])
    rest = list(range(first, blocks))
    for start, stop in chunks:
        if stop <= head:
            if rest:
                scaled(rest.pop(0))
        else:
            while rest:
                scaled(rest.pop(0))
        g_ref[start:stop, 0:head] = dot3((sh_ref[start:stop], sl_ref[start:stop]), left, NT)
    low = (sh_ref[head:n], sl_ref[head:n])
    g_ref[head:n, head:n] = dot3(low, low, NT)
    g_ref[0:head, head:n] = jnp.transpose(g_ref[head:n, 0:head])
    g = g_ref[...]
    square = jnp.sum(jnp.sum(g * g, axis=0, keepdims=True), axis=1, keepdims=True)
    norm = jnp.sqrt(square) * (1.0 + 1e-5)
    size = square[0, 0]
    limits = step_limits()
    pairs = jnp.int32(0)
    for k in range(7, MOST_STEPS - 2, 2):
        limit = limits[k] * (1.0 - 1e-4)
        pairs = pairs + (size > limit * limit).astype(jnp.int32)
    n_ref[0] = (size > 1.6e7).astype(jnp.int32) + (size > 1e8).astype(jnp.int32)
    eye_ref[...] = diagonal(n, n, 0).astype(F32)
    eye = eye_ref[...]
    first = 2.0 / (2.0 + norm)
    rho = norm * (0.5 * first)
    rho2 = rho * rho
    weight = 2.0 / (2.0 - rho2)
    keep = 0.5 * rho2 * weight
    r = (1.0 - first) * eye - first * g
    parts = split(r)
    x = (weight * first) * (eye + r)
    x_ref[...] = x
    for i, part in enumerate(split(x)):
        wa[i, :, n : 2 * n] = part

    def store(targets, start, left, corner):
        blocks = [(slice(0, n), slice(start, start + head), left)]
        blocks.append((slice(head, n), slice(start + head, start + n), corner))
        blocks.append((slice(0, head), slice(start + head, start + n), jnp.transpose(left[head:n])))
        for rows, columns, block in blocks:
            for target, part in zip(targets, split(block)):
                target[rows, columns] = part

    def corner_of(weight, keep, left, corner):
        left = weight * left - keep * eye_ref[:, 0:head]
        return left, weight * corner - keep * eye_ref[head:n, head:n]

    left = dot3(parts, [part[:, 0:head] for part in parts])
    corner = dot3([part[head:n] for part in parts], [part[:, head:n] for part in parts])
    store((wa.at[0], wa.at[1]), 0, *corner_of(weight, keep, left, corner))

    def advance(source, target, rho2):
        weight = 2.0 / (2.0 - rho2)
        keep = 0.5 * rho2 * weight
        parts = (source[0, :, 0:n], source[1, :, 0:n])
        ends = [jnp.concatenate([source[i, :, head:n], source[i, :, n + head : 2 * n]], axis=1) for i in (0, 1)]
        left = dot3(parts, (source[0, :, 0:head], source[1, :, 0:head]))
        corners = dot3([part[head:n] for part in parts], ends)
        both = (target.at[0], target.at[1])
        store(both, 0, *corner_of(weight, keep, left, corners[:, 0:tail]))
        left = dot3(parts, (source[0, :, n : n + head], source[1, :, n : n + head]))
        left = weight * (x_ref[:, 0:head] + left)
        corner = weight * (x_ref[head:n, head:n] + corners[:, tail : 2 * tail])
        x_ref[:, 0:head] = left
        x_ref[head:n, head:n] = corner
        store(both, n, left, corner)
        return keep * keep

    rho2 = keep * keep

    def sides(source, span):
        return [source[i, span[0] : span[1], 0:n] for i in (0, 1)]

    def put(targets, start, span, block):
        for target, part in zip(targets, split(block)):
            target[span[0] : span[1], start : start + head] = part
        low = max(span[0], head)
        if low < span[1]:
            for target, part in zip(targets, split(jnp.transpose(block[low - span[0] :]))):
                target[0:head, start + low : start + span[1]] = part

    def put_corner(targets, start, block):
        for target, part in zip(targets, split(block)):
            target[head:n, start + head : start + n] = part

    def put_x(targets, start, weight, span, product):
        x = weight * (x_ref[span[0] : span[1], 0:head] + product)
        x_ref[span[0] : span[1], 0:head] = x
        put(targets, start, span, x)

    def put_x_corner(targets, start, weight, product):
        x = weight * (x_ref[head:n, head:n] + product)
        x_ref[head:n, head:n] = x
        put_corner(targets, start, x)

    waiting = None
    source, target = wa, wb
    for _ in range(5):
        weight = 2.0 / (2.0 - rho2)
        keep = 0.5 * rho2 * weight
        first = (source[0, :, 0:head], source[1, :, 0:head])
        r = []
        for k, span in enumerate(chunks):
            r.append(dot3(sides(source, span), first))
            if waiting is not None:
                put_x((source.at[0], source.at[1]), n, waiting[0], span, waiting[1][k])
        if waiting is not None:
            put_x_corner((source.at[0], source.at[1]), n, waiting[0], waiting[2])
        ends = [jnp.concatenate([source[i, :, head:n], source[i, :, n + head : 2 * n]], axis=1) for i in (0, 1)]
        corners = dot3(sides(source, (head, n)), ends)
        first = (source[0, :, n : n + head], source[1, :, n : n + head])
        both = (target.at[0], target.at[1])
        x = []
        for k, span in enumerate(chunks):
            x.append(dot3(sides(source, span), first))
            put(both, 0, span, weight * r[k] - keep * eye_ref[span[0] : span[1], 0:head])
        put_corner(both, 0, weight * corners[:, 0:tail] - keep * eye_ref[head:n, head:n])
        waiting = (weight, x, corners[:, tail : 2 * tail])
        rho2 = keep * keep
        source, target = target, source
    for k, span in enumerate(chunks):
        put_x((source.at[0], source.at[1]), n, waiting[0], span, waiting[1][k])
    put_x_corner((source.at[0], source.at[1]), n, waiting[0], waiting[2])

    def twice(_, rho2):
        return advance(target, source, advance(source, target, rho2))

    rho2 = lax.fori_loop(0, pairs, twice, rho2)
    weight = 2.0 / (2.0 - rho2)
    first = (source[0, :, n : n + head], source[1, :, n : n + head])
    done = (xh_ref, xl_ref)
    ends = [source[i, :, n + head : 2 * n] for i in (0, 1)]
    put_x_corner(done, 0, weight, dot3(sides(source, (head, n)), ends))
    x = [dot3(sides(source, span), first) for span in chunks]
    for k, span in enumerate(chunks):
        put_x(done, 0, weight, span, x[k])


def centred(fields):
    members = sum(field.shape[0] for field in fields)
    mean = sum(jnp.sum(field, axis=0, keepdims=True) for field in fields) * (1.0 / members)
    pairs = [split(field - mean) for field in fields]
    return [jnp.concatenate(parts, axis=0) for parts in zip(*pairs)], mean


def in_chunks(count, product, work):
    waiting = None
    for start in range(0, count, CHUNK):
        span = slice(start, min(start + CHUNK, count))
        result = product(span)
        if waiting is not None:
            work(*waiting)
        waiting = (span, result)
    work(*waiting)


def solve(n_ref, s, g_ref, x, anomaly, z_ref, cross_ref, parts_ref):
    n = z_ref.shape[0]

    def keep(slot, span, value):
        for i, part in enumerate(split(value)):
            parts_ref[slot, i, span] = part

    def kept(slot):
        return parts_ref[slot, 0], parts_ref[slot, 1]

    def some(parts, span):
        return [part[span] for part in parts]

    def crossed(span, value):
        cross_ref[span] = value
        keep(0, span, value)

    def solved(span, value):
        z_ref[span] = value
        keep(1, span, value)

    def left(span, value):
        keep(0, span, cross_ref[span] - z_ref[span] - value)

    def refined(span, value):
        z_ref[span] = z_ref[span] + value

    in_chunks(n, lambda span: dot3(some(s, span), anomaly), crossed)
    in_chunks(n, lambda span: dot3(some(x, span), kept(0)), solved)
    in_chunks(n, lambda span: dot3(split(g_ref[span]), kept(1)), left)
    in_chunks(n, lambda span: dot3(some(x, span), kept(0)), refined)

    def refine(_, carry):
        z = z_ref[...]
        gz = lax.dot_general(g_ref[...], z, NN, precision=HIGHEST, preferred_element_type=F32)
        z_ref[...] = z + dot3([part[...] for part in x], split(cross_ref[...] - z - gz))
        return carry

    lax.fori_loop(0, n_ref[0], refine, 0)


def gain_kernel(batch, parts, own_of, place_ref, n_ref, cells_ref, sh_ref, sl_ref, d_ref, g_ref, xh_ref, xl_ref, *refs):
    states = refs[:parts]
    z_ref, rows_ref, scratch, cross_ref, parts_ref = refs[parts:]
    anomaly, mean = centred([state[...] for state in states])
    solve(n_ref, (sh_ref, sl_ref), g_ref, (xh_ref, xl_ref), anomaly, z_ref, cross_ref, parts_ref)
    s = (sh_ref[...], sl_ref[...])
    picks = cells_ref[pl.ds(own_of(place_ref), 1), batch, :]
    hot = selector(picks, mean.shape[1], scratch)
    zt = split(select(hot, split(z_ref[...]), NT))
    base = jnp.sum(hot * mean, axis=1, keepdims=True) + dot3(zt, split(d_ref[...]))[:, 0:1]
    rows_ref[...] = base + select(hot, anomaly, NT) - 0.5 * dot3(zt, s)


def updated(field, start, s, shift, z):
    size = field.shape[0]
    return field + shift - 0.5 * dot3([h[:, start : start + size] for h in s], z, TN)


def shift_of(z, d_ref):
    return jnp.sum(z * d_ref[:, 0:1], axis=0, keepdims=True)


def update_kernel(starts, sh_ref, sl_ref, d_ref, z_ref, *refs):
    count = len(starts)
    states, outs, parts = refs[:count], refs[count : 2 * count], refs[2 * count :]
    z = z_ref[...]
    shift = shift_of(z, d_ref)
    s, zs = (sh_ref[...], sl_ref[...]), split(z)
    for start, state, out in zip(starts, states, outs):
        out[...] = updated(state[...], start, s, shift, zs)
    if parts:
        anomaly, _ = centred([out[...] for out in outs])
        for ref, part in zip(parts, anomaly):
            ref[...] = part


def last_kernel(n_ref, sh_ref, sl_ref, d_ref, g_ref, xh_ref, xl_ref, *refs):
    (state_ref, *parts), (z_ref, out_ref, cross_ref, parts_ref) = refs[:-4], refs[-4:]
    anomaly = [part[...] for part in parts] if parts else centred([state_ref[...]])[0]
    solve(n_ref, (sh_ref, sl_ref), g_ref, (xh_ref, xl_ref), anomaly, z_ref, cross_ref, parts_ref)
    z = z_ref[...]
    start = sh_ref.shape[1] - state_ref.shape[0]
    s = (sh_ref[...], sl_ref[...])
    out_ref[...] = updated(state_ref[...], start, s, shift_of(z, d_ref), split(z))


def join_kernel(place_ref, mine_ref, theirs_ref, out_ref, both, sems):
    chunks = sems.shape[0]
    size = both.shape[0] // chunks
    column = place_ref[1]
    copies = []
    for i in range(chunks):
        at = slice(i * size, (i + 1) * size)
        mine, theirs = mine_ref[at, :], theirs_ref[at, :]
        both[at, 0, :] = jnp.where(column == 0, mine, theirs)
        both[at, 1, :] = jnp.where(column == 0, theirs, mine)
        span = pl.ds(i * size, size)
        copies.append(pltpu.make_async_copy(both.at[span], out_ref.at[span], sems.at[i]))
        copies[-1].start()
    for copy in copies:
        copy.wait()


def factor(pieces, batch, members, chunk, patches_of, place, near, values, var, sources):
    per_patch = values.shape[2]
    n = len(pieces) * per_patch
    outs = [
        ((n, members), BF16, VMEM),
        ((n, members), BF16, VMEM),
        ((n, 128), F32, VMEM),
        ((n, n), F32, VMEM),
        ((n, n), BF16, VMEM),
        ((n, n), BF16, VMEM),
        ((1,), jnp.int32, SMEM),
    ]
    scratch = [
        pltpu.VMEM((128, 128), F32),
        pltpu.VMEM((n, n), F32),
        pltpu.VMEM((n, n), F32),
        pltpu.VMEM((2, n, 2 * n), BF16),
        pltpu.VMEM((2, n, 2 * n), BF16),
    ]
    kernel = functools.partial(factor_kernel, pieces, batch, members, chunk, patches_of)
    args = [place, near, values, var, *sources]
    flops = 6 * n * n * members + 60 * n * n * n
    return call(kernel, outs, [SMEM, SMEM] + [VMEM] * (2 + len(sources)), args, scratch, flops, FACTOR_LIMIT)


def solver_scratch(n, width):
    return [pltpu.VMEM((n, width), F32), pltpu.VMEM((2, 2, n, width), BF16)]


def gain(batch, own_of, place, cells, factored, states):
    sh, sl, d, g, xh, xl, more = factored
    n, members = sh.shape
    width = states[0].shape[1]
    kernel = functools.partial(gain_kernel, batch, len(states), own_of)
    outs = [((n, width), F32, VMEM), ((cells.shape[2], members), F32, VMEM)]
    ins = [SMEM, SMEM] + [VMEM] * (7 + len(states))
    args = [place, more, cells, sh, sl, d, g, xh, xl, *states]
    flops = 8 * n * members * width
    scratch = [pltpu.VMEM((8, 128), jnp.int32)] + solver_scratch(n, width)
    return call(kernel, outs, ins, args, scratch, flops)


def update(factored, z, states, starts, more=False):
    sh, sl, d = factored[:3]
    kernel = functools.partial(update_kernel, starts)
    outs = [(state.shape, F32, VMEM) for state in states]
    if more:
        outs += [((sh.shape[1], z.shape[1]), BF16, VMEM)] * 2
    flops = 6 * sh.shape[0] * sh.shape[1] * z.shape[1]
    return call(kernel, outs, [VMEM] * (4 + len(states)), [sh, sl, d, z, *states], (), flops)


def last(factored, state, anomaly=()):
    sh, sl, d, g, xh, xl, more = factored
    n, width = sh.shape[0], state.shape[1]
    outs = [((n, width), F32, VMEM), (state.shape, F32, VMEM)]
    args = [more, sh, sl, d, g, xh, xl, state, *anomaly]
    flops = 12 * sh.shape[0] * sh.shape[1] * width
    ins = [SMEM] + [VMEM] * (len(args) - 1)
    return call(last_kernel, outs, ins, args, solver_scratch(n, width), flops)


def rings(size):
    up = [(i, (i + 1) % size) for i in range(size)]
    return up, [(j, i) for i, j in up]


BOTH = ("region", "member")


def permute(x, moves, regions):
    table = []
    for region in range(regions):
        for column in range(2):
            pair, parity, to = moves(region // 2, region % 2, column)
            pair %= regions // 2
            table.append((region * 2 + column, (pair * 2 + parity) * 2 + to))
    return lax.ppermute(x, BOTH, table)


def paired(state, neighbours, obs_cell, obs_values, obs_var):
    half, _, cells = state.shape
    members = 2 * half
    regions = lax.axis_size("region")
    region, column = lax.axis_index("region"), lax.axis_index("member")
    place = jnp.stack([region, column]).astype(jnp.int32)
    near = neighbours.T

    def own_of(place_ref):
        return place_ref[0] * 2 + place_ref[1]

    def around(place_ref, within):
        region = place_ref[0]
        side = 2 * lax.rem(region, 2) - 1
        outer = lax.rem(region + regions + side, regions)
        return [r * 2 + p for r in (region, region - side, outer) for p in within], own_of(place_ref)

    def patches_first(place_ref):
        return around(place_ref, (0, 1))

    def patches_next(place_ref):
        return around(place_ref, (place_ref[1], 1 - place_ref[1]))

    def across(x):
        return permute(x, lambda c, q, m: (c, q, 1 - m), regions)

    def beside(x):
        return permute(x, lambda c, q, m: (c, 1 - q, m), regions)

    def outside(x):
        return permute(x, lambda c, q, m: (c + 2 * q - 1, 1 - q, m), regions)

    anywhere = pl.BlockSpec(memory_space=pl.ANY)
    (rows,) = call(
        pick_kernel,
        [((2, obs_cell.shape[2], half), F32, VMEM)],
        [SMEM, VMEM, VMEM],
        [place, obs_cell, state],
        [pltpu.VMEM((8, 128), jnp.int32), pltpu.VMEM((2, half, cells), F32)],
    )
    other = across(rows)
    sources = [rows, beside(rows), outside(rows), other, beside(other), outside(other)]
    shape = ((half, cells), F32, VMEM)
    keep, send, values, var = call(
        sort_kernel,
        [shape, shape, (obs_values.shape, F32, VMEM), (obs_var.shape, F32, VMEM)],
        [SMEM, anywhere, anywhere, VMEM, anywhere],
        [place, obs_values, obs_var, state, other],
        [pltpu.SemaphoreType.DMA((2,))],
    )
    pieces = [[(i, (p,), 0), (3 + i, (p,), 1)] for i in range(3) for p in range(2)]
    states = [keep, across(send)]
    factored = factor(pieces, 0, members, CHUNK, patches_first, place, near, values, var, sources)
    everything = slice(None)
    low, high = (everything, slice(0, half)), (everything, slice(half, members))
    pieces = []
    for i in range(3):
        pieces += [[(i, low, 0), (i, high, 1)], [(3 + i, high, 0), (3 + i, low, 1)]]
    for batch in range(1, NBATCH):
        z, rows = gain(batch, own_of, place, obs_cell, factored, states)
        other = across(rows)
        sources = [rows, beside(rows), outside(rows), other, beside(other), outside(other)]
        mine, theirs, *anomaly = update(factored, z, states, (0, half), True)
        states = [mine, theirs]
        factored = factor(pieces, batch, members, CHUNK // 2, patches_next, place, near, values, var, sources)
    z, theirs = last(factored, states[1], anomaly)
    theirs = across(theirs)
    (mine,) = update(factored, z, states[:1], (0,))
    return pl.pallas_call(
        join_kernel,
        out_shape=jax.ShapeDtypeStruct(state.shape, F32),
        in_specs=[SMEM, VMEM, VMEM],
        out_specs=anywhere,
        scratch_shapes=[pltpu.VMEM(state.shape, F32), pltpu.SemaphoreType.DMA((4,))],
        compiler_params=pltpu.CompilerParams(vmem_limit_bytes=16 * 1024 * 1024),
    )(place, mine, theirs)


def listed(table_ref):
    blocks = table_ref.shape[0] - 1
    return [table_ref[i] for i in range(blocks)], table_ref[blocks]


def general(state, neighbours, obs_cell, obs_values, obs_var):
    ensemble = lax.all_to_all(state, "member", split_axis=1, concat_axis=0, tiled=True)
    members, owned, cells = ensemble.shape
    regions = lax.axis_size("region")
    region_patches = owned * lax.axis_size("member")
    region = lax.axis_index("region")
    first = region * region_patches + lax.axis_index("member") * owned
    up, down = rings(regions)
    fields = [ensemble[:, p, :] for p in range(owned)]
    grid = jnp.arange(cells, dtype=jnp.int32)
    for batch in range(NBATCH):
        picks = lax.dynamic_slice_in_dim(obs_cell, first, owned, 0)[:, batch, :]
        hot = (picks[:, :, None] == grid[None, None, :]).astype(F32)
        own_rows = jnp.einsum("poc,pkc->pok", hot, jnp.stack(fields), precision=HIGHEST)
        region_rows = lax.all_gather(own_rows, "member", axis=0, tiled=True)
        before = lax.ppermute(region_rows, "region", up)
        after = lax.ppermute(region_rows, "region", down)
        beside = jnp.concatenate([before, region_rows, after], axis=0)
        new = []
        for p in range(owned):
            own = first + p
            links = lax.dynamic_index_in_dim(neighbours, own, 0, keepdims=False)
            ids = jnp.concatenate([own[None], links]).astype(jnp.int32)
            table = jnp.concatenate([ids, own[None]]).astype(jnp.int32)
            home = (ids // region_patches - region + 1) % regions
            rows = jnp.take(beside, home * region_patches + ids % region_patches, axis=0)
            pieces = [[(0, (i,), 0)] for i in range(ids.shape[0])]
            factored = factor(
                pieces, batch, members, CHUNK, listed, table, neighbours.T, obs_values, obs_var, [rows]
            )
            new.append(last(factored, fields[p])[1])
        fields = new
    ensemble = jnp.stack(fields, axis=1)
    return lax.all_to_all(ensemble, "member", split_axis=0, concat_axis=1, tiled=True)


def on_device(state, neighbours, obs_cell, obs_values, obs_var):
    patches, links = state.shape[1], neighbours.shape[1]
    even = lax.axis_size("region") % 2 == 0
    if even and patches == 2 and lax.axis_size("member") == 2 and links + 1 == 3 * patches:
        return paired(state, neighbours, obs_cell, obs_values, obs_var)
    return general(state, neighbours, obs_cell, obs_values, obs_var)


def solution(mesh):
    in_specs = (P("member", "region", None), P(), P(), P(), P())
    out_specs = P("member", "region", None)
    return jax.shard_map(
        on_device, mesh=mesh, in_specs=in_specs, out_specs=out_specs, check_vma=False
    )
```

```python
import functools
import math

import jax
import jax.numpy as jnp
from jax import lax
from jax.experimental import pallas as pl
from jax.experimental.pallas import tpu as pltpu
from jax.sharding import PartitionSpec as P

NBATCH = 2
HIGHEST = lax.Precision.HIGHEST
F32 = jnp.float32
BF16 = jnp.bfloat16
VMEM = pl.BlockSpec(memory_space=pltpu.VMEM)
SMEM = pl.BlockSpec(memory_space=pltpu.SMEM)
NN = (((1,), (0,)), ((), ()))
NT = (((1,), (1,)), ((), ()))
TN = (((0,), (0,)), ((), ()))
RESIDUAL = 1e-3
FACTOR_LIMIT = 24
MOST_STEPS = 15
TILE = 256
CHUNK = 128


def call(kernel, outs, ins, args, scratch=(), flops=0, limit=16):
    shapes = [jax.ShapeDtypeStruct(shape, dtype) for shape, dtype, _ in outs]
    moved = sum(math.prod(s.shape) * s.dtype.itemsize for s in shapes)
    moved += sum(a.size * a.dtype.itemsize for a in args)
    return pl.pallas_call(
        kernel,
        out_shape=shapes,
        in_specs=ins,
        out_specs=[space for _, _, space in outs],
        scratch_shapes=list(scratch),
        compiler_params=pltpu.CompilerParams(vmem_limit_bytes=limit * 1024 * 1024),
        cost_estimate=pl.CostEstimate(flops=flops, bytes_accessed=moved, transcendentals=0),
    )(*args)


def split(x):
    high = x.astype(BF16)
    return high, (x - high.astype(F32)).astype(BF16)


def dot(a, b, dims=NN):
    return lax.dot_general(a, b, dims, preferred_element_type=F32)


def dot3(a, b, dims=NN):
    (left,), (right,) = dims[0]
    lhs = jnp.concatenate([a[0], a[0], a[1]], axis=left)
    rhs = jnp.concatenate([b[0], b[1], b[0]], axis=right)
    return dot(lhs, rhs, dims)


def select(hot, parts, dims):
    (left,), (right,) = dims[0]
    hot = hot.astype(BF16)
    lhs = jnp.concatenate([hot] * len(parts), axis=left)
    return dot(lhs, jnp.concatenate(parts, axis=right), dims)


def split_all(x):
    high, middle = split(x)
    low = x - high.astype(F32) - middle.astype(F32)
    return high, middle, low.astype(BF16)


def step_limits():
    limits = []
    for steps in range(MOST_STEPS):
        rho = RESIDUAL
        for _ in range(steps):
            rho = math.sqrt(2.0 * rho / (1.0 + rho))
        limits.append(2.0 * rho / (1.0 - rho) if rho < 1.0 else math.inf)
    return limits


def diagonal(n, columns, first):
    row = lax.broadcasted_iota(jnp.int32, (n, columns), 0)
    column = lax.broadcasted_iota(jnp.int32, (n, columns), 1)
    return row + first == column


def selector(picks, cells, scratch):
    per_patch = picks.shape[1]
    scratch[...] = jnp.full_like(scratch, -1)
    scratch[0:1, 0:per_patch] = picks
    grid = lax.broadcasted_iota(jnp.int32, (cells, scratch.shape[1]), 0)
    hot = (grid == scratch[0:1, :]).astype(F32)
    return jnp.transpose(hot)[0:per_patch, :]


def pick_kernel(region_ref, cells_ref, state_ref, rows_ref, scratch, field_ref):
    patches, cells = state_ref.shape[1:]
    for p in range(patches):
        field_ref[p] = state_ref[:, p, :]
        hot = selector(cells_ref[pl.ds(region_ref[0] * patches + p, 1), 0, :], cells, scratch)
        rows_ref[p] = select(hot, split_all(field_ref[p]), NT)


def sort_kernel(column_ref, values_hbm, var_hbm, state_ref, *refs):
    keep_ref, send_ref, values_ref, var_ref, sems = refs[-5:]
    copies = [
        pltpu.make_async_copy(values_hbm, values_ref, sems.at[0]),
        pltpu.make_async_copy(var_hbm, var_ref, sems.at[1]),
    ]
    for copy in copies:
        copy.start()
    column = column_ref[0]
    first, second = state_ref[:, 0, :], state_ref[:, 1, :]
    keep_ref[...] = jnp.where(column == 0, first, second)
    send_ref[...] = jnp.where(column == 0, second, first)
    for copy in copies:
        copy.wait()


def factor_kernel(pieces, batch, members, chunk, patches_of, places, *refs):
    place_refs, refs = refs[:places], refs[places:]
    near_ref, values_ref, var_ref, *refs = refs
    count = len(refs) - 12
    sources = refs[:count]
    sh_ref, sl_ref, d_ref, g_ref, xh_ref, xl_ref, n_ref, flat, eye_ref, x_ref, wa, wb = refs[count:]
    per_patch = values_ref.shape[2]
    flat[...] = jnp.ones_like(flat)
    blocks = len(pieces)
    ids, own = patches_of(*place_refs)
    for i in range(blocks):
        patch = ids[i]
        widening = (patch == own).astype(jnp.int32)
        for j in range(near_ref.shape[0]):
            widening = widening + (near_ref[j, own] == patch).astype(jnp.int32) * (j + 2)
        flat[i : i + 1, 0:per_patch] = values_ref[pl.ds(patch, 1), batch, :]
        noise = var_ref[pl.ds(patch, 1), batch, :] * widening.astype(F32)
        flat[blocks + i : blocks + i + 1, 0:per_patch] = noise
    upright = jnp.transpose(flat[...])

    def scaled(i):
        rows = [sources[which][index] for which, index, _ in pieces[i]]
        total = sum(jnp.sum(part, axis=1, keepdims=True) for part in rows)
        mean = total * (1.0 / members)
        noise = upright[0:per_patch, blocks + i : blocks + i + 1]
        scale = lax.rsqrt(noise * (members - 1.0))
        at = slice(i * per_patch, (i + 1) * per_patch)
        for part, (_, _, start) in zip(rows, pieces[i]):
            size = part.shape[1]
            lanes = slice(start * size, (start + 1) * size)
            sh_ref[at, lanes], sl_ref[at, lanes] = split((part - mean) * scale)
        shift = (upright[0:per_patch, i : i + 1] - mean) * scale
        d_ref[at, :] = jnp.broadcast_to(shift, (per_patch, d_ref.shape[1]))

    n = sh_ref.shape[0]
    head = min(TILE, n)
    tail = n - head
    chunks = [(i, min(i + chunk, n)) for i in range(0, n, chunk)]
    first = head // per_patch
    for i in range(first):
        scaled(i)
    left = (sh_ref[0:head], sl_ref[0:head])
    for i in range(first, blocks):
        scaled(i)
    g_ref[:, 0:head] = dot3((sh_ref[...], sl_ref[...]), left, NT)
    low = (sh_ref[head:n], sl_ref[head:n])
    g_ref[head:n, head:n] = dot3(low, low, NT)
    g_ref[0:head, head:n] = jnp.transpose(g_ref[head:n, 0:head])
    g = g_ref[...]
    square = jnp.sum(jnp.sum(g * g, axis=0, keepdims=True), axis=1, keepdims=True)
    norm = jnp.sqrt(square) * (1.0 + 1e-5)
    size = square[0, 0]
    limits = step_limits()
    pairs = jnp.int32(0)
    for k in range(7, MOST_STEPS - 2, 2):
        limit = limits[k] * (1.0 - 1e-4)
        pairs = pairs + (size > limit * limit).astype(jnp.int32)
    n_ref[0] = (size > 1.6e7).astype(jnp.int32) + (size > 1e8).astype(jnp.int32)
    eye_ref[...] = diagonal(n, n, 0).astype(F32)
    eye = eye_ref[...]
    first = 2.0 / (2.0 + norm)
    rho = norm * (0.5 * first)
    rho2 = rho * rho
    weight = 2.0 / (2.0 - rho2)
    keep = 0.5 * rho2 * weight
    r = (1.0 - first) * eye - first * g
    parts = split(r)
    x = (weight * first) * (eye + r)
    x_ref[...] = x
    for i, part in enumerate(split(x)):
        wa[i, :, n : 2 * n] = part

    def store(targets, start, left, corner):
        blocks = [(slice(0, n), slice(start, start + head), left)]
        blocks.append((slice(head, n), slice(start + head, start + n), corner))
        blocks.append((slice(0, head), slice(start + head, start + n), jnp.transpose(left[head:n])))
        for rows, columns, block in blocks:
            for target, part in zip(targets, split(block)):
                target[rows, columns] = part

    def corner_of(weight, keep, left, corner):
        left = weight * left - keep * eye_ref[:, 0:head]
        return left, weight * corner - keep * eye_ref[head:n, head:n]

    left = dot3(parts, [part[:, 0:head] for part in parts])
    corner = dot3([part[head:n] for part in parts], [part[:, head:n] for part in parts])
    store((wa.at[0], wa.at[1]), 0, *corner_of(weight, keep, left, corner))

    def advance(source, target, rho2):
        weight = 2.0 / (2.0 - rho2)
        keep = 0.5 * rho2 * weight
        parts = (source[0, :, 0:n], source[1, :, 0:n])
        ends = [jnp.concatenate([source[i, :, head:n], source[i, :, n + head : 2 * n]], axis=1) for i in (0, 1)]
        left = dot3(parts, (source[0, :, 0:head], source[1, :, 0:head]))
        corners = dot3([part[head:n] for part in parts], ends)
        both = (target.at[0], target.at[1])
        store(both, 0, *corner_of(weight, keep, left, corners[:, 0:tail]))
        left = dot3(parts, (source[0, :, n : n + head], source[1, :, n : n + head]))
        left = weight * (x_ref[:, 0:head] + left)
        corner = weight * (x_ref[head:n, head:n] + corners[:, tail : 2 * tail])
        x_ref[:, 0:head] = left
        x_ref[head:n, head:n] = corner
        store(both, n, left, corner)
        return keep * keep

    rho2 = keep * keep

    def sides(source, span):
        return [source[i, span[0] : span[1], 0:n] for i in (0, 1)]

    def put(targets, start, span, block):
        for target, part in zip(targets, split(block)):
            target[span[0] : span[1], start : start + head] = part
        low = max(span[0], head)
        if low < span[1]:
            for target, part in zip(targets, split(jnp.transpose(block[low - span[0] :]))):
                target[0:head, start + low : start + span[1]] = part

    def put_corner(targets, start, block):
        for target, part in zip(targets, split(block)):
            target[head:n, start + head : start + n] = part

    def put_x(targets, start, weight, span, product):
        x = weight * (x_ref[span[0] : span[1], 0:head] + product)
        x_ref[span[0] : span[1], 0:head] = x
        put(targets, start, span, x)

    def put_x_corner(targets, start, weight, product):
        x = weight * (x_ref[head:n, head:n] + product)
        x_ref[head:n, head:n] = x
        put_corner(targets, start, x)

    waiting = None
    source, target = wa, wb
    for _ in range(5):
        weight = 2.0 / (2.0 - rho2)
        keep = 0.5 * rho2 * weight
        first = (source[0, :, 0:head], source[1, :, 0:head])
        r = []
        for k, span in enumerate(chunks):
            r.append(dot3(sides(source, span), first))
            if waiting is not None:
                put_x((source.at[0], source.at[1]), n, waiting[0], span, waiting[1][k])
        if waiting is not None:
            put_x_corner((source.at[0], source.at[1]), n, waiting[0], waiting[2])
        ends = [jnp.concatenate([source[i, :, head:n], source[i, :, n + head : 2 * n]], axis=1) for i in (0, 1)]
        corners = dot3(sides(source, (head, n)), ends)
        first = (source[0, :, n : n + head], source[1, :, n : n + head])
        both = (target.at[0], target.at[1])
        x = []
        for k, span in enumerate(chunks):
            x.append(dot3(sides(source, span), first))
            put(both, 0, span, weight * r[k] - keep * eye_ref[span[0] : span[1], 0:head])
        put_corner(both, 0, weight * corners[:, 0:tail] - keep * eye_ref[head:n, head:n])
        waiting = (weight, x, corners[:, tail : 2 * tail])
        rho2 = keep * keep
        source, target = target, source
    for k, span in enumerate(chunks):
        put_x((source.at[0], source.at[1]), n, waiting[0], span, waiting[1][k])
    put_x_corner((source.at[0], source.at[1]), n, waiting[0], waiting[2])

    def twice(_, rho2):
        return advance(target, source, advance(source, target, rho2))

    rho2 = lax.fori_loop(0, pairs, twice, rho2)
    weight = 2.0 / (2.0 - rho2)
    first = (source[0, :, n : n + head], source[1, :, n : n + head])
    done = (xh_ref, xl_ref)
    ends = [source[i, :, n + head : 2 * n] for i in (0, 1)]
    put_x_corner(done, 0, weight, dot3(sides(source, (head, n)), ends))
    x = [dot3(sides(source, span), first) for span in chunks]
    for k, span in enumerate(chunks):
        put_x(done, 0, weight, span, x[k])


def centred(fields):
    members = sum(field.shape[0] for field in fields)
    mean = sum(jnp.sum(field, axis=0, keepdims=True) for field in fields) * (1.0 / members)
    pairs = [split(field - mean) for field in fields]
    return [jnp.concatenate(parts, axis=0) for parts in zip(*pairs)], mean


def in_chunks(count, product, work):
    waiting = None
    for start in range(0, count, CHUNK):
        span = slice(start, min(start + CHUNK, count))
        result = product(span)
        if waiting is not None:
            work(*waiting)
        waiting = (span, result)
    work(*waiting)


def solve(n_ref, s, g_ref, x, anomaly, z_ref, cross_ref, parts_ref):
    n = z_ref.shape[0]

    def keep(slot, span, value):
        for i, part in enumerate(split(value)):
            parts_ref[slot, i, span] = part

    def kept(slot):
        return parts_ref[slot, 0], parts_ref[slot, 1]

    def some(parts, span):
        return [part[span] for part in parts]

    def crossed(span, value):
        cross_ref[span] = value
        keep(0, span, value)

    def solved(span, value):
        z_ref[span] = value
        keep(1, span, value)

    def left(span, value):
        keep(0, span, cross_ref[span] - z_ref[span] - value)

    def refined(span, value):
        z_ref[span] = z_ref[span] + value

    in_chunks(n, lambda span: dot3(some(s, span), [part[...] for part in anomaly]), crossed)
    in_chunks(n, lambda span: dot3(some(x, span), kept(0)), solved)
    in_chunks(n, lambda span: dot3(split(g_ref[span]), kept(1)), left)
    in_chunks(n, lambda span: dot3(some(x, span), kept(0)), refined)

    def refine(_, carry):
        z = z_ref[...]
        gz = lax.dot_general(g_ref[...], z, NN, precision=HIGHEST, preferred_element_type=F32)
        z_ref[...] = z + dot3([part[...] for part in x], split(cross_ref[...] - z - gz))
        return carry

    lax.fori_loop(0, n_ref[0], refine, 0)


def gain_kernel(batch, parts, own_of, region_ref, column_ref, n_ref, cells_ref, sh_ref, sl_ref, d_ref, g_ref, *refs):
    xh_ref, xl_ref, *refs = refs
    states = refs[:parts]
    z_ref, rows_ref, scratch, anomaly_ref, cross_ref, parts_ref = refs[parts:]
    anomaly, mean = centred([state[...] for state in states])
    for i, part in enumerate(anomaly):
        anomaly_ref[i] = part
    anomaly = (anomaly_ref.at[0], anomaly_ref.at[1])
    solve(n_ref, (sh_ref, sl_ref), g_ref, (xh_ref, xl_ref), anomaly, z_ref, cross_ref, parts_ref)
    s = (sh_ref[...], sl_ref[...])
    picks = cells_ref[pl.ds(own_of(region_ref, column_ref), 1), batch, :]
    hot = selector(picks, mean.shape[1], scratch)
    zt = split(select(hot, split(z_ref[...]), NT))
    base = jnp.sum(hot * mean, axis=1, keepdims=True) + dot3(zt, split(d_ref[...]))[:, 0:1]
    picked = select(hot, [part[...] for part in anomaly], NT)
    rows_ref[...] = base + picked - 0.5 * dot3(zt, s)


def updated(field, start, s, shift, z):
    size = field.shape[0]
    return field + shift - 0.5 * dot3([h[:, start : start + size] for h in s], z, TN)


def shift_of(z, d_ref):
    return jnp.sum(z * d_ref[:, 0:1], axis=0, keepdims=True)


def update_kernel(starts, sh_ref, sl_ref, d_ref, z_ref, *refs):
    count = len(starts)
    states, outs, parts = refs[:count], refs[count : 2 * count], refs[2 * count :]
    z = z_ref[...]
    shift = shift_of(z, d_ref)
    s, zs = (sh_ref[...], sl_ref[...]), split(z)
    for start, state, out in zip(starts, states, outs):
        out[...] = updated(state[...], start, s, shift, zs)
    if parts:
        anomaly, _ = centred([out[...] for out in outs])
        for ref, part in zip(parts, anomaly):
            ref[...] = part


def last_kernel(n_ref, sh_ref, sl_ref, d_ref, g_ref, xh_ref, xl_ref, *refs):
    (state_ref, *parts), (z_ref, out_ref, cross_ref, parts_ref) = refs[:-4], refs[-4:]
    anomaly = parts or centred([state_ref[...]])[0]
    solve(n_ref, (sh_ref, sl_ref), g_ref, (xh_ref, xl_ref), anomaly, z_ref, cross_ref, parts_ref)
    z = z_ref[...]
    start = sh_ref.shape[1] - state_ref.shape[0]
    s = (sh_ref[...], sl_ref[...])
    out_ref[...] = updated(state_ref[...], start, s, shift_of(z, d_ref), split(z))


def join_kernel(column_ref, mine_ref, theirs_ref, out_ref, both, sems):
    chunks = sems.shape[0]
    size = both.shape[0] // chunks
    column = column_ref[0]
    copies = []
    for i in range(chunks):
        at = slice(i * size, (i + 1) * size)
        mine, theirs = mine_ref[at, :], theirs_ref[at, :]
        both[at, 0, :] = jnp.where(column == 0, mine, theirs)
        both[at, 1, :] = jnp.where(column == 0, theirs, mine)
        span = pl.ds(i * size, size)
        copies.append(pltpu.make_async_copy(both.at[span], out_ref.at[span], sems.at[i]))
        copies[-1].start()
    for copy in copies:
        copy.wait()


def factor(pieces, batch, members, chunk, patches_of, place, near, values, var, sources):
    per_patch = values.shape[2]
    n = len(pieces) * per_patch
    outs = [
        ((n, members), BF16, VMEM),
        ((n, members), BF16, VMEM),
        ((n, 128), F32, VMEM),
        ((n, n), F32, VMEM),
        ((n, n), BF16, VMEM),
        ((n, n), BF16, VMEM),
        ((1,), jnp.int32, SMEM),
    ]
    scratch = [
        pltpu.VMEM((128, 128), F32),
        pltpu.VMEM((n, n), F32),
        pltpu.VMEM((n, n), F32),
        pltpu.VMEM((2, n, 2 * n), BF16),
        pltpu.VMEM((2, n, 2 * n), BF16),
    ]
    kernel = functools.partial(factor_kernel, pieces, batch, members, chunk, patches_of, len(place))
    args = [*place, near, values, var, *sources]
    flops = 6 * n * n * members + 60 * n * n * n
    return call(kernel, outs, [SMEM] * (len(place) + 1) + [VMEM] * (2 + len(sources)), args, scratch, flops, FACTOR_LIMIT)


def solver_scratch(n, width):
    return [pltpu.VMEM((n, width), F32), pltpu.VMEM((2, 2, n, width), BF16)]


def gain(batch, own_of, place, cells, factored, states):
    sh, sl, d, g, xh, xl, more = factored
    n, members = sh.shape
    width = states[0].shape[1]
    kernel = functools.partial(gain_kernel, batch, len(states), own_of)
    outs = [((n, width), F32, VMEM), ((cells.shape[2], members), F32, VMEM)]
    ins = [SMEM] * 3 + [VMEM] * (7 + len(states))
    args = [*place, more, cells, sh, sl, d, g, xh, xl, *states]
    flops = 8 * n * members * width
    scratch = [pltpu.VMEM((8, 128), jnp.int32), pltpu.VMEM((2, members, width), BF16)]
    scratch += solver_scratch(n, width)
    return call(kernel, outs, ins, args, scratch, flops)


def update(factored, z, states, starts, more=False):
    sh, sl, d = factored[:3]
    kernel = functools.partial(update_kernel, starts)
    outs = [(state.shape, F32, VMEM) for state in states]
    if more:
        outs += [((sh.shape[1], z.shape[1]), BF16, VMEM)] * 2
    flops = 6 * sh.shape[0] * sh.shape[1] * z.shape[1]
    return call(kernel, outs, [VMEM] * (4 + len(states)), [sh, sl, d, z, *states], (), flops)


def last(factored, state, anomaly=()):
    sh, sl, d, g, xh, xl, more = factored
    n, width = sh.shape[0], state.shape[1]
    outs = [((n, width), F32, VMEM), (state.shape, F32, VMEM)]
    args = [more, sh, sl, d, g, xh, xl, state, *anomaly]
    flops = 12 * sh.shape[0] * sh.shape[1] * width
    ins = [SMEM] + [VMEM] * (len(args) - 1)
    return call(last_kernel, outs, ins, args, solver_scratch(n, width), flops)


def rings(size):
    up = [(i, (i + 1) % size) for i in range(size)]
    return up, [(j, i) for i, j in up]


BOTH = ("region", "member")


def permute(x, moves, regions):
    table = []
    for region in range(regions):
        for column in range(2):
            pair, parity, to = moves(region // 2, region % 2, column)
            pair %= regions // 2
            table.append((region * 2 + column, (pair * 2 + parity) * 2 + to))
    return lax.ppermute(x, BOTH, table)


def paired(state, neighbours, obs_cell, obs_values, obs_var):
    half, _, cells = state.shape
    members = 2 * half
    regions = lax.axis_size("region")
    region, column = lax.axis_index("region"), lax.axis_index("member")
    place = (region.astype(jnp.int32)[None], column.astype(jnp.int32)[None])
    near = neighbours.T

    def own_of(region_ref, column_ref):
        return region_ref[0] * 2 + column_ref[0]

    def around(region, within):
        side = 2 * lax.rem(region, 2) - 1
        outer = lax.rem(region + regions + side, regions)
        return [r * 2 + p for r in (region, region - side, outer) for p in within]

    def patches_first(region_ref, column_ref):
        return around(region_ref[0], (0, 1)), own_of(region_ref, column_ref)

    def patches_next(region_ref, column_ref):
        column = column_ref[0]
        return around(region_ref[0], (column, 1 - column)), own_of(region_ref, column_ref)

    def across(x):
        return permute(x, lambda c, q, m: (c, q, 1 - m), regions)

    def beside(x):
        return permute(x, lambda c, q, m: (c, 1 - q, m), regions)

    def outside(x):
        return permute(x, lambda c, q, m: (c + 2 * q - 1, 1 - q, m), regions)

    anywhere = pl.BlockSpec(memory_space=pl.ANY)
    (rows,) = call(
        pick_kernel,
        [((2, obs_cell.shape[2], half), F32, VMEM)],
        [SMEM, VMEM, VMEM],
        [place[0], obs_cell, state],
        [pltpu.VMEM((8, 128), jnp.int32), pltpu.VMEM((2, half, cells), F32)],
    )
    other = across(rows)
    sources = [rows, beside(rows), outside(rows), other, beside(other), outside(other)]
    shape = ((half, cells), F32, VMEM)
    keep, send, values, var = call(
        sort_kernel,
        [shape, shape, (obs_values.shape, F32, VMEM), (obs_var.shape, F32, VMEM)],
        [SMEM, anywhere, anywhere, VMEM, anywhere],
        [place[1], obs_values, obs_var, state, other],
        [pltpu.SemaphoreType.DMA((2,))],
    )
    pieces = [[(i, (p,), 0), (3 + i, (p,), 1)] for i in range(3) for p in range(2)]
    states = [keep, across(send)]
    factored = factor(pieces, 0, members, CHUNK, patches_first, place, near, values, var, sources)
    everything = slice(None)
    low, high = (everything, slice(0, half)), (everything, slice(half, members))
    pieces = []
    for i in range(3):
        pieces += [[(i, low, 0), (i, high, 1)], [(3 + i, high, 0), (3 + i, low, 1)]]
    for batch in range(1, NBATCH):
        z, rows = gain(batch, own_of, place, obs_cell, factored, states)
        other = across(rows)
        sources = [rows, beside(rows), outside(rows), other, beside(other), outside(other)]
        mine, theirs, *anomaly = update(factored, z, states, (0, half), True)
        states = [mine, theirs]
        factored = factor(pieces, batch, members, 192, patches_next, place, near, values, var, sources)
    z, theirs = last(factored, states[1], anomaly)
    theirs = across(theirs)
    (mine,) = update(factored, z, states[:1], (0,))
    return pl.pallas_call(
        join_kernel,
        out_shape=jax.ShapeDtypeStruct(state.shape, F32),
        in_specs=[SMEM, VMEM, VMEM],
        out_specs=anywhere,
        scratch_shapes=[pltpu.VMEM(state.shape, F32), pltpu.SemaphoreType.DMA((4,))],
        compiler_params=pltpu.CompilerParams(vmem_limit_bytes=16 * 1024 * 1024),
    )(place[1], mine, theirs)


def listed(table_ref):
    blocks = table_ref.shape[0] - 1
    return [table_ref[i] for i in range(blocks)], table_ref[blocks]


def general(state, neighbours, obs_cell, obs_values, obs_var):
    ensemble = lax.all_to_all(state, "member", split_axis=1, concat_axis=0, tiled=True)
    members, owned, cells = ensemble.shape
    regions = lax.axis_size("region")
    region_patches = owned * lax.axis_size("member")
    region = lax.axis_index("region")
    first = region * region_patches + lax.axis_index("member") * owned
    up, down = rings(regions)
    fields = [ensemble[:, p, :] for p in range(owned)]
    grid = jnp.arange(cells, dtype=jnp.int32)
    for batch in range(NBATCH):
        picks = lax.dynamic_slice_in_dim(obs_cell, first, owned, 0)[:, batch, :]
        hot = (picks[:, :, None] == grid[None, None, :]).astype(F32)
        own_rows = jnp.einsum("poc,pkc->pok", hot, jnp.stack(fields), precision=HIGHEST)
        region_rows = lax.all_gather(own_rows, "member", axis=0, tiled=True)
        before = lax.ppermute(region_rows, "region", up)
        after = lax.ppermute(region_rows, "region", down)
        beside = jnp.concatenate([before, region_rows, after], axis=0)
        new = []
        for p in range(owned):
            own = first + p
            links = lax.dynamic_index_in_dim(neighbours, own, 0, keepdims=False)
            ids = jnp.concatenate([own[None], links]).astype(jnp.int32)
            table = jnp.concatenate([ids, own[None]]).astype(jnp.int32)
            home = (ids // region_patches - region + 1) % regions
            rows = jnp.take(beside, home * region_patches + ids % region_patches, axis=0)
            pieces = [[(0, (i,), 0)] for i in range(ids.shape[0])]
            factored = factor(
                pieces, batch, members, CHUNK, listed, [table], neighbours.T, obs_values, obs_var, [rows]
            )
            new.append(last(factored, fields[p])[1])
        fields = new
    ensemble = jnp.stack(fields, axis=1)
    return lax.all_to_all(ensemble, "member", split_axis=0, concat_axis=1, tiled=True)


def on_device(state, neighbours, obs_cell, obs_values, obs_var):
    patches, links = state.shape[1], neighbours.shape[1]
    even = lax.axis_size("region") % 2 == 0
    if even and patches == 2 and lax.axis_size("member") == 2 and links + 1 == 3 * patches:
        return paired(state, neighbours, obs_cell, obs_values, obs_var)
    return general(state, neighbours, obs_cell, obs_values, obs_var)


def solution(mesh):
    in_specs = (P("member", "region", None), P(), P(), P(), P())
    out_specs = P("member", "region", None)
    return jax.shard_map(
        on_device, mesh=mesh, in_specs=in_specs, out_specs=out_specs, check_vma=False
    )
```

```python
import functools
import math

import jax
import jax.numpy as jnp
from jax import lax
from jax.experimental import pallas as pl
from jax.experimental.pallas import tpu as pltpu
from jax.sharding import PartitionSpec as P

NBATCH = 2
HIGHEST = lax.Precision.HIGHEST
F32 = jnp.float32
BF16 = jnp.bfloat16
VMEM = pl.BlockSpec(memory_space=pltpu.VMEM)
SMEM = pl.BlockSpec(memory_space=pltpu.SMEM)
NN = (((1,), (0,)), ((), ()))
NT = (((1,), (1,)), ((), ()))
TN = (((0,), (0,)), ((), ()))
RESIDUAL = 1e-3
FACTOR_LIMIT = 24
MOST_STEPS = 15
TILE = 256
CHUNK = 128


def call(kernel, outs, ins, args, scratch=(), flops=0, limit=16):
    shapes = [jax.ShapeDtypeStruct(shape, dtype) for shape, dtype, _ in outs]
    moved = sum(math.prod(s.shape) * s.dtype.itemsize for s in shapes)
    moved += sum(a.size * a.dtype.itemsize for a in args)
    return pl.pallas_call(
        kernel,
        out_shape=shapes,
        in_specs=ins,
        out_specs=[space for _, _, space in outs],
        scratch_shapes=list(scratch),
        compiler_params=pltpu.CompilerParams(vmem_limit_bytes=limit * 1024 * 1024),
        cost_estimate=pl.CostEstimate(flops=flops, bytes_accessed=moved, transcendentals=0),
    )(*args)


def split(x):
    high = x.astype(BF16)
    return high, (x - high.astype(F32)).astype(BF16)


def dot(a, b, dims=NN):
    return lax.dot_general(a, b, dims, preferred_element_type=F32)


def dot3(a, b, dims=NN):
    (left,), (right,) = dims[0]
    lhs = jnp.concatenate([a[0], a[0], a[1]], axis=left)
    rhs = jnp.concatenate([b[0], b[1], b[0]], axis=right)
    return dot(lhs, rhs, dims)


def select(hot, parts, dims):
    (left,), (right,) = dims[0]
    hot = hot.astype(BF16)
    lhs = jnp.concatenate([hot] * len(parts), axis=left)
    return dot(lhs, jnp.concatenate(parts, axis=right), dims)


def split_all(x):
    high, middle = split(x)
    low = x - high.astype(F32) - middle.astype(F32)
    return high, middle, low.astype(BF16)


def step_limits():
    limits = []
    for steps in range(MOST_STEPS):
        rho = RESIDUAL
        for _ in range(steps):
            rho = math.sqrt(2.0 * rho / (1.0 + rho))
        limits.append(2.0 * rho / (1.0 - rho) if rho < 1.0 else math.inf)
    return limits


def diagonal(n, columns, first):
    row = lax.broadcasted_iota(jnp.int32, (n, columns), 0)
    column = lax.broadcasted_iota(jnp.int32, (n, columns), 1)
    return row + first == column


def selector(picks, cells, scratch):
    per_patch = picks.shape[1]
    scratch[...] = jnp.full_like(scratch, -1)
    scratch[0:1, 0:per_patch] = picks
    grid = lax.broadcasted_iota(jnp.int32, (cells, scratch.shape[1]), 0)
    hot = (grid == scratch[0:1, :]).astype(F32)
    return jnp.transpose(hot)[0:per_patch, :]


def pick_kernel(region_ref, cells_ref, state_ref, rows_ref, scratch, field_ref):
    patches, cells = state_ref.shape[1:]
    for p in range(patches):
        field_ref[p] = state_ref[:, p, :]
        hot = selector(cells_ref[pl.ds(region_ref[0] * patches + p, 1), 0, :], cells, scratch)
        rows_ref[p] = select(hot, split_all(field_ref[p]), NT)


def sort_kernel(column_ref, values_hbm, var_hbm, state_ref, *refs):
    keep_ref, send_ref, values_ref, var_ref, sems = refs[-5:]
    copies = [
        pltpu.make_async_copy(values_hbm, values_ref, sems.at[0]),
        pltpu.make_async_copy(var_hbm, var_ref, sems.at[1]),
    ]
    for copy in copies:
        copy.start()
    column = column_ref[0]
    first, second = state_ref[:, 0, :], state_ref[:, 1, :]
    keep_ref[...] = jnp.where(column == 0, first, second)
    send_ref[...] = jnp.where(column == 0, second, first)
    for copy in copies:
        copy.wait()


def factor_kernel(pieces, batch, members, chunk, patches_of, places, *refs):
    place_refs, refs = refs[:places], refs[places:]
    near_ref, values_ref, var_ref, *refs = refs
    count = len(refs) - 12
    sources = refs[:count]
    sh_ref, sl_ref, d_ref, g_ref, xh_ref, xl_ref, n_ref, flat, eye_ref, x_ref, wa, wb = refs[count:]
    per_patch = values_ref.shape[2]
    flat[...] = jnp.ones_like(flat)
    blocks = len(pieces)
    ids, own = patches_of(*place_refs)
    for i in range(blocks):
        patch = ids[i]
        widening = (patch == own).astype(jnp.int32)
        for j in range(near_ref.shape[0]):
            widening = widening + (near_ref[j, own] == patch).astype(jnp.int32) * (j + 2)
        flat[i : i + 1, 0:per_patch] = values_ref[pl.ds(patch, 1), batch, :]
        noise = var_ref[pl.ds(patch, 1), batch, :] * widening.astype(F32)
        flat[blocks + i : blocks + i + 1, 0:per_patch] = noise
    upright = jnp.transpose(flat[...])

    def fetch(which, index):
        if isinstance(which, int):
            return sources[which][index]
        odd = lax.rem(place_refs[0][0], 2) == 1
        return jnp.where(odd, sources[which[1]][index], sources[which[0]][index])

    def scaled(i):
        rows = [fetch(which, index) for which, index, _ in pieces[i]]
        total = sum(jnp.sum(part, axis=1, keepdims=True) for part in rows)
        mean = total * (1.0 / members)
        noise = upright[0:per_patch, blocks + i : blocks + i + 1]
        scale = lax.rsqrt(noise * (members - 1.0))
        at = slice(i * per_patch, (i + 1) * per_patch)
        for part, (_, _, start) in zip(rows, pieces[i]):
            size = part.shape[1]
            lanes = slice(start * size, (start + 1) * size)
            sh_ref[at, lanes], sl_ref[at, lanes] = split((part - mean) * scale)
        shift = (upright[0:per_patch, i : i + 1] - mean) * scale
        d_ref[at, :] = jnp.broadcast_to(shift, (per_patch, d_ref.shape[1]))

    n = sh_ref.shape[0]
    head = min(TILE, n)
    tail = n - head
    chunks = [(i, min(i + chunk, n)) for i in range(0, n, chunk)]
    first = head // per_patch
    for i in range(first):
        scaled(i)
    left = (sh_ref[0:head], sl_ref[0:head])
    for i in range(first, blocks):
        scaled(i)
    g_ref[:, 0:head] = dot3((sh_ref[...], sl_ref[...]), left, NT)
    low = (sh_ref[head:n], sl_ref[head:n])
    g_ref[head:n, head:n] = dot3(low, low, NT)
    g_ref[0:head, head:n] = jnp.transpose(g_ref[head:n, 0:head])
    g = g_ref[...]
    square = jnp.sum(jnp.sum(g * g, axis=0, keepdims=True), axis=1, keepdims=True)
    norm = jnp.sqrt(square) * (1.0 + 1e-5)
    size = square[0, 0]
    limits = step_limits()
    pairs = jnp.int32(0)
    for k in range(7, MOST_STEPS - 2, 2):
        limit = limits[k] * (1.0 - 1e-4)
        pairs = pairs + (size > limit * limit).astype(jnp.int32)
    n_ref[0] = (size > 1.6e7).astype(jnp.int32) + (size > 1e8).astype(jnp.int32)
    eye_ref[...] = diagonal(n, n, 0).astype(F32)
    eye = eye_ref[...]
    first = 2.0 / (2.0 + norm)
    rho = norm * (0.5 * first)
    rho2 = rho * rho
    weight = 2.0 / (2.0 - rho2)
    keep = 0.5 * rho2 * weight
    r = (1.0 - first) * eye - first * g
    parts = split(r)
    x = (weight * first) * (eye + r)
    x_ref[...] = x
    for i, part in enumerate(split(x)):
        wa[i, :, n : 2 * n] = part

    def store(targets, start, left, corner):
        blocks = [(slice(0, n), slice(start, start + head), left)]
        blocks.append((slice(head, n), slice(start + head, start + n), corner))
        blocks.append((slice(0, head), slice(start + head, start + n), jnp.transpose(left[head:n])))
        for rows, columns, block in blocks:
            for target, part in zip(targets, split(block)):
                target[rows, columns] = part

    def corner_of(weight, keep, left, corner):
        left = weight * left - keep * eye_ref[:, 0:head]
        return left, weight * corner - keep * eye_ref[head:n, head:n]

    left = dot3(parts, [part[:, 0:head] for part in parts])
    corner = dot3([part[head:n] for part in parts], [part[:, head:n] for part in parts])
    store((wa.at[0], wa.at[1]), 0, *corner_of(weight, keep, left, corner))

    def advance(source, target, rho2):
        weight = 2.0 / (2.0 - rho2)
        keep = 0.5 * rho2 * weight
        parts = (source[0, :, 0:n], source[1, :, 0:n])
        ends = [jnp.concatenate([source[i, :, head:n], source[i, :, n + head : 2 * n]], axis=1) for i in (0, 1)]
        left = dot3(parts, (source[0, :, 0:head], source[1, :, 0:head]))
        corners = dot3([part[head:n] for part in parts], ends)
        both = (target.at[0], target.at[1])
        store(both, 0, *corner_of(weight, keep, left, corners[:, 0:tail]))
        left = dot3(parts, (source[0, :, n : n + head], source[1, :, n : n + head]))
        left = weight * (x_ref[:, 0:head] + left)
        corner = weight * (x_ref[head:n, head:n] + corners[:, tail : 2 * tail])
        x_ref[:, 0:head] = left
        x_ref[head:n, head:n] = corner
        store(both, n, left, corner)
        return keep * keep

    rho2 = keep * keep

    def sides(source, span):
        return [source[i, span[0] : span[1], 0:n] for i in (0, 1)]

    def put(targets, start, span, block):
        for target, part in zip(targets, split(block)):
            target[span[0] : span[1], start : start + head] = part
        low = max(span[0], head)
        if low < span[1]:
            for target, part in zip(targets, split(jnp.transpose(block[low - span[0] :]))):
                target[0:head, start + low : start + span[1]] = part

    def put_corner(targets, start, block):
        for target, part in zip(targets, split(block)):
            target[head:n, start + head : start + n] = part

    def put_x(targets, start, weight, span, product):
        x = weight * (x_ref[span[0] : span[1], 0:head] + product)
        x_ref[span[0] : span[1], 0:head] = x
        put(targets, start, span, x)

    def put_x_corner(targets, start, weight, product):
        x = weight * (x_ref[head:n, head:n] + product)
        x_ref[head:n, head:n] = x
        put_corner(targets, start, x)

    waiting = None
    source, target = wa, wb
    for _ in range(5):
        weight = 2.0 / (2.0 - rho2)
        keep = 0.5 * rho2 * weight
        first = (source[0, :, 0:head], source[1, :, 0:head])
        r = []
        for k, span in enumerate(chunks):
            r.append(dot3(sides(source, span), first))
            if waiting is not None:
                put_x((source.at[0], source.at[1]), n, waiting[0], span, waiting[1][k])
        if waiting is not None:
            put_x_corner((source.at[0], source.at[1]), n, waiting[0], waiting[2])
        ends = [jnp.concatenate([source[i, :, head:n], source[i, :, n + head : 2 * n]], axis=1) for i in (0, 1)]
        corners = dot3(sides(source, (head, n)), ends)
        first = (source[0, :, n : n + head], source[1, :, n : n + head])
        both = (target.at[0], target.at[1])
        x = []
        for k, span in enumerate(chunks):
            x.append(dot3(sides(source, span), first))
            put(both, 0, span, weight * r[k] - keep * eye_ref[span[0] : span[1], 0:head])
        put_corner(both, 0, weight * corners[:, 0:tail] - keep * eye_ref[head:n, head:n])
        waiting = (weight, x, corners[:, tail : 2 * tail])
        rho2 = keep * keep
        source, target = target, source
    for k, span in enumerate(chunks):
        put_x((source.at[0], source.at[1]), n, waiting[0], span, waiting[1][k])
    put_x_corner((source.at[0], source.at[1]), n, waiting[0], waiting[2])

    def twice(_, rho2):
        return advance(target, source, advance(source, target, rho2))

    rho2 = lax.fori_loop(0, pairs, twice, rho2)
    weight = 2.0 / (2.0 - rho2)
    first = (source[0, :, n : n + head], source[1, :, n : n + head])
    done = (xh_ref, xl_ref)
    ends = [source[i, :, n + head : 2 * n] for i in (0, 1)]
    put_x_corner(done, 0, weight, dot3(sides(source, (head, n)), ends))
    x = [dot3(sides(source, span), first) for span in chunks]
    for k, span in enumerate(chunks):
        put_x(done, 0, weight, span, x[k])


def centred(fields):
    members = sum(field.shape[0] for field in fields)
    mean = sum(jnp.sum(field, axis=0, keepdims=True) for field in fields) * (1.0 / members)
    pairs = [split(field - mean) for field in fields]
    return [jnp.concatenate(parts, axis=0) for parts in zip(*pairs)], mean


def in_chunks(count, product, work):
    waiting = None
    for start in range(0, count, CHUNK):
        span = slice(start, min(start + CHUNK, count))
        result = product(span)
        if waiting is not None:
            work(*waiting)
        waiting = (span, result)
    work(*waiting)


def solve(n_ref, s, g_ref, x, anomaly, z_ref, cross_ref, parts_ref):
    n = z_ref.shape[0]

    def keep(slot, span, value):
        for i, part in enumerate(split(value)):
            parts_ref[slot, i, span] = part

    def kept(slot):
        return parts_ref[slot, 0], parts_ref[slot, 1]

    def some(parts, span):
        return [part[span] for part in parts]

    def crossed(span, value):
        cross_ref[span] = value
        keep(0, span, value)

    def solved(span, value):
        z_ref[span] = value
        keep(1, span, value)

    def left(span, value):
        keep(0, span, cross_ref[span] - z_ref[span] - value)

    def refined(span, value):
        z_ref[span] = z_ref[span] + value

    in_chunks(n, lambda span: dot3(some(s, span), [part[...] for part in anomaly]), crossed)
    in_chunks(n, lambda span: dot3(some(x, span), kept(0)), solved)
    in_chunks(n, lambda span: dot3(split(g_ref[span]), kept(1)), left)
    in_chunks(n, lambda span: dot3(some(x, span), kept(0)), refined)

    def refine(_, carry):
        z = z_ref[...]
        gz = lax.dot_general(g_ref[...], z, NN, precision=HIGHEST, preferred_element_type=F32)
        z_ref[...] = z + dot3([part[...] for part in x], split(cross_ref[...] - z - gz))
        return carry

    lax.fori_loop(0, n_ref[0], refine, 0)


def gain_kernel(batch, parts, own_of, region_ref, column_ref, n_ref, cells_ref, sh_ref, sl_ref, d_ref, g_ref, *refs):
    xh_ref, xl_ref, *refs = refs
    states = refs[:parts]
    z_ref, rows_ref, scratch, anomaly_ref, cross_ref, parts_ref = refs[parts:]
    anomaly, mean = centred([state[...] for state in states])
    for i, part in enumerate(anomaly):
        anomaly_ref[i] = part
    anomaly = (anomaly_ref.at[0], anomaly_ref.at[1])
    solve(n_ref, (sh_ref, sl_ref), g_ref, (xh_ref, xl_ref), anomaly, z_ref, cross_ref, parts_ref)
    s = (sh_ref[...], sl_ref[...])
    picks = cells_ref[pl.ds(own_of(region_ref, column_ref), 1), batch, :]
    hot = selector(picks, mean.shape[1], scratch)
    zt = split(select(hot, split(z_ref[...]), NT))
    base = jnp.sum(hot * mean, axis=1, keepdims=True) + dot3(zt, split(d_ref[...]))[:, 0:1]
    picked = select(hot, [part[...] for part in anomaly], NT)
    rows_ref[...] = base + picked - 0.5 * dot3(zt, s)


def updated(field, start, s, shift, z):
    size = field.shape[0]
    return field + shift - 0.5 * dot3([h[:, start : start + size] for h in s], z, TN)


def shift_of(z, d_ref):
    return jnp.sum(z * d_ref[:, 0:1], axis=0, keepdims=True)


def update_kernel(starts, sh_ref, sl_ref, d_ref, z_ref, *refs):
    count = len(starts)
    states, outs, parts = refs[:count], refs[count : 2 * count], refs[2 * count :]
    z = z_ref[...]
    shift = shift_of(z, d_ref)
    s, zs = (sh_ref[...], sl_ref[...]), split(z)
    for start, state, out in zip(starts, states, outs):
        out[...] = updated(state[...], start, s, shift, zs)
    if parts:
        anomaly, _ = centred([out[...] for out in outs])
        for ref, part in zip(parts, anomaly):
            ref[...] = part


def last_kernel(n_ref, sh_ref, sl_ref, d_ref, g_ref, xh_ref, xl_ref, *refs):
    (state_ref, *parts), (z_ref, out_ref, cross_ref, parts_ref) = refs[:-4], refs[-4:]
    anomaly = parts or centred([state_ref[...]])[0]
    solve(n_ref, (sh_ref, sl_ref), g_ref, (xh_ref, xl_ref), anomaly, z_ref, cross_ref, parts_ref)
    z = z_ref[...]
    start = sh_ref.shape[1] - state_ref.shape[0]
    s = (sh_ref[...], sl_ref[...])
    out_ref[...] = updated(state_ref[...], start, s, shift_of(z, d_ref), split(z))


def join_kernel(column_ref, mine_ref, theirs_ref, out_ref, both, sems):
    chunks = sems.shape[0]
    size = both.shape[0] // chunks
    column = column_ref[0]
    copies = []
    for i in range(chunks):
        at = slice(i * size, (i + 1) * size)
        mine, theirs = mine_ref[at, :], theirs_ref[at, :]
        both[at, 0, :] = jnp.where(column == 0, mine, theirs)
        both[at, 1, :] = jnp.where(column == 0, theirs, mine)
        span = pl.ds(i * size, size)
        copies.append(pltpu.make_async_copy(both.at[span], out_ref.at[span], sems.at[i]))
        copies[-1].start()
    for copy in copies:
        copy.wait()


def factor(pieces, batch, members, chunk, patches_of, place, near, values, var, sources):
    per_patch = values.shape[2]
    n = len(pieces) * per_patch
    outs = [
        ((n, members), BF16, VMEM),
        ((n, members), BF16, VMEM),
        ((n, 128), F32, VMEM),
        ((n, n), F32, VMEM),
        ((n, n), BF16, VMEM),
        ((n, n), BF16, VMEM),
        ((1,), jnp.int32, SMEM),
    ]
    scratch = [
        pltpu.VMEM((128, 128), F32),
        pltpu.VMEM((n, n), F32),
        pltpu.VMEM((n, n), F32),
        pltpu.VMEM((2, n, 2 * n), BF16),
        pltpu.VMEM((2, n, 2 * n), BF16),
    ]
    kernel = functools.partial(factor_kernel, pieces, batch, members, chunk, patches_of, len(place))
    args = [*place, near, values, var, *sources]
    flops = 6 * n * n * members + 60 * n * n * n
    return call(kernel, outs, [SMEM] * (len(place) + 1) + [VMEM] * (2 + len(sources)), args, scratch, flops, FACTOR_LIMIT)


def solver_scratch(n, width):
    return [pltpu.VMEM((n, width), F32), pltpu.VMEM((2, 2, n, width), BF16)]


def gain(batch, own_of, place, cells, factored, states):
    sh, sl, d, g, xh, xl, more = factored
    n, members = sh.shape
    width = states[0].shape[1]
    kernel = functools.partial(gain_kernel, batch, len(states), own_of)
    outs = [((n, width), F32, VMEM), ((cells.shape[2], members), F32, VMEM)]
    ins = [SMEM] * 3 + [VMEM] * (7 + len(states))
    args = [*place, more, cells, sh, sl, d, g, xh, xl, *states]
    flops = 8 * n * members * width
    scratch = [pltpu.VMEM((8, 128), jnp.int32), pltpu.VMEM((2, members, width), BF16)]
    scratch += solver_scratch(n, width)
    return call(kernel, outs, ins, args, scratch, flops)


def update(factored, z, states, starts, more=False):
    sh, sl, d = factored[:3]
    kernel = functools.partial(update_kernel, starts)
    outs = [(state.shape, F32, VMEM) for state in states]
    if more:
        outs += [((sh.shape[1], z.shape[1]), BF16, VMEM)] * 2
    flops = 6 * sh.shape[0] * sh.shape[1] * z.shape[1]
    return call(kernel, outs, [VMEM] * (4 + len(states)), [sh, sl, d, z, *states], (), flops)


def last(factored, state, anomaly=()):
    sh, sl, d, g, xh, xl, more = factored
    n, width = sh.shape[0], state.shape[1]
    outs = [((n, width), F32, VMEM), (state.shape, F32, VMEM)]
    args = [more, sh, sl, d, g, xh, xl, state, *anomaly]
    flops = 12 * sh.shape[0] * sh.shape[1] * width
    ins = [SMEM] + [VMEM] * (len(args) - 1)
    return call(last_kernel, outs, ins, args, solver_scratch(n, width), flops)


def rings(size):
    up = [(i, (i + 1) % size) for i in range(size)]
    return up, [(j, i) for i, j in up]


BOTH = ("region", "member")


def permute(x, moves, regions):
    table = []
    for region in range(regions):
        for column in range(2):
            move = moves(region // 2, region % 2, column)
            if move is None:
                continue
            pair, parity, to = move
            pair %= regions // 2
            table.append((region * 2 + column, (pair * 2 + parity) * 2 + to))
    return lax.ppermute(x, BOTH, table)


def paired(state, neighbours, obs_cell, obs_values, obs_var):
    half, _, cells = state.shape
    members = 2 * half
    regions = lax.axis_size("region")
    region, column = lax.axis_index("region"), lax.axis_index("member")
    place = (region.astype(jnp.int32)[None], column.astype(jnp.int32)[None])
    near = neighbours.T

    def own_of(region_ref, column_ref):
        return region_ref[0] * 2 + column_ref[0]

    def around(region, within):
        side = 2 * lax.rem(region, 2) - 1
        outer = lax.rem(region + regions + side, regions)
        return [r * 2 + p for r in (region, region - side, outer) for p in within]

    def patches_first(region_ref, column_ref):
        return around(region_ref[0], (0, 1)), own_of(region_ref, column_ref)

    def patches_next(region_ref, column_ref):
        column = column_ref[0]
        return around(region_ref[0], (column, 1 - column)), own_of(region_ref, column_ref)

    def across(x):
        return permute(x, lambda c, q, m: (c, q, 1 - m), regions)

    def beside(x):
        return permute(x, lambda c, q, m: (c, 1 - q, m), regions)

    def outside(x):
        return permute(x, lambda c, q, m: (c + 2 * q - 1, 1 - q, m), regions)

    def exchanged(rows):
        other, out = across(rows), outside(rows)
        forward = permute(other, lambda c, q, m: (c + 1, 0, m) if q == 1 else None, regions)
        over = permute(out, lambda c, q, m: (c, 1, 1 - m) if q == 1 else None, regions)
        return [rows, beside(rows), out, other, beside(other), forward, over]

    anywhere = pl.BlockSpec(memory_space=pl.ANY)
    (rows,) = call(
        pick_kernel,
        [((2, obs_cell.shape[2], half), F32, VMEM)],
        [SMEM, VMEM, VMEM],
        [place[0], obs_cell, state],
        [pltpu.VMEM((8, 128), jnp.int32), pltpu.VMEM((2, half, cells), F32)],
    )
    sources = exchanged(rows)
    shape = ((half, cells), F32, VMEM)
    keep, send, values, var = call(
        sort_kernel,
        [shape, shape, (obs_values.shape, F32, VMEM), (obs_var.shape, F32, VMEM)],
        [SMEM, anywhere, anywhere, VMEM, anywhere],
        [place[1], obs_values, obs_var, state, sources[3]],
        [pltpu.SemaphoreType.DMA((2,))],
    )
    far = (3, 4, (5, 6))
    pieces = [[(i, (p,), 0), (far[i], (p,), 1)] for i in range(3) for p in range(2)]
    states = [keep, across(send)]
    factored = factor(pieces, 0, members, CHUNK, patches_first, place, near, values, var, sources)
    everything = slice(None)
    low, high = (everything, slice(0, half)), (everything, slice(half, members))
    pieces = []
    for i in range(3):
        pieces += [[(i, low, 0), (i, high, 1)], [(far[i], high, 0), (far[i], low, 1)]]
    for batch in range(1, NBATCH):
        z, rows = gain(batch, own_of, place, obs_cell, factored, states)
        sources = exchanged(rows)
        mine, theirs, *anomaly = update(factored, z, states, (0, half), True)
        states = [mine, theirs]
        factored = factor(pieces, batch, members, CHUNK, patches_next, place, near, values, var, sources)
    z, theirs = last(factored, states[1], anomaly)
    theirs = across(theirs)
    (mine,) = update(factored, z, states[:1], (0,))
    return pl.pallas_call(
        join_kernel,
        out_shape=jax.ShapeDtypeStruct(state.shape, F32),
        in_specs=[SMEM, VMEM, VMEM],
        out_specs=anywhere,
        scratch_shapes=[pltpu.VMEM(state.shape, F32), pltpu.SemaphoreType.DMA((4,))],
        compiler_params=pltpu.CompilerParams(vmem_limit_bytes=16 * 1024 * 1024),
    )(place[1], mine, theirs)


def listed(table_ref):
    blocks = table_ref.shape[0] - 1
    return [table_ref[i] for i in range(blocks)], table_ref[blocks]


def general(state, neighbours, obs_cell, obs_values, obs_var):
    ensemble = lax.all_to_all(state, "member", split_axis=1, concat_axis=0, tiled=True)
    members, owned, cells = ensemble.shape
    regions = lax.axis_size("region")
    region_patches = owned * lax.axis_size("member")
    region = lax.axis_index("region")
    first = region * region_patches + lax.axis_index("member") * owned
    up, down = rings(regions)
    fields = [ensemble[:, p, :] for p in range(owned)]
    grid = jnp.arange(cells, dtype=jnp.int32)
    for batch in range(NBATCH):
        picks = lax.dynamic_slice_in_dim(obs_cell, first, owned, 0)[:, batch, :]
        hot = (picks[:, :, None] == grid[None, None, :]).astype(F32)
        own_rows = jnp.einsum("poc,pkc->pok", hot, jnp.stack(fields), precision=HIGHEST)
        region_rows = lax.all_gather(own_rows, "member", axis=0, tiled=True)
        before = lax.ppermute(region_rows, "region", up)
        after = lax.ppermute(region_rows, "region", down)
        beside = jnp.concatenate([before, region_rows, after], axis=0)
        new = []
        for p in range(owned):
            own = first + p
            links = lax.dynamic_index_in_dim(neighbours, own, 0, keepdims=False)
            ids = jnp.concatenate([own[None], links]).astype(jnp.int32)
            table = jnp.concatenate([ids, own[None]]).astype(jnp.int32)
            home = (ids // region_patches - region + 1) % regions
            rows = jnp.take(beside, home * region_patches + ids % region_patches, axis=0)
            pieces = [[(0, (i,), 0)] for i in range(ids.shape[0])]
            factored = factor(
                pieces, batch, members, CHUNK, listed, [table], neighbours.T, obs_values, obs_var, [rows]
            )
            new.append(last(factored, fields[p])[1])
        fields = new
    ensemble = jnp.stack(fields, axis=1)
    return lax.all_to_all(ensemble, "member", split_axis=0, concat_axis=1, tiled=True)


def on_device(state, neighbours, obs_cell, obs_values, obs_var):
    patches, links = state.shape[1], neighbours.shape[1]
    even = lax.axis_size("region") % 2 == 0
    if even and patches == 2 and lax.axis_size("member") == 2 and links + 1 == 3 * patches:
        return paired(state, neighbours, obs_cell, obs_values, obs_var)
    return general(state, neighbours, obs_cell, obs_values, obs_var)


def solution(mesh):
    in_specs = (P("member", "region", None), P(), P(), P(), P())
    out_specs = P("member", "region", None)
    return jax.shard_map(
        on_device, mesh=mesh, in_specs=in_specs, out_specs=out_specs, check_vma=False
    )
```

```python
import functools
import math

import jax
import jax.numpy as jnp
from jax import lax
from jax.experimental import pallas as pl
from jax.experimental.pallas import tpu as pltpu
from jax.sharding import PartitionSpec as P

NBATCH = 2
HIGHEST = lax.Precision.HIGHEST
F32 = jnp.float32
BF16 = jnp.bfloat16
VMEM = pl.BlockSpec(memory_space=pltpu.VMEM)
SMEM = pl.BlockSpec(memory_space=pltpu.SMEM)
NN = (((1,), (0,)), ((), ()))
NT = (((1,), (1,)), ((), ()))
TN = (((0,), (0,)), ((), ()))
RESIDUAL = 1e-3
FACTOR_LIMIT = 24
MOST_STEPS = 15
TILE = 256
CHUNK = 128


def call(kernel, outs, ins, args, scratch=(), flops=0, limit=16, aliases=None):
    shapes = [jax.ShapeDtypeStruct(shape, dtype) for shape, dtype, _ in outs]
    moved = sum(math.prod(s.shape) * s.dtype.itemsize for s in shapes)
    moved += sum(a.size * a.dtype.itemsize for a in args)
    return pl.pallas_call(
        kernel,
        out_shape=shapes,
        in_specs=ins,
        out_specs=[space for _, _, space in outs],
        scratch_shapes=list(scratch),
        input_output_aliases=aliases or {},
        compiler_params=pltpu.CompilerParams(vmem_limit_bytes=limit * 1024 * 1024),
        cost_estimate=pl.CostEstimate(flops=flops, bytes_accessed=moved, transcendentals=0),
    )(*args)


def split(x):
    high = x.astype(BF16)
    return high, (x - high.astype(F32)).astype(BF16)


def dot(a, b, dims=NN):
    return lax.dot_general(a, b, dims, preferred_element_type=F32)


def dot3(a, b, dims=NN):
    (left,), (right,) = dims[0]
    lhs = jnp.concatenate([a[0], a[0], a[1]], axis=left)
    rhs = jnp.concatenate([b[0], b[1], b[0]], axis=right)
    return dot(lhs, rhs, dims)


def select(hot, parts, dims):
    (left,), (right,) = dims[0]
    hot = hot.astype(BF16)
    lhs = jnp.concatenate([hot] * len(parts), axis=left)
    return dot(lhs, jnp.concatenate(parts, axis=right), dims)


def split_all(x):
    high, middle = split(x)
    low = x - high.astype(F32) - middle.astype(F32)
    return high, middle, low.astype(BF16)


def step_limits():
    limits = []
    for steps in range(MOST_STEPS):
        rho = RESIDUAL
        for _ in range(steps):
            rho = math.sqrt(2.0 * rho / (1.0 + rho))
        limits.append(2.0 * rho / (1.0 - rho) if rho < 1.0 else math.inf)
    return limits


def diagonal(n, columns, first):
    row = lax.broadcasted_iota(jnp.int32, (n, columns), 0)
    column = lax.broadcasted_iota(jnp.int32, (n, columns), 1)
    return row + first == column


def selector(picks, cells, scratch):
    per_patch = picks.shape[1]
    scratch[...] = jnp.full_like(scratch, -1)
    scratch[0:1, 0:per_patch] = picks
    grid = lax.broadcasted_iota(jnp.int32, (cells, scratch.shape[1]), 0)
    hot = (grid == scratch[0:1, :]).astype(F32)
    return jnp.transpose(hot)[0:per_patch, :]


def pick_kernel(region_ref, cells_ref, state_ref, rows_ref, scratch, field_ref):
    patches, cells = state_ref.shape[1:]
    for p in range(patches):
        field_ref[p] = state_ref[:, p, :]
        hot = selector(cells_ref[pl.ds(region_ref[0] * patches + p, 1), 0, :], cells, scratch)
        rows_ref[p] = select(hot, split_all(field_ref[p]), NT)


def sort_kernel(column_ref, values_hbm, var_hbm, state_ref, *refs):
    keep_ref, send_ref, values_ref, var_ref, sems = refs[-5:]
    copies = [
        pltpu.make_async_copy(values_hbm, values_ref, sems.at[0]),
        pltpu.make_async_copy(var_hbm, var_ref, sems.at[1]),
    ]
    for copy in copies:
        copy.start()
    column = column_ref[0]
    first, second = state_ref[:, 0, :], state_ref[:, 1, :]
    keep_ref[...] = jnp.where(column == 0, first, second)
    send_ref[...] = jnp.where(column == 0, second, first)
    for copy in copies:
        copy.wait()


def table(patches, own, near_ref, values_ref, var_ref, batch, flat):
    per_patch = values_ref.shape[2]
    blocks = len(patches)
    flat[...] = jnp.ones_like(flat)
    for i, patch in enumerate(patches):
        widening = (patch == own).astype(jnp.int32)
        for j in range(near_ref.shape[0]):
            widening = widening + (near_ref[j, own] == patch).astype(jnp.int32) * (j + 2)
        flat[i : i + 1, 0:per_patch] = values_ref[pl.ds(patch, 1), batch, :]
        noise = var_ref[pl.ds(patch, 1), batch, :] * widening.astype(F32)
        flat[blocks + i : blocks + i + 1, 0:per_patch] = noise
    upright = jnp.transpose(flat[...])[0:per_patch]
    return [(upright[:, i : i + 1], upright[:, blocks + i : blocks + i + 1]) for i in range(blocks)]


def scale_block(i, piece, sources, column, members, sh_ref, sl_ref, d_ref):
    value, noise = column
    rows = [sources[which][index] for which, index, _ in piece]
    total = sum(jnp.sum(part, axis=1, keepdims=True) for part in rows)
    mean = total * (1.0 / members)
    scale = lax.rsqrt(noise * (members - 1.0))
    per_patch = value.shape[0]
    at = slice(i * per_patch, (i + 1) * per_patch)
    for part, (_, _, start) in zip(rows, piece):
        size = part.shape[1]
        lanes = slice(start * size, (start + 1) * size)
        sh_ref[at, lanes], sl_ref[at, lanes] = split((part - mean) * scale)
    d_ref[at, :] = jnp.broadcast_to((value - mean) * scale, (per_patch, d_ref.shape[1]))


def prepare_kernel(pieces, batch, members, patches_of, places, *refs):
    place_refs, refs = refs[:places], refs[places:]
    near_ref, values_ref, var_ref, ah_ref, al_ref, *refs = refs
    sources, (sh_ref, sl_ref, d_ref, g_ref, cross_ref, flat) = refs[:-6], refs[-6:]
    patches, own = patches_of(*place_refs)
    columns = table(patches[: len(pieces)], own, near_ref, values_ref, var_ref, batch, flat)
    for i, piece in enumerate(pieces):
        scale_block(i, piece, sources, columns[i], members, sh_ref, sl_ref, d_ref)
    count = len(pieces) * values_ref.shape[2]
    s = (sh_ref[0:count], sl_ref[0:count])
    g_ref[0:count, 0:count] = dot3(s, s, NT)
    cross_ref[0:count] = dot3(s, (ah_ref[...], al_ref[...]))


def factor_kernel(pieces, batch, members, chunk, patches_of, places, ready, *refs):
    place_refs, refs = refs[:places], refs[places:]
    near_ref, values_ref, var_ref, *refs = refs
    refs, (flat, eye_ref, x_ref, wa, wb) = refs[:-5], refs[-5:]
    if ready:
        refs, cross_ref = refs[:-1], refs[-1]
    refs, (sh_ref, sl_ref, d_ref, g_ref, xh_ref, xl_ref, n_ref) = refs[:-7], refs[-7:]
    if ready:
        refs, (ah_ref, al_ref) = refs[:-7], refs[-7:-5]
    sources = refs
    per_patch = values_ref.shape[2]
    blocks = len(pieces)
    patches, own = patches_of(*place_refs)
    columns = table(patches[ready:], own, near_ref, values_ref, var_ref, batch, flat)
    for i in range(ready, blocks):
        scale_block(i, pieces[i], sources, columns[i - ready], members, sh_ref, sl_ref, d_ref)
    n = sh_ref.shape[0]
    head = min(TILE, n)
    tail = n - head
    chunks = [(i, min(i + chunk, n)) for i in range(0, n, chunk)]
    left = (sh_ref[0:head], sl_ref[0:head])
    fresh = ready * per_patch
    g_ref[fresh:n, 0:head] = dot3((sh_ref[fresh:n], sl_ref[fresh:n]), left, NT)
    low = (sh_ref[head:n], sl_ref[head:n])
    g_ref[head:n, head:n] = dot3(low, low, NT)
    g_ref[0:head, head:n] = jnp.transpose(g_ref[head:n, 0:head])
    if ready:
        cross_ref[fresh:n] = dot3((sh_ref[fresh:n], sl_ref[fresh:n]), (ah_ref[...], al_ref[...]))
    g = g_ref[...]
    square = jnp.sum(jnp.sum(g * g, axis=0, keepdims=True), axis=1, keepdims=True)
    norm = jnp.sqrt(square) * (1.0 + 1e-5)
    size = square[0, 0]
    limits = step_limits()
    pairs = jnp.int32(0)
    for k in range(7, MOST_STEPS - 2, 2):
        limit = limits[k] * (1.0 - 1e-4)
        pairs = pairs + (size > limit * limit).astype(jnp.int32)
    n_ref[0] = (size > 1.6e7).astype(jnp.int32) + (size > 1e8).astype(jnp.int32)
    eye_ref[...] = diagonal(n, n, 0).astype(F32)
    eye = eye_ref[...]
    first = 2.0 / (2.0 + norm)
    rho = norm * (0.5 * first)
    rho2 = rho * rho
    weight = 2.0 / (2.0 - rho2)
    keep = 0.5 * rho2 * weight
    r = (1.0 - first) * eye - first * g
    parts = split(r)
    x = (weight * first) * (eye + r)
    x_ref[...] = x
    for i, part in enumerate(split(x)):
        wa[i, :, n : 2 * n] = part

    def store(targets, start, left, corner):
        blocks = [(slice(0, n), slice(start, start + head), left)]
        blocks.append((slice(head, n), slice(start + head, start + n), corner))
        blocks.append((slice(0, head), slice(start + head, start + n), jnp.transpose(left[head:n])))
        for rows, columns, block in blocks:
            for target, part in zip(targets, split(block)):
                target[rows, columns] = part

    def corner_of(weight, keep, left, corner):
        left = weight * left - keep * eye_ref[:, 0:head]
        return left, weight * corner - keep * eye_ref[head:n, head:n]

    left = dot3(parts, [part[:, 0:head] for part in parts])
    corner = dot3([part[head:n] for part in parts], [part[:, head:n] for part in parts])
    store((wa.at[0], wa.at[1]), 0, *corner_of(weight, keep, left, corner))

    def advance(source, target, rho2):
        weight = 2.0 / (2.0 - rho2)
        keep = 0.5 * rho2 * weight
        parts = (source[0, :, 0:n], source[1, :, 0:n])
        ends = [jnp.concatenate([source[i, :, head:n], source[i, :, n + head : 2 * n]], axis=1) for i in (0, 1)]
        left = dot3(parts, (source[0, :, 0:head], source[1, :, 0:head]))
        corners = dot3([part[head:n] for part in parts], ends)
        both = (target.at[0], target.at[1])
        store(both, 0, *corner_of(weight, keep, left, corners[:, 0:tail]))
        left = dot3(parts, (source[0, :, n : n + head], source[1, :, n : n + head]))
        left = weight * (x_ref[:, 0:head] + left)
        corner = weight * (x_ref[head:n, head:n] + corners[:, tail : 2 * tail])
        x_ref[:, 0:head] = left
        x_ref[head:n, head:n] = corner
        store(both, n, left, corner)
        return keep * keep

    rho2 = keep * keep

    def sides(source, span):
        return [source[i, span[0] : span[1], 0:n] for i in (0, 1)]

    def put(targets, start, span, block):
        for target, part in zip(targets, split(block)):
            target[span[0] : span[1], start : start + head] = part
        low = max(span[0], head)
        if low < span[1]:
            for target, part in zip(targets, split(jnp.transpose(block[low - span[0] :]))):
                target[0:head, start + low : start + span[1]] = part

    def put_corner(targets, start, block):
        for target, part in zip(targets, split(block)):
            target[head:n, start + head : start + n] = part

    def put_x(targets, start, weight, span, product):
        x = weight * (x_ref[span[0] : span[1], 0:head] + product)
        x_ref[span[0] : span[1], 0:head] = x
        put(targets, start, span, x)

    def put_x_corner(targets, start, weight, product):
        x = weight * (x_ref[head:n, head:n] + product)
        x_ref[head:n, head:n] = x
        put_corner(targets, start, x)

    waiting = None
    source, target = wa, wb
    for _ in range(5):
        weight = 2.0 / (2.0 - rho2)
        keep = 0.5 * rho2 * weight
        first = (source[0, :, 0:head], source[1, :, 0:head])
        r = []
        for k, span in enumerate(chunks):
            r.append(dot3(sides(source, span), first))
            if waiting is not None:
                put_x((source.at[0], source.at[1]), n, waiting[0], span, waiting[1][k])
        if waiting is not None:
            put_x_corner((source.at[0], source.at[1]), n, waiting[0], waiting[2])
        ends = [jnp.concatenate([source[i, :, head:n], source[i, :, n + head : 2 * n]], axis=1) for i in (0, 1)]
        corners = dot3(sides(source, (head, n)), ends)
        first = (source[0, :, n : n + head], source[1, :, n : n + head])
        both = (target.at[0], target.at[1])
        x = []
        for k, span in enumerate(chunks):
            x.append(dot3(sides(source, span), first))
            put(both, 0, span, weight * r[k] - keep * eye_ref[span[0] : span[1], 0:head])
        put_corner(both, 0, weight * corners[:, 0:tail] - keep * eye_ref[head:n, head:n])
        waiting = (weight, x, corners[:, tail : 2 * tail])
        rho2 = keep * keep
        source, target = target, source
    for k, span in enumerate(chunks):
        put_x((source.at[0], source.at[1]), n, waiting[0], span, waiting[1][k])
    put_x_corner((source.at[0], source.at[1]), n, waiting[0], waiting[2])

    def twice(_, rho2):
        return advance(target, source, advance(source, target, rho2))

    rho2 = lax.fori_loop(0, pairs, twice, rho2)
    weight = 2.0 / (2.0 - rho2)
    first = (source[0, :, n : n + head], source[1, :, n : n + head])
    done = (xh_ref, xl_ref)
    ends = [source[i, :, n + head : 2 * n] for i in (0, 1)]
    put_x_corner(done, 0, weight, dot3(sides(source, (head, n)), ends))
    x = [dot3(sides(source, span), first) for span in chunks]
    for k, span in enumerate(chunks):
        put_x(done, 0, weight, span, x[k])


def centred(fields):
    members = sum(field.shape[0] for field in fields)
    mean = sum(jnp.sum(field, axis=0, keepdims=True) for field in fields) * (1.0 / members)
    pairs = [split(field - mean) for field in fields]
    return [jnp.concatenate(parts, axis=0) for parts in zip(*pairs)], mean


def in_chunks(count, product, work):
    waiting = None
    for start in range(0, count, CHUNK):
        span = slice(start, min(start + CHUNK, count))
        result = product(span)
        if waiting is not None:
            work(*waiting)
        waiting = (span, result)
    work(*waiting)


def solve(n_ref, s, g_ref, x, anomaly, z_ref, cross_ref, parts_ref, crossed_already=False):
    n = z_ref.shape[0]

    def keep(slot, span, value):
        for i, part in enumerate(split(value)):
            parts_ref[slot, i, span] = part

    def kept(slot):
        return parts_ref[slot, 0], parts_ref[slot, 1]

    def some(parts, span):
        return [part[span] for part in parts]

    def crossed(span, value):
        cross_ref[span] = value
        keep(0, span, value)

    def solved(span, value):
        z_ref[span] = value
        keep(1, span, value)

    def left(span, value):
        keep(0, span, cross_ref[span] - z_ref[span] - value)

    def refined(span, value):
        z_ref[span] = z_ref[span] + value

    if crossed_already:
        keep(0, slice(0, n), cross_ref[...])
    else:
        in_chunks(n, lambda span: dot3(some(s, span), [part[...] for part in anomaly]), crossed)
    in_chunks(n, lambda span: dot3(some(x, span), kept(0)), solved)
    in_chunks(n, lambda span: dot3(split(g_ref[span]), kept(1)), left)
    in_chunks(n, lambda span: dot3(some(x, span), kept(0)), refined)

    def refine(_, carry):
        z = z_ref[...]
        gz = lax.dot_general(g_ref[...], z, NN, precision=HIGHEST, preferred_element_type=F32)
        z_ref[...] = z + dot3([part[...] for part in x], split(cross_ref[...] - z - gz))
        return carry

    lax.fori_loop(0, n_ref[0], refine, 0)


def gain_kernel(batch, parts, own_of, region_ref, column_ref, n_ref, cells_ref, sh_ref, sl_ref, d_ref, g_ref, *refs):
    xh_ref, xl_ref, *refs = refs
    states = refs[:parts]
    z_ref, rows_ref, scratch, anomaly_ref, cross_ref, parts_ref = refs[parts:]
    anomaly, mean = centred([state[...] for state in states])
    for i, part in enumerate(anomaly):
        anomaly_ref[i] = part
    anomaly = (anomaly_ref.at[0], anomaly_ref.at[1])
    solve(n_ref, (sh_ref, sl_ref), g_ref, (xh_ref, xl_ref), anomaly, z_ref, cross_ref, parts_ref)
    s = (sh_ref[...], sl_ref[...])
    picks = cells_ref[pl.ds(own_of(region_ref, column_ref), 1), batch, :]
    hot = selector(picks, mean.shape[1], scratch)
    zt = split(select(hot, split(z_ref[...]), NT))
    base = jnp.sum(hot * mean, axis=1, keepdims=True) + dot3(zt, split(d_ref[...]))[:, 0:1]
    picked = select(hot, [part[...] for part in anomaly], NT)
    rows_ref[...] = base + picked - 0.5 * dot3(zt, s)


def updated(field, start, s, shift, z):
    size = field.shape[0]
    return field + shift - 0.5 * dot3([h[:, start : start + size] for h in s], z, TN)


def shift_of(z, d_ref):
    return jnp.sum(z * d_ref[:, 0:1], axis=0, keepdims=True)


def update_kernel(starts, sh_ref, sl_ref, d_ref, z_ref, *refs):
    count = len(starts)
    states, outs, parts = refs[:count], refs[count : 2 * count], refs[2 * count :]
    z = z_ref[...]
    shift = shift_of(z, d_ref)
    s, zs = (sh_ref[...], sl_ref[...]), split(z)
    for start, state, out in zip(starts, states, outs):
        out[...] = updated(state[...], start, s, shift, zs)
    if parts:
        anomaly, _ = centred([out[...] for out in outs])
        for ref, part in zip(parts, anomaly):
            ref[...] = part


def last_kernel(n_ref, sh_ref, sl_ref, d_ref, g_ref, xh_ref, xl_ref, state_ref, *refs):
    cross, z_ref, out_ref, scratch_ref, parts_ref = refs if len(refs) == 5 else (None, *refs)
    given = cross is not None
    cross_ref = cross if given else scratch_ref
    anomaly = None if given else centred([state_ref[...]])[0]
    x = (xh_ref, xl_ref)
    solve(n_ref, (sh_ref, sl_ref), g_ref, x, anomaly, z_ref, cross_ref, parts_ref, given)
    z = z_ref[...]
    start = sh_ref.shape[1] - state_ref.shape[0]
    s = (sh_ref[...], sl_ref[...])
    out_ref[...] = updated(state_ref[...], start, s, shift_of(z, d_ref), split(z))


def join_kernel(column_ref, mine_ref, theirs_ref, out_ref, both, sems):
    chunks = sems.shape[0]
    size = both.shape[0] // chunks
    column = column_ref[0]
    copies = []
    for i in range(chunks):
        at = slice(i * size, (i + 1) * size)
        mine, theirs = mine_ref[at, :], theirs_ref[at, :]
        both[at, 0, :] = jnp.where(column == 0, mine, theirs)
        both[at, 1, :] = jnp.where(column == 0, theirs, mine)
        span = pl.ds(i * size, size)
        copies.append(pltpu.make_async_copy(both.at[span], out_ref.at[span], sems.at[i]))
        copies[-1].start()
    for copy in copies:
        copy.wait()


def prepare(pieces, batch, members, patches_of, place, near, values, var, anomaly, sources, n):
    width = anomaly[0].shape[1]
    outs = [
        ((n, members), BF16, VMEM),
        ((n, members), BF16, VMEM),
        ((n, 128), F32, VMEM),
        ((n, n), F32, VMEM),
        ((n, width), F32, VMEM),
    ]
    kernel = functools.partial(prepare_kernel, pieces, batch, members, patches_of, len(place))
    args = [*place, near, values, var, *anomaly, *sources]
    ins = [SMEM] * (len(place) + 1) + [VMEM] * (len(args) - len(place) - 1)
    return call(kernel, outs, ins, args, [pltpu.VMEM((128, 128), F32)], 6 * n * width * members)


def factor(pieces, batch, members, chunk, patches_of, place, near, values, var, sources, ready=0, before=()):
    per_patch = values.shape[2]
    n = len(pieces) * per_patch
    outs = [
        ((n, members), BF16, VMEM),
        ((n, members), BF16, VMEM),
        ((n, 128), F32, VMEM),
        ((n, n), F32, VMEM),
        ((n, n), BF16, VMEM),
        ((n, n), BF16, VMEM),
        ((1,), jnp.int32, SMEM),
    ]
    args = [*place, near, values, var, *sources, *before]
    aliases = {}
    if ready:
        outs.append((before[-1].shape, F32, VMEM))
        first = len(args) - 5
        aliases = {first: 0, first + 1: 1, first + 2: 2, first + 3: 3, first + 4: 7}
    scratch = [
        pltpu.VMEM((128, 128), F32),
        pltpu.VMEM((n, n), F32),
        pltpu.VMEM((n, n), F32),
        pltpu.VMEM((2, n, 2 * n), BF16),
        pltpu.VMEM((2, n, 2 * n), BF16),
    ]
    kernel = functools.partial(factor_kernel, pieces, batch, members, chunk, patches_of, len(place), ready)
    flops = 6 * n * n * members + 60 * n * n * n
    ins = [SMEM] * (len(place) + 1) + [VMEM] * (len(args) - len(place) - 1)
    return call(kernel, outs, ins, args, scratch, flops, FACTOR_LIMIT, aliases)


def solver_scratch(n, width):
    return [pltpu.VMEM((n, width), F32), pltpu.VMEM((2, 2, n, width), BF16)]


def gain(batch, own_of, place, cells, factored, states):
    sh, sl, d, g, xh, xl, more = factored[:7]
    n, members = sh.shape
    width = states[0].shape[1]
    kernel = functools.partial(gain_kernel, batch, len(states), own_of)
    outs = [((n, width), F32, VMEM), ((cells.shape[2], members), F32, VMEM)]
    ins = [SMEM] * 3 + [VMEM] * (7 + len(states))
    args = [*place, more, cells, sh, sl, d, g, xh, xl, *states]
    flops = 8 * n * members * width
    scratch = [pltpu.VMEM((8, 128), jnp.int32), pltpu.VMEM((2, members, width), BF16)]
    scratch += solver_scratch(n, width)
    return call(kernel, outs, ins, args, scratch, flops)


def update(factored, z, states, starts, more=False):
    sh, sl, d = factored[:3]
    kernel = functools.partial(update_kernel, starts)
    outs = [(state.shape, F32, VMEM) for state in states]
    if more:
        outs += [((sh.shape[1], z.shape[1]), BF16, VMEM)] * 2
    flops = 6 * sh.shape[0] * sh.shape[1] * z.shape[1]
    return call(kernel, outs, [VMEM] * (4 + len(states)), [sh, sl, d, z, *states], (), flops)


def last(factored, state):
    sh, sl, d, g, xh, xl, more, *cross = factored
    n, width = sh.shape[0], state.shape[1]
    outs = [((n, width), F32, VMEM), (state.shape, F32, VMEM)]
    args = [more, sh, sl, d, g, xh, xl, state, *cross]
    flops = 12 * sh.shape[0] * sh.shape[1] * width
    ins = [SMEM] + [VMEM] * (len(args) - 1)
    return call(last_kernel, outs, ins, args, solver_scratch(n, width), flops)


def rings(size):
    up = [(i, (i + 1) % size) for i in range(size)]
    return up, [(j, i) for i, j in up]


BOTH = ("region", "member")


def permute(x, moves, regions):
    table = []
    for region in range(regions):
        for column in range(2):
            pair, parity, to = moves(region // 2, region % 2, column)
            pair %= regions // 2
            table.append((region * 2 + column, (pair * 2 + parity) * 2 + to))
    return lax.ppermute(x, BOTH, table)


def paired(state, neighbours, obs_cell, obs_values, obs_var):
    half, _, cells = state.shape
    members = 2 * half
    regions = lax.axis_size("region")
    region, column = lax.axis_index("region"), lax.axis_index("member")
    place = (region.astype(jnp.int32)[None], column.astype(jnp.int32)[None])
    near = neighbours.T

    def own_of(region_ref, column_ref):
        return region_ref[0] * 2 + column_ref[0]

    def around(region, within):
        side = 2 * lax.rem(region, 2) - 1
        outer = lax.rem(region + regions + side, regions)
        return [r * 2 + p for p in within for r in (region, region - side, outer)]

    def patches_first(region_ref, column_ref):
        return around(region_ref[0], (0, 1)), own_of(region_ref, column_ref)

    def patches_next(region_ref, column_ref):
        column = column_ref[0]
        return around(region_ref[0], (column, 1 - column)), own_of(region_ref, column_ref)

    def across(x):
        return permute(x, lambda c, q, m: (c, q, 1 - m), regions)

    def beside(x):
        return permute(x, lambda c, q, m: (c, 1 - q, m), regions)

    def outside(x):
        return permute(x, lambda c, q, m: (c + 2 * q - 1, 1 - q, m), regions)

    anywhere = pl.BlockSpec(memory_space=pl.ANY)
    (rows,) = call(
        pick_kernel,
        [((2, obs_cell.shape[2], half), F32, VMEM)],
        [SMEM, VMEM, VMEM],
        [place[0], obs_cell, state],
        [pltpu.VMEM((8, 128), jnp.int32), pltpu.VMEM((2, half, cells), F32)],
    )
    other = across(rows)
    far = permute(rows, lambda c, q, m: (c + 2 * q - 1, 1 - q, 1 - m), regions)
    sources = [rows, beside(rows), outside(rows), other, beside(other), far]
    shape = ((half, cells), F32, VMEM)
    keep, send, values, var = call(
        sort_kernel,
        [shape, shape, (obs_values.shape, F32, VMEM), (obs_var.shape, F32, VMEM)],
        [SMEM, anywhere, anywhere, VMEM, anywhere],
        [place[1], obs_values, obs_var, state, other],
        [pltpu.SemaphoreType.DMA((2,))],
    )
    pieces = [[(i, (p,), 0), (3 + i, (p,), 1)] for p in range(2) for i in range(3)]
    states = [keep, across(send)]
    factored = factor(pieces, 0, members, CHUNK, patches_first, place, near, values, var, sources)
    everything = slice(None)
    low, high = (everything, slice(0, half)), (everything, slice(half, members))
    pieces = [[(i, low, 0), (i, high, 1)] for i in range(3)]
    pieces += [[(i, high, 0), (i, low, 1)] for i in range(3, 6)]
    early = 4
    for batch in range(1, NBATCH):
        z, rows = gain(batch, own_of, place, obs_cell, factored, states)
        other = across(rows)
        sources = [rows, beside(rows), outside(rows), other, beside(other), outside(other)]
        mine, theirs, *anomaly = update(factored, z, states, (0, half), True)
        states = [mine, theirs]
        given = (place, near, values, var)
        n = factored[0].shape[0]
        done = prepare(pieces[:early], batch, members, patches_next, *given, anomaly, sources[:early], n)
        factored = factor(
            pieces, batch, members, CHUNK, patches_next, *given, sources, early, [*anomaly, *done]
        )
    z, theirs = last(factored, states[1])
    theirs = across(theirs)
    (mine,) = update(factored, z, states[:1], (0,))
    return pl.pallas_call(
        join_kernel,
        out_shape=jax.ShapeDtypeStruct(state.shape, F32),
        in_specs=[SMEM, VMEM, VMEM],
        out_specs=anywhere,
        scratch_shapes=[pltpu.VMEM(state.shape, F32), pltpu.SemaphoreType.DMA((4,))],
        compiler_params=pltpu.CompilerParams(vmem_limit_bytes=16 * 1024 * 1024),
    )(place[1], mine, theirs)


def listed(table_ref):
    blocks = table_ref.shape[0] - 1
    return [table_ref[i] for i in range(blocks)], table_ref[blocks]


def general(state, neighbours, obs_cell, obs_values, obs_var):
    ensemble = lax.all_to_all(state, "member", split_axis=1, concat_axis=0, tiled=True)
    members, owned, cells = ensemble.shape
    regions = lax.axis_size("region")
    region_patches = owned * lax.axis_size("member")
    region = lax.axis_index("region")
    first = region * region_patches + lax.axis_index("member") * owned
    up, down = rings(regions)
    fields = [ensemble[:, p, :] for p in range(owned)]
    grid = jnp.arange(cells, dtype=jnp.int32)
    for batch in range(NBATCH):
        picks = lax.dynamic_slice_in_dim(obs_cell, first, owned, 0)[:, batch, :]
        hot = (picks[:, :, None] == grid[None, None, :]).astype(F32)
        own_rows = jnp.einsum("poc,pkc->pok", hot, jnp.stack(fields), precision=HIGHEST)
        region_rows = lax.all_gather(own_rows, "member", axis=0, tiled=True)
        before = lax.ppermute(region_rows, "region", up)
        after = lax.ppermute(region_rows, "region", down)
        beside = jnp.concatenate([before, region_rows, after], axis=0)
        new = []
        for p in range(owned):
            own = first + p
            links = lax.dynamic_index_in_dim(neighbours, own, 0, keepdims=False)
            ids = jnp.concatenate([own[None], links]).astype(jnp.int32)
            table = jnp.concatenate([ids, own[None]]).astype(jnp.int32)
            home = (ids // region_patches - region + 1) % regions
            rows = jnp.take(beside, home * region_patches + ids % region_patches, axis=0)
            pieces = [[(0, (i,), 0)] for i in range(ids.shape[0])]
            factored = factor(
                pieces, batch, members, CHUNK, listed, [table], neighbours.T, obs_values, obs_var, [rows]
            )
            new.append(last(factored, fields[p])[1])
        fields = new
    ensemble = jnp.stack(fields, axis=1)
    return lax.all_to_all(ensemble, "member", split_axis=0, concat_axis=1, tiled=True)


def on_device(state, neighbours, obs_cell, obs_values, obs_var):
    patches, links = state.shape[1], neighbours.shape[1]
    even = lax.axis_size("region") % 2 == 0
    if even and patches == 2 and lax.axis_size("member") == 2 and links + 1 == 3 * patches:
        return paired(state, neighbours, obs_cell, obs_values, obs_var)
    return general(state, neighbours, obs_cell, obs_values, obs_var)


def solution(mesh):
    in_specs = (P("member", "region", None), P(), P(), P(), P())
    out_specs = P("member", "region", None)
    return jax.shard_map(
        on_device, mesh=mesh, in_specs=in_specs, out_specs=out_specs, check_vma=False
    )
```

```python
import functools
import math

import jax
import jax.numpy as jnp
from jax import lax
from jax.experimental import pallas as pl
from jax.experimental.pallas import tpu as pltpu
from jax.sharding import PartitionSpec as P

NBATCH = 2
HIGHEST = lax.Precision.HIGHEST
F32 = jnp.float32
BF16 = jnp.bfloat16
VMEM = pl.BlockSpec(memory_space=pltpu.VMEM)
SMEM = pl.BlockSpec(memory_space=pltpu.SMEM)
NN = (((1,), (0,)), ((), ()))
NT = (((1,), (1,)), ((), ()))
TN = (((0,), (0,)), ((), ()))
RESIDUAL = 1e-3
FACTOR_LIMIT = 24
MOST_STEPS = 15
TILE = 256
CHUNK = 128


def call(kernel, outs, ins, args, scratch=(), flops=0, limit=16, aliases=None):
    shapes = [jax.ShapeDtypeStruct(shape, dtype) for shape, dtype, _ in outs]
    moved = sum(math.prod(s.shape) * s.dtype.itemsize for s in shapes)
    moved += sum(a.size * a.dtype.itemsize for a in args)
    return pl.pallas_call(
        kernel,
        out_shape=shapes,
        in_specs=ins,
        out_specs=[space for _, _, space in outs],
        scratch_shapes=list(scratch),
        input_output_aliases=aliases or {},
        compiler_params=pltpu.CompilerParams(vmem_limit_bytes=limit * 1024 * 1024),
        cost_estimate=pl.CostEstimate(flops=flops, bytes_accessed=moved, transcendentals=0),
    )(*args)


def split(x):
    high = x.astype(BF16)
    return high, (x - high.astype(F32)).astype(BF16)


def dot(a, b, dims=NN):
    return lax.dot_general(a, b, dims, preferred_element_type=F32)


def dot3(a, b, dims=NN):
    (left,), (right,) = dims[0]
    lhs = jnp.concatenate([a[0], a[0], a[1]], axis=left)
    rhs = jnp.concatenate([b[0], b[1], b[0]], axis=right)
    return dot(lhs, rhs, dims)


def select(hot, parts, dims):
    (left,), (right,) = dims[0]
    hot = hot.astype(BF16)
    lhs = jnp.concatenate([hot] * len(parts), axis=left)
    return dot(lhs, jnp.concatenate(parts, axis=right), dims)


def split_all(x):
    high, middle = split(x)
    low = x - high.astype(F32) - middle.astype(F32)
    return high, middle, low.astype(BF16)


def step_limits():
    limits = []
    for steps in range(MOST_STEPS):
        rho = RESIDUAL
        for _ in range(steps):
            rho = math.sqrt(2.0 * rho / (1.0 + rho))
        limits.append(2.0 * rho / (1.0 - rho) if rho < 1.0 else math.inf)
    return limits


def diagonal(n, columns, first):
    row = lax.broadcasted_iota(jnp.int32, (n, columns), 0)
    column = lax.broadcasted_iota(jnp.int32, (n, columns), 1)
    return row + first == column


def selector(picks, cells, scratch):
    per_patch = picks.shape[1]
    scratch[...] = jnp.full_like(scratch, -1)
    scratch[0:1, 0:per_patch] = picks
    grid = lax.broadcasted_iota(jnp.int32, (cells, scratch.shape[1]), 0)
    hot = (grid == scratch[0:1, :]).astype(F32)
    return jnp.transpose(hot)[0:per_patch, :]


def pick_kernel(region_ref, cells_ref, state_ref, rows_ref, scratch, field_ref):
    patches, cells = state_ref.shape[1:]
    for p in range(patches):
        field_ref[p] = state_ref[:, p, :]
        hot = selector(cells_ref[pl.ds(region_ref[0] * patches + p, 1), 0, :], cells, scratch)
        rows_ref[p] = select(hot, split_all(field_ref[p]), NT)


def sort_kernel(column_ref, values_hbm, var_hbm, state_ref, *refs):
    keep_ref, send_ref, values_ref, var_ref, sems = refs[-5:]
    copies = [
        pltpu.make_async_copy(values_hbm, values_ref, sems.at[0]),
        pltpu.make_async_copy(var_hbm, var_ref, sems.at[1]),
    ]
    for copy in copies:
        copy.start()
    column = column_ref[0]
    first, second = state_ref[:, 0, :], state_ref[:, 1, :]
    keep_ref[...] = jnp.where(column == 0, first, second)
    send_ref[...] = jnp.where(column == 0, second, first)
    for copy in copies:
        copy.wait()


def table(patches, own, near_ref, values_ref, var_ref, batch, flat):
    per_patch = values_ref.shape[2]
    blocks = len(patches)
    flat[...] = jnp.ones_like(flat)
    for i, patch in enumerate(patches):
        widening = (patch == own).astype(jnp.int32)
        for j in range(near_ref.shape[0]):
            widening = widening + (near_ref[j, own] == patch).astype(jnp.int32) * (j + 2)
        flat[i : i + 1, 0:per_patch] = values_ref[pl.ds(patch, 1), batch, :]
        noise = var_ref[pl.ds(patch, 1), batch, :] * widening.astype(F32)
        flat[blocks + i : blocks + i + 1, 0:per_patch] = noise
    upright = jnp.transpose(flat[...])[0:per_patch]
    return [(upright[:, i : i + 1], upright[:, blocks + i : blocks + i + 1]) for i in range(blocks)]


def scale_block(i, piece, sources, column, members, sh_ref, sl_ref, d_ref):
    value, noise = column
    rows = [sources[which][index] for which, index, _ in piece]
    total = sum(jnp.sum(part, axis=1, keepdims=True) for part in rows)
    mean = total * (1.0 / members)
    scale = lax.rsqrt(noise * (members - 1.0))
    per_patch = value.shape[0]
    at = slice(i * per_patch, (i + 1) * per_patch)
    for part, (_, _, start) in zip(rows, piece):
        size = part.shape[1]
        lanes = slice(start * size, (start + 1) * size)
        sh_ref[at, lanes], sl_ref[at, lanes] = split((part - mean) * scale)
    d_ref[at, :] = jnp.broadcast_to((value - mean) * scale, (per_patch, d_ref.shape[1]))


def prepare_kernel(pieces, batch, members, patches_of, places, *refs):
    place_refs, refs = refs[:places], refs[places:]
    near_ref, values_ref, var_ref, ah_ref, al_ref, *refs = refs
    sources, (sh_ref, sl_ref, d_ref, g_ref, cross_ref, flat) = refs[:-6], refs[-6:]
    patches, own = patches_of(*place_refs)
    columns = table(patches[: len(pieces)], own, near_ref, values_ref, var_ref, batch, flat)
    for i, piece in enumerate(pieces):
        scale_block(i, piece, sources, columns[i], members, sh_ref, sl_ref, d_ref)
    count = len(pieces) * values_ref.shape[2]
    s = (sh_ref[0:count], sl_ref[0:count])
    g_ref[0:count, 0:count] = dot3(s, s, NT)
    cross_ref[0:count] = dot3(s, (ah_ref[...], al_ref[...]))


def factor_kernel(pieces, batch, members, chunk, patches_of, places, ready, *refs):
    place_refs, refs = refs[:places], refs[places:]
    near_ref, values_ref, var_ref, *refs = refs
    refs, (flat, eye_ref, x_ref, wa, wb) = refs[:-5], refs[-5:]
    if ready:
        refs, cross_ref = refs[:-1], refs[-1]
    refs, (sh_ref, sl_ref, d_ref, g_ref, xh_ref, xl_ref, n_ref) = refs[:-7], refs[-7:]
    if ready:
        refs, (ah_ref, al_ref) = refs[:-7], refs[-7:-5]
    sources = refs
    per_patch = values_ref.shape[2]
    blocks = len(pieces)
    patches, own = patches_of(*place_refs)
    columns = table(patches[ready:], own, near_ref, values_ref, var_ref, batch, flat)
    for i in range(ready, blocks):
        scale_block(i, pieces[i], sources, columns[i - ready], members, sh_ref, sl_ref, d_ref)
    n = sh_ref.shape[0]
    head = min(TILE, n)
    tail = n - head
    chunks = [(i, min(i + chunk, n)) for i in range(0, n, chunk)]
    left = (sh_ref[0:head], sl_ref[0:head])
    fresh = ready * per_patch
    g_ref[fresh:n, 0:head] = dot3((sh_ref[fresh:n], sl_ref[fresh:n]), left, NT)
    low = (sh_ref[head:n], sl_ref[head:n])
    g_ref[head:n, head:n] = dot3(low, low, NT)
    g_ref[0:head, head:n] = jnp.transpose(g_ref[head:n, 0:head])
    if ready:
        cross_ref[fresh:n] = dot3((sh_ref[fresh:n], sl_ref[fresh:n]), (ah_ref[...], al_ref[...]))
    g = g_ref[...]
    square = jnp.sum(jnp.sum(g * g, axis=0, keepdims=True), axis=1, keepdims=True)
    norm = jnp.sqrt(square) * (1.0 + 1e-5)
    size = square[0, 0]
    limits = step_limits()
    pairs = jnp.int32(0)
    for k in range(7, MOST_STEPS - 2, 2):
        limit = limits[k] * (1.0 - 1e-4)
        pairs = pairs + (size > limit * limit).astype(jnp.int32)
    n_ref[0] = (size > 1.6e7).astype(jnp.int32) + (size > 1e8).astype(jnp.int32)
    eye_ref[...] = diagonal(n, n, 0).astype(F32)
    eye = eye_ref[...]
    first = 2.0 / (2.0 + norm)
    rho = norm * (0.5 * first)
    rho2 = rho * rho
    weight = 2.0 / (2.0 - rho2)
    keep = 0.5 * rho2 * weight
    r = (1.0 - first) * eye - first * g
    parts = split(r)
    x = (weight * first) * (eye + r)
    x_ref[...] = x
    for i, part in enumerate(split(x)):
        wa[i, :, n : 2 * n] = part

    def store(targets, start, left, corner):
        blocks = [(slice(0, n), slice(start, start + head), left)]
        blocks.append((slice(head, n), slice(start + head, start + n), corner))
        blocks.append((slice(0, head), slice(start + head, start + n), jnp.transpose(left[head:n])))
        for rows, columns, block in blocks:
            for target, part in zip(targets, split(block)):
                target[rows, columns] = part

    def corner_of(weight, keep, left, corner):
        left = weight * left - keep * eye_ref[:, 0:head]
        return left, weight * corner - keep * eye_ref[head:n, head:n]

    left = dot3(parts, [part[:, 0:head] for part in parts])
    corner = dot3([part[head:n] for part in parts], [part[:, head:n] for part in parts])
    store((wa.at[0], wa.at[1]), 0, *corner_of(weight, keep, left, corner))

    def advance(source, target, rho2):
        weight = 2.0 / (2.0 - rho2)
        keep = 0.5 * rho2 * weight
        parts = (source[0, :, 0:n], source[1, :, 0:n])
        ends = [jnp.concatenate([source[i, :, head:n], source[i, :, n + head : 2 * n]], axis=1) for i in (0, 1)]
        left = dot3(parts, (source[0, :, 0:head], source[1, :, 0:head]))
        corners = dot3([part[head:n] for part in parts], ends)
        both = (target.at[0], target.at[1])
        store(both, 0, *corner_of(weight, keep, left, corners[:, 0:tail]))
        left = dot3(parts, (source[0, :, n : n + head], source[1, :, n : n + head]))
        left = weight * (x_ref[:, 0:head] + left)
        corner = weight * (x_ref[head:n, head:n] + corners[:, tail : 2 * tail])
        x_ref[:, 0:head] = left
        x_ref[head:n, head:n] = corner
        store(both, n, left, corner)
        return keep * keep

    rho2 = keep * keep

    def sides(source, span):
        return [source[i, span[0] : span[1], 0:n] for i in (0, 1)]

    def put(targets, start, span, block):
        for target, part in zip(targets, split(block)):
            target[span[0] : span[1], start : start + head] = part
        low = max(span[0], head)
        if low < span[1]:
            for target, part in zip(targets, split(jnp.transpose(block[low - span[0] :]))):
                target[0:head, start + low : start + span[1]] = part

    def put_corner(targets, start, block):
        for target, part in zip(targets, split(block)):
            target[head:n, start + head : start + n] = part

    def put_x(targets, start, weight, span, product):
        x = weight * (x_ref[span[0] : span[1], 0:head] + product)
        x_ref[span[0] : span[1], 0:head] = x
        put(targets, start, span, x)

    def put_x_corner(targets, start, weight, product):
        x = weight * (x_ref[head:n, head:n] + product)
        x_ref[head:n, head:n] = x
        put_corner(targets, start, x)

    waiting = None
    source, target = wa, wb
    for _ in range(5):
        weight = 2.0 / (2.0 - rho2)
        keep = 0.5 * rho2 * weight
        first = (source[0, :, 0:head], source[1, :, 0:head])
        r = []
        for k, span in enumerate(chunks):
            r.append(dot3(sides(source, span), first))
            if waiting is not None:
                put_x((source.at[0], source.at[1]), n, waiting[0], span, waiting[1][k])
        if waiting is not None:
            put_x_corner((source.at[0], source.at[1]), n, waiting[0], waiting[2])
        ends = [jnp.concatenate([source[i, :, head:n], source[i, :, n + head : 2 * n]], axis=1) for i in (0, 1)]
        corners = dot3(sides(source, (head, n)), ends)
        first = (source[0, :, n : n + head], source[1, :, n : n + head])
        both = (target.at[0], target.at[1])
        x = []
        for k, span in enumerate(chunks):
            x.append(dot3(sides(source, span), first))
            put(both, 0, span, weight * r[k] - keep * eye_ref[span[0] : span[1], 0:head])
        put_corner(both, 0, weight * corners[:, 0:tail] - keep * eye_ref[head:n, head:n])
        waiting = (weight, x, corners[:, tail : 2 * tail])
        rho2 = keep * keep
        source, target = target, source
    for k, span in enumerate(chunks):
        put_x((source.at[0], source.at[1]), n, waiting[0], span, waiting[1][k])
    put_x_corner((source.at[0], source.at[1]), n, waiting[0], waiting[2])

    def twice(_, rho2):
        return advance(target, source, advance(source, target, rho2))

    rho2 = lax.fori_loop(0, pairs, twice, rho2)
    weight = 2.0 / (2.0 - rho2)
    first = (source[0, :, n : n + head], source[1, :, n : n + head])
    done = (xh_ref, xl_ref)
    ends = [source[i, :, n + head : 2 * n] for i in (0, 1)]
    put_x_corner(done, 0, weight, dot3(sides(source, (head, n)), ends))
    x = [dot3(sides(source, span), first) for span in chunks]
    for k, span in enumerate(chunks):
        put_x(done, 0, weight, span, x[k])


def centred(fields):
    members = sum(field.shape[0] for field in fields)
    mean = sum(jnp.sum(field, axis=0, keepdims=True) for field in fields) * (1.0 / members)
    pairs = [split(field - mean) for field in fields]
    return [jnp.concatenate(parts, axis=0) for parts in zip(*pairs)], mean


def in_chunks(count, product, work):
    waiting = None
    for start in range(0, count, CHUNK):
        span = slice(start, min(start + CHUNK, count))
        result = product(span)
        if waiting is not None:
            work(*waiting)
        waiting = (span, result)
    work(*waiting)


def solve(n_ref, s, g_ref, x, anomaly, z_ref, cross_ref, parts_ref, crossed_already=False):
    n = z_ref.shape[0]

    def keep(slot, span, value):
        for i, part in enumerate(split(value)):
            parts_ref[slot, i, span] = part

    def kept(slot):
        return parts_ref[slot, 0], parts_ref[slot, 1]

    def some(parts, span):
        return [part[span] for part in parts]

    def crossed(span, value):
        cross_ref[span] = value
        keep(0, span, value)

    def solved(span, value):
        z_ref[span] = value
        keep(1, span, value)

    def left(span, value):
        keep(0, span, cross_ref[span] - z_ref[span] - value)

    def refined(span, value):
        z_ref[span] = z_ref[span] + value

    if crossed_already:
        keep(0, slice(0, n), cross_ref[...])
    else:
        in_chunks(n, lambda span: dot3(some(s, span), [part[...] for part in anomaly]), crossed)
    in_chunks(n, lambda span: dot3(some(x, span), kept(0)), solved)
    in_chunks(n, lambda span: dot3(split(g_ref[span]), kept(1)), left)
    in_chunks(n, lambda span: dot3(some(x, span), kept(0)), refined)

    def refine(_, carry):
        z = z_ref[...]
        gz = lax.dot_general(g_ref[...], z, NN, precision=HIGHEST, preferred_element_type=F32)
        z_ref[...] = z + dot3([part[...] for part in x], split(cross_ref[...] - z - gz))
        return carry

    lax.fori_loop(0, n_ref[0], refine, 0)


def gain_kernel(batch, parts, own_of, region_ref, column_ref, n_ref, cells_ref, sh_ref, sl_ref, d_ref, g_ref, *refs):
    xh_ref, xl_ref, *refs = refs
    states = refs[:parts]
    z_ref, rows_ref, scratch, anomaly_ref, cross_ref, parts_ref = refs[parts:]
    anomaly, mean = centred([state[...] for state in states])
    for i, part in enumerate(anomaly):
        anomaly_ref[i] = part
    anomaly = (anomaly_ref.at[0], anomaly_ref.at[1])
    solve(n_ref, (sh_ref, sl_ref), g_ref, (xh_ref, xl_ref), anomaly, z_ref, cross_ref, parts_ref)
    s = (sh_ref[...], sl_ref[...])
    picks = cells_ref[pl.ds(own_of(region_ref, column_ref), 1), batch, :]
    hot = selector(picks, mean.shape[1], scratch)
    zt = split(select(hot, split(z_ref[...]), NT))
    base = jnp.sum(hot * mean, axis=1, keepdims=True) + dot3(zt, split(d_ref[...]))[:, 0:1]
    picked = select(hot, [part[...] for part in anomaly], NT)
    rows_ref[...] = base + picked - 0.5 * dot3(zt, s)


def updated(field, start, s, shift, z):
    size = field.shape[0]
    return field + shift - 0.5 * dot3([h[:, start : start + size] for h in s], z, TN)


def shift_of(z, d_ref):
    return jnp.sum(z * d_ref[:, 0:1], axis=0, keepdims=True)


def update_kernel(starts, sh_ref, sl_ref, d_ref, z_ref, *refs):
    count = len(starts)
    states, outs, parts = refs[:count], refs[count : 2 * count], refs[2 * count :]
    z = z_ref[...]
    shift = shift_of(z, d_ref)
    s, zs = (sh_ref[...], sl_ref[...]), split(z)
    for start, state, out in zip(starts, states, outs):
        out[...] = updated(state[...], start, s, shift, zs)
    if parts:
        anomaly, _ = centred([out[...] for out in outs])
        for ref, part in zip(parts, anomaly):
            ref[...] = part


def last_kernel(n_ref, sh_ref, sl_ref, d_ref, g_ref, xh_ref, xl_ref, state_ref, *refs):
    cross, z_ref, out_ref, scratch_ref, parts_ref = refs if len(refs) == 5 else (None, *refs)
    given = cross is not None
    cross_ref = cross if given else scratch_ref
    anomaly = None if given else centred([state_ref[...]])[0]
    x = (xh_ref, xl_ref)
    solve(n_ref, (sh_ref, sl_ref), g_ref, x, anomaly, z_ref, cross_ref, parts_ref, given)
    z = z_ref[...]
    start = sh_ref.shape[1] - state_ref.shape[0]
    s = (sh_ref[...], sl_ref[...])
    out_ref[...] = updated(state_ref[...], start, s, shift_of(z, d_ref), split(z))


def join_kernel(column_ref, mine_ref, theirs_ref, out_ref, both, sems):
    chunks = sems.shape[0]
    size = both.shape[0] // chunks
    column = column_ref[0]
    copies = []
    for i in range(chunks):
        at = slice(i * size, (i + 1) * size)
        mine, theirs = mine_ref[at, :], theirs_ref[at, :]
        both[at, 0, :] = jnp.where(column == 0, mine, theirs)
        both[at, 1, :] = jnp.where(column == 0, theirs, mine)
        span = pl.ds(i * size, size)
        copies.append(pltpu.make_async_copy(both.at[span], out_ref.at[span], sems.at[i]))
        copies[-1].start()
    for copy in copies:
        copy.wait()


def prepare(pieces, batch, members, patches_of, place, near, values, var, anomaly, sources, n):
    width = anomaly[0].shape[1]
    outs = [
        ((n, members), BF16, VMEM),
        ((n, members), BF16, VMEM),
        ((n, 128), F32, VMEM),
        ((n, n), F32, VMEM),
        ((n, width), F32, VMEM),
    ]
    kernel = functools.partial(prepare_kernel, pieces, batch, members, patches_of, len(place))
    args = [*place, near, values, var, *anomaly, *sources]
    ins = [SMEM] * (len(place) + 1) + [VMEM] * (len(args) - len(place) - 1)
    return call(kernel, outs, ins, args, [pltpu.VMEM((128, 128), F32)], 6 * n * width * members)


def factor(pieces, batch, members, chunk, patches_of, place, near, values, var, sources, ready=0, before=()):
    per_patch = values.shape[2]
    n = len(pieces) * per_patch
    outs = [
        ((n, members), BF16, VMEM),
        ((n, members), BF16, VMEM),
        ((n, 128), F32, VMEM),
        ((n, n), F32, VMEM),
        ((n, n), BF16, VMEM),
        ((n, n), BF16, VMEM),
        ((1,), jnp.int32, SMEM),
    ]
    args = [*place, near, values, var, *sources, *before]
    aliases = {}
    if ready:
        outs.append((before[-1].shape, F32, VMEM))
        first = len(args) - 5
        aliases = {first: 0, first + 1: 1, first + 2: 2, first + 3: 3, first + 4: 7}
    scratch = [
        pltpu.VMEM((128, 128), F32),
        pltpu.VMEM((n, n), F32),
        pltpu.VMEM((n, n), F32),
        pltpu.VMEM((2, n, 2 * n), BF16),
        pltpu.VMEM((2, n, 2 * n), BF16),
    ]
    kernel = functools.partial(factor_kernel, pieces, batch, members, chunk, patches_of, len(place), ready)
    flops = 6 * n * n * members + 60 * n * n * n
    ins = [SMEM] * (len(place) + 1) + [VMEM] * (len(args) - len(place) - 1)
    return call(kernel, outs, ins, args, scratch, flops, FACTOR_LIMIT, aliases)


def solver_scratch(n, width):
    return [pltpu.VMEM((n, width), F32), pltpu.VMEM((2, 2, n, width), BF16)]


def gain(batch, own_of, place, cells, factored, states):
    sh, sl, d, g, xh, xl, more = factored[:7]
    n, members = sh.shape
    width = states[0].shape[1]
    kernel = functools.partial(gain_kernel, batch, len(states), own_of)
    outs = [((n, width), F32, VMEM), ((cells.shape[2], members), F32, VMEM)]
    ins = [SMEM] * 3 + [VMEM] * (7 + len(states))
    args = [*place, more, cells, sh, sl, d, g, xh, xl, *states]
    flops = 8 * n * members * width
    scratch = [pltpu.VMEM((8, 128), jnp.int32), pltpu.VMEM((2, members, width), BF16)]
    scratch += solver_scratch(n, width)
    return call(kernel, outs, ins, args, scratch, flops)


def update(factored, z, states, starts, more=False):
    sh, sl, d = factored[:3]
    kernel = functools.partial(update_kernel, starts)
    outs = [(state.shape, F32, VMEM) for state in states]
    if more:
        outs += [((sh.shape[1], z.shape[1]), BF16, VMEM)] * 2
    flops = 6 * sh.shape[0] * sh.shape[1] * z.shape[1]
    return call(kernel, outs, [VMEM] * (4 + len(states)), [sh, sl, d, z, *states], (), flops)


def last(factored, state):
    sh, sl, d, g, xh, xl, more, *cross = factored
    n, width = sh.shape[0], state.shape[1]
    outs = [((n, width), F32, VMEM), (state.shape, F32, VMEM)]
    args = [more, sh, sl, d, g, xh, xl, state, *cross]
    flops = 12 * sh.shape[0] * sh.shape[1] * width
    ins = [SMEM] + [VMEM] * (len(args) - 1)
    return call(last_kernel, outs, ins, args, solver_scratch(n, width), flops)


def rings(size):
    up = [(i, (i + 1) % size) for i in range(size)]
    return up, [(j, i) for i, j in up]


BOTH = ("region", "member")


def permute(x, moves, regions):
    table = []
    for region in range(regions):
        for column in range(2):
            pair, parity, to = moves(region // 2, region % 2, column)
            pair %= regions // 2
            table.append((region * 2 + column, (pair * 2 + parity) * 2 + to))
    return lax.ppermute(x, BOTH, table)


def paired(state, neighbours, obs_cell, obs_values, obs_var):
    half, _, cells = state.shape
    members = 2 * half
    regions = lax.axis_size("region")
    region, column = lax.axis_index("region"), lax.axis_index("member")
    place = (region.astype(jnp.int32)[None], column.astype(jnp.int32)[None])
    near = neighbours.T

    def own_of(region_ref, column_ref):
        return region_ref[0] * 2 + column_ref[0]

    def around(region, within):
        side = 2 * lax.rem(region, 2) - 1
        outer = lax.rem(region + regions + side, regions)
        return [r * 2 + p for p in within for r in (region, region - side, outer)]

    def patches_first(region_ref, column_ref):
        return around(region_ref[0], (0, 1)), own_of(region_ref, column_ref)

    def patches_next(region_ref, column_ref):
        column = column_ref[0]
        return around(region_ref[0], (column, 1 - column)), own_of(region_ref, column_ref)

    def across(x):
        return permute(x, lambda c, q, m: (c, q, 1 - m), regions)

    def beside(x):
        return permute(x, lambda c, q, m: (c, 1 - q, m), regions)

    def outside(x):
        return permute(x, lambda c, q, m: (c + 2 * q - 1, 1 - q, m), regions)

    anywhere = pl.BlockSpec(memory_space=pl.ANY)
    (rows,) = call(
        pick_kernel,
        [((2, obs_cell.shape[2], half), F32, VMEM)],
        [SMEM, VMEM, VMEM],
        [place[0], obs_cell, state],
        [pltpu.VMEM((8, 128), jnp.int32), pltpu.VMEM((2, half, cells), F32)],
    )
    other = across(rows)
    sources = [rows, beside(rows), outside(rows), other, beside(other), outside(other)]
    shape = ((half, cells), F32, VMEM)
    keep, send, values, var = call(
        sort_kernel,
        [shape, shape, (obs_values.shape, F32, VMEM), (obs_var.shape, F32, VMEM)],
        [SMEM, anywhere, anywhere, VMEM, anywhere],
        [place[1], obs_values, obs_var, state, other],
        [pltpu.SemaphoreType.DMA((2,))],
    )
    pieces = [[(i, (p,), 0), (3 + i, (p,), 1)] for p in range(2) for i in range(3)]
    states = [keep, across(send)]
    factored = factor(pieces, 0, members, CHUNK, patches_first, place, near, values, var, sources)
    everything = slice(None)
    low, high = (everything, slice(0, half)), (everything, slice(half, members))
    pieces = [[(i, low, 0), (i, high, 1)] for i in range(3)]
    pieces += [[(i, high, 0), (i, low, 1)] for i in range(3, 6)]
    early = 4
    for batch in range(1, NBATCH):
        z, rows = gain(batch, own_of, place, obs_cell, factored, states)
        other = across(rows)
        far = permute(rows, lambda c, q, m: (c + 2 * q - 1, 1 - q, 1 - m), regions)
        sources = [rows, beside(rows), outside(rows), other, beside(other), far]
        mine, theirs, *anomaly = update(factored, z, states, (0, half), True)
        states = [mine, theirs]
        given = (place, near, values, var)
        n = factored[0].shape[0]
        done = prepare(pieces[:early], batch, members, patches_next, *given, anomaly, sources[:early], n)
        factored = factor(
            pieces, batch, members, CHUNK, patches_next, *given, sources, early, [*anomaly, *done]
        )
    z, theirs = last(factored, states[1])
    theirs = across(theirs)
    (mine,) = update(factored, z, states[:1], (0,))
    return pl.pallas_call(
        join_kernel,
        out_shape=jax.ShapeDtypeStruct(state.shape, F32),
        in_specs=[SMEM, VMEM, VMEM],
        out_specs=anywhere,
        scratch_shapes=[pltpu.VMEM(state.shape, F32), pltpu.SemaphoreType.DMA((4,))],
        compiler_params=pltpu.CompilerParams(vmem_limit_bytes=16 * 1024 * 1024),
    )(place[1], mine, theirs)


def listed(table_ref):
    blocks = table_ref.shape[0] - 1
    return [table_ref[i] for i in range(blocks)], table_ref[blocks]


def general(state, neighbours, obs_cell, obs_values, obs_var):
    ensemble = lax.all_to_all(state, "member", split_axis=1, concat_axis=0, tiled=True)
    members, owned, cells = ensemble.shape
    regions = lax.axis_size("region")
    region_patches = owned * lax.axis_size("member")
    region = lax.axis_index("region")
    first = region * region_patches + lax.axis_index("member") * owned
    up, down = rings(regions)
    fields = [ensemble[:, p, :] for p in range(owned)]
    grid = jnp.arange(cells, dtype=jnp.int32)
    for batch in range(NBATCH):
        picks = lax.dynamic_slice_in_dim(obs_cell, first, owned, 0)[:, batch, :]
        hot = (picks[:, :, None] == grid[None, None, :]).astype(F32)
        own_rows = jnp.einsum("poc,pkc->pok", hot, jnp.stack(fields), precision=HIGHEST)
        region_rows = lax.all_gather(own_rows, "member", axis=0, tiled=True)
        before = lax.ppermute(region_rows, "region", up)
        after = lax.ppermute(region_rows, "region", down)
        beside = jnp.concatenate([before, region_rows, after], axis=0)
        new = []
        for p in range(owned):
            own = first + p
            links = lax.dynamic_index_in_dim(neighbours, own, 0, keepdims=False)
            ids = jnp.concatenate([own[None], links]).astype(jnp.int32)
            table = jnp.concatenate([ids, own[None]]).astype(jnp.int32)
            home = (ids // region_patches - region + 1) % regions
            rows = jnp.take(beside, home * region_patches + ids % region_patches, axis=0)
            pieces = [[(0, (i,), 0)] for i in range(ids.shape[0])]
            factored = factor(
                pieces, batch, members, CHUNK, listed, [table], neighbours.T, obs_values, obs_var, [rows]
            )
            new.append(last(factored, fields[p])[1])
        fields = new
    ensemble = jnp.stack(fields, axis=1)
    return lax.all_to_all(ensemble, "member", split_axis=0, concat_axis=1, tiled=True)


def on_device(state, neighbours, obs_cell, obs_values, obs_var):
    patches, links = state.shape[1], neighbours.shape[1]
    even = lax.axis_size("region") % 2 == 0
    if even and patches == 2 and lax.axis_size("member") == 2 and links + 1 == 3 * patches:
        return paired(state, neighbours, obs_cell, obs_values, obs_var)
    return general(state, neighbours, obs_cell, obs_values, obs_var)


def solution(mesh):
    in_specs = (P("member", "region", None), P(), P(), P(), P())
    out_specs = P("member", "region", None)
    return jax.shard_map(
        on_device, mesh=mesh, in_specs=in_specs, out_specs=out_specs, check_vma=False
    )
```

```python
import functools
import math

import jax
import jax.numpy as jnp
from jax import lax
from jax.experimental import pallas as pl
from jax.experimental.pallas import tpu as pltpu
from jax.sharding import PartitionSpec as P

NBATCH = 2
HIGHEST = lax.Precision.HIGHEST
F32 = jnp.float32
BF16 = jnp.bfloat16
VMEM = pl.BlockSpec(memory_space=pltpu.VMEM)
SMEM = pl.BlockSpec(memory_space=pltpu.SMEM)
NN = (((1,), (0,)), ((), ()))
NT = (((1,), (1,)), ((), ()))
TN = (((0,), (0,)), ((), ()))
RESIDUAL = 1e-3
FACTOR_LIMIT = 24
MOST_STEPS = 15
TILE = 256
CHUNK = 128


def call(kernel, outs, ins, args, scratch=(), flops=0, limit=16, aliases=None):
    shapes = [jax.ShapeDtypeStruct(shape, dtype) for shape, dtype, _ in outs]
    moved = sum(math.prod(s.shape) * s.dtype.itemsize for s in shapes)
    moved += sum(a.size * a.dtype.itemsize for a in args)
    return pl.pallas_call(
        kernel,
        out_shape=shapes,
        in_specs=ins,
        out_specs=[space for _, _, space in outs],
        scratch_shapes=list(scratch),
        input_output_aliases=aliases or {},
        compiler_params=pltpu.CompilerParams(vmem_limit_bytes=limit * 1024 * 1024),
        cost_estimate=pl.CostEstimate(flops=flops, bytes_accessed=moved, transcendentals=0),
    )(*args)


def split(x):
    high = x.astype(BF16)
    return high, (x - high.astype(F32)).astype(BF16)


def dot(a, b, dims=NN):
    return lax.dot_general(a, b, dims, preferred_element_type=F32)


def dot3(a, b, dims=NN):
    (left,), (right,) = dims[0]
    lhs = jnp.concatenate([a[0], a[0], a[1]], axis=left)
    rhs = jnp.concatenate([b[0], b[1], b[0]], axis=right)
    return dot(lhs, rhs, dims)


def select(hot, parts, dims):
    (left,), (right,) = dims[0]
    hot = hot.astype(BF16)
    lhs = jnp.concatenate([hot] * len(parts), axis=left)
    return dot(lhs, jnp.concatenate(parts, axis=right), dims)


def split_all(x):
    high, middle = split(x)
    low = x - high.astype(F32) - middle.astype(F32)
    return high, middle, low.astype(BF16)


def step_limits():
    limits = []
    for steps in range(MOST_STEPS):
        rho = RESIDUAL
        for _ in range(steps):
            rho = math.sqrt(2.0 * rho / (1.0 + rho))
        limits.append(2.0 * rho / (1.0 - rho) if rho < 1.0 else math.inf)
    return limits


def diagonal(n, columns, first):
    row = lax.broadcasted_iota(jnp.int32, (n, columns), 0)
    column = lax.broadcasted_iota(jnp.int32, (n, columns), 1)
    return row + first == column


def selector(picks, cells, scratch):
    per_patch = picks.shape[1]
    scratch[...] = jnp.full_like(scratch, -1)
    scratch[0:1, 0:per_patch] = picks
    grid = lax.broadcasted_iota(jnp.int32, (cells, scratch.shape[1]), 0)
    hot = (grid == scratch[0:1, :]).astype(F32)
    return jnp.transpose(hot)[0:per_patch, :]


def sort_kernel(column_ref, state_ref, keep_ref, send_ref):
    column = column_ref[0]
    first, second = state_ref[:, 0, :], state_ref[:, 1, :]
    keep_ref[...] = jnp.where(column == 0, first, second)
    send_ref[...] = jnp.where(column == 0, second, first)


def pick_kernel(region_ref, column_ref, cells_ref, keep_ref, send_ref, rows_ref, scratch):
    column = column_ref[0]
    for patch, field_ref in ((column, keep_ref), (1 - column, send_ref)):
        picks = cells_ref[pl.ds(region_ref[0] * 2 + patch, 1), 0, :]
        hot = selector(picks, field_ref.shape[1], scratch)
        rows_ref[pl.ds(patch, 1)] = select(hot, split_all(field_ref[...]), NT)[None]


def gate_kernel(values_hbm, var_hbm, send_ref, after_ref, out_ref, values_ref, var_ref, sems):
    copies = [
        pltpu.make_async_copy(values_hbm, values_ref, sems.at[0]),
        pltpu.make_async_copy(var_hbm, var_ref, sems.at[1]),
    ]
    for copy in copies:
        copy.start()
    for copy in copies:
        copy.wait()


def table(patches, own, near_ref, values_ref, var_ref, batch, flat):
    per_patch = values_ref.shape[2]
    blocks = len(patches)
    flat[...] = jnp.ones_like(flat)
    for i, patch in enumerate(patches):
        widening = (patch == own).astype(jnp.int32)
        for j in range(near_ref.shape[0]):
            widening = widening + (near_ref[j, own] == patch).astype(jnp.int32) * (j + 2)
        flat[i : i + 1, 0:per_patch] = values_ref[pl.ds(patch, 1), batch, :]
        noise = var_ref[pl.ds(patch, 1), batch, :] * widening.astype(F32)
        flat[blocks + i : blocks + i + 1, 0:per_patch] = noise
    upright = jnp.transpose(flat[...])[0:per_patch]
    return [(upright[:, i : i + 1], upright[:, blocks + i : blocks + i + 1]) for i in range(blocks)]


def scale_block(i, piece, sources, column, members, sh_ref, sl_ref, d_ref):
    value, noise = column
    rows = [sources[which][index] for which, index, _ in piece]
    total = sum(jnp.sum(part, axis=1, keepdims=True) for part in rows)
    mean = total * (1.0 / members)
    scale = lax.rsqrt(noise * (members - 1.0))
    per_patch = value.shape[0]
    at = slice(i * per_patch, (i + 1) * per_patch)
    for part, (_, _, start) in zip(rows, piece):
        size = part.shape[1]
        lanes = slice(start * size, (start + 1) * size)
        sh_ref[at, lanes], sl_ref[at, lanes] = split((part - mean) * scale)
    d_ref[at, :] = jnp.broadcast_to((value - mean) * scale, (per_patch, d_ref.shape[1]))


def prepare_kernel(pieces, batch, members, patches_of, places, *refs):
    place_refs, refs = refs[:places], refs[places:]
    near_ref, values_ref, var_ref, ah_ref, al_ref, *refs = refs
    sources, (sh_ref, sl_ref, d_ref, g_ref, cross_ref, flat) = refs[:-6], refs[-6:]
    patches, own = patches_of(*place_refs)
    columns = table(patches[: len(pieces)], own, near_ref, values_ref, var_ref, batch, flat)
    for i, piece in enumerate(pieces):
        scale_block(i, piece, sources, columns[i], members, sh_ref, sl_ref, d_ref)
    count = len(pieces) * values_ref.shape[2]
    s = (sh_ref[0:count], sl_ref[0:count])
    g_ref[0:count, 0:count] = dot3(s, s, NT)
    cross_ref[0:count] = dot3(s, (ah_ref[...], al_ref[...]))


def factor_kernel(pieces, batch, members, chunk, patches_of, places, ready, *refs):
    place_refs, refs = refs[:places], refs[places:]
    near_ref, values_ref, var_ref, *refs = refs
    refs, (flat, eye_ref, x_ref, wa, wb) = refs[:-5], refs[-5:]
    if ready:
        refs, cross_ref = refs[:-1], refs[-1]
    refs, (sh_ref, sl_ref, d_ref, g_ref, xh_ref, xl_ref, n_ref) = refs[:-7], refs[-7:]
    if ready:
        refs, (ah_ref, al_ref) = refs[:-7], refs[-7:-5]
    sources = refs
    per_patch = values_ref.shape[2]
    blocks = len(pieces)
    patches, own = patches_of(*place_refs)
    columns = table(patches[ready:], own, near_ref, values_ref, var_ref, batch, flat)
    for i in range(ready, blocks):
        scale_block(i, pieces[i], sources, columns[i - ready], members, sh_ref, sl_ref, d_ref)
    n = sh_ref.shape[0]
    head = min(TILE, n)
    tail = n - head
    chunks = [(i, min(i + chunk, n)) for i in range(0, n, chunk)]
    left = (sh_ref[0:head], sl_ref[0:head])
    fresh = ready * per_patch
    g_ref[fresh:n, 0:head] = dot3((sh_ref[fresh:n], sl_ref[fresh:n]), left, NT)
    low = (sh_ref[head:n], sl_ref[head:n])
    g_ref[head:n, head:n] = dot3(low, low, NT)
    g_ref[0:head, head:n] = jnp.transpose(g_ref[head:n, 0:head])
    if ready:
        cross_ref[fresh:n] = dot3((sh_ref[fresh:n], sl_ref[fresh:n]), (ah_ref[...], al_ref[...]))
    g = g_ref[...]
    square = jnp.sum(jnp.sum(g * g, axis=0, keepdims=True), axis=1, keepdims=True)
    norm = jnp.sqrt(square) * (1.0 + 1e-5)
    size = square[0, 0]
    limits = step_limits()
    pairs = jnp.int32(0)
    for k in range(7, MOST_STEPS - 2, 2):
        limit = limits[k] * (1.0 - 1e-4)
        pairs = pairs + (size > limit * limit).astype(jnp.int32)
    n_ref[0] = (size > 1.6e7).astype(jnp.int32) + (size > 1e8).astype(jnp.int32)
    eye_ref[...] = diagonal(n, n, 0).astype(F32)
    eye = eye_ref[...]
    first = 2.0 / (2.0 + norm)
    rho = norm * (0.5 * first)
    rho2 = rho * rho
    weight = 2.0 / (2.0 - rho2)
    keep = 0.5 * rho2 * weight
    r = (1.0 - first) * eye - first * g
    parts = split(r)
    x = (weight * first) * (eye + r)
    x_ref[...] = x
    for i, part in enumerate(split(x)):
        wa[i, :, n : 2 * n] = part

    def store(targets, start, left, corner):
        blocks = [(slice(0, n), slice(start, start + head), left)]
        blocks.append((slice(head, n), slice(start + head, start + n), corner))
        blocks.append((slice(0, head), slice(start + head, start + n), jnp.transpose(left[head:n])))
        for rows, columns, block in blocks:
            for target, part in zip(targets, split(block)):
                target[rows, columns] = part

    def corner_of(weight, keep, left, corner):
        left = weight * left - keep * eye_ref[:, 0:head]
        return left, weight * corner - keep * eye_ref[head:n, head:n]

    left = dot3(parts, [part[:, 0:head] for part in parts])
    corner = dot3([part[head:n] for part in parts], [part[:, head:n] for part in parts])
    store((wa.at[0], wa.at[1]), 0, *corner_of(weight, keep, left, corner))

    def corners_of(source):
        ends = [
            jnp.concatenate([source[i, head:n, 0:n], source[i, head:n, n : 2 * n]], axis=0) for i in (0, 1)
        ]
        return dot3(ends, (source[0, :, head:n], source[1, :, head:n]))

    def advance(source, target, rho2):
        weight = 2.0 / (2.0 - rho2)
        keep = 0.5 * rho2 * weight
        parts = (source[0, :, 0:n], source[1, :, 0:n])
        left = dot3(parts, (source[0, :, 0:head], source[1, :, 0:head]))
        corners = corners_of(source)
        both = (target.at[0], target.at[1])
        store(both, 0, *corner_of(weight, keep, left, corners[0:tail]))
        left = dot3(parts, (source[0, :, n : n + head], source[1, :, n : n + head]))
        left = weight * (x_ref[:, 0:head] + left)
        corner = weight * (x_ref[head:n, head:n] + corners[tail : 2 * tail])
        x_ref[:, 0:head] = left
        x_ref[head:n, head:n] = corner
        store(both, n, left, corner)
        return keep * keep

    rho2 = keep * keep

    def sides(source, span):
        return [source[i, span[0] : span[1], 0:n] for i in (0, 1)]

    def put(targets, start, span, block, mirror):
        for target, part in zip(targets, split(block)):
            target[span[0] : span[1], start : start + head] = part
        low = max(span[0], head)
        if mirror and low < span[1]:
            for target, part in zip(targets, split(jnp.transpose(block[low - span[0] :]))):
                target[0:head, start + low : start + span[1]] = part

    def put_corner(targets, start, block):
        for target, part in zip(targets, split(block)):
            target[head:n, start + head : start + n] = part

    def put_x(targets, start, weight, span, product, mirror=False):
        x = weight * (x_ref[span[0] : span[1], 0:head] + product)
        x_ref[span[0] : span[1], 0:head] = x
        put(targets, start, span, x, mirror)

    def put_x_corner(targets, start, weight, product):
        x = weight * (x_ref[head:n, head:n] + product)
        x_ref[head:n, head:n] = x
        put_corner(targets, start, x)

    waiting = None
    source, target = wa, wb
    for _ in range(5):
        weight = 2.0 / (2.0 - rho2)
        keep = 0.5 * rho2 * weight
        first = (source[0, :, 0:head], source[1, :, 0:head])
        r = []
        for k, span in enumerate(chunks):
            r.append(dot3(sides(source, span), first))
            if waiting is not None:
                put_x((source.at[0], source.at[1]), n, waiting[0], span, waiting[1][k])
        if waiting is not None:
            put_x_corner((source.at[0], source.at[1]), n, waiting[0], waiting[2])
        corners = corners_of(source)
        first = (source[0, :, n : n + head], source[1, :, n : n + head])
        both = (target.at[0], target.at[1])
        x = []
        for k, span in enumerate(chunks):
            x.append(dot3(sides(source, span), first))
            put(both, 0, span, weight * r[k] - keep * eye_ref[span[0] : span[1], 0:head], True)
        put_corner(both, 0, weight * corners[0:tail] - keep * eye_ref[head:n, head:n])
        waiting = (weight, x, corners[tail : 2 * tail])
        rho2 = keep * keep
        source, target = target, source
    for k, span in enumerate(chunks):
        put_x((source.at[0], source.at[1]), n, waiting[0], span, waiting[1][k])
    put_x_corner((source.at[0], source.at[1]), n, waiting[0], waiting[2])

    def twice(_, rho2):
        return advance(target, source, advance(source, target, rho2))

    rho2 = lax.fori_loop(0, pairs, twice, rho2)
    weight = 2.0 / (2.0 - rho2)
    first = (source[0, :, n : n + head], source[1, :, n : n + head])
    done = (xh_ref, xl_ref)
    ends = [source[i, head:n, n : 2 * n] for i in (0, 1)]
    put_x_corner(done, 0, weight, dot3(ends, (source[0, :, head:n], source[1, :, head:n])))
    x = [dot3(sides(source, span), first) for span in chunks]
    for k, span in enumerate(chunks):
        put_x(done, 0, weight, span, x[k], True)


def centred(fields):
    members = sum(field.shape[0] for field in fields)
    mean = sum(jnp.sum(field, axis=0, keepdims=True) for field in fields) * (1.0 / members)
    pairs = [split(field - mean) for field in fields]
    return [jnp.concatenate(parts, axis=0) for parts in zip(*pairs)], mean


def in_chunks(count, product, work):
    waiting = None
    for start in range(0, count, CHUNK):
        span = slice(start, min(start + CHUNK, count))
        result = product(span)
        if waiting is not None:
            work(*waiting)
        waiting = (span, result)
    work(*waiting)


def solve(n_ref, s, g_ref, x, anomaly, z_ref, cross_ref, parts_ref, crossed_already=False, between=()):
    n = z_ref.shape[0]

    def keep(slot, span, value):
        for i, part in enumerate(split(value)):
            parts_ref[slot, i, span] = part

    def kept(slot):
        return parts_ref[slot, 0], parts_ref[slot, 1]

    def some(parts, span):
        return [part[span] for part in parts]

    def crossed(span, value):
        cross_ref[span] = value
        keep(0, span, value)

    def solved(span, value):
        z_ref[span] = value
        keep(1, span, value)

    def left(span, value):
        keep(0, span, cross_ref[span] - z_ref[span] - value)

    def refined(span, value):
        z_ref[span] = z_ref[span] + value

    if crossed_already:
        keep(0, slice(0, n), cross_ref[...])
    else:
        in_chunks(n, lambda span: dot3(some(s, span), [part[...] for part in anomaly]), crossed)
    stages = [
        (lambda span: dot3(some(x, span), kept(0)), solved),
        (lambda span: dot3(split(g_ref[span]), kept(1)), left),
        (lambda span: dot3(some(x, span), kept(0)), refined),
    ]
    for i, (product, work) in enumerate(stages):
        for extra in between[i : i + 1]:
            extra()
        in_chunks(n, product, work)

    def refine(_, carry):
        z = z_ref[...]
        gz = lax.dot_general(g_ref[...], z, NN, precision=HIGHEST, preferred_element_type=F32)
        z_ref[...] = z + dot3([part[...] for part in x], split(cross_ref[...] - z - gz))
        return carry

    lax.fori_loop(0, n_ref[0], refine, 0)


def gain_kernel(batch, parts, own_of, region_ref, column_ref, n_ref, cells_ref, sh_ref, sl_ref, d_ref, g_ref, *refs):
    xh_ref, xl_ref, *refs = refs
    states = refs[:parts]
    z_ref, rows_ref, scratch, anomaly_ref, cross_ref, parts_ref = refs[parts:]
    anomaly, mean = centred([state[...] for state in states])
    for i, part in enumerate(anomaly):
        anomaly_ref[i] = part
    anomaly = (anomaly_ref.at[0], anomaly_ref.at[1])
    picks = cells_ref[pl.ds(own_of(region_ref, column_ref), 1), batch, :]
    hot = selector(picks, mean.shape[1], scratch)
    base = jnp.sum(hot * mean, axis=1, keepdims=True)
    members = anomaly_ref.shape[1]
    count = 3
    size = -(-members // (count * 128)) * 128

    def pick(start, stop):
        picked = select(hot, [part[start:stop] for part in anomaly], NT)
        rows_ref[:, start:stop] = base + picked

    between = [
        functools.partial(pick, i * size, min((i + 1) * size, members)) for i in range(count)
    ]
    x = (xh_ref, xl_ref)
    solve(n_ref, (sh_ref, sl_ref), g_ref, x, anomaly, z_ref, cross_ref, parts_ref, False, between)
    zt = split(select(hot, split(z_ref[...]), NT))
    shift = dot3(zt, split(d_ref[...]))[:, 0:1]
    rows_ref[...] = rows_ref[...] + shift - 0.5 * dot3(zt, (sh_ref[...], sl_ref[...]))


def updated(field, start, s, shift, z):
    size = field.shape[0]
    return field + shift - 0.5 * dot3([h[:, start : start + size] for h in s], z, TN)


def shift_of(z, d_ref):
    return jnp.sum(z * d_ref[:, 0:1], axis=0, keepdims=True)


def update_kernel(starts, sh_ref, sl_ref, d_ref, z_ref, *refs):
    count = len(starts)
    states, outs, parts = refs[:count], refs[count : 2 * count], refs[2 * count :]
    z = z_ref[...]
    shift = shift_of(z, d_ref)
    s, zs = (sh_ref[...], sl_ref[...]), split(z)
    for start, state, out in zip(starts, states, outs):
        out[...] = updated(state[...], start, s, shift, zs)
    if parts:
        anomaly, _ = centred([out[...] for out in outs])
        for ref, part in zip(parts, anomaly):
            ref[...] = part


def last_kernel(n_ref, sh_ref, sl_ref, d_ref, g_ref, xh_ref, xl_ref, state_ref, *refs):
    cross, z_ref, out_ref, scratch_ref, parts_ref = refs if len(refs) == 5 else (None, *refs)
    given = cross is not None
    cross_ref = cross if given else scratch_ref
    anomaly = None if given else centred([state_ref[...]])[0]
    x = (xh_ref, xl_ref)
    solve(n_ref, (sh_ref, sl_ref), g_ref, x, anomaly, z_ref, cross_ref, parts_ref, given)
    z = z_ref[...]
    start = sh_ref.shape[1] - state_ref.shape[0]
    s = (sh_ref[...], sl_ref[...])
    out_ref[...] = updated(state_ref[...], start, s, shift_of(z, d_ref), split(z))


def join_kernel(column_ref, mine_ref, theirs_ref, out_ref, both, sems):
    chunks = sems.shape[0]
    size = both.shape[0] // chunks
    column = column_ref[0]
    copies = []
    for i in range(chunks):
        at = slice(i * size, (i + 1) * size)
        mine, theirs = mine_ref[at, :], theirs_ref[at, :]
        both[at, 0, :] = jnp.where(column == 0, mine, theirs)
        both[at, 1, :] = jnp.where(column == 0, theirs, mine)
        span = pl.ds(i * size, size)
        copies.append(pltpu.make_async_copy(both.at[span], out_ref.at[span], sems.at[i]))
        copies[-1].start()
    for copy in copies:
        copy.wait()


def prepare(pieces, batch, members, patches_of, place, near, values, var, anomaly, sources, n):
    width = anomaly[0].shape[1]
    outs = [
        ((n, members), BF16, VMEM),
        ((n, members), BF16, VMEM),
        ((n, 128), F32, VMEM),
        ((n, n), F32, VMEM),
        ((n, width), F32, VMEM),
    ]
    kernel = functools.partial(prepare_kernel, pieces, batch, members, patches_of, len(place))
    args = [*place, near, values, var, *anomaly, *sources]
    ins = [SMEM] * (len(place) + 1) + [VMEM] * (len(args) - len(place) - 1)
    return call(kernel, outs, ins, args, [pltpu.VMEM((128, 128), F32)], 6 * n * width * members)


def factor(pieces, batch, members, chunk, patches_of, place, near, values, var, sources, ready=0, before=()):
    per_patch = values.shape[2]
    n = len(pieces) * per_patch
    outs = [
        ((n, members), BF16, VMEM),
        ((n, members), BF16, VMEM),
        ((n, 128), F32, VMEM),
        ((n, n), F32, VMEM),
        ((n, n), BF16, VMEM),
        ((n, n), BF16, VMEM),
        ((1,), jnp.int32, SMEM),
    ]
    args = [*place, near, values, var, *sources, *before]
    aliases = {}
    if ready:
        outs.append((before[-1].shape, F32, VMEM))
        first = len(args) - 5
        aliases = {first: 0, first + 1: 1, first + 2: 2, first + 3: 3, first + 4: 7}
    scratch = [
        pltpu.VMEM((128, 128), F32),
        pltpu.VMEM((n, n), F32),
        pltpu.VMEM((n, n), F32),
        pltpu.VMEM((2, n, 2 * n), BF16),
        pltpu.VMEM((2, n, 2 * n), BF16),
    ]
    kernel = functools.partial(factor_kernel, pieces, batch, members, chunk, patches_of, len(place), ready)
    flops = 6 * n * n * members + 60 * n * n * n
    ins = [SMEM] * (len(place) + 1) + [VMEM] * (len(args) - len(place) - 1)
    return call(kernel, outs, ins, args, scratch, flops, FACTOR_LIMIT, aliases)


def solver_scratch(n, width):
    return [pltpu.VMEM((n, width), F32), pltpu.VMEM((2, 2, n, width), BF16)]


def gain(batch, own_of, place, cells, factored, states):
    sh, sl, d, g, xh, xl, more = factored[:7]
    n, members = sh.shape
    width = states[0].shape[1]
    kernel = functools.partial(gain_kernel, batch, len(states), own_of)
    outs = [((n, width), F32, VMEM), ((cells.shape[2], members), F32, VMEM)]
    ins = [SMEM] * 3 + [VMEM] * (7 + len(states))
    args = [*place, more, cells, sh, sl, d, g, xh, xl, *states]
    flops = 8 * n * members * width
    scratch = [pltpu.VMEM((8, 128), jnp.int32), pltpu.VMEM((2, members, width), BF16)]
    scratch += solver_scratch(n, width)
    return call(kernel, outs, ins, args, scratch, flops)


def update(factored, z, states, starts, more=False):
    sh, sl, d = factored[:3]
    kernel = functools.partial(update_kernel, starts)
    outs = [(state.shape, F32, VMEM) for state in states]
    if more:
        outs += [((sh.shape[1], z.shape[1]), BF16, VMEM)] * 2
    flops = 6 * sh.shape[0] * sh.shape[1] * z.shape[1]
    return call(kernel, outs, [VMEM] * (4 + len(states)), [sh, sl, d, z, *states], (), flops)


def last(factored, state):
    sh, sl, d, g, xh, xl, more, *cross = factored
    n, width = sh.shape[0], state.shape[1]
    outs = [((n, width), F32, VMEM), (state.shape, F32, VMEM)]
    args = [more, sh, sl, d, g, xh, xl, state, *cross]
    flops = 12 * sh.shape[0] * sh.shape[1] * width
    ins = [SMEM] + [VMEM] * (len(args) - 1)
    return call(last_kernel, outs, ins, args, solver_scratch(n, width), flops)


def rings(size):
    up = [(i, (i + 1) % size) for i in range(size)]
    return up, [(j, i) for i, j in up]


BOTH = ("region", "member")


def permute(x, moves, regions):
    table = []
    for region in range(regions):
        for column in range(2):
            pair, parity, to = moves(region // 2, region % 2, column)
            pair %= regions // 2
            table.append((region * 2 + column, (pair * 2 + parity) * 2 + to))
    return lax.ppermute(x, BOTH, table)


def paired(state, neighbours, obs_cell, obs_values, obs_var):
    half, _, cells = state.shape
    members = 2 * half
    regions = lax.axis_size("region")
    region, column = lax.axis_index("region"), lax.axis_index("member")
    place = (region.astype(jnp.int32)[None], column.astype(jnp.int32)[None])
    near = neighbours.T

    def own_of(region_ref, column_ref):
        return region_ref[0] * 2 + column_ref[0]

    def around(region, within):
        side = 2 * lax.rem(region, 2) - 1
        outer = lax.rem(region + regions + side, regions)
        return [r * 2 + p for p in within for r in (region, region - side, outer)]

    def patches_first(region_ref, column_ref):
        return around(region_ref[0], (0, 1)), own_of(region_ref, column_ref)

    def patches_next(region_ref, column_ref):
        column = column_ref[0]
        return around(region_ref[0], (column, 1 - column)), own_of(region_ref, column_ref)

    def across(x):
        return permute(x, lambda c, q, m: (c, q, 1 - m), regions)

    def beside(x):
        return permute(x, lambda c, q, m: (c, 1 - q, m), regions)

    def outside(x):
        return permute(x, lambda c, q, m: (c + 2 * q - 1, 1 - q, m), regions)

    anywhere = pl.BlockSpec(memory_space=pl.ANY)
    shape = ((half, cells), F32, VMEM)
    keep, send = call(sort_kernel, [shape] * 2, [SMEM, VMEM], [place[1], state])
    (rows,) = call(
        pick_kernel,
        [((2, obs_cell.shape[2], half), F32, VMEM)],
        [SMEM, SMEM, VMEM, VMEM, VMEM],
        [*place, obs_cell, keep, send],
        [pltpu.VMEM((8, 128), jnp.int32)],
    )
    other = across(rows)
    sources = [rows, beside(rows), outside(rows), other, beside(other), outside(other)]
    send, values, var = call(
        gate_kernel,
        [((half, cells), F32, anywhere), (obs_values.shape, F32, VMEM), (obs_var.shape, F32, VMEM)],
        [anywhere] * 4,
        [obs_values, obs_var, send, other],
        [pltpu.SemaphoreType.DMA((2,))],
        aliases={2: 0},
    )
    pieces = [[(i, (p,), 0), (3 + i, (p,), 1)] for p in range(2) for i in range(3)]
    states = [keep, across(send)]
    factored = factor(pieces, 0, members, CHUNK, patches_first, place, near, values, var, sources)
    everything = slice(None)
    low, high = (everything, slice(0, half)), (everything, slice(half, members))
    pieces = [[(i, low, 0), (i, high, 1)] for i in range(3)]
    pieces += [[(i, high, 0), (i, low, 1)] for i in range(3, 6)]
    early = 4
    for batch in range(1, NBATCH):
        z, rows = gain(batch, own_of, place, obs_cell, factored, states)
        other = across(rows)
        far = permute(rows, lambda c, q, m: (c + 2 * q - 1, 1 - q, 1 - m), regions)
        sources = [rows, beside(rows), outside(rows), other, beside(other), far]
        mine, theirs, *anomaly = update(factored, z, states, (0, half), True)
        states = [mine, theirs]
        given = (place, near, values, var)
        n = factored[0].shape[0]
        done = prepare(pieces[:early], batch, members, patches_next, *given, anomaly, sources[:early], n)
        factored = factor(
            pieces, batch, members, CHUNK, patches_next, *given, sources, early, [*anomaly, *done]
        )
    z, theirs = last(factored, states[1])
    theirs = across(theirs)
    (mine,) = update(factored, z, states[:1], (0,))
    return pl.pallas_call(
        join_kernel,
        out_shape=jax.ShapeDtypeStruct(state.shape, F32),
        in_specs=[SMEM, VMEM, VMEM],
        out_specs=anywhere,
        scratch_shapes=[pltpu.VMEM(state.shape, F32), pltpu.SemaphoreType.DMA((4,))],
        compiler_params=pltpu.CompilerParams(vmem_limit_bytes=16 * 1024 * 1024),
    )(place[1], mine, theirs)


def listed(table_ref):
    blocks = table_ref.shape[0] - 1
    return [table_ref[i] for i in range(blocks)], table_ref[blocks]


def general(state, neighbours, obs_cell, obs_values, obs_var):
    ensemble = lax.all_to_all(state, "member", split_axis=1, concat_axis=0, tiled=True)
    members, owned, cells = ensemble.shape
    regions = lax.axis_size("region")
    region_patches = owned * lax.axis_size("member")
    region = lax.axis_index("region")
    first = region * region_patches + lax.axis_index("member") * owned
    up, down = rings(regions)
    fields = [ensemble[:, p, :] for p in range(owned)]
    grid = jnp.arange(cells, dtype=jnp.int32)
    for batch in range(NBATCH):
        picks = lax.dynamic_slice_in_dim(obs_cell, first, owned, 0)[:, batch, :]
        hot = (picks[:, :, None] == grid[None, None, :]).astype(F32)
        own_rows = jnp.einsum("poc,pkc->pok", hot, jnp.stack(fields), precision=HIGHEST)
        region_rows = lax.all_gather(own_rows, "member", axis=0, tiled=True)
        before = lax.ppermute(region_rows, "region", up)
        after = lax.ppermute(region_rows, "region", down)
        beside = jnp.concatenate([before, region_rows, after], axis=0)
        new = []
        for p in range(owned):
            own = first + p
            links = lax.dynamic_index_in_dim(neighbours, own, 0, keepdims=False)
            ids = jnp.concatenate([own[None], links]).astype(jnp.int32)
            table = jnp.concatenate([ids, own[None]]).astype(jnp.int32)
            home = (ids // region_patches - region + 1) % regions
            rows = jnp.take(beside, home * region_patches + ids % region_patches, axis=0)
            pieces = [[(0, (i,), 0)] for i in range(ids.shape[0])]
            factored = factor(
                pieces, batch, members, CHUNK, listed, [table], neighbours.T, obs_values, obs_var, [rows]
            )
            new.append(last(factored, fields[p])[1])
        fields = new
    ensemble = jnp.stack(fields, axis=1)
    return lax.all_to_all(ensemble, "member", split_axis=0, concat_axis=1, tiled=True)


def on_device(state, neighbours, obs_cell, obs_values, obs_var):
    patches, links = state.shape[1], neighbours.shape[1]
    even = lax.axis_size("region") % 2 == 0
    if even and patches == 2 and lax.axis_size("member") == 2 and links + 1 == 3 * patches:
        return paired(state, neighbours, obs_cell, obs_values, obs_var)
    return general(state, neighbours, obs_cell, obs_values, obs_var)


def solution(mesh):
    in_specs = (P("member", "region", None), P(), P(), P(), P())
    out_specs = P("member", "region", None)
    return jax.shard_map(
        on_device, mesh=mesh, in_specs=in_specs, out_specs=out_specs, check_vma=False
    )
```

```python
import functools
import math

import jax
import jax.numpy as jnp
from jax import lax
from jax.experimental import pallas as pl
from jax.experimental.pallas import tpu as pltpu
from jax.sharding import PartitionSpec as P

NBATCH = 2
HIGHEST = lax.Precision.HIGHEST
F32 = jnp.float32
BF16 = jnp.bfloat16
VMEM = pl.BlockSpec(memory_space=pltpu.VMEM)
SMEM = pl.BlockSpec(memory_space=pltpu.SMEM)
NN = (((1,), (0,)), ((), ()))
NT = (((1,), (1,)), ((), ()))
TN = (((0,), (0,)), ((), ()))
RESIDUAL = 1e-3
FACTOR_LIMIT = 24
MOST_STEPS = 15
TILE = 256
CHUNK = 128


def call(kernel, outs, ins, args, scratch=(), flops=0, limit=16, aliases=None):
    shapes = [jax.ShapeDtypeStruct(shape, dtype) for shape, dtype, _ in outs]
    moved = sum(math.prod(s.shape) * s.dtype.itemsize for s in shapes)
    moved += sum(a.size * a.dtype.itemsize for a in args)
    return pl.pallas_call(
        kernel,
        out_shape=shapes,
        in_specs=ins,
        out_specs=[space for _, _, space in outs],
        scratch_shapes=list(scratch),
        input_output_aliases=aliases or {},
        compiler_params=pltpu.CompilerParams(vmem_limit_bytes=limit * 1024 * 1024),
        cost_estimate=pl.CostEstimate(flops=flops, bytes_accessed=moved, transcendentals=0),
    )(*args)


def split(x):
    high = x.astype(BF16)
    return high, (x - high.astype(F32)).astype(BF16)


def dot(a, b, dims=NN):
    return lax.dot_general(a, b, dims, preferred_element_type=F32)


def dot3(a, b, dims=NN):
    (left,), (right,) = dims[0]
    lhs = jnp.concatenate([a[0], a[0], a[1]], axis=left)
    rhs = jnp.concatenate([b[0], b[1], b[0]], axis=right)
    return dot(lhs, rhs, dims)


def select(hot, parts, dims):
    (left,), (right,) = dims[0]
    hot = hot.astype(BF16)
    lhs = jnp.concatenate([hot] * len(parts), axis=left)
    return dot(lhs, jnp.concatenate(parts, axis=right), dims)


def split_all(x):
    high, middle = split(x)
    low = x - high.astype(F32) - middle.astype(F32)
    return high, middle, low.astype(BF16)


def step_limits():
    limits = []
    for steps in range(MOST_STEPS):
        rho = RESIDUAL
        for _ in range(steps):
            rho = math.sqrt(2.0 * rho / (1.0 + rho))
        limits.append(2.0 * rho / (1.0 - rho) if rho < 1.0 else math.inf)
    return limits


def diagonal(n, columns, first):
    row = lax.broadcasted_iota(jnp.int32, (n, columns), 0)
    column = lax.broadcasted_iota(jnp.int32, (n, columns), 1)
    return row + first == column


def selector(picks, cells, scratch):
    per_patch = picks.shape[1]
    scratch[...] = jnp.full_like(scratch, -1)
    scratch[0:1, 0:per_patch] = picks
    grid = lax.broadcasted_iota(jnp.int32, (cells, scratch.shape[1]), 0)
    hot = (grid == scratch[0:1, :]).astype(F32)
    return jnp.transpose(hot)[0:per_patch, :]


def sort_kernel(column_ref, state_ref, keep_ref, send_ref):
    column = column_ref[0]
    first, second = state_ref[:, 0, :], state_ref[:, 1, :]
    keep_ref[...] = jnp.where(column == 0, first, second)
    send_ref[...] = jnp.where(column == 0, second, first)


def pick_kernel(region_ref, column_ref, cells_ref, keep_ref, send_ref, rows_ref, scratch):
    column = column_ref[0]
    for patch, field_ref in ((column, keep_ref), (1 - column, send_ref)):
        picks = cells_ref[pl.ds(region_ref[0] * 2 + patch, 1), 0, :]
        hot = selector(picks, field_ref.shape[1], scratch)
        rows_ref[pl.ds(patch, 1)] = select(hot, split_all(field_ref[...]), NT)[None]


def gate_kernel(values_hbm, var_hbm, send_ref, after_ref, out_ref, values_ref, var_ref, sems):
    copies = [
        pltpu.make_async_copy(values_hbm, values_ref, sems.at[0]),
        pltpu.make_async_copy(var_hbm, var_ref, sems.at[1]),
    ]
    for copy in copies:
        copy.start()
    for copy in copies:
        copy.wait()


def table(patches, own, near_ref, values_ref, var_ref, batch, flat):
    per_patch = values_ref.shape[2]
    blocks = len(patches)
    flat[...] = jnp.ones_like(flat)
    for i, patch in enumerate(patches):
        widening = (patch == own).astype(jnp.int32)
        for j in range(near_ref.shape[0]):
            widening = widening + (near_ref[j, own] == patch).astype(jnp.int32) * (j + 2)
        flat[i : i + 1, 0:per_patch] = values_ref[pl.ds(patch, 1), batch, :]
        noise = var_ref[pl.ds(patch, 1), batch, :] * widening.astype(F32)
        flat[blocks + i : blocks + i + 1, 0:per_patch] = noise
    upright = jnp.transpose(flat[...])[0:per_patch]
    return [(upright[:, i : i + 1], upright[:, blocks + i : blocks + i + 1]) for i in range(blocks)]


def scale_block(i, piece, sources, column, members, sh_ref, sl_ref, d_ref):
    value, noise = column
    rows = [sources[which][index] for which, index, _ in piece]
    total = sum(jnp.sum(part, axis=1, keepdims=True) for part in rows)
    mean = total * (1.0 / members)
    scale = lax.rsqrt(noise * (members - 1.0))
    per_patch = value.shape[0]
    at = slice(i * per_patch, (i + 1) * per_patch)
    for part, (_, _, start) in zip(rows, piece):
        size = part.shape[1]
        lanes = slice(start * size, (start + 1) * size)
        sh_ref[at, lanes], sl_ref[at, lanes] = split((part - mean) * scale)
    d_ref[at, :] = jnp.broadcast_to((value - mean) * scale, (per_patch, d_ref.shape[1]))


def prepare_kernel(pieces, batch, members, patches_of, places, crossing, *refs):
    place_refs, refs = refs[:places], refs[places:]
    near_ref, values_ref, var_ref, *refs = refs
    refs, flat = refs[:-1], refs[-1]
    if crossing:
        (ah_ref, al_ref, *refs), cross_ref = refs[:-1], refs[-1]
    sources, (sh_ref, sl_ref, d_ref, g_ref) = refs[:-4], refs[-4:]
    patches, own = patches_of(*place_refs)
    columns = table(patches[: len(pieces)], own, near_ref, values_ref, var_ref, batch, flat)
    for i, piece in enumerate(pieces):
        scale_block(i, piece, sources, columns[i], members, sh_ref, sl_ref, d_ref)
    count = len(pieces) * values_ref.shape[2]
    s = (sh_ref[0:count], sl_ref[0:count])
    g_ref[0:count, 0:count] = dot3(s, s, NT)
    if crossing:
        cross_ref[0:count] = dot3(s, (ah_ref[...], al_ref[...]))


def factor_kernel(pieces, batch, members, chunk, patches_of, places, ready, crossing, *refs):
    place_refs, refs = refs[:places], refs[places:]
    near_ref, values_ref, var_ref, *refs = refs
    refs, (flat, eye_ref, x_ref, wa, wb) = refs[:-5], refs[-5:]
    if crossing:
        refs, cross_ref = refs[:-1], refs[-1]
    refs, (sh_ref, sl_ref, d_ref, g_ref, xh_ref, xl_ref, n_ref) = refs[:-7], refs[-7:]
    if crossing:
        refs, (ah_ref, al_ref) = refs[:-7], refs[-7:-5]
    elif ready:
        refs = refs[:-4]
    sources = refs
    per_patch = values_ref.shape[2]
    blocks = len(pieces)
    patches, own = patches_of(*place_refs)
    columns = table(patches[ready:], own, near_ref, values_ref, var_ref, batch, flat)
    for i in range(ready, blocks):
        scale_block(i, pieces[i], sources, columns[i - ready], members, sh_ref, sl_ref, d_ref)
    n = sh_ref.shape[0]
    head = min(TILE, n)
    tail = n - head
    chunks = [(i, min(i + chunk, n)) for i in range(0, n, chunk)]
    left = (sh_ref[0:head], sl_ref[0:head])
    fresh = ready * per_patch
    g_ref[fresh:n, 0:head] = dot3((sh_ref[fresh:n], sl_ref[fresh:n]), left, NT)
    if 0 < fresh < head:
        g_ref[0:fresh, fresh:head] = jnp.transpose(g_ref[fresh:head, 0:fresh])
    low = (sh_ref[head:n], sl_ref[head:n])
    g_ref[head:n, head:n] = dot3(low, low, NT)
    g_ref[0:head, head:n] = jnp.transpose(g_ref[head:n, 0:head])
    if crossing:
        cross_ref[fresh:n] = dot3((sh_ref[fresh:n], sl_ref[fresh:n]), (ah_ref[...], al_ref[...]))
    g = g_ref[...]
    square = jnp.sum(jnp.sum(g * g, axis=0, keepdims=True), axis=1, keepdims=True)
    norm = jnp.sqrt(square) * (1.0 + 1e-5)
    size = square[0, 0]
    limits = step_limits()
    pairs = jnp.int32(0)
    for k in range(7, MOST_STEPS - 2, 2):
        limit = limits[k] * (1.0 - 1e-4)
        pairs = pairs + (size > limit * limit).astype(jnp.int32)
    n_ref[0] = (size > 1.6e7).astype(jnp.int32) + (size > 1e8).astype(jnp.int32)
    eye_ref[...] = diagonal(n, n, 0).astype(F32)
    eye = eye_ref[...]
    first = 2.0 / (2.0 + norm)
    rho = norm * (0.5 * first)
    rho2 = rho * rho
    weight = 2.0 / (2.0 - rho2)
    keep = 0.5 * rho2 * weight
    r = (1.0 - first) * eye - first * g
    parts = split(r)
    x = (weight * first) * (eye + r)
    x_ref[...] = x
    for i, part in enumerate(split(x)):
        wa[i, :, n : 2 * n] = part

    def store(targets, start, left, corner):
        blocks = [(slice(0, n), slice(start, start + head), left)]
        blocks.append((slice(head, n), slice(start + head, start + n), corner))
        blocks.append((slice(0, head), slice(start + head, start + n), jnp.transpose(left[head:n])))
        for rows, columns, block in blocks:
            for target, part in zip(targets, split(block)):
                target[rows, columns] = part

    def corner_of(weight, keep, left, corner):
        left = weight * left - keep * eye_ref[:, 0:head]
        return left, weight * corner - keep * eye_ref[head:n, head:n]

    left = dot3(parts, [part[:, 0:head] for part in parts])
    corner = dot3([part[head:n] for part in parts], [part[:, head:n] for part in parts])
    store((wa.at[0], wa.at[1]), 0, *corner_of(weight, keep, left, corner))

    def corners_of(source):
        ends = [jnp.concatenate([source[i, :, head:n], source[i, :, n + head : 2 * n]], axis=1) for i in (0, 1)]
        return dot3([source[i, head:n, 0:n] for i in (0, 1)], ends)

    def advance(source, target, rho2):
        weight = 2.0 / (2.0 - rho2)
        keep = 0.5 * rho2 * weight
        parts = (source[0, :, 0:n], source[1, :, 0:n])
        left = dot3(parts, (source[0, :, 0:head], source[1, :, 0:head]))
        corners = corners_of(source)
        both = (target.at[0], target.at[1])
        store(both, 0, *corner_of(weight, keep, left, corners[:, 0:tail]))
        left = dot3(parts, (source[0, :, n : n + head], source[1, :, n : n + head]))
        left = weight * (x_ref[:, 0:head] + left)
        corner = weight * (x_ref[head:n, head:n] + corners[:, tail : 2 * tail])
        x_ref[:, 0:head] = left
        x_ref[head:n, head:n] = corner
        store(both, n, left, corner)
        return keep * keep

    rho2 = keep * keep

    def sides(source, span):
        return [source[i, span[0] : span[1], 0:n] for i in (0, 1)]

    def put(targets, start, span, block):
        for target, part in zip(targets, split(block)):
            target[span[0] : span[1], start : start + head] = part
        low = max(span[0], head)
        if low < span[1]:
            for target, part in zip(targets, split(jnp.transpose(block[low - span[0] :]))):
                target[0:head, start + low : start + span[1]] = part

    def put_corner(targets, start, block):
        for target, part in zip(targets, split(block)):
            target[head:n, start + head : start + n] = part

    def put_x(targets, start, weight, span, product):
        x = weight * (x_ref[span[0] : span[1], 0:head] + product)
        x_ref[span[0] : span[1], 0:head] = x
        put(targets, start, span, x)

    def put_x_corner(targets, start, weight, product):
        x = weight * (x_ref[head:n, head:n] + product)
        x_ref[head:n, head:n] = x
        put_corner(targets, start, x)

    waiting = None
    source, target = wa, wb
    for _ in range(5):
        weight = 2.0 / (2.0 - rho2)
        keep = 0.5 * rho2 * weight
        first = (source[0, :, 0:head], source[1, :, 0:head])
        r = []
        for k, span in enumerate(chunks):
            r.append(dot3(sides(source, span), first))
            if waiting is not None:
                put_x((source.at[0], source.at[1]), n, waiting[0], span, waiting[1][k])
        if waiting is not None:
            put_x_corner((source.at[0], source.at[1]), n, waiting[0], waiting[2])
        corners = corners_of(source)
        first = (source[0, :, n : n + head], source[1, :, n : n + head])
        both = (target.at[0], target.at[1])
        x = []
        for k, span in enumerate(chunks):
            x.append(dot3(sides(source, span), first))
            put(both, 0, span, weight * r[k] - keep * eye_ref[span[0] : span[1], 0:head])
        put_corner(both, 0, weight * corners[:, 0:tail] - keep * eye_ref[head:n, head:n])
        waiting = (weight, x, corners[:, tail : 2 * tail])
        rho2 = keep * keep
        source, target = target, source
    for k, span in enumerate(chunks):
        put_x((source.at[0], source.at[1]), n, waiting[0], span, waiting[1][k])
    put_x_corner((source.at[0], source.at[1]), n, waiting[0], waiting[2])

    def twice(_, rho2):
        return advance(target, source, advance(source, target, rho2))

    rho2 = lax.fori_loop(0, pairs, twice, rho2)
    weight = 2.0 / (2.0 - rho2)
    first = (source[0, :, n : n + head], source[1, :, n : n + head])
    done = (xh_ref, xl_ref)
    ends = [source[i, :, n + head : 2 * n] for i in (0, 1)]
    put_x_corner(done, 0, weight, dot3(sides(source, (head, n)), ends))
    x = [dot3(sides(source, span), first) for span in chunks]
    for k, span in enumerate(chunks):
        put_x(done, 0, weight, span, x[k])


def centred(fields):
    members = sum(field.shape[0] for field in fields)
    mean = sum(jnp.sum(field, axis=0, keepdims=True) for field in fields) * (1.0 / members)
    pairs = [split(field - mean) for field in fields]
    return [jnp.concatenate(parts, axis=0) for parts in zip(*pairs)], mean


def in_chunks(count, product, work):
    waiting = None
    for start in range(0, count, CHUNK):
        span = slice(start, min(start + CHUNK, count))
        result = product(span)
        if waiting is not None:
            work(*waiting)
        waiting = (span, result)
    work(*waiting)


def solve(n_ref, s, g_ref, x, anomaly, z_ref, cross_ref, parts_ref, crossed_already=False, between=()):
    n = z_ref.shape[0]

    def keep(slot, span, value):
        for i, part in enumerate(split(value)):
            parts_ref[slot, i, span] = part

    def kept(slot):
        return parts_ref[slot, 0], parts_ref[slot, 1]

    def some(parts, span):
        return [part[span] for part in parts]

    def crossed(span, value):
        cross_ref[span] = value
        keep(0, span, value)

    def solved(span, value):
        z_ref[span] = value
        keep(1, span, value)

    def left(span, value):
        keep(0, span, cross_ref[span] - z_ref[span] - value)

    def refined(span, value):
        z_ref[span] = z_ref[span] + value

    if crossed_already:
        keep(0, slice(0, n), cross_ref[...])
    else:
        in_chunks(n, lambda span: dot3(some(s, span), [part[...] for part in anomaly]), crossed)
    stages = [
        (lambda span: dot3(some(x, span), kept(0)), solved),
        (lambda span: dot3(split(g_ref[span]), kept(1)), left),
        (lambda span: dot3(some(x, span), kept(0)), refined),
    ]
    for i, (product, work) in enumerate(stages):
        for extra in between[i : i + 1]:
            extra()
        in_chunks(n, product, work)

    def refine(_, carry):
        z = z_ref[...]
        gz = lax.dot_general(g_ref[...], z, NN, precision=HIGHEST, preferred_element_type=F32)
        z_ref[...] = z + dot3([part[...] for part in x], split(cross_ref[...] - z - gz))
        return carry

    lax.fori_loop(0, n_ref[0], refine, 0)


def gain_kernel(batch, parts, own_of, region_ref, column_ref, n_ref, cells_ref, sh_ref, sl_ref, d_ref, g_ref, *refs):
    xh_ref, xl_ref, *refs = refs
    states = refs[:parts]
    z_ref, rows_ref, scratch, anomaly_ref, cross_ref, parts_ref = refs[parts:]
    anomaly, mean = centred([state[...] for state in states])
    for i, part in enumerate(anomaly):
        anomaly_ref[i] = part
    anomaly = (anomaly_ref.at[0], anomaly_ref.at[1])
    picks = cells_ref[pl.ds(own_of(region_ref, column_ref), 1), batch, :]
    hot = selector(picks, mean.shape[1], scratch)
    base = jnp.sum(hot * mean, axis=1, keepdims=True)
    members = anomaly_ref.shape[1]
    count = 3
    size = -(-members // (count * 128)) * 128

    def pick(start, stop):
        picked = select(hot, [part[start:stop] for part in anomaly], NT)
        rows_ref[:, start:stop] = base + picked

    between = [
        functools.partial(pick, i * size, min((i + 1) * size, members)) for i in range(count)
    ]
    x = (xh_ref, xl_ref)
    solve(n_ref, (sh_ref, sl_ref), g_ref, x, anomaly, z_ref, cross_ref, parts_ref, False, between)
    zt = split(select(hot, split(z_ref[...]), NT))
    shift = dot3(zt, split(d_ref[...]))[:, 0:1]
    rows_ref[...] = rows_ref[...] + shift - 0.5 * dot3(zt, (sh_ref[...], sl_ref[...]))


def updated(field, start, s, shift, z):
    size = field.shape[0]
    return field + shift - 0.5 * dot3([h[:, start : start + size] for h in s], z, TN)


def shift_of(z, d_ref):
    return jnp.sum(z * d_ref[:, 0:1], axis=0, keepdims=True)


def update_kernel(starts, sh_ref, sl_ref, d_ref, z_ref, *refs):
    count = len(starts)
    states, outs, parts = refs[:count], refs[count : 2 * count], refs[2 * count :]
    z = z_ref[...]
    shift = shift_of(z, d_ref)
    s, zs = (sh_ref[...], sl_ref[...]), split(z)
    for start, state, out in zip(starts, states, outs):
        out[...] = updated(state[...], start, s, shift, zs)
    if parts:
        anomaly, _ = centred([out[...] for out in outs])
        for ref, part in zip(parts, anomaly):
            ref[...] = part


def last_kernel(given, n_ref, sh_ref, sl_ref, d_ref, g_ref, xh_ref, xl_ref, state_ref, *refs):
    refs, (cross_ref, parts_ref) = refs[:-2], refs[-2:]
    if given:
        cross_ref, *refs = refs
    z_ref, *out_refs = refs
    anomaly = None if given else centred([state_ref[...]])[0]
    x = (xh_ref, xl_ref)
    solve(n_ref, (sh_ref, sl_ref), g_ref, x, anomaly, z_ref, cross_ref, parts_ref, given)
    z = z_ref[...]
    shift, zs = shift_of(z, d_ref), split(z)
    start = sh_ref.shape[1] - state_ref.shape[0]
    s = (sh_ref[...], sl_ref[...])
    count = out_refs[0].shape[0]
    for i, out_ref in enumerate(out_refs):
        out_ref[...] = updated(state_ref[i * count : (i + 1) * count], start + i * count, s, shift, zs)


def join_kernel(first, column_ref, mine_ref, theirs_ref, *refs):
    out_ref, both, sems = refs[-3:]
    chunks = sems.shape[0]
    size = both.shape[0] // chunks
    column = column_ref[0]
    copies = []
    for i in range(chunks):
        at = slice(i * size, (i + 1) * size)
        mine, theirs = mine_ref[first + i * size : first + (i + 1) * size, :], theirs_ref[at, :]
        both[at, 0, :] = jnp.where(column == 0, mine, theirs)
        both[at, 1, :] = jnp.where(column == 0, theirs, mine)
        target = out_ref.at[pl.ds(first + i * size, size)]
        copies.append(pltpu.make_async_copy(both.at[pl.ds(i * size, size)], target, sems.at[i]))
        copies[-1].start()
    for copy in copies:
        copy.wait()


def prepare(pieces, batch, members, patches_of, place, near, values, var, anomaly, sources, n):
    width = anomaly[0].shape[1] if anomaly else 0
    outs = [
        ((n, members), BF16, VMEM),
        ((n, members), BF16, VMEM),
        ((n, 128), F32, VMEM),
        ((n, n), F32, VMEM),
    ]
    if anomaly:
        outs.append(((n, width), F32, VMEM))
    kernel = functools.partial(
        prepare_kernel, pieces, batch, members, patches_of, len(place), bool(anomaly)
    )
    args = [*place, near, values, var, *anomaly, *sources]
    ins = [SMEM] * (len(place) + 1) + [VMEM] * (len(args) - len(place) - 1)
    return call(kernel, outs, ins, args, [pltpu.VMEM((128, 128), F32)], 6 * n * (width + n // 3) * members)


def factor(pieces, batch, members, chunk, patches_of, place, near, values, var, sources, ready=0, before=()):
    per_patch = values.shape[2]
    n = len(pieces) * per_patch
    outs = [
        ((n, members), BF16, VMEM),
        ((n, members), BF16, VMEM),
        ((n, 128), F32, VMEM),
        ((n, n), F32, VMEM),
        ((n, n), BF16, VMEM),
        ((n, n), BF16, VMEM),
        ((1,), jnp.int32, SMEM),
    ]
    args = [*place, near, values, var, *sources, *before]
    aliases = {}
    crossing = len(before) > 4
    if crossing:
        outs.append((before[-1].shape, F32, VMEM))
    if ready:
        first = len(args) - 4 - crossing
        aliases = {first: 0, first + 1: 1, first + 2: 2, first + 3: 3}
        if crossing:
            aliases[first + 4] = 7
    scratch = [
        pltpu.VMEM((128, 128), F32),
        pltpu.VMEM((n, n), F32),
        pltpu.VMEM((n, n), F32),
        pltpu.VMEM((2, n, 2 * n), BF16),
        pltpu.VMEM((2, n, 2 * n), BF16),
    ]
    kernel = functools.partial(
        factor_kernel, pieces, batch, members, chunk, patches_of, len(place), ready, crossing
    )
    flops = 6 * n * n * members + 60 * n * n * n
    ins = [SMEM] * (len(place) + 1) + [VMEM] * (len(args) - len(place) - 1)
    return call(kernel, outs, ins, args, scratch, flops, FACTOR_LIMIT, aliases)


def solver_scratch(n, width):
    return [pltpu.VMEM((n, width), F32), pltpu.VMEM((2, 2, n, width), BF16)]


def gain(batch, own_of, place, cells, factored, states):
    sh, sl, d, g, xh, xl, more = factored[:7]
    n, members = sh.shape
    width = states[0].shape[1]
    kernel = functools.partial(gain_kernel, batch, len(states), own_of)
    outs = [((n, width), F32, VMEM), ((cells.shape[2], members), F32, VMEM)]
    ins = [SMEM] * 3 + [VMEM] * (7 + len(states))
    args = [*place, more, cells, sh, sl, d, g, xh, xl, *states]
    flops = 8 * n * members * width
    scratch = [pltpu.VMEM((8, 128), jnp.int32), pltpu.VMEM((2, members, width), BF16)]
    scratch += solver_scratch(n, width)
    return call(kernel, outs, ins, args, scratch, flops)


def update(factored, z, states, starts, more=False):
    sh, sl, d = factored[:3]
    kernel = functools.partial(update_kernel, starts)
    outs = [(state.shape, F32, VMEM) for state in states]
    if more:
        outs += [((sh.shape[1], z.shape[1]), BF16, VMEM)] * 2
    flops = 6 * sh.shape[0] * sh.shape[1] * z.shape[1]
    return call(kernel, outs, [VMEM] * (4 + len(states)), [sh, sl, d, z, *states], (), flops)


def last(factored, state, parts=1):
    sh, sl, d, g, xh, xl, more, *cross = factored
    n, width = sh.shape[0], state.shape[1]
    outs = [((n, width), F32, VMEM)] + [((state.shape[0] // parts, width), F32, VMEM)] * parts
    args = [more, sh, sl, d, g, xh, xl, state, *cross]
    flops = 12 * sh.shape[0] * sh.shape[1] * width
    ins = [SMEM] + [VMEM] * (len(args) - 1)
    kernel = functools.partial(last_kernel, bool(cross))
    return call(kernel, outs, ins, args, solver_scratch(n, width), flops)


def rings(size):
    up = [(i, (i + 1) % size) for i in range(size)]
    return up, [(j, i) for i, j in up]


BOTH = ("region", "member")


def permute(x, moves, regions):
    table = []
    for region in range(regions):
        for column in range(2):
            pair, parity, to = moves(region // 2, region % 2, column)
            pair %= regions // 2
            table.append((region * 2 + column, (pair * 2 + parity) * 2 + to))
    return lax.ppermute(x, BOTH, table)


def paired(state, neighbours, obs_cell, obs_values, obs_var):
    half, _, cells = state.shape
    members = 2 * half
    regions = lax.axis_size("region")
    region, column = lax.axis_index("region"), lax.axis_index("member")
    place = (region.astype(jnp.int32)[None], column.astype(jnp.int32)[None])
    near = neighbours.T

    def own_of(region_ref, column_ref):
        return region_ref[0] * 2 + column_ref[0]

    def around(region):
        side = 2 * lax.rem(region, 2) - 1
        return region, region - side, lax.rem(region + regions + side, regions)

    def patches_first(region_ref, column_ref):
        return [r * 2 + p for r in around(region_ref[0]) for p in (0, 1)], own_of(region_ref, column_ref)

    def patches_next(region_ref, column_ref):
        column = column_ref[0]
        within = (column, 1 - column)
        return [r * 2 + p for p in within for r in around(region_ref[0])], own_of(region_ref, column_ref)

    def across(x):
        return permute(x, lambda c, q, m: (c, q, 1 - m), regions)

    def beside(x):
        return permute(x, lambda c, q, m: (c, 1 - q, m), regions)

    def outside(x):
        return permute(x, lambda c, q, m: (c + 2 * q - 1, 1 - q, m), regions)

    anywhere = pl.BlockSpec(memory_space=pl.ANY)
    shape = ((half, cells), F32, VMEM)
    keep, send = call(sort_kernel, [shape] * 2, [SMEM, VMEM], [place[1], state])
    (rows,) = call(
        pick_kernel,
        [((2, obs_cell.shape[2], half), F32, VMEM)],
        [SMEM, SMEM, VMEM, VMEM, VMEM],
        [*place, obs_cell, keep, send],
        [pltpu.VMEM((8, 128), jnp.int32)],
    )
    other = across(rows)
    sources = [rows, beside(rows), outside(rows), other, beside(other), outside(other)]
    send, values, var = call(
        gate_kernel,
        [((half, cells), F32, anywhere), (obs_values.shape, F32, VMEM), (obs_var.shape, F32, VMEM)],
        [anywhere] * 4,
        [obs_values, obs_var, send, other],
        [pltpu.SemaphoreType.DMA((2,))],
        aliases={2: 0},
    )
    pieces = [[(i, (p,), 0), (3 + i, (p,), 1)] for i in range(3) for p in range(2)]
    states = [keep, across(send)]
    given = (place, near, values, var)
    n = len(pieces) * obs_cell.shape[2]
    early = [[(0, (p,), 0), (1, (p,), 1)] for p in range(2)]
    done = prepare(early, 0, members, patches_first, *given, (), [rows, other], n)
    factored = factor(pieces, 0, members, CHUNK, patches_first, *given, sources, 2, done)
    everything = slice(None)
    low, high = (everything, slice(0, half)), (everything, slice(half, members))
    pieces = [[(i, low, 0), (i, high, 1)] for i in range(3)]
    pieces += [[(i, high, 0), (i, low, 1)] for i in range(3, 6)]
    early = 4
    for batch in range(1, NBATCH):
        z, rows = gain(batch, own_of, place, obs_cell, factored, states)
        other = across(rows)
        far = permute(rows, lambda c, q, m: (c + 2 * q - 1, 1 - q, 1 - m), regions)
        sources = [rows, beside(rows), outside(rows), other, beside(other), far]
        mine, theirs, *anomaly = update(factored, z, states, (0, half), True)
        states = [mine, theirs]
        done = prepare(pieces[:early], batch, members, patches_next, *given, anomaly, sources[:early], n)
        factored = factor(
            pieces, batch, members, CHUNK, patches_next, *given, sources, early, [*anomaly, *done]
        )
    z, *theirs = last(factored, states[1], 2)
    theirs = [across(part) for part in theirs]
    (mine,) = update(factored, z, states[:1], (0,))
    joined = []
    for part, other in enumerate(theirs):
        count = other.shape[0]
        (out,) = call(
            functools.partial(join_kernel, part * count),
            [(state.shape, F32, anywhere)],
            [SMEM, VMEM, VMEM] + [anywhere] * len(joined),
            [place[1], mine, other, *joined],
            [pltpu.VMEM((count, *state.shape[1:]), F32), pltpu.SemaphoreType.DMA((2,))],
            aliases={3: 0} if joined else {},
        )
        joined = [out]
    return out


def listed(table_ref):
    blocks = table_ref.shape[0] - 1
    return [table_ref[i] for i in range(blocks)], table_ref[blocks]


def general(state, neighbours, obs_cell, obs_values, obs_var):
    ensemble = lax.all_to_all(state, "member", split_axis=1, concat_axis=0, tiled=True)
    members, owned, cells = ensemble.shape
    regions = lax.axis_size("region")
    region_patches = owned * lax.axis_size("member")
    region = lax.axis_index("region")
    first = region * region_patches + lax.axis_index("member") * owned
    up, down = rings(regions)
    fields = [ensemble[:, p, :] for p in range(owned)]
    grid = jnp.arange(cells, dtype=jnp.int32)
    for batch in range(NBATCH):
        picks = lax.dynamic_slice_in_dim(obs_cell, first, owned, 0)[:, batch, :]
        hot = (picks[:, :, None] == grid[None, None, :]).astype(F32)
        own_rows = jnp.einsum("poc,pkc->pok", hot, jnp.stack(fields), precision=HIGHEST)
        region_rows = lax.all_gather(own_rows, "member", axis=0, tiled=True)
        before = lax.ppermute(region_rows, "region", up)
        after = lax.ppermute(region_rows, "region", down)
        beside = jnp.concatenate([before, region_rows, after], axis=0)
        new = []
        for p in range(owned):
            own = first + p
            links = lax.dynamic_index_in_dim(neighbours, own, 0, keepdims=False)
            ids = jnp.concatenate([own[None], links]).astype(jnp.int32)
            table = jnp.concatenate([ids, own[None]]).astype(jnp.int32)
            home = (ids // region_patches - region + 1) % regions
            rows = jnp.take(beside, home * region_patches + ids % region_patches, axis=0)
            pieces = [[(0, (i,), 0)] for i in range(ids.shape[0])]
            factored = factor(
                pieces, batch, members, CHUNK, listed, [table], neighbours.T, obs_values, obs_var, [rows]
            )
            new.append(last(factored, fields[p])[1])
        fields = new
    ensemble = jnp.stack(fields, axis=1)
    return lax.all_to_all(ensemble, "member", split_axis=0, concat_axis=1, tiled=True)


def on_device(state, neighbours, obs_cell, obs_values, obs_var):
    patches, links = state.shape[1], neighbours.shape[1]
    even = lax.axis_size("region") % 2 == 0
    if even and patches == 2 and lax.axis_size("member") == 2 and links + 1 == 3 * patches:
        return paired(state, neighbours, obs_cell, obs_values, obs_var)
    return general(state, neighbours, obs_cell, obs_values, obs_var)


def solution(mesh):
    in_specs = (P("member", "region", None), P(), P(), P(), P())
    out_specs = P("member", "region", None)
    return jax.shard_map(
        on_device, mesh=mesh, in_specs=in_specs, out_specs=out_specs, check_vma=False
    )
```

```python
import functools
import math

import jax
import jax.numpy as jnp
from jax import lax
from jax.experimental import pallas as pl
from jax.experimental.pallas import tpu as pltpu
from jax.sharding import PartitionSpec as P

NBATCH = 2
HIGHEST = lax.Precision.HIGHEST
F32 = jnp.float32
BF16 = jnp.bfloat16
VMEM = pl.BlockSpec(memory_space=pltpu.VMEM)
SMEM = pl.BlockSpec(memory_space=pltpu.SMEM)
NN = (((1,), (0,)), ((), ()))
NT = (((1,), (1,)), ((), ()))
TN = (((0,), (0,)), ((), ()))
RESIDUAL = 0.03
REFINEMENTS = 2
STEPS = 6
FACTOR_LIMIT = 24
MOST_STEPS = 15
TILE = 256
CHUNK = 128


def call(kernel, outs, ins, args, scratch=(), flops=0, limit=16, aliases=None):
    shapes = [jax.ShapeDtypeStruct(shape, dtype) for shape, dtype, _ in outs]
    moved = sum(math.prod(s.shape) * s.dtype.itemsize for s in shapes)
    moved += sum(a.size * a.dtype.itemsize for a in args)
    return pl.pallas_call(
        kernel,
        out_shape=shapes,
        in_specs=ins,
        out_specs=[space for _, _, space in outs],
        scratch_shapes=list(scratch),
        input_output_aliases=aliases or {},
        compiler_params=pltpu.CompilerParams(vmem_limit_bytes=limit * 1024 * 1024),
        cost_estimate=pl.CostEstimate(flops=flops, bytes_accessed=moved, transcendentals=0),
    )(*args)


def split(x):
    high = x.astype(BF16)
    return high, (x - high.astype(F32)).astype(BF16)


def dot(a, b, dims=NN):
    return lax.dot_general(a, b, dims, preferred_element_type=F32)


def dot3(a, b, dims=NN):
    (left,), (right,) = dims[0]
    lhs = jnp.concatenate([a[0], a[0], a[1]], axis=left)
    rhs = jnp.concatenate([b[0], b[1], b[0]], axis=right)
    return dot(lhs, rhs, dims)


def select(hot, parts, dims):
    (left,), (right,) = dims[0]
    hot = hot.astype(BF16)
    lhs = jnp.concatenate([hot] * len(parts), axis=left)
    return dot(lhs, jnp.concatenate(parts, axis=right), dims)


def split_all(x):
    high, middle = split(x)
    low = x - high.astype(F32) - middle.astype(F32)
    return high, middle, low.astype(BF16)


def step_limits():
    limits = []
    for steps in range(MOST_STEPS):
        rho = RESIDUAL
        for _ in range(steps):
            rho = math.sqrt(2.0 * rho / (1.0 + rho))
        limits.append(2.0 * rho / (1.0 - rho) if rho < 1.0 else math.inf)
    return limits


def diagonal(n, columns, first):
    row = lax.broadcasted_iota(jnp.int32, (n, columns), 0)
    column = lax.broadcasted_iota(jnp.int32, (n, columns), 1)
    return row + first == column


def selector(picks, cells, scratch):
    per_patch = picks.shape[1]
    scratch[...] = jnp.full_like(scratch, -1)
    scratch[0:1, 0:per_patch] = picks
    grid = lax.broadcasted_iota(jnp.int32, (cells, scratch.shape[1]), 0)
    hot = (grid == scratch[0:1, :]).astype(F32)
    return jnp.transpose(hot)[0:per_patch, :]


def sort_kernel(column_ref, state_ref, keep_ref, send_ref):
    column = column_ref[0]
    first, second = state_ref[:, 0, :], state_ref[:, 1, :]
    keep_ref[...] = jnp.where(column == 0, first, second)
    send_ref[...] = jnp.where(column == 0, second, first)


def pick_kernel(region_ref, column_ref, cells_ref, keep_ref, send_ref, rows_ref, scratch):
    column = column_ref[0]
    for patch, field_ref in ((column, keep_ref), (1 - column, send_ref)):
        picks = cells_ref[pl.ds(region_ref[0] * 2 + patch, 1), 0, :]
        hot = selector(picks, field_ref.shape[1], scratch)
        rows_ref[pl.ds(patch, 1)] = select(hot, split_all(field_ref[...]), NT)[None]


def gate_kernel(values_hbm, var_hbm, send_ref, after_ref, out_ref, values_ref, var_ref, sems):
    copies = [
        pltpu.make_async_copy(values_hbm, values_ref, sems.at[0]),
        pltpu.make_async_copy(var_hbm, var_ref, sems.at[1]),
    ]
    for copy in copies:
        copy.start()
    for copy in copies:
        copy.wait()


def table(patches, own, near_ref, values_ref, var_ref, batch, flat):
    per_patch = values_ref.shape[2]
    blocks = len(patches)
    flat[...] = jnp.ones_like(flat)
    for i, patch in enumerate(patches):
        widening = (patch == own).astype(jnp.int32)
        for j in range(near_ref.shape[0]):
            widening = widening + (near_ref[j, own] == patch).astype(jnp.int32) * (j + 2)
        flat[i : i + 1, 0:per_patch] = values_ref[pl.ds(patch, 1), batch, :]
        noise = var_ref[pl.ds(patch, 1), batch, :] * widening.astype(F32)
        flat[blocks + i : blocks + i + 1, 0:per_patch] = noise
    upright = jnp.transpose(flat[...])[0:per_patch]
    return [(upright[:, i : i + 1], upright[:, blocks + i : blocks + i + 1]) for i in range(blocks)]


def scale_block(i, piece, sources, column, members, sh_ref, sl_ref, d_ref):
    value, noise = column
    rows = [sources[which][index] for which, index, _ in piece]
    total = sum(jnp.sum(part, axis=1, keepdims=True) for part in rows)
    mean = total * (1.0 / members)
    scale = lax.rsqrt(noise * (members - 1.0))
    per_patch = value.shape[0]
    at = slice(i * per_patch, (i + 1) * per_patch)
    for part, (_, _, start) in zip(rows, piece):
        size = part.shape[1]
        lanes = slice(start * size, (start + 1) * size)
        sh_ref[at, lanes], sl_ref[at, lanes] = split((part - mean) * scale)
    d_ref[at, :] = jnp.broadcast_to((value - mean) * scale, (per_patch, d_ref.shape[1]))


def prepare_kernel(pieces, batch, members, patches_of, places, crossing, *refs):
    place_refs, refs = refs[:places], refs[places:]
    near_ref, values_ref, var_ref, *refs = refs
    refs, flat = refs[:-1], refs[-1]
    if crossing:
        (ah_ref, al_ref, *refs), cross_ref = refs[:-1], refs[-1]
    sources, (sh_ref, sl_ref, d_ref, g_ref) = refs[:-4], refs[-4:]
    patches, own = patches_of(*place_refs)
    columns = table(patches[: len(pieces)], own, near_ref, values_ref, var_ref, batch, flat)
    for i, piece in enumerate(pieces):
        scale_block(i, piece, sources, columns[i], members, sh_ref, sl_ref, d_ref)
    count = len(pieces) * values_ref.shape[2]
    s = (sh_ref[0:count], sl_ref[0:count])
    g_ref[0:count, 0:count] = dot3(s, s, NT)
    if crossing:
        cross_ref[0:count] = dot3(s, (ah_ref[...], al_ref[...]))


def factor_kernel(pieces, batch, members, chunk, patches_of, places, ready, crossing, *refs):
    place_refs, refs = refs[:places], refs[places:]
    near_ref, values_ref, var_ref, *refs = refs
    refs, (flat, eye_ref, x_ref, wa, wb) = refs[:-5], refs[-5:]
    if crossing:
        refs, cross_ref = refs[:-1], refs[-1]
    refs, (sh_ref, sl_ref, d_ref, g_ref, xh_ref, xl_ref, n_ref) = refs[:-7], refs[-7:]
    if crossing:
        refs, (ah_ref, al_ref) = refs[:-7], refs[-7:-5]
    elif ready:
        refs = refs[:-4]
    sources = refs
    per_patch = values_ref.shape[2]
    blocks = len(pieces)
    patches, own = patches_of(*place_refs)
    columns = table(patches[ready:], own, near_ref, values_ref, var_ref, batch, flat)
    for i in range(ready, blocks):
        scale_block(i, pieces[i], sources, columns[i - ready], members, sh_ref, sl_ref, d_ref)
    n = sh_ref.shape[0]
    head = min(TILE, n)
    tail = n - head
    chunks = [(i, min(i + chunk, n)) for i in range(0, n, chunk)]
    left = (sh_ref[0:head], sl_ref[0:head])
    fresh = ready * per_patch
    g_ref[fresh:n, 0:head] = dot3((sh_ref[fresh:n], sl_ref[fresh:n]), left, NT)
    if 0 < fresh < head:
        g_ref[0:fresh, fresh:head] = jnp.transpose(g_ref[fresh:head, 0:fresh])
    low = (sh_ref[head:n], sl_ref[head:n])
    g_ref[head:n, head:n] = dot3(low, low, NT)
    g_ref[0:head, head:n] = jnp.transpose(g_ref[head:n, 0:head])
    if crossing:
        cross_ref[fresh:n] = dot3((sh_ref[fresh:n], sl_ref[fresh:n]), (ah_ref[...], al_ref[...]))
    g = g_ref[...]
    square = jnp.sum(jnp.sum(g * g, axis=0, keepdims=True), axis=1, keepdims=True)
    norm = jnp.sqrt(square) * (1.0 + 1e-5)
    size = square[0, 0]
    limits = step_limits()
    pairs = jnp.int32(0)
    for k in range(STEPS, MOST_STEPS - 2, 2):
        limit = limits[k] * (1.0 - 1e-4)
        pairs = pairs + (size > limit * limit).astype(jnp.int32)
    n_ref[0] = (size > 1.6e7).astype(jnp.int32) + (size > 1e8).astype(jnp.int32)
    eye_ref[...] = diagonal(n, n, 0).astype(F32)
    eye = eye_ref[...]
    first = 2.0 / (2.0 + norm)
    rho = norm * (0.5 * first)
    rho2 = rho * rho
    weight = 2.0 / (2.0 - rho2)
    keep = 0.5 * rho2 * weight
    r = (1.0 - first) * eye - first * g
    parts = split(r)
    x = (weight * first) * (eye + r)
    x_ref[...] = x
    for i, part in enumerate(split(x)):
        wa[i, :, n : 2 * n] = part

    def store(targets, start, left, corner):
        blocks = [(slice(0, n), slice(start, start + head), left)]
        blocks.append((slice(head, n), slice(start + head, start + n), corner))
        blocks.append((slice(0, head), slice(start + head, start + n), jnp.transpose(left[head:n])))
        for rows, columns, block in blocks:
            for target, part in zip(targets, split(block)):
                target[rows, columns] = part

    def corner_of(weight, keep, left, corner):
        left = weight * left - keep * eye_ref[:, 0:head]
        return left, weight * corner - keep * eye_ref[head:n, head:n]

    left = dot3(parts, [part[:, 0:head] for part in parts])
    corner = dot3([part[head:n] for part in parts], [part[:, head:n] for part in parts])
    store((wa.at[0], wa.at[1]), 0, *corner_of(weight, keep, left, corner))

    def corners_of(source):
        ends = [jnp.concatenate([source[i, :, head:n], source[i, :, n + head : 2 * n]], axis=1) for i in (0, 1)]
        return dot3([source[i, head:n, 0:n] for i in (0, 1)], ends)

    def advance(source, target, rho2):
        weight = 2.0 / (2.0 - rho2)
        keep = 0.5 * rho2 * weight
        parts = (source[0, :, 0:n], source[1, :, 0:n])
        left = dot3(parts, (source[0, :, 0:head], source[1, :, 0:head]))
        corners = corners_of(source)
        both = (target.at[0], target.at[1])
        store(both, 0, *corner_of(weight, keep, left, corners[:, 0:tail]))
        left = dot3(parts, (source[0, :, n : n + head], source[1, :, n : n + head]))
        left = weight * (x_ref[:, 0:head] + left)
        corner = weight * (x_ref[head:n, head:n] + corners[:, tail : 2 * tail])
        x_ref[:, 0:head] = left
        x_ref[head:n, head:n] = corner
        store(both, n, left, corner)
        return keep * keep

    rho2 = keep * keep

    def sides(source, span):
        return [source[i, span[0] : span[1], 0:n] for i in (0, 1)]

    def put(targets, start, span, block):
        for target, part in zip(targets, split(block)):
            target[span[0] : span[1], start : start + head] = part
        low = max(span[0], head)
        if low < span[1]:
            for target, part in zip(targets, split(jnp.transpose(block[low - span[0] :]))):
                target[0:head, start + low : start + span[1]] = part

    def put_corner(targets, start, block):
        for target, part in zip(targets, split(block)):
            target[head:n, start + head : start + n] = part

    def put_x(targets, start, weight, span, product):
        x = weight * (x_ref[span[0] : span[1], 0:head] + product)
        x_ref[span[0] : span[1], 0:head] = x
        put(targets, start, span, x)

    def put_x_corner(targets, start, weight, product):
        x = weight * (x_ref[head:n, head:n] + product)
        x_ref[head:n, head:n] = x
        put_corner(targets, start, x)

    waiting = None
    source, target = wa, wb
    for _ in range(STEPS - 2):
        weight = 2.0 / (2.0 - rho2)
        keep = 0.5 * rho2 * weight
        first = (source[0, :, 0:head], source[1, :, 0:head])
        r = []
        for k, span in enumerate(chunks):
            r.append(dot3(sides(source, span), first))
            if waiting is not None:
                put_x((source.at[0], source.at[1]), n, waiting[0], span, waiting[1][k])
        if waiting is not None:
            put_x_corner((source.at[0], source.at[1]), n, waiting[0], waiting[2])
        corners = corners_of(source)
        first = (source[0, :, n : n + head], source[1, :, n : n + head])
        both = (target.at[0], target.at[1])
        x = []
        for k, span in enumerate(chunks):
            x.append(dot3(sides(source, span), first))
            put(both, 0, span, weight * r[k] - keep * eye_ref[span[0] : span[1], 0:head])
        put_corner(both, 0, weight * corners[:, 0:tail] - keep * eye_ref[head:n, head:n])
        waiting = (weight, x, corners[:, tail : 2 * tail])
        rho2 = keep * keep
        source, target = target, source
    for k, span in enumerate(chunks):
        put_x((source.at[0], source.at[1]), n, waiting[0], span, waiting[1][k])
    put_x_corner((source.at[0], source.at[1]), n, waiting[0], waiting[2])

    def twice(_, rho2):
        return advance(target, source, advance(source, target, rho2))

    rho2 = lax.fori_loop(0, pairs, twice, rho2)
    weight = 2.0 / (2.0 - rho2)
    first = (source[0, :, n : n + head], source[1, :, n : n + head])
    done = (xh_ref, xl_ref)
    ends = [source[i, :, n + head : 2 * n] for i in (0, 1)]
    put_x_corner(done, 0, weight, dot3(sides(source, (head, n)), ends))
    x = [dot3(sides(source, span), first) for span in chunks]
    for k, span in enumerate(chunks):
        put_x(done, 0, weight, span, x[k])


def centred(fields):
    members = sum(field.shape[0] for field in fields)
    mean = sum(jnp.sum(field, axis=0, keepdims=True) for field in fields) * (1.0 / members)
    pairs = [split(field - mean) for field in fields]
    return [jnp.concatenate(parts, axis=0) for parts in zip(*pairs)], mean


def in_chunks(count, product, work):
    waiting = None
    for start in range(0, count, CHUNK):
        span = slice(start, min(start + CHUNK, count))
        result = product(span)
        if waiting is not None:
            work(*waiting)
        waiting = (span, result)
    work(*waiting)


def solve(n_ref, s, g_ref, x, anomaly, z_ref, cross_ref, parts_ref, crossed_already=False, between=()):
    n = z_ref.shape[0]

    def keep(slot, span, value):
        for i, part in enumerate(split(value)):
            parts_ref[slot, i, span] = part

    def kept(slot):
        return parts_ref[slot, 0], parts_ref[slot, 1]

    def some(parts, span):
        return [part[span] for part in parts]

    def crossed(span, value):
        cross_ref[span] = value
        keep(0, span, value)

    def solved(span, value):
        z_ref[span] = value
        keep(1, span, value)

    def left(span, value):
        keep(0, span, cross_ref[span] - z_ref[span] - value)

    def refined(span, value):
        solved(span, z_ref[span] + value)

    if crossed_already:
        keep(0, slice(0, n), cross_ref[...])
    else:
        in_chunks(n, lambda span: dot3(some(s, span), [part[...] for part in anomaly]), crossed)
    stages = [
        (lambda span: dot3(some(x, span), kept(0)), solved),
        (lambda span: dot3(split(g_ref[span]), kept(1)), left),
        (lambda span: dot3(some(x, span), kept(0)), refined),
    ]
    stages += stages[1:] * (REFINEMENTS - 1)
    for i, (product, work) in enumerate(stages):
        for extra in between[i : i + 1]:
            extra()
        in_chunks(n, product, work)

    def refine(_, carry):
        z = z_ref[...]
        gz = lax.dot_general(g_ref[...], z, NN, precision=HIGHEST, preferred_element_type=F32)
        z_ref[...] = z + dot3([part[...] for part in x], split(cross_ref[...] - z - gz))
        return carry

    lax.fori_loop(0, n_ref[0], refine, 0)


def gain_kernel(batch, parts, own_of, region_ref, column_ref, n_ref, cells_ref, sh_ref, sl_ref, d_ref, g_ref, *refs):
    xh_ref, xl_ref, *refs = refs
    states = refs[:parts]
    z_ref, rows_ref, scratch, anomaly_ref, cross_ref, parts_ref = refs[parts:]
    anomaly, mean = centred([state[...] for state in states])
    for i, part in enumerate(anomaly):
        anomaly_ref[i] = part
    anomaly = (anomaly_ref.at[0], anomaly_ref.at[1])
    picks = cells_ref[pl.ds(own_of(region_ref, column_ref), 1), batch, :]
    hot = selector(picks, mean.shape[1], scratch)
    base = jnp.sum(hot * mean, axis=1, keepdims=True)
    members = anomaly_ref.shape[1]
    count = 3
    size = -(-members // (count * 128)) * 128

    def pick(start, stop):
        picked = select(hot, [part[start:stop] for part in anomaly], NT)
        rows_ref[:, start:stop] = base + picked

    between = [
        functools.partial(pick, i * size, min((i + 1) * size, members)) for i in range(count)
    ]
    x = (xh_ref, xl_ref)
    solve(n_ref, (sh_ref, sl_ref), g_ref, x, anomaly, z_ref, cross_ref, parts_ref, False, between)
    zt = split(select(hot, split(z_ref[...]), NT))
    shift = dot3(zt, split(d_ref[...]))[:, 0:1]
    rows_ref[...] = rows_ref[...] + shift - 0.5 * dot3(zt, (sh_ref[...], sl_ref[...]))


def updated(field, start, s, shift, z):
    size = field.shape[0]
    return field + shift - 0.5 * dot3([h[:, start : start + size] for h in s], z, TN)


def shift_of(z, d_ref):
    return jnp.sum(z * d_ref[:, 0:1], axis=0, keepdims=True)


def update_kernel(starts, sh_ref, sl_ref, d_ref, z_ref, *refs):
    count = len(starts)
    states, outs, parts = refs[:count], refs[count : 2 * count], refs[2 * count :]
    z = z_ref[...]
    shift = shift_of(z, d_ref)
    s, zs = (sh_ref[...], sl_ref[...]), split(z)
    for start, state, out in zip(starts, states, outs):
        out[...] = updated(state[...], start, s, shift, zs)
    if parts:
        anomaly, _ = centred([out[...] for out in outs])
        for ref, part in zip(parts, anomaly):
            ref[...] = part


def last_kernel(given, n_ref, sh_ref, sl_ref, d_ref, g_ref, xh_ref, xl_ref, state_ref, *refs):
    refs, (cross_ref, parts_ref) = refs[:-2], refs[-2:]
    if given:
        cross_ref, *refs = refs
    z_ref, *out_refs = refs
    anomaly = None if given else centred([state_ref[...]])[0]
    x = (xh_ref, xl_ref)
    solve(n_ref, (sh_ref, sl_ref), g_ref, x, anomaly, z_ref, cross_ref, parts_ref, given)
    z = z_ref[...]
    shift, zs = shift_of(z, d_ref), split(z)
    start = sh_ref.shape[1] - state_ref.shape[0]
    s = (sh_ref[...], sl_ref[...])
    first = 0
    for out_ref in out_refs:
        stop = first + out_ref.shape[0]
        out_ref[...] = updated(state_ref[first:stop], start + first, s, shift, zs)
        first = stop


def join_kernel(first, column_ref, mine_ref, theirs_ref, *refs):
    out_ref, both, sems = refs[-3:]
    chunks = sems.shape[0]
    size = both.shape[0] // chunks
    column = column_ref[0]
    copies = []
    for i in range(chunks):
        at = slice(i * size, (i + 1) * size)
        mine, theirs = mine_ref[first + i * size : first + (i + 1) * size, :], theirs_ref[at, :]
        both[at, 0, :] = jnp.where(column == 0, mine, theirs)
        both[at, 1, :] = jnp.where(column == 0, theirs, mine)
        target = out_ref.at[pl.ds(first + i * size, size)]
        copies.append(pltpu.make_async_copy(both.at[pl.ds(i * size, size)], target, sems.at[i]))
        copies[-1].start()
    for copy in copies:
        copy.wait()


def prepare(pieces, batch, members, patches_of, place, near, values, var, anomaly, sources, n):
    width = anomaly[0].shape[1] if anomaly else 0
    outs = [
        ((n, members), BF16, VMEM),
        ((n, members), BF16, VMEM),
        ((n, 128), F32, VMEM),
        ((n, n), F32, VMEM),
    ]
    if anomaly:
        outs.append(((n, width), F32, VMEM))
    kernel = functools.partial(
        prepare_kernel, pieces, batch, members, patches_of, len(place), bool(anomaly)
    )
    args = [*place, near, values, var, *anomaly, *sources]
    ins = [SMEM] * (len(place) + 1) + [VMEM] * (len(args) - len(place) - 1)
    return call(kernel, outs, ins, args, [pltpu.VMEM((128, 128), F32)], 6 * n * (width + n // 3) * members)


def factor(pieces, batch, members, chunk, patches_of, place, near, values, var, sources, ready=0, before=()):
    per_patch = values.shape[2]
    n = len(pieces) * per_patch
    outs = [
        ((n, members), BF16, VMEM),
        ((n, members), BF16, VMEM),
        ((n, 128), F32, VMEM),
        ((n, n), F32, VMEM),
        ((n, n), BF16, VMEM),
        ((n, n), BF16, VMEM),
        ((1,), jnp.int32, SMEM),
    ]
    args = [*place, near, values, var, *sources, *before]
    aliases = {}
    crossing = len(before) > 4
    if crossing:
        outs.append((before[-1].shape, F32, VMEM))
    if ready:
        first = len(args) - 4 - crossing
        aliases = {first: 0, first + 1: 1, first + 2: 2, first + 3: 3}
        if crossing:
            aliases[first + 4] = 7
    scratch = [
        pltpu.VMEM((128, 128), F32),
        pltpu.VMEM((n, n), F32),
        pltpu.VMEM((n, n), F32),
        pltpu.VMEM((2, n, 2 * n), BF16),
        pltpu.VMEM((2, n, 2 * n), BF16),
    ]
    kernel = functools.partial(
        factor_kernel, pieces, batch, members, chunk, patches_of, len(place), ready, crossing
    )
    flops = 6 * n * n * members + 60 * n * n * n
    ins = [SMEM] * (len(place) + 1) + [VMEM] * (len(args) - len(place) - 1)
    return call(kernel, outs, ins, args, scratch, flops, FACTOR_LIMIT, aliases)


def solver_scratch(n, width):
    return [pltpu.VMEM((n, width), F32), pltpu.VMEM((2, 2, n, width), BF16)]


def gain(batch, own_of, place, cells, factored, states):
    sh, sl, d, g, xh, xl, more = factored[:7]
    n, members = sh.shape
    width = states[0].shape[1]
    kernel = functools.partial(gain_kernel, batch, len(states), own_of)
    outs = [((n, width), F32, VMEM), ((cells.shape[2], members), F32, VMEM)]
    ins = [SMEM] * 3 + [VMEM] * (7 + len(states))
    args = [*place, more, cells, sh, sl, d, g, xh, xl, *states]
    flops = 8 * n * members * width
    scratch = [pltpu.VMEM((8, 128), jnp.int32), pltpu.VMEM((2, members, width), BF16)]
    scratch += solver_scratch(n, width)
    return call(kernel, outs, ins, args, scratch, flops)


def update(factored, z, states, starts, more=False):
    sh, sl, d = factored[:3]
    kernel = functools.partial(update_kernel, starts)
    outs = [(state.shape, F32, VMEM) for state in states]
    if more:
        outs += [((sh.shape[1], z.shape[1]), BF16, VMEM)] * 2
    flops = 6 * sh.shape[0] * sh.shape[1] * z.shape[1]
    return call(kernel, outs, [VMEM] * (4 + len(states)), [sh, sl, d, z, *states], (), flops)


def last(factored, state, counts=None):
    sh, sl, d, g, xh, xl, more, *cross = factored
    n, width = sh.shape[0], state.shape[1]
    outs = [((n, width), F32, VMEM)] + [((count, width), F32, VMEM) for count in counts or state.shape[:1]]
    args = [more, sh, sl, d, g, xh, xl, state, *cross]
    flops = 12 * sh.shape[0] * sh.shape[1] * width
    ins = [SMEM] + [VMEM] * (len(args) - 1)
    kernel = functools.partial(last_kernel, bool(cross))
    return call(kernel, outs, ins, args, solver_scratch(n, width), flops)


def rings(size):
    up = [(i, (i + 1) % size) for i in range(size)]
    return up, [(j, i) for i, j in up]


BOTH = ("region", "member")


def permute(x, moves, regions):
    table = []
    for region in range(regions):
        for column in range(2):
            pair, parity, to = moves(region // 2, region % 2, column)
            pair %= regions // 2
            table.append((region * 2 + column, (pair * 2 + parity) * 2 + to))
    return lax.ppermute(x, BOTH, table)


def paired(state, neighbours, obs_cell, obs_values, obs_var):
    half, _, cells = state.shape
    members = 2 * half
    regions = lax.axis_size("region")
    region, column = lax.axis_index("region"), lax.axis_index("member")
    place = (region.astype(jnp.int32)[None], column.astype(jnp.int32)[None])
    near = neighbours.T

    def own_of(region_ref, column_ref):
        return region_ref[0] * 2 + column_ref[0]

    def around(region):
        side = 2 * lax.rem(region, 2) - 1
        return region, region - side, lax.rem(region + regions + side, regions)

    def patches_first(region_ref, column_ref):
        return [r * 2 + p for r in around(region_ref[0]) for p in (0, 1)], own_of(region_ref, column_ref)

    def patches_next(region_ref, column_ref):
        column = column_ref[0]
        within = (column, 1 - column)
        return [r * 2 + p for p in within for r in around(region_ref[0])], own_of(region_ref, column_ref)

    def across(x):
        return permute(x, lambda c, q, m: (c, q, 1 - m), regions)

    def beside(x):
        return permute(x, lambda c, q, m: (c, 1 - q, m), regions)

    def outside(x):
        return permute(x, lambda c, q, m: (c + 2 * q - 1, 1 - q, m), regions)

    anywhere = pl.BlockSpec(memory_space=pl.ANY)
    shape = ((half, cells), F32, VMEM)
    keep, send = call(sort_kernel, [shape] * 2, [SMEM, VMEM], [place[1], state])
    (rows,) = call(
        pick_kernel,
        [((2, obs_cell.shape[2], half), F32, VMEM)],
        [SMEM, SMEM, VMEM, VMEM, VMEM],
        [*place, obs_cell, keep, send],
        [pltpu.VMEM((8, 128), jnp.int32)],
    )
    other = across(rows)
    sources = [rows, beside(rows), outside(rows), other, beside(other), outside(other)]
    send, values, var = call(
        gate_kernel,
        [((half, cells), F32, anywhere), (obs_values.shape, F32, VMEM), (obs_var.shape, F32, VMEM)],
        [anywhere] * 4,
        [obs_values, obs_var, send, other],
        [pltpu.SemaphoreType.DMA((2,))],
        aliases={2: 0},
    )
    pieces = [[(i, (p,), 0), (3 + i, (p,), 1)] for i in range(3) for p in range(2)]
    states = [keep, across(send)]
    given = (place, near, values, var)
    n = len(pieces) * obs_cell.shape[2]
    early = [[(0, (p,), 0), (1, (p,), 1)] for p in range(2)]
    done = prepare(early, 0, members, patches_first, *given, (), [rows, other], n)
    factored = factor(pieces, 0, members, CHUNK, patches_first, *given, sources, 2, done)
    everything = slice(None)
    low, high = (everything, slice(0, half)), (everything, slice(half, members))
    pieces = [[(i, low, 0), (i, high, 1)] for i in range(3)]
    pieces += [[(i, high, 0), (i, low, 1)] for i in range(3, 6)]
    early = 4
    for batch in range(1, NBATCH):
        z, rows = gain(batch, own_of, place, obs_cell, factored, states)
        other = across(rows)
        far = permute(rows, lambda c, q, m: (c + 2 * q - 1, 1 - q, 1 - m), regions)
        sources = [rows, beside(rows), outside(rows), other, beside(other), far]
        mine, theirs, *anomaly = update(factored, z, states, (0, half), True)
        states = [mine, theirs]
        done = prepare(pieces[:early], batch, members, patches_next, *given, anomaly, sources[:early], n)
        factored = factor(
            pieces, batch, members, CHUNK, patches_next, *given, sources, early, [*anomaly, *done]
        )
    most = half - half // 4
    z, *theirs = last(factored, states[1], (most, half - most))
    theirs = [across(part) for part in theirs]
    (mine,) = update(factored, z, states[:1], (0,))
    joined = []
    for first, other in zip((0, most), theirs):
        count = other.shape[0]
        (out,) = call(
            functools.partial(join_kernel, first),
            [(state.shape, F32, anywhere)],
            [SMEM, VMEM, VMEM] + [anywhere] * len(joined),
            [place[1], mine, other, *joined],
            [pltpu.VMEM((count, *state.shape[1:]), F32), pltpu.SemaphoreType.DMA((2,))],
            aliases={3: 0} if joined else {},
        )
        joined = [out]
    return out


def listed(table_ref):
    blocks = table_ref.shape[0] - 1
    return [table_ref[i] for i in range(blocks)], table_ref[blocks]


def general(state, neighbours, obs_cell, obs_values, obs_var):
    ensemble = lax.all_to_all(state, "member", split_axis=1, concat_axis=0, tiled=True)
    members, owned, cells = ensemble.shape
    regions = lax.axis_size("region")
    region_patches = owned * lax.axis_size("member")
    region = lax.axis_index("region")
    first = region * region_patches + lax.axis_index("member") * owned
    up, down = rings(regions)
    fields = [ensemble[:, p, :] for p in range(owned)]
    grid = jnp.arange(cells, dtype=jnp.int32)
    for batch in range(NBATCH):
        picks = lax.dynamic_slice_in_dim(obs_cell, first, owned, 0)[:, batch, :]
        hot = (picks[:, :, None] == grid[None, None, :]).astype(F32)
        own_rows = jnp.einsum("poc,pkc->pok", hot, jnp.stack(fields), precision=HIGHEST)
        region_rows = lax.all_gather(own_rows, "member", axis=0, tiled=True)
        before = lax.ppermute(region_rows, "region", up)
        after = lax.ppermute(region_rows, "region", down)
        beside = jnp.concatenate([before, region_rows, after], axis=0)
        new = []
        for p in range(owned):
            own = first + p
            links = lax.dynamic_index_in_dim(neighbours, own, 0, keepdims=False)
            ids = jnp.concatenate([own[None], links]).astype(jnp.int32)
            table = jnp.concatenate([ids, own[None]]).astype(jnp.int32)
            home = (ids // region_patches - region + 1) % regions
            rows = jnp.take(beside, home * region_patches + ids % region_patches, axis=0)
            pieces = [[(0, (i,), 0)] for i in range(ids.shape[0])]
            factored = factor(
                pieces, batch, members, CHUNK, listed, [table], neighbours.T, obs_values, obs_var, [rows]
            )
            new.append(last(factored, fields[p])[1])
        fields = new
    ensemble = jnp.stack(fields, axis=1)
    return lax.all_to_all(ensemble, "member", split_axis=0, concat_axis=1, tiled=True)


def on_device(state, neighbours, obs_cell, obs_values, obs_var):
    patches, links = state.shape[1], neighbours.shape[1]
    even = lax.axis_size("region") % 2 == 0
    if even and patches == 2 and lax.axis_size("member") == 2 and links + 1 == 3 * patches:
        return paired(state, neighbours, obs_cell, obs_values, obs_var)
    return general(state, neighbours, obs_cell, obs_values, obs_var)


def solution(mesh):
    in_specs = (P("member", "region", None), P(), P(), P(), P())
    out_specs = P("member", "region", None)
    return jax.shard_map(
        on_device, mesh=mesh, in_specs=in_specs, out_specs=out_specs, check_vma=False
    )
```

```python
import functools
import math

import jax
import jax.numpy as jnp
from jax import lax
from jax.experimental import pallas as pl
from jax.experimental.pallas import tpu as pltpu
from jax.sharding import PartitionSpec as P

NBATCH = 2
HIGHEST = lax.Precision.HIGHEST
F32 = jnp.float32
BF16 = jnp.bfloat16
VMEM = pl.BlockSpec(memory_space=pltpu.VMEM)
SMEM = pl.BlockSpec(memory_space=pltpu.SMEM)
NN = (((1,), (0,)), ((), ()))
NT = (((1,), (1,)), ((), ()))
TN = (((0,), (0,)), ((), ()))
RESIDUAL = 1e-3
FACTOR_LIMIT = 24
MOST_STEPS = 15
TILE = 256
CHUNK = 128


def call(kernel, outs, ins, args, scratch=(), flops=0, limit=16, aliases=None):
    shapes = [jax.ShapeDtypeStruct(shape, dtype) for shape, dtype, _ in outs]
    moved = sum(math.prod(s.shape) * s.dtype.itemsize for s in shapes)
    moved += sum(a.size * a.dtype.itemsize for a in args)
    return pl.pallas_call(
        kernel,
        out_shape=shapes,
        in_specs=ins,
        out_specs=[space for _, _, space in outs],
        scratch_shapes=list(scratch),
        input_output_aliases=aliases or {},
        compiler_params=pltpu.CompilerParams(vmem_limit_bytes=limit * 1024 * 1024),
        cost_estimate=pl.CostEstimate(flops=flops, bytes_accessed=moved, transcendentals=0),
    )(*args)


def split(x):
    high = x.astype(BF16)
    return high, (x - high.astype(F32)).astype(BF16)


def dot(a, b, dims=NN):
    return lax.dot_general(a, b, dims, preferred_element_type=F32)


def dot3(a, b, dims=NN):
    (left,), (right,) = dims[0]
    lhs = jnp.concatenate([a[0], a[0], a[1]], axis=left)
    rhs = jnp.concatenate([b[0], b[1], b[0]], axis=right)
    return dot(lhs, rhs, dims)


def select(hot, parts, dims):
    (left,), (right,) = dims[0]
    hot = hot.astype(BF16)
    lhs = jnp.concatenate([hot] * len(parts), axis=left)
    return dot(lhs, jnp.concatenate(parts, axis=right), dims)


def split_all(x):
    high, middle = split(x)
    low = x - high.astype(F32) - middle.astype(F32)
    return high, middle, low.astype(BF16)


def step_limits():
    limits = []
    for steps in range(MOST_STEPS):
        rho = RESIDUAL
        for _ in range(steps):
            rho = math.sqrt(2.0 * rho / (1.0 + rho))
        limits.append(2.0 * rho / (1.0 - rho) if rho < 1.0 else math.inf)
    return limits


def diagonal(n, columns, first):
    row = lax.broadcasted_iota(jnp.int32, (n, columns), 0)
    column = lax.broadcasted_iota(jnp.int32, (n, columns), 1)
    return row + first == column


def selector(picks, cells, scratch):
    per_patch = picks.shape[1]
    scratch[...] = jnp.full_like(scratch, -1)
    scratch[0:1, 0:per_patch] = picks
    grid = lax.broadcasted_iota(jnp.int32, (cells, scratch.shape[1]), 0)
    hot = (grid == scratch[0:1, :]).astype(F32)
    return jnp.transpose(hot)[0:per_patch, :]


def sort_kernel(column_ref, state_ref, keep_ref, send_ref):
    column = column_ref[0]
    first, second = state_ref[:, 0, :], state_ref[:, 1, :]
    keep_ref[...] = jnp.where(column == 0, first, second)
    send_ref[...] = jnp.where(column == 0, second, first)


def pick_kernel(region_ref, column_ref, cells_ref, keep_ref, send_ref, rows_ref, scratch):
    column = column_ref[0]
    for patch, field_ref in ((column, keep_ref), (1 - column, send_ref)):
        picks = cells_ref[pl.ds(region_ref[0] * 2 + patch, 1), 0, :]
        hot = selector(picks, field_ref.shape[1], scratch)
        rows_ref[pl.ds(patch, 1)] = select(hot, split_all(field_ref[...]), NT)[None]


def gate_kernel(values_hbm, var_hbm, send_ref, after_ref, out_ref, values_ref, var_ref, sems):
    copies = [
        pltpu.make_async_copy(values_hbm, values_ref, sems.at[0]),
        pltpu.make_async_copy(var_hbm, var_ref, sems.at[1]),
    ]
    for copy in copies:
        copy.start()
    for copy in copies:
        copy.wait()


def table(patches, own, near_ref, values_ref, var_ref, batch, flat):
    per_patch = values_ref.shape[2]
    blocks = len(patches)
    flat[...] = jnp.ones_like(flat)
    for i, patch in enumerate(patches):
        widening = (patch == own).astype(jnp.int32)
        for j in range(near_ref.shape[0]):
            widening = widening + (near_ref[j, own] == patch).astype(jnp.int32) * (j + 2)
        flat[i : i + 1, 0:per_patch] = values_ref[pl.ds(patch, 1), batch, :]
        noise = var_ref[pl.ds(patch, 1), batch, :] * widening.astype(F32)
        flat[blocks + i : blocks + i + 1, 0:per_patch] = noise
    return jnp.transpose(flat[...])[0:per_patch]


def column_of(upright, i, blocks):
    return upright[:, i : i + 1], upright[:, blocks + i : blocks + i + 1]


def scale_block(i, piece, sources, column, members, sh_ref, sl_ref, d_ref):
    value, noise = column
    rows = [sources[which][index] for which, index, _ in piece]
    total = sum(jnp.sum(part, axis=1, keepdims=True) for part in rows)
    mean = total * (1.0 / members)
    scale = lax.rsqrt(noise * (members - 1.0))
    per_patch = value.shape[0]
    at = slice(i * per_patch, (i + 1) * per_patch)
    for part, (_, _, start) in zip(rows, piece):
        size = part.shape[1]
        lanes = slice(start * size, (start + 1) * size)
        sh_ref[at, lanes], sl_ref[at, lanes] = split((part - mean) * scale)
    d_ref[at, :] = jnp.broadcast_to((value - mean) * scale, (per_patch, d_ref.shape[1]))


def prepare_kernel(pieces, batch, members, patches_of, places, crossing, *refs):
    place_refs, refs = refs[:places], refs[places:]
    near_ref, values_ref, var_ref, *refs = refs
    refs, (upright_ref, flat) = refs[:-2], refs[-2:]
    if crossing:
        (ah_ref, al_ref, *refs), cross_ref = refs[:-1], refs[-1]
    sources, (sh_ref, sl_ref, d_ref, g_ref) = refs[:-4], refs[-4:]
    patches, own = patches_of(*place_refs)
    upright = table(patches, own, near_ref, values_ref, var_ref, batch, flat)
    upright_ref[...] = upright
    for i, piece in enumerate(pieces):
        column = column_of(upright, i, len(patches))
        scale_block(i, piece, sources, column, members, sh_ref, sl_ref, d_ref)
    count = len(pieces) * values_ref.shape[2]
    s = (sh_ref[0:count], sl_ref[0:count])
    g_ref[0:count, 0:count] = dot3(s, s, NT)
    if crossing:
        cross_ref[0:count] = dot3(s, (ah_ref[...], al_ref[...]))


def factor_kernel(pieces, batch, members, chunk, patches_of, places, ready, crossing, *refs):
    if ready:
        upright_ref, *refs = refs
    else:
        place_refs, refs = refs[:places], refs[places:]
        near_ref, values_ref, var_ref, *refs = refs
    refs, (flat, eye_ref, x_ref, wa, wb) = refs[:-5], refs[-5:]
    if crossing:
        refs, cross_ref = refs[:-1], refs[-1]
    refs, (sh_ref, sl_ref, d_ref, g_ref, xh_ref, xl_ref, n_ref) = refs[:-7], refs[-7:]
    if crossing:
        refs, (ah_ref, al_ref) = refs[:-7], refs[-7:-5]
    elif ready:
        refs = refs[:-4]
    sources = refs
    blocks = len(pieces)
    if ready:
        upright = upright_ref[...]
    else:
        patches, own = patches_of(*place_refs)
        upright = table(patches, own, near_ref, values_ref, var_ref, batch, flat)
    per_patch = upright.shape[0]
    for i in range(ready, blocks):
        column = column_of(upright, i, blocks)
        scale_block(i, pieces[i], sources, column, members, sh_ref, sl_ref, d_ref)
    n = sh_ref.shape[0]
    head = min(TILE, n)
    tail = n - head
    chunks = [(i, min(i + chunk, n)) for i in range(0, n, chunk)]
    left = (sh_ref[0:head], sl_ref[0:head])
    fresh = ready * per_patch
    g_ref[fresh:n, 0:head] = dot3((sh_ref[fresh:n], sl_ref[fresh:n]), left, NT)
    if 0 < fresh < head:
        g_ref[0:fresh, fresh:head] = jnp.transpose(g_ref[fresh:head, 0:fresh])
    low = (sh_ref[head:n], sl_ref[head:n])
    g_ref[head:n, head:n] = dot3(low, low, NT)
    g_ref[0:head, head:n] = jnp.transpose(g_ref[head:n, 0:head])
    if crossing:
        cross_ref[fresh:n] = dot3((sh_ref[fresh:n], sl_ref[fresh:n]), (ah_ref[...], al_ref[...]))
    g = g_ref[...]
    square = jnp.sum(jnp.sum(g * g, axis=0, keepdims=True), axis=1, keepdims=True)
    norm = jnp.sqrt(square) * (1.0 + 1e-5)
    size = square[0, 0]
    limits = step_limits()
    pairs = jnp.int32(0)
    for k in range(7, MOST_STEPS - 2, 2):
        limit = limits[k] * (1.0 - 1e-4)
        pairs = pairs + (size > limit * limit).astype(jnp.int32)
    n_ref[0] = (size > 1.6e7).astype(jnp.int32) + (size > 1e8).astype(jnp.int32)
    eye_ref[...] = diagonal(n, n, 0).astype(F32)
    eye = eye_ref[...]
    first = 2.0 / (2.0 + norm)
    rho = norm * (0.5 * first)
    rho2 = rho * rho
    weight = 2.0 / (2.0 - rho2)
    keep = 0.5 * rho2 * weight
    x = (weight * first * (2.0 - first)) * eye - (weight * first * first) * g
    x_ref[...] = x
    for i, part in enumerate(split(x)):
        wa[i, :, n : 2 * n] = part

    def store(targets, start, left, corner):
        blocks = [(slice(0, n), slice(start, start + head), left)]
        blocks.append((slice(head, n), slice(start + head, start + n), corner))
        blocks.append((slice(0, head), slice(start + head, start + n), jnp.transpose(left[head:n])))
        for rows, columns, block in blocks:
            for target, part in zip(targets, split(block)):
                target[rows, columns] = part

    def corner_of(weight, keep, left, corner):
        left = weight * left - keep * eye_ref[:, 0:head]
        return left, weight * corner - keep * eye_ref[head:n, head:n]

    parts = split(g)
    square_left = dot3(parts, [part[:, 0:head] for part in parts])
    square_corner = dot3([part[head:n] for part in parts], [part[:, head:n] for part in parts])
    two = weight * first * first
    one = -2.0 * weight * first * (1.0 - first)
    none = weight * (1.0 - first) * (1.0 - first) - keep
    left = two * square_left + one * g[:, 0:head] + none * eye[:, 0:head]
    corner = two * square_corner + one * g[head:n, head:n] + none * eye[head:n, head:n]
    store((wa.at[0], wa.at[1]), 0, left, corner)

    def corners_of(source):
        ends = [jnp.concatenate([source[i, :, head:n], source[i, :, n + head : 2 * n]], axis=1) for i in (0, 1)]
        return dot3([source[i, head:n, 0:n] for i in (0, 1)], ends)

    def advance(source, target, rho2):
        weight = 2.0 / (2.0 - rho2)
        keep = 0.5 * rho2 * weight
        parts = (source[0, :, 0:n], source[1, :, 0:n])
        left = dot3(parts, (source[0, :, 0:head], source[1, :, 0:head]))
        corners = corners_of(source)
        both = (target.at[0], target.at[1])
        store(both, 0, *corner_of(weight, keep, left, corners[:, 0:tail]))
        left = dot3(parts, (source[0, :, n : n + head], source[1, :, n : n + head]))
        left = weight * (x_ref[:, 0:head] + left)
        corner = weight * (x_ref[head:n, head:n] + corners[:, tail : 2 * tail])
        x_ref[:, 0:head] = left
        x_ref[head:n, head:n] = corner
        store(both, n, left, corner)
        return keep * keep

    rho2 = keep * keep

    def sides(source, span):
        return [source[i, span[0] : span[1], 0:n] for i in (0, 1)]

    def put(targets, start, span, block):
        for target, part in zip(targets, split(block)):
            target[span[0] : span[1], start : start + head] = part
        low = max(span[0], head)
        if low < span[1]:
            for target, part in zip(targets, split(jnp.transpose(block[low - span[0] :]))):
                target[0:head, start + low : start + span[1]] = part

    def put_corner(targets, start, block):
        for target, part in zip(targets, split(block)):
            target[head:n, start + head : start + n] = part

    def put_x(targets, start, weight, span, product):
        x = weight * (x_ref[span[0] : span[1], 0:head] + product)
        x_ref[span[0] : span[1], 0:head] = x
        put(targets, start, span, x)

    def put_x_corner(targets, start, weight, product):
        x = weight * (x_ref[head:n, head:n] + product)
        x_ref[head:n, head:n] = x
        put_corner(targets, start, x)

    waiting = None
    source, target = wa, wb
    for _ in range(5):
        weight = 2.0 / (2.0 - rho2)
        keep = 0.5 * rho2 * weight
        first = (source[0, :, 0:head], source[1, :, 0:head])
        r = []
        for k, span in enumerate(chunks):
            r.append(dot3(sides(source, span), first))
            if waiting is not None:
                put_x((source.at[0], source.at[1]), n, waiting[0], span, waiting[1][k])
        if waiting is not None:
            put_x_corner((source.at[0], source.at[1]), n, waiting[0], waiting[2])
        corners = corners_of(source)
        first = (source[0, :, n : n + head], source[1, :, n : n + head])
        both = (target.at[0], target.at[1])
        x = []
        for k, span in enumerate(chunks):
            x.append(dot3(sides(source, span), first))
            put(both, 0, span, weight * r[k] - keep * eye_ref[span[0] : span[1], 0:head])
        put_corner(both, 0, weight * corners[:, 0:tail] - keep * eye_ref[head:n, head:n])
        waiting = (weight, x, corners[:, tail : 2 * tail])
        rho2 = keep * keep
        source, target = target, source
    for k, span in enumerate(chunks):
        put_x((source.at[0], source.at[1]), n, waiting[0], span, waiting[1][k])
    put_x_corner((source.at[0], source.at[1]), n, waiting[0], waiting[2])

    def twice(_, rho2):
        return advance(target, source, advance(source, target, rho2))

    rho2 = lax.fori_loop(0, pairs, twice, rho2)
    weight = 2.0 / (2.0 - rho2)
    first = (source[0, :, n : n + head], source[1, :, n : n + head])
    done = (xh_ref, xl_ref)
    ends = [source[i, :, n + head : 2 * n] for i in (0, 1)]
    put_x_corner(done, 0, weight, dot3(sides(source, (head, n)), ends))
    x = [dot3(sides(source, span), first) for span in chunks]
    for k, span in enumerate(chunks):
        put_x(done, 0, weight, span, x[k])


def centred(fields):
    members = sum(field.shape[0] for field in fields)
    mean = sum(jnp.sum(field, axis=0, keepdims=True) for field in fields) * (1.0 / members)
    pairs = [split(field - mean) for field in fields]
    return [jnp.concatenate(parts, axis=0) for parts in zip(*pairs)], mean


def in_chunks(count, product, work):
    waiting = None
    for start in range(0, count, CHUNK):
        span = slice(start, min(start + CHUNK, count))
        result = product(span)
        if waiting is not None:
            work(*waiting)
        waiting = (span, result)
    work(*waiting)


def solve(n_ref, s, g_ref, x, anomaly, z_ref, cross_ref, parts_ref, crossed_already=False, between=()):
    n = z_ref.shape[0]

    def keep(slot, span, value):
        for i, part in enumerate(split(value)):
            parts_ref[slot, i, span] = part

    def kept(slot):
        return parts_ref[slot, 0], parts_ref[slot, 1]

    def some(parts, span):
        return [part[span] for part in parts]

    def crossed(span, value):
        cross_ref[span] = value
        keep(0, span, value)

    def solved(span, value):
        z_ref[span] = value
        keep(1, span, value)

    def left(span, value):
        keep(0, span, cross_ref[span] - z_ref[span] - value)

    def refined(span, value):
        z_ref[span] = z_ref[span] + value

    if crossed_already:
        keep(0, slice(0, n), cross_ref[...])
    else:
        in_chunks(n, lambda span: dot3(some(s, span), [part[...] for part in anomaly]), crossed)
    stages = [
        (lambda span: dot3(some(x, span), kept(0)), solved),
        (lambda span: dot3(split(g_ref[span]), kept(1)), left),
        (lambda span: dot3(some(x, span), kept(0)), refined),
    ]
    for i, (product, work) in enumerate(stages):
        for extra in between[i : i + 1]:
            extra()
        in_chunks(n, product, work)

    def refine(_, carry):
        z = z_ref[...]
        gz = lax.dot_general(g_ref[...], z, NN, precision=HIGHEST, preferred_element_type=F32)
        z_ref[...] = z + dot3([part[...] for part in x], split(cross_ref[...] - z - gz))
        return carry

    lax.fori_loop(0, n_ref[0], refine, 0)


def gain_kernel(batch, parts, own_of, region_ref, column_ref, n_ref, cells_ref, sh_ref, sl_ref, d_ref, g_ref, *refs):
    xh_ref, xl_ref, *refs = refs
    states = refs[:parts]
    z_ref, rows_ref, scratch, anomaly_ref, cross_ref, parts_ref = refs[parts:]
    anomaly, mean = centred([state[...] for state in states])
    for i, part in enumerate(anomaly):
        anomaly_ref[i] = part
    anomaly = (anomaly_ref.at[0], anomaly_ref.at[1])
    picks = cells_ref[pl.ds(own_of(region_ref, column_ref), 1), batch, :]
    hot = selector(picks, mean.shape[1], scratch)
    base = jnp.sum(hot * mean, axis=1, keepdims=True)
    members = anomaly_ref.shape[1]
    count = 3
    size = -(-members // (count * 128)) * 128

    def pick(start, stop):
        picked = select(hot, [part[start:stop] for part in anomaly], NT)
        rows_ref[:, start:stop] = base + picked

    between = [
        functools.partial(pick, i * size, min((i + 1) * size, members)) for i in range(count)
    ]
    x = (xh_ref, xl_ref)
    solve(n_ref, (sh_ref, sl_ref), g_ref, x, anomaly, z_ref, cross_ref, parts_ref, False, between)
    zt = split(select(hot, split(z_ref[...]), NT))
    shift = dot3(zt, split(d_ref[...]))[:, 0:1]
    rows_ref[...] = rows_ref[...] + shift - 0.5 * dot3(zt, (sh_ref[...], sl_ref[...]))


def updated(field, start, s, shift, z):
    size = field.shape[0]
    return field + shift - 0.5 * dot3([h[:, start : start + size] for h in s], z, TN)


def shift_of(z, d_ref):
    return jnp.sum(z * d_ref[:, 0:1], axis=0, keepdims=True)


def update_kernel(starts, sh_ref, sl_ref, d_ref, z_ref, *refs):
    count = len(starts)
    states, outs, parts = refs[:count], refs[count : 2 * count], refs[2 * count :]
    z = z_ref[...]
    shift = shift_of(z, d_ref)
    s, zs = (sh_ref[...], sl_ref[...]), split(z)
    for start, state, out in zip(starts, states, outs):
        out[...] = updated(state[...], start, s, shift, zs)
    if parts:
        anomaly, _ = centred([out[...] for out in outs])
        for ref, part in zip(parts, anomaly):
            ref[...] = part


def last_kernel(given, n_ref, sh_ref, sl_ref, d_ref, g_ref, xh_ref, xl_ref, state_ref, *refs):
    refs, (cross_ref, parts_ref) = refs[:-2], refs[-2:]
    if given:
        cross_ref, *refs = refs
    z_ref, *out_refs = refs
    anomaly = None if given else centred([state_ref[...]])[0]
    x = (xh_ref, xl_ref)
    solve(n_ref, (sh_ref, sl_ref), g_ref, x, anomaly, z_ref, cross_ref, parts_ref, given)
    z = z_ref[...]
    shift, zs = shift_of(z, d_ref), split(z)
    start = sh_ref.shape[1] - state_ref.shape[0]
    s = (sh_ref[...], sl_ref[...])
    count = out_refs[0].shape[0]
    for i, out_ref in enumerate(out_refs):
        out_ref[...] = updated(state_ref[i * count : (i + 1) * count], start + i * count, s, shift, zs)


def join_kernel(first, column_ref, mine_ref, theirs_ref, *refs):
    out_ref, both, sems = refs[-3:]
    chunks = sems.shape[0]
    size = both.shape[0] // chunks
    column = column_ref[0]
    copies = []
    for i in range(chunks):
        at = slice(i * size, (i + 1) * size)
        mine, theirs = mine_ref[first + i * size : first + (i + 1) * size, :], theirs_ref[at, :]
        both[at, 0, :] = jnp.where(column == 0, mine, theirs)
        both[at, 1, :] = jnp.where(column == 0, theirs, mine)
        target = out_ref.at[pl.ds(first + i * size, size)]
        copies.append(pltpu.make_async_copy(both.at[pl.ds(i * size, size)], target, sems.at[i]))
        copies[-1].start()
    for copy in copies:
        copy.wait()


def prepare(pieces, batch, members, patches_of, place, near, values, var, anomaly, sources, n):
    width = anomaly[0].shape[1] if anomaly else 0
    outs = [
        ((n, members), BF16, VMEM),
        ((n, members), BF16, VMEM),
        ((n, 128), F32, VMEM),
        ((n, n), F32, VMEM),
    ]
    if anomaly:
        outs.append(((n, width), F32, VMEM))
    outs.append(((values.shape[2], 128), F32, VMEM))
    kernel = functools.partial(
        prepare_kernel, pieces, batch, members, patches_of, len(place), bool(anomaly)
    )
    args = [*place, near, values, var, *anomaly, *sources]
    ins = [SMEM] * (len(place) + 1) + [VMEM] * (len(args) - len(place) - 1)
    return call(kernel, outs, ins, args, [pltpu.VMEM((128, 128), F32)], 6 * n * (width + n // 3) * members)


def factor(pieces, batch, members, chunk, patches_of, place, near, values, var, sources, ready=0, before=()):
    per_patch = values.shape[2]
    n = len(pieces) * per_patch
    outs = [
        ((n, members), BF16, VMEM),
        ((n, members), BF16, VMEM),
        ((n, 128), F32, VMEM),
        ((n, n), F32, VMEM),
        ((n, n), BF16, VMEM),
        ((n, n), BF16, VMEM),
        ((1,), jnp.int32, SMEM),
    ]
    if ready:
        *before, upright = before
        args = [upright, *sources, *before]
        ins = [VMEM] * len(args)
    else:
        args = [*place, near, values, var, *sources]
        ins = [SMEM] * (len(place) + 1) + [VMEM] * (2 + len(sources))
    aliases = {}
    crossing = len(before) > 4
    if crossing:
        outs.append((before[-1].shape, F32, VMEM))
    if ready:
        first = len(args) - 4 - crossing
        aliases = {first: 0, first + 1: 1, first + 2: 2, first + 3: 3}
        if crossing:
            aliases[first + 4] = 7
    scratch = [
        pltpu.VMEM((128, 128), F32),
        pltpu.VMEM((n, n), F32),
        pltpu.VMEM((n, n), F32),
        pltpu.VMEM((2, n, 2 * n), BF16),
        pltpu.VMEM((2, n, 2 * n), BF16),
    ]
    kernel = functools.partial(
        factor_kernel, pieces, batch, members, chunk, patches_of, len(place), ready, crossing
    )
    flops = 6 * n * n * members + 60 * n * n * n
    return call(kernel, outs, ins, args, scratch, flops, FACTOR_LIMIT, aliases)


def solver_scratch(n, width):
    return [pltpu.VMEM((n, width), F32), pltpu.VMEM((2, 2, n, width), BF16)]


def gain(batch, own_of, place, cells, factored, states):
    sh, sl, d, g, xh, xl, more = factored[:7]
    n, members = sh.shape
    width = states[0].shape[1]
    kernel = functools.partial(gain_kernel, batch, len(states), own_of)
    outs = [((n, width), F32, VMEM), ((cells.shape[2], members), F32, VMEM)]
    ins = [SMEM] * 3 + [VMEM] * (7 + len(states))
    args = [*place, more, cells, sh, sl, d, g, xh, xl, *states]
    flops = 8 * n * members * width
    scratch = [pltpu.VMEM((8, 128), jnp.int32), pltpu.VMEM((2, members, width), BF16)]
    scratch += solver_scratch(n, width)
    return call(kernel, outs, ins, args, scratch, flops)


def update(factored, z, states, starts, more=False):
    sh, sl, d = factored[:3]
    kernel = functools.partial(update_kernel, starts)
    outs = [(state.shape, F32, VMEM) for state in states]
    if more:
        outs += [((sh.shape[1], z.shape[1]), BF16, VMEM)] * 2
    flops = 6 * sh.shape[0] * sh.shape[1] * z.shape[1]
    return call(kernel, outs, [VMEM] * (4 + len(states)), [sh, sl, d, z, *states], (), flops)


def last(factored, state, parts=1):
    sh, sl, d, g, xh, xl, more, *cross = factored
    n, width = sh.shape[0], state.shape[1]
    outs = [((n, width), F32, VMEM)] + [((state.shape[0] // parts, width), F32, VMEM)] * parts
    args = [more, sh, sl, d, g, xh, xl, state, *cross]
    flops = 12 * sh.shape[0] * sh.shape[1] * width
    ins = [SMEM] + [VMEM] * (len(args) - 1)
    kernel = functools.partial(last_kernel, bool(cross))
    return call(kernel, outs, ins, args, solver_scratch(n, width), flops)


def rings(size):
    up = [(i, (i + 1) % size) for i in range(size)]
    return up, [(j, i) for i, j in up]


BOTH = ("region", "member")


def permute(x, moves, regions):
    table = []
    for region in range(regions):
        for column in range(2):
            pair, parity, to = moves(region // 2, region % 2, column)
            pair %= regions // 2
            table.append((region * 2 + column, (pair * 2 + parity) * 2 + to))
    return lax.ppermute(x, BOTH, table)


def paired(state, neighbours, obs_cell, obs_values, obs_var):
    half, _, cells = state.shape
    members = 2 * half
    regions = lax.axis_size("region")
    region, column = lax.axis_index("region"), lax.axis_index("member")
    place = (region.astype(jnp.int32)[None], column.astype(jnp.int32)[None])
    near = neighbours.T

    def own_of(region_ref, column_ref):
        return region_ref[0] * 2 + column_ref[0]

    def around(region):
        side = 2 * lax.rem(region, 2) - 1
        return region, region - side, lax.rem(region + regions + side, regions)

    def patches_first(region_ref, column_ref):
        return [r * 2 + p for r in around(region_ref[0]) for p in (0, 1)], own_of(region_ref, column_ref)

    def patches_next(region_ref, column_ref):
        column = column_ref[0]
        within = (column, 1 - column)
        return [r * 2 + p for p in within for r in around(region_ref[0])], own_of(region_ref, column_ref)

    def across(x):
        return permute(x, lambda c, q, m: (c, q, 1 - m), regions)

    def beside(x):
        return permute(x, lambda c, q, m: (c, 1 - q, m), regions)

    def outside(x):
        return permute(x, lambda c, q, m: (c + 2 * q - 1, 1 - q, m), regions)

    anywhere = pl.BlockSpec(memory_space=pl.ANY)
    shape = ((half, cells), F32, VMEM)
    keep, send = call(sort_kernel, [shape] * 2, [SMEM, VMEM], [place[1], state])
    (rows,) = call(
        pick_kernel,
        [((2, obs_cell.shape[2], half), F32, VMEM)],
        [SMEM, SMEM, VMEM, VMEM, VMEM],
        [*place, obs_cell, keep, send],
        [pltpu.VMEM((8, 128), jnp.int32)],
    )
    other = across(rows)
    sources = [rows, beside(rows), outside(rows), other, beside(other), outside(other)]
    send, values, var = call(
        gate_kernel,
        [((half, cells), F32, anywhere), (obs_values.shape, F32, VMEM), (obs_var.shape, F32, VMEM)],
        [anywhere] * 4,
        [obs_values, obs_var, send, other],
        [pltpu.SemaphoreType.DMA((2,))],
        aliases={2: 0},
    )
    pieces = [[(i, (p,), 0), (3 + i, (p,), 1)] for i in range(3) for p in range(2)]
    states = [keep, across(send)]
    given = (place, near, values, var)
    n = len(pieces) * obs_cell.shape[2]
    early = [[(0, (p,), 0), (1, (p,), 1)] for p in range(2)]
    done = prepare(early, 0, members, patches_first, *given, (), [rows, other], n)
    factored = factor(pieces, 0, members, CHUNK, patches_first, *given, sources, 2, done)
    everything = slice(None)
    low, high = (everything, slice(0, half)), (everything, slice(half, members))
    pieces = [[(i, low, 0), (i, high, 1)] for i in range(3)]
    pieces += [[(i, high, 0), (i, low, 1)] for i in range(3, 6)]
    early = 4
    for batch in range(1, NBATCH):
        z, rows = gain(batch, own_of, place, obs_cell, factored, states)
        other = across(rows)
        far = permute(rows, lambda c, q, m: (c + 2 * q - 1, 1 - q, 1 - m), regions)
        sources = [rows, beside(rows), outside(rows), other, beside(other), far]
        mine, theirs, *anomaly = update(factored, z, states, (0, half), True)
        states = [mine, theirs]
        done = prepare(pieces[:early], batch, members, patches_next, *given, anomaly, sources[:early], n)
        factored = factor(
            pieces, batch, members, CHUNK, patches_next, *given, sources, early, [*anomaly, *done]
        )
    z, *theirs = last(factored, states[1], 2)
    theirs = [across(part) for part in theirs]
    (mine,) = update(factored, z, states[:1], (0,))
    joined = []
    for part, other in enumerate(theirs):
        count = other.shape[0]
        (out,) = call(
            functools.partial(join_kernel, part * count),
            [(state.shape, F32, anywhere)],
            [SMEM, VMEM, VMEM] + [anywhere] * len(joined),
            [place[1], mine, other, *joined],
            [pltpu.VMEM((count, *state.shape[1:]), F32), pltpu.SemaphoreType.DMA((2,))],
            aliases={3: 0} if joined else {},
        )
        joined = [out]
    return out


def listed(table_ref):
    blocks = table_ref.shape[0] - 1
    return [table_ref[i] for i in range(blocks)], table_ref[blocks]


def general(state, neighbours, obs_cell, obs_values, obs_var):
    ensemble = lax.all_to_all(state, "member", split_axis=1, concat_axis=0, tiled=True)
    members, owned, cells = ensemble.shape
    regions = lax.axis_size("region")
    region_patches = owned * lax.axis_size("member")
    region = lax.axis_index("region")
    first = region * region_patches + lax.axis_index("member") * owned
    up, down = rings(regions)
    fields = [ensemble[:, p, :] for p in range(owned)]
    grid = jnp.arange(cells, dtype=jnp.int32)
    for batch in range(NBATCH):
        picks = lax.dynamic_slice_in_dim(obs_cell, first, owned, 0)[:, batch, :]
        hot = (picks[:, :, None] == grid[None, None, :]).astype(F32)
        own_rows = jnp.einsum("poc,pkc->pok", hot, jnp.stack(fields), precision=HIGHEST)
        region_rows = lax.all_gather(own_rows, "member", axis=0, tiled=True)
        before = lax.ppermute(region_rows, "region", up)
        after = lax.ppermute(region_rows, "region", down)
        beside = jnp.concatenate([before, region_rows, after], axis=0)
        new = []
        for p in range(owned):
            own = first + p
            links = lax.dynamic_index_in_dim(neighbours, own, 0, keepdims=False)
            ids = jnp.concatenate([own[None], links]).astype(jnp.int32)
            table = jnp.concatenate([ids, own[None]]).astype(jnp.int32)
            home = (ids // region_patches - region + 1) % regions
            rows = jnp.take(beside, home * region_patches + ids % region_patches, axis=0)
            pieces = [[(0, (i,), 0)] for i in range(ids.shape[0])]
            factored = factor(
                pieces, batch, members, CHUNK, listed, [table], neighbours.T, obs_values, obs_var, [rows]
            )
            new.append(last(factored, fields[p])[1])
        fields = new
    ensemble = jnp.stack(fields, axis=1)
    return lax.all_to_all(ensemble, "member", split_axis=0, concat_axis=1, tiled=True)


def on_device(state, neighbours, obs_cell, obs_values, obs_var):
    patches, links = state.shape[1], neighbours.shape[1]
    even = lax.axis_size("region") % 2 == 0
    if even and patches == 2 and lax.axis_size("member") == 2 and links + 1 == 3 * patches:
        return paired(state, neighbours, obs_cell, obs_values, obs_var)
    return general(state, neighbours, obs_cell, obs_values, obs_var)


def solution(mesh):
    in_specs = (P("member", "region", None), P(), P(), P(), P())
    out_specs = P("member", "region", None)
    return jax.shard_map(
        on_device, mesh=mesh, in_specs=in_specs, out_specs=out_specs, check_vma=False
    )
```

```python
import functools
import math

import jax
import jax.numpy as jnp
from jax import lax
from jax.experimental import pallas as pl
from jax.experimental.pallas import tpu as pltpu
from jax.sharding import PartitionSpec as P

NBATCH = 2
HIGHEST = lax.Precision.HIGHEST
F32 = jnp.float32
BF16 = jnp.bfloat16
VMEM = pl.BlockSpec(memory_space=pltpu.VMEM)
SMEM = pl.BlockSpec(memory_space=pltpu.SMEM)
NN = (((1,), (0,)), ((), ()))
NT = (((1,), (1,)), ((), ()))
TN = (((0,), (0,)), ((), ()))
RESIDUAL = 1e-3
FACTOR_LIMIT = 24
MOST_STEPS = 15
TILE = 256
CHUNK = 128


def call(kernel, outs, ins, args, scratch=(), flops=0, limit=16, aliases=None):
    shapes = [jax.ShapeDtypeStruct(shape, dtype) for shape, dtype, _ in outs]
    moved = sum(math.prod(s.shape) * s.dtype.itemsize for s in shapes)
    moved += sum(a.size * a.dtype.itemsize for a in args)
    return pl.pallas_call(
        kernel,
        out_shape=shapes,
        in_specs=ins,
        out_specs=[space for _, _, space in outs],
        scratch_shapes=list(scratch),
        input_output_aliases=aliases or {},
        compiler_params=pltpu.CompilerParams(vmem_limit_bytes=limit * 1024 * 1024),
        cost_estimate=pl.CostEstimate(flops=flops, bytes_accessed=moved, transcendentals=0),
    )(*args)


def split(x):
    high = x.astype(BF16)
    return high, (x - high.astype(F32)).astype(BF16)


def dot(a, b, dims=NN):
    return lax.dot_general(a, b, dims, preferred_element_type=F32)


def dot3(a, b, dims=NN):
    (left,), (right,) = dims[0]
    lhs = jnp.concatenate([a[0], a[0], a[1]], axis=left)
    rhs = jnp.concatenate([b[0], b[1], b[0]], axis=right)
    return dot(lhs, rhs, dims)


def select(hot, parts, dims):
    (left,), (right,) = dims[0]
    hot = hot.astype(BF16)
    lhs = jnp.concatenate([hot] * len(parts), axis=left)
    return dot(lhs, jnp.concatenate(parts, axis=right), dims)


def split_all(x):
    high, middle = split(x)
    low = x - high.astype(F32) - middle.astype(F32)
    return high, middle, low.astype(BF16)


def step_limits():
    limits = []
    for steps in range(MOST_STEPS):
        rho = RESIDUAL
        for _ in range(steps):
            rho = math.sqrt(2.0 * rho / (1.0 + rho))
        limits.append(2.0 * rho / (1.0 - rho) if rho < 1.0 else math.inf)
    return limits


def diagonal(n, columns, first):
    row = lax.broadcasted_iota(jnp.int32, (n, columns), 0)
    column = lax.broadcasted_iota(jnp.int32, (n, columns), 1)
    return row + first == column


def selector(picks, cells, scratch):
    per_patch = picks.shape[1]
    scratch[...] = jnp.full_like(scratch, -1)
    scratch[0:1, 0:per_patch] = picks
    grid = lax.broadcasted_iota(jnp.int32, (cells, scratch.shape[1]), 0)
    hot = (grid == scratch[0:1, :]).astype(F32)
    return jnp.transpose(hot)[0:per_patch, :]


def sort_kernel(column_ref, state_ref, keep_ref, send_ref):
    column = column_ref[0]
    first, second = state_ref[:, 0, :], state_ref[:, 1, :]
    keep_ref[...] = jnp.where(column == 0, first, second)
    send_ref[...] = jnp.where(column == 0, second, first)


def pick_kernel(region_ref, column_ref, cells_ref, keep_ref, send_ref, rows_ref, scratch):
    column = column_ref[0]
    for patch, field_ref in ((column, keep_ref), (1 - column, send_ref)):
        picks = cells_ref[pl.ds(region_ref[0] * 2 + patch, 1), 0, :]
        hot = selector(picks, field_ref.shape[1], scratch)
        rows_ref[pl.ds(patch, 1)] = select(hot, split_all(field_ref[...]), NT)[None]


def gate_kernel(values_hbm, var_hbm, send_ref, after_ref, out_ref, values_ref, var_ref, sems):
    copies = [
        pltpu.make_async_copy(values_hbm, values_ref, sems.at[0]),
        pltpu.make_async_copy(var_hbm, var_ref, sems.at[1]),
    ]
    for copy in copies:
        copy.start()
    for copy in copies:
        copy.wait()


def table(patches, own, near_ref, values_ref, var_ref, batch, flat):
    per_patch = values_ref.shape[2]
    blocks = len(patches)
    flat[...] = jnp.ones_like(flat)
    for i, patch in enumerate(patches):
        widening = (patch == own).astype(jnp.int32)
        for j in range(near_ref.shape[0]):
            widening = widening + (near_ref[j, own] == patch).astype(jnp.int32) * (j + 2)
        flat[i : i + 1, 0:per_patch] = values_ref[pl.ds(patch, 1), batch, :]
        noise = var_ref[pl.ds(patch, 1), batch, :] * widening.astype(F32)
        flat[blocks + i : blocks + i + 1, 0:per_patch] = noise
    return jnp.transpose(flat[...])[0:per_patch]


def column_of(upright, i, blocks):
    return upright[:, i : i + 1], upright[:, blocks + i : blocks + i + 1]


def scale_block(i, piece, sources, column, members, sh_ref, sl_ref, d_ref):
    value, noise = column
    rows = [sources[which][index] for which, index, _ in piece]
    total = sum(jnp.sum(part, axis=1, keepdims=True) for part in rows)
    mean = total * (1.0 / members)
    scale = lax.rsqrt(noise * (members - 1.0))
    per_patch = value.shape[0]
    at = slice(i * per_patch, (i + 1) * per_patch)
    for part, (_, _, start) in zip(rows, piece):
        size = part.shape[1]
        lanes = slice(start * size, (start + 1) * size)
        sh_ref[at, lanes], sl_ref[at, lanes] = split((part - mean) * scale)
    d_ref[at, :] = jnp.broadcast_to((value - mean) * scale, (per_patch, d_ref.shape[1]))


def prepare_kernel(pieces, batch, members, patches_of, places, crossing, *refs):
    place_refs, refs = refs[:places], refs[places:]
    near_ref, values_ref, var_ref, *refs = refs
    refs, (upright_ref, flat) = refs[:-2], refs[-2:]
    if crossing:
        (ah_ref, al_ref, *refs), cross_ref = refs[:-1], refs[-1]
    sources, (sh_ref, sl_ref, d_ref, g_ref) = refs[:-4], refs[-4:]
    patches, own = patches_of(*place_refs)
    upright = table(patches, own, near_ref, values_ref, var_ref, batch, flat)
    upright_ref[...] = upright
    for i, piece in enumerate(pieces):
        column = column_of(upright, i, len(patches))
        scale_block(i, piece, sources, column, members, sh_ref, sl_ref, d_ref)
    count = len(pieces) * values_ref.shape[2]
    s = (sh_ref[0:count], sl_ref[0:count])
    g_ref[0:count, 0:count] = dot3(s, s, NT)
    if crossing:
        cross_ref[0:count] = dot3(s, (ah_ref[...], al_ref[...]))


def factor_kernel(pieces, batch, members, chunk, patches_of, places, ready, crossing, *refs):
    if ready:
        upright_ref, *refs = refs
    else:
        place_refs, refs = refs[:places], refs[places:]
        near_ref, values_ref, var_ref, *refs = refs
    refs, (flat, eye_ref, x_ref, wa, wb) = refs[:-5], refs[-5:]
    if crossing:
        refs, cross_ref = refs[:-1], refs[-1]
    refs, (sh_ref, sl_ref, d_ref, g_ref, xh_ref, xl_ref, n_ref) = refs[:-7], refs[-7:]
    if crossing:
        refs, (ah_ref, al_ref) = refs[:-7], refs[-7:-5]
    elif ready:
        refs = refs[:-4]
    sources = refs
    blocks = len(pieces)
    if ready:
        upright = upright_ref[...]
    else:
        patches, own = patches_of(*place_refs)
        upright = table(patches, own, near_ref, values_ref, var_ref, batch, flat)
    per_patch = upright.shape[0]
    for i in range(ready, blocks):
        column = column_of(upright, i, blocks)
        scale_block(i, pieces[i], sources, column, members, sh_ref, sl_ref, d_ref)
    n = sh_ref.shape[0]
    head = min(TILE, n)
    tail = n - head
    chunks = [(i, min(i + chunk, n)) for i in range(0, n, chunk)]
    left = (sh_ref[0:head], sl_ref[0:head])
    fresh = ready * per_patch
    g_ref[fresh:n, 0:head] = dot3((sh_ref[fresh:n], sl_ref[fresh:n]), left, NT)
    if 0 < fresh < head:
        g_ref[0:fresh, fresh:head] = jnp.transpose(g_ref[fresh:head, 0:fresh])
    low = (sh_ref[head:n], sl_ref[head:n])
    g_ref[head:n, head:n] = dot3(low, low, NT)
    g_ref[0:head, head:n] = jnp.transpose(g_ref[head:n, 0:head])
    if crossing:
        cross_ref[fresh:n] = dot3((sh_ref[fresh:n], sl_ref[fresh:n]), (ah_ref[...], al_ref[...]))
    g = g_ref[...]
    square = jnp.sum(jnp.sum(g * g, axis=0, keepdims=True), axis=1, keepdims=True)
    norm = jnp.sqrt(square) * (1.0 + 1e-5)
    size = square[0, 0]
    limits = step_limits()
    pairs = jnp.int32(0)
    for k in range(7, MOST_STEPS - 2, 2):
        limit = limits[k] * (1.0 - 1e-4)
        pairs = pairs + (size > limit * limit).astype(jnp.int32)
    n_ref[0] = (size > 1.6e7).astype(jnp.int32) + (size > 1e8).astype(jnp.int32)
    eye_ref[...] = diagonal(n, n, 0).astype(F32)
    eye = eye_ref[...]
    first = 2.0 / (2.0 + norm)
    rho = norm * (0.5 * first)
    rho2 = rho * rho
    weight = 2.0 / (2.0 - rho2)
    keep = 0.5 * rho2 * weight
    x = (weight * first * (2.0 - first)) * eye - (weight * first * first) * g
    x_ref[...] = x
    for i, part in enumerate(split(x)):
        wa[i, :, n : 2 * n] = part

    def store(targets, start, left, corner):
        blocks = [(slice(0, n), slice(start, start + head), left)]
        blocks.append((slice(head, n), slice(start + head, start + n), corner))
        blocks.append((slice(0, head), slice(start + head, start + n), jnp.transpose(left[head:n])))
        for rows, columns, block in blocks:
            for target, part in zip(targets, split(block)):
                target[rows, columns] = part

    def corner_of(weight, keep, left, corner):
        left = weight * left - keep * eye_ref[:, 0:head]
        return left, weight * corner - keep * eye_ref[head:n, head:n]

    parts = split(g)
    square_left = dot3(parts, [part[:, 0:head] for part in parts])
    square_corner = dot3([part[head:n] for part in parts], [part[:, head:n] for part in parts])
    two = weight * first * first
    one = -2.0 * weight * first * (1.0 - first)
    none = weight * (1.0 - first) * (1.0 - first) - keep
    left = two * square_left + one * g[:, 0:head] + none * eye[:, 0:head]
    corner = two * square_corner + one * g[head:n, head:n] + none * eye[head:n, head:n]
    store((wa.at[0], wa.at[1]), 0, left, corner)

    def corners_of(source):
        ends = [jnp.concatenate([source[i, :, head:n], source[i, :, n + head : 2 * n]], axis=1) for i in (0, 1)]
        return dot3([source[i, head:n, 0:n] for i in (0, 1)], ends)

    def advance(source, target, rho2):
        weight = 2.0 / (2.0 - rho2)
        keep = 0.5 * rho2 * weight
        parts = (source[0, :, 0:n], source[1, :, 0:n])
        left = dot3(parts, (source[0, :, 0:head], source[1, :, 0:head]))
        corners = corners_of(source)
        both = (target.at[0], target.at[1])
        store(both, 0, *corner_of(weight, keep, left, corners[:, 0:tail]))
        left = dot3(parts, (source[0, :, n : n + head], source[1, :, n : n + head]))
        left = weight * (x_ref[:, 0:head] + left)
        corner = weight * (x_ref[head:n, head:n] + corners[:, tail : 2 * tail])
        x_ref[:, 0:head] = left
        x_ref[head:n, head:n] = corner
        store(both, n, left, corner)
        return keep * keep

    rho2 = keep * keep

    def sides(source, span):
        return [source[i, span[0] : span[1], 0:n] for i in (0, 1)]

    def put(targets, start, span, block):
        for target, part in zip(targets, split(block)):
            target[span[0] : span[1], start : start + head] = part
        low = max(span[0], head)
        if low < span[1]:
            for target, part in zip(targets, split(jnp.transpose(block[low - span[0] :]))):
                target[0:head, start + low : start + span[1]] = part

    def put_corner(targets, start, block):
        for target, part in zip(targets, split(block)):
            target[head:n, start + head : start + n] = part

    def put_x(targets, start, weight, span, product):
        x = weight * (x_ref[span[0] : span[1], 0:head] + product)
        x_ref[span[0] : span[1], 0:head] = x
        put(targets, start, span, x)

    def put_x_corner(targets, start, weight, product):
        x = weight * (x_ref[head:n, head:n] + product)
        x_ref[head:n, head:n] = x
        put_corner(targets, start, x)

    waiting = None
    source, target = wa, wb
    for _ in range(5):
        weight = 2.0 / (2.0 - rho2)
        keep = 0.5 * rho2 * weight
        first = (source[0, :, 0:head], source[1, :, 0:head])
        r = []
        for k, span in enumerate(chunks):
            r.append(dot3(sides(source, span), first))
            if waiting is not None:
                put_x((source.at[0], source.at[1]), n, waiting[0], span, waiting[1][k])
        if waiting is not None:
            put_x_corner((source.at[0], source.at[1]), n, waiting[0], waiting[2])
        corners = corners_of(source)
        first = (source[0, :, n : n + head], source[1, :, n : n + head])
        both = (target.at[0], target.at[1])
        x = []
        for k, span in enumerate(chunks):
            x.append(dot3(sides(source, span), first))
            put(both, 0, span, weight * r[k] - keep * eye_ref[span[0] : span[1], 0:head])
        put_corner(both, 0, weight * corners[:, 0:tail] - keep * eye_ref[head:n, head:n])
        waiting = (weight, x, corners[:, tail : 2 * tail])
        rho2 = keep * keep
        source, target = target, source
    for k, span in enumerate(chunks):
        put_x((source.at[0], source.at[1]), n, waiting[0], span, waiting[1][k])
    put_x_corner((source.at[0], source.at[1]), n, waiting[0], waiting[2])

    def twice(_, rho2):
        return advance(target, source, advance(source, target, rho2))

    rho2 = lax.fori_loop(0, pairs, twice, rho2)
    weight = 2.0 / (2.0 - rho2)
    first = (source[0, :, n : n + head], source[1, :, n : n + head])
    done = (xh_ref, xl_ref)
    ends = [source[i, :, n + head : 2 * n] for i in (0, 1)]
    put_x_corner(done, 0, weight, dot3(sides(source, (head, n)), ends))
    x = [dot3(sides(source, span), first) for span in chunks]
    for k, span in enumerate(chunks):
        put_x(done, 0, weight, span, x[k])


def centred(fields):
    members = sum(field.shape[0] for field in fields)
    mean = sum(jnp.sum(field, axis=0, keepdims=True) for field in fields) * (1.0 / members)
    pairs = [split(field - mean) for field in fields]
    return [jnp.concatenate(parts, axis=0) for parts in zip(*pairs)], mean


def in_chunks(count, product, work):
    waiting = None
    for start in range(0, count, CHUNK):
        span = slice(start, min(start + CHUNK, count))
        result = product(span)
        if waiting is not None:
            work(*waiting)
        waiting = (span, result)
    work(*waiting)


def solve(n_ref, s, g_ref, x, anomaly, z_ref, cross_ref, parts_ref, crossed_already=False, between=()):
    n = z_ref.shape[0]

    def keep(slot, span, value):
        for i, part in enumerate(split(value)):
            parts_ref[slot, i, span] = part

    def kept(slot):
        return parts_ref[slot, 0], parts_ref[slot, 1]

    def some(parts, span):
        return [part[span] for part in parts]

    def crossed(span, value):
        cross_ref[span] = value
        keep(0, span, value)

    def solved(span, value):
        z_ref[span] = value
        keep(1, span, value)

    def left(span, value):
        keep(0, span, cross_ref[span] - z_ref[span] - value)

    def refined(span, value):
        z_ref[span] = z_ref[span] + value

    if crossed_already:
        keep(0, slice(0, n), cross_ref[...])
    else:
        in_chunks(n, lambda span: dot3(some(s, span), [part[...] for part in anomaly]), crossed)
    stages = [
        (lambda span: dot3(some(x, span), kept(0)), solved),
        (lambda span: dot3(split(g_ref[span]), kept(1)), left),
        (lambda span: dot3(some(x, span), kept(0)), refined),
    ]
    for i, (product, work) in enumerate(stages):
        for extra in between[i : i + 1]:
            extra()
        in_chunks(n, product, work)

    def refine(_, carry):
        z = z_ref[...]
        gz = lax.dot_general(g_ref[...], z, NN, precision=HIGHEST, preferred_element_type=F32)
        z_ref[...] = z + dot3([part[...] for part in x], split(cross_ref[...] - z - gz))
        return carry

    lax.fori_loop(0, n_ref[0], refine, 0)


def gain_kernel(batch, parts, own_of, region_ref, column_ref, n_ref, cells_ref, sh_ref, sl_ref, d_ref, g_ref, *refs):
    xh_ref, xl_ref, *refs = refs
    states = refs[:parts]
    z_ref, rows_ref, scratch, anomaly_ref, cross_ref, parts_ref = refs[parts:]
    anomaly, mean = centred([state[...] for state in states])
    for i, part in enumerate(anomaly):
        anomaly_ref[i] = part
    anomaly = (anomaly_ref.at[0], anomaly_ref.at[1])
    picks = cells_ref[pl.ds(own_of(region_ref, column_ref), 1), batch, :]
    hot = selector(picks, mean.shape[1], scratch)
    base = jnp.sum(hot * mean, axis=1, keepdims=True)
    members = anomaly_ref.shape[1]
    count = 3
    size = -(-members // (count * 128)) * 128

    def pick(start, stop):
        picked = select(hot, [part[start:stop] for part in anomaly], NT)
        rows_ref[:, start:stop] = base + picked

    between = [
        functools.partial(pick, i * size, min((i + 1) * size, members)) for i in range(count)
    ]
    x = (xh_ref, xl_ref)
    solve(n_ref, (sh_ref, sl_ref), g_ref, x, anomaly, z_ref, cross_ref, parts_ref, False, between)
    zt = split(select(hot, split(z_ref[...]), NT))
    shift = dot3(zt, split(d_ref[...]))[:, 0:1]
    rows_ref[...] = rows_ref[...] + shift - 0.5 * dot3(zt, (sh_ref[...], sl_ref[...]))


def updated(field, start, s, shift, z):
    size = field.shape[0]
    return field + shift - 0.5 * dot3([h[:, start : start + size] for h in s], z, TN)


def shift_of(z, d_ref):
    return jnp.sum(z * d_ref[:, 0:1], axis=0, keepdims=True)


def update_kernel(starts, sh_ref, sl_ref, d_ref, z_ref, *refs):
    count = len(starts)
    states, outs, parts = refs[:count], refs[count : 2 * count], refs[2 * count :]
    z = z_ref[...]
    shift = shift_of(z, d_ref)
    s, zs = (sh_ref[...], sl_ref[...]), split(z)
    for start, state, out in zip(starts, states, outs):
        out[...] = updated(state[...], start, s, shift, zs)
    if parts:
        anomaly, _ = centred([out[...] for out in outs])
        for ref, part in zip(parts, anomaly):
            ref[...] = part


def last_kernel(given, n_ref, sh_ref, sl_ref, d_ref, g_ref, xh_ref, xl_ref, state_ref, *refs):
    refs, (cross_ref, parts_ref) = refs[:-2], refs[-2:]
    if given:
        cross_ref, *refs = refs
    z_ref, *out_refs = refs
    anomaly = None if given else centred([state_ref[...]])[0]
    x = (xh_ref, xl_ref)
    solve(n_ref, (sh_ref, sl_ref), g_ref, x, anomaly, z_ref, cross_ref, parts_ref, given)
    z = z_ref[...]
    shift, zs = shift_of(z, d_ref), split(z)
    start = sh_ref.shape[1] - state_ref.shape[0]
    s = (sh_ref[...], sl_ref[...])
    count = out_refs[0].shape[0]
    for i, out_ref in enumerate(out_refs):
        out_ref[...] = updated(state_ref[i * count : (i + 1) * count], start + i * count, s, shift, zs)


def join_kernel(first, column_ref, mine_ref, theirs_ref, *refs):
    out_ref, both, sems = refs[-3:]
    chunks = sems.shape[0]
    size = both.shape[0] // chunks
    column = column_ref[0]
    copies = []
    for i in range(chunks):
        at = slice(i * size, (i + 1) * size)
        mine, theirs = mine_ref[first + i * size : first + (i + 1) * size, :], theirs_ref[at, :]
        both[at, 0, :] = jnp.where(column == 0, mine, theirs)
        both[at, 1, :] = jnp.where(column == 0, theirs, mine)
        target = out_ref.at[pl.ds(first + i * size, size)]
        copies.append(pltpu.make_async_copy(both.at[pl.ds(i * size, size)], target, sems.at[i]))
        copies[-1].start()
    for copy in copies:
        copy.wait()


def prepare(pieces, batch, members, patches_of, place, near, values, var, anomaly, sources, n):
    width = anomaly[0].shape[1] if anomaly else 0
    outs = [
        ((n, members), BF16, VMEM),
        ((n, members), BF16, VMEM),
        ((n, 128), F32, VMEM),
        ((n, n), F32, VMEM),
    ]
    if anomaly:
        outs.append(((n, width), F32, VMEM))
    outs.append(((values.shape[2], 128), F32, VMEM))
    kernel = functools.partial(
        prepare_kernel, pieces, batch, members, patches_of, len(place), bool(anomaly)
    )
    args = [*place, near, values, var, *anomaly, *sources]
    ins = [SMEM] * (len(place) + 1) + [VMEM] * (len(args) - len(place) - 1)
    return call(kernel, outs, ins, args, [pltpu.VMEM((128, 128), F32)], 6 * n * (width + n // 3) * members)


def factor(pieces, batch, members, chunk, patches_of, place, near, values, var, sources, ready=0, before=()):
    per_patch = values.shape[2]
    n = len(pieces) * per_patch
    outs = [
        ((n, members), BF16, VMEM),
        ((n, members), BF16, VMEM),
        ((n, 128), F32, VMEM),
        ((n, n), F32, VMEM),
        ((n, n), BF16, VMEM),
        ((n, n), BF16, VMEM),
        ((1,), jnp.int32, SMEM),
    ]
    if ready:
        *before, upright = before
        args = [upright, *sources, *before]
        ins = [VMEM] * len(args)
    else:
        args = [*place, near, values, var, *sources]
        ins = [SMEM] * (len(place) + 1) + [VMEM] * (2 + len(sources))
    aliases = {}
    crossing = len(before) > 4
    if crossing:
        outs.append((before[-1].shape, F32, VMEM))
    if ready:
        first = len(args) - 4 - crossing
        aliases = {first: 0, first + 1: 1, first + 2: 2, first + 3: 3}
        if crossing:
            aliases[first + 4] = 7
    scratch = [
        pltpu.VMEM((128, 128), F32),
        pltpu.VMEM((n, n), F32),
        pltpu.VMEM((n, n), F32),
        pltpu.VMEM((2, n, 2 * n), BF16),
        pltpu.VMEM((2, n, 2 * n), BF16),
    ]
    kernel = functools.partial(
        factor_kernel, pieces, batch, members, chunk, patches_of, len(place), ready, crossing
    )
    flops = 6 * n * n * members + (30 if crossing else 20) * n * n * n
    return call(kernel, outs, ins, args, scratch, flops, FACTOR_LIMIT, aliases)


def solver_scratch(n, width):
    return [pltpu.VMEM((n, width), F32), pltpu.VMEM((2, 2, n, width), BF16)]


def gain(batch, own_of, place, cells, factored, states):
    sh, sl, d, g, xh, xl, more = factored[:7]
    n, members = sh.shape
    width = states[0].shape[1]
    kernel = functools.partial(gain_kernel, batch, len(states), own_of)
    outs = [((n, width), F32, VMEM), ((cells.shape[2], members), F32, VMEM)]
    ins = [SMEM] * 3 + [VMEM] * (7 + len(states))
    args = [*place, more, cells, sh, sl, d, g, xh, xl, *states]
    flops = 8 * n * members * width
    scratch = [pltpu.VMEM((8, 128), jnp.int32), pltpu.VMEM((2, members, width), BF16)]
    scratch += solver_scratch(n, width)
    return call(kernel, outs, ins, args, scratch, flops)


def update(factored, z, states, starts, more=False):
    sh, sl, d = factored[:3]
    kernel = functools.partial(update_kernel, starts)
    outs = [(state.shape, F32, VMEM) for state in states]
    if more:
        outs += [((sh.shape[1], z.shape[1]), BF16, VMEM)] * 2
    flops = 6 * sh.shape[0] * sh.shape[1] * z.shape[1]
    return call(kernel, outs, [VMEM] * (4 + len(states)), [sh, sl, d, z, *states], (), flops)


def last(factored, state, parts=1):
    sh, sl, d, g, xh, xl, more, *cross = factored
    n, width = sh.shape[0], state.shape[1]
    outs = [((n, width), F32, VMEM)] + [((state.shape[0] // parts, width), F32, VMEM)] * parts
    args = [more, sh, sl, d, g, xh, xl, state, *cross]
    flops = 12 * sh.shape[0] * sh.shape[1] * width
    ins = [SMEM] + [VMEM] * (len(args) - 1)
    kernel = functools.partial(last_kernel, bool(cross))
    return call(kernel, outs, ins, args, solver_scratch(n, width), flops)


def rings(size):
    up = [(i, (i + 1) % size) for i in range(size)]
    return up, [(j, i) for i, j in up]


BOTH = ("region", "member")


def permute(x, moves, regions):
    table = []
    for region in range(regions):
        for column in range(2):
            pair, parity, to = moves(region // 2, region % 2, column)
            pair %= regions // 2
            table.append((region * 2 + column, (pair * 2 + parity) * 2 + to))
    return lax.ppermute(x, BOTH, table)


def paired(state, neighbours, obs_cell, obs_values, obs_var):
    half, _, cells = state.shape
    members = 2 * half
    regions = lax.axis_size("region")
    region, column = lax.axis_index("region"), lax.axis_index("member")
    place = (region.astype(jnp.int32)[None], column.astype(jnp.int32)[None])
    near = neighbours.T

    def own_of(region_ref, column_ref):
        return region_ref[0] * 2 + column_ref[0]

    def around(region):
        side = 2 * lax.rem(region, 2) - 1
        return region, region - side, lax.rem(region + regions + side, regions)

    def patches_first(region_ref, column_ref):
        return [r * 2 + p for r in around(region_ref[0]) for p in (0, 1)], own_of(region_ref, column_ref)

    def patches_next(region_ref, column_ref):
        column = column_ref[0]
        within = (column, 1 - column)
        return [r * 2 + p for p in within for r in around(region_ref[0])], own_of(region_ref, column_ref)

    def across(x):
        return permute(x, lambda c, q, m: (c, q, 1 - m), regions)

    def beside(x):
        return permute(x, lambda c, q, m: (c, 1 - q, m), regions)

    def outside(x):
        return permute(x, lambda c, q, m: (c + 2 * q - 1, 1 - q, m), regions)

    anywhere = pl.BlockSpec(memory_space=pl.ANY)
    shape = ((half, cells), F32, VMEM)
    keep, send = call(sort_kernel, [shape] * 2, [SMEM, VMEM], [place[1], state])
    (rows,) = call(
        pick_kernel,
        [((2, obs_cell.shape[2], half), F32, VMEM)],
        [SMEM, SMEM, VMEM, VMEM, VMEM],
        [*place, obs_cell, keep, send],
        [pltpu.VMEM((8, 128), jnp.int32)],
    )
    other = across(rows)
    sources = [rows, beside(rows), outside(rows), other, beside(other), outside(other)]
    send, values, var = call(
        gate_kernel,
        [((half, cells), F32, anywhere), (obs_values.shape, F32, VMEM), (obs_var.shape, F32, VMEM)],
        [anywhere] * 4,
        [obs_values, obs_var, send, rows],
        [pltpu.SemaphoreType.DMA((2,))],
        aliases={2: 0},
    )
    pieces = [[(i, (p,), 0), (3 + i, (p,), 1)] for i in range(3) for p in range(2)]
    states = [keep, across(send)]
    given = (place, near, values, var)
    n = len(pieces) * obs_cell.shape[2]
    early = [[(0, (p,), 0), (1, (p,), 1)] for p in range(2)]
    done = prepare(early, 0, members, patches_first, *given, (), [rows, other], n)
    factored = factor(pieces, 0, members, CHUNK, patches_first, *given, sources, 2, done)
    everything = slice(None)
    low, high = (everything, slice(0, half)), (everything, slice(half, members))
    pieces = [[(i, low, 0), (i, high, 1)] for i in range(3)]
    pieces += [[(i, high, 0), (i, low, 1)] for i in range(3, 6)]
    early = 4
    for batch in range(1, NBATCH):
        z, rows = gain(batch, own_of, place, obs_cell, factored, states)
        other = across(rows)
        far = permute(rows, lambda c, q, m: (c + 2 * q - 1, 1 - q, 1 - m), regions)
        sources = [rows, beside(rows), outside(rows), other, beside(other), far]
        mine, theirs, *anomaly = update(factored, z, states, (0, half), True)
        states = [mine, theirs]
        done = prepare(pieces[:early], batch, members, patches_next, *given, anomaly, sources[:early], n)
        factored = factor(
            pieces, batch, members, CHUNK, patches_next, *given, sources, early, [*anomaly, *done]
        )
    z, *theirs = last(factored, states[1], 2)
    theirs = [across(part) for part in theirs]
    (mine,) = update(factored, z, states[:1], (0,))
    joined = []
    for part, other in enumerate(theirs):
        count = other.shape[0]
        (out,) = call(
            functools.partial(join_kernel, part * count),
            [(state.shape, F32, anywhere)],
            [SMEM, VMEM, VMEM] + [anywhere] * len(joined),
            [place[1], mine, other, *joined],
            [pltpu.VMEM((count, *state.shape[1:]), F32), pltpu.SemaphoreType.DMA((2,))],
            aliases={3: 0} if joined else {},
        )
        joined = [out]
    return out


def listed(table_ref):
    blocks = table_ref.shape[0] - 1
    return [table_ref[i] for i in range(blocks)], table_ref[blocks]


def general(state, neighbours, obs_cell, obs_values, obs_var):
    ensemble = lax.all_to_all(state, "member", split_axis=1, concat_axis=0, tiled=True)
    members, owned, cells = ensemble.shape
    regions = lax.axis_size("region")
    region_patches = owned * lax.axis_size("member")
    region = lax.axis_index("region")
    first = region * region_patches + lax.axis_index("member") * owned
    up, down = rings(regions)
    fields = [ensemble[:, p, :] for p in range(owned)]
    grid = jnp.arange(cells, dtype=jnp.int32)
    for batch in range(NBATCH):
        picks = lax.dynamic_slice_in_dim(obs_cell, first, owned, 0)[:, batch, :]
        hot = (picks[:, :, None] == grid[None, None, :]).astype(F32)
        own_rows = jnp.einsum("poc,pkc->pok", hot, jnp.stack(fields), precision=HIGHEST)
        region_rows = lax.all_gather(own_rows, "member", axis=0, tiled=True)
        before = lax.ppermute(region_rows, "region", up)
        after = lax.ppermute(region_rows, "region", down)
        beside = jnp.concatenate([before, region_rows, after], axis=0)
        new = []
        for p in range(owned):
            own = first + p
            links = lax.dynamic_index_in_dim(neighbours, own, 0, keepdims=False)
            ids = jnp.concatenate([own[None], links]).astype(jnp.int32)
            table = jnp.concatenate([ids, own[None]]).astype(jnp.int32)
            home = (ids // region_patches - region + 1) % regions
            rows = jnp.take(beside, home * region_patches + ids % region_patches, axis=0)
            pieces = [[(0, (i,), 0)] for i in range(ids.shape[0])]
            factored = factor(
                pieces, batch, members, CHUNK, listed, [table], neighbours.T, obs_values, obs_var, [rows]
            )
            new.append(last(factored, fields[p])[1])
        fields = new
    ensemble = jnp.stack(fields, axis=1)
    return lax.all_to_all(ensemble, "member", split_axis=0, concat_axis=1, tiled=True)


def on_device(state, neighbours, obs_cell, obs_values, obs_var):
    patches, links = state.shape[1], neighbours.shape[1]
    even = lax.axis_size("region") % 2 == 0
    if even and patches == 2 and lax.axis_size("member") == 2 and links + 1 == 3 * patches:
        return paired(state, neighbours, obs_cell, obs_values, obs_var)
    return general(state, neighbours, obs_cell, obs_values, obs_var)


def solution(mesh):
    in_specs = (P("member", "region", None), P(), P(), P(), P())
    out_specs = P("member", "region", None)
    return jax.shard_map(
        on_device, mesh=mesh, in_specs=in_specs, out_specs=out_specs, check_vma=False
    )
```

```python
import functools
import math

import jax
import jax.numpy as jnp
from jax import lax
from jax.experimental import pallas as pl
from jax.experimental.pallas import tpu as pltpu
from jax.sharding import PartitionSpec as P

NBATCH = 2
HIGHEST = lax.Precision.HIGHEST
F32 = jnp.float32
BF16 = jnp.bfloat16
VMEM = pl.BlockSpec(memory_space=pltpu.VMEM)
SMEM = pl.BlockSpec(memory_space=pltpu.SMEM)
NN = (((1,), (0,)), ((), ()))
NT = (((1,), (1,)), ((), ()))
TN = (((0,), (0,)), ((), ()))
RESIDUAL = 1e-3
FACTOR_LIMIT = 24
MOST_STEPS = 15
TILE = 256
CHUNK = 128


def call(kernel, outs, ins, args, scratch=(), flops=0, limit=16, aliases=None):
    shapes = [jax.ShapeDtypeStruct(shape, dtype) for shape, dtype, _ in outs]
    moved = sum(math.prod(s.shape) * s.dtype.itemsize for s in shapes)
    moved += sum(a.size * a.dtype.itemsize for a in args)
    return pl.pallas_call(
        kernel,
        out_shape=shapes,
        in_specs=ins,
        out_specs=[space for _, _, space in outs],
        scratch_shapes=list(scratch),
        input_output_aliases=aliases or {},
        compiler_params=pltpu.CompilerParams(vmem_limit_bytes=limit * 1024 * 1024),
        cost_estimate=pl.CostEstimate(flops=flops, bytes_accessed=moved, transcendentals=0),
    )(*args)


def split(x):
    high = x.astype(BF16)
    return high, (x - high.astype(F32)).astype(BF16)


def dot(a, b, dims=NN):
    return lax.dot_general(a, b, dims, preferred_element_type=F32)


def dot3(a, b, dims=NN):
    (left,), (right,) = dims[0]
    lhs = jnp.concatenate([a[0], a[0], a[1]], axis=left)
    rhs = jnp.concatenate([b[0], b[1], b[0]], axis=right)
    return dot(lhs, rhs, dims)


def select(hot, parts, dims):
    (left,), (right,) = dims[0]
    hot = hot.astype(BF16)
    lhs = jnp.concatenate([hot] * len(parts), axis=left)
    return dot(lhs, jnp.concatenate(parts, axis=right), dims)


def split_all(x):
    high, middle = split(x)
    low = x - high.astype(F32) - middle.astype(F32)
    return high, middle, low.astype(BF16)


def step_limits():
    limits = []
    for steps in range(MOST_STEPS):
        rho = RESIDUAL
        for _ in range(steps):
            rho = math.sqrt(2.0 * rho / (1.0 + rho))
        limits.append(2.0 * rho / (1.0 - rho) if rho < 1.0 else math.inf)
    return limits


def diagonal(n, columns, first):
    row = lax.broadcasted_iota(jnp.int32, (n, columns), 0)
    column = lax.broadcasted_iota(jnp.int32, (n, columns), 1)
    return row + first == column


def selector(picks, cells, scratch):
    per_patch = picks.shape[1]
    scratch[...] = jnp.full_like(scratch, -1)
    scratch[0:1, 0:per_patch] = picks
    grid = lax.broadcasted_iota(jnp.int32, (cells, scratch.shape[1]), 0)
    hot = (grid == scratch[0:1, :]).astype(F32)
    return jnp.transpose(hot)[0:per_patch, :]


def sort_kernel(column_ref, state_ref, keep_ref, send_ref):
    column = column_ref[0]
    first, second = state_ref[:, 0, :], state_ref[:, 1, :]
    keep_ref[...] = jnp.where(column == 0, first, second)
    send_ref[...] = jnp.where(column == 0, second, first)


def pick_kernel(region_ref, column_ref, cells_ref, keep_ref, send_ref, rows_ref, scratch):
    column = column_ref[0]
    for patch, field_ref in ((column, keep_ref), (1 - column, send_ref)):
        picks = cells_ref[pl.ds(region_ref[0] * 2 + patch, 1), 0, :]
        hot = selector(picks, field_ref.shape[1], scratch)
        rows_ref[pl.ds(patch, 1)] = select(hot, split_all(field_ref[...]), NT)[None]


def gate_kernel(values_hbm, var_hbm, send_ref, after_ref, out_ref, values_ref, var_ref, sems):
    copies = [
        pltpu.make_async_copy(values_hbm, values_ref, sems.at[0]),
        pltpu.make_async_copy(var_hbm, var_ref, sems.at[1]),
    ]
    for copy in copies:
        copy.start()
    for copy in copies:
        copy.wait()


def table(patches, own, near_ref, values_ref, var_ref, batch, flat):
    per_patch = values_ref.shape[2]
    blocks = len(patches)
    flat[...] = jnp.ones_like(flat)
    for i, patch in enumerate(patches):
        widening = (patch == own).astype(jnp.int32)
        for j in range(near_ref.shape[0]):
            widening = widening + (near_ref[j, own] == patch).astype(jnp.int32) * (j + 2)
        flat[i : i + 1, 0:per_patch] = values_ref[pl.ds(patch, 1), batch, :]
        noise = var_ref[pl.ds(patch, 1), batch, :] * widening.astype(F32)
        flat[blocks + i : blocks + i + 1, 0:per_patch] = noise
    return jnp.transpose(flat[...])[0:per_patch]


def column_of(upright, i, blocks):
    return upright[:, i : i + 1], upright[:, blocks + i : blocks + i + 1]


def scale_block(i, piece, sources, column, members, sh_ref, sl_ref, d_ref):
    value, noise = column
    rows = [sources[which][index] for which, index, _ in piece]
    total = sum(jnp.sum(part, axis=1, keepdims=True) for part in rows)
    mean = total * (1.0 / members)
    scale = lax.rsqrt(noise * (members - 1.0))
    per_patch = value.shape[0]
    at = slice(i * per_patch, (i + 1) * per_patch)
    for part, (_, _, start) in zip(rows, piece):
        size = part.shape[1]
        lanes = slice(start * size, (start + 1) * size)
        sh_ref[at, lanes], sl_ref[at, lanes] = split((part - mean) * scale)
    d_ref[at, :] = jnp.broadcast_to((value - mean) * scale, (per_patch, d_ref.shape[1]))


def prepare_kernel(pieces, batch, members, patches_of, places, crossing, *refs):
    place_refs, refs = refs[:places], refs[places:]
    near_ref, values_ref, var_ref, *refs = refs
    refs, (upright_ref, flat) = refs[:-2], refs[-2:]
    if crossing:
        (ah_ref, al_ref, *refs), cross_ref = refs[:-1], refs[-1]
    sources, (sh_ref, sl_ref, d_ref, g_ref) = refs[:-4], refs[-4:]
    patches, own = patches_of(*place_refs)
    upright = table(patches, own, near_ref, values_ref, var_ref, batch, flat)
    upright_ref[...] = upright
    for i, piece in enumerate(pieces):
        column = column_of(upright, i, len(patches))
        scale_block(i, piece, sources, column, members, sh_ref, sl_ref, d_ref)
    count = len(pieces) * values_ref.shape[2]
    s = (sh_ref[0:count], sl_ref[0:count])
    g_ref[0:count, 0:count] = dot3(s, s, NT)
    if crossing:
        cross_ref[0:count] = dot3(s, (ah_ref[...], al_ref[...]))


def factor_kernel(pieces, batch, members, chunk, patches_of, places, ready, crossing, *refs):
    if ready:
        upright_ref, *refs = refs
    else:
        place_refs, refs = refs[:places], refs[places:]
        near_ref, values_ref, var_ref, *refs = refs
    refs, (flat, eye_ref, x_ref, wa, wb) = refs[:-5], refs[-5:]
    if crossing:
        refs, cross_ref = refs[:-1], refs[-1]
    refs, (sh_ref, sl_ref, d_ref, g_ref, xh_ref, xl_ref, n_ref) = refs[:-7], refs[-7:]
    if crossing:
        refs, (ah_ref, al_ref) = refs[:-7], refs[-7:-5]
    elif ready:
        refs = refs[:-4]
    sources = refs
    blocks = len(pieces)
    if ready:
        upright = upright_ref[...]
    else:
        patches, own = patches_of(*place_refs)
        upright = table(patches, own, near_ref, values_ref, var_ref, batch, flat)
    per_patch = upright.shape[0]
    for i in range(ready, blocks):
        column = column_of(upright, i, blocks)
        scale_block(i, pieces[i], sources, column, members, sh_ref, sl_ref, d_ref)
    n = sh_ref.shape[0]
    head = min(TILE, n)
    tail = n - head
    chunks = [(i, min(i + chunk, n)) for i in range(0, n, chunk)]
    left = (sh_ref[0:head], sl_ref[0:head])
    fresh = ready * per_patch
    g_ref[fresh:n, 0:head] = dot3((sh_ref[fresh:n], sl_ref[fresh:n]), left, NT)
    if 0 < fresh < head:
        g_ref[0:fresh, fresh:head] = jnp.transpose(g_ref[fresh:head, 0:fresh])
    low = (sh_ref[head:n], sl_ref[head:n])
    g_ref[head:n, head:n] = dot3(low, low, NT)
    g_ref[0:head, head:n] = jnp.transpose(g_ref[head:n, 0:head])
    if crossing:
        cross_ref[fresh:n] = dot3((sh_ref[fresh:n], sl_ref[fresh:n]), (ah_ref[...], al_ref[...]))
    g = g_ref[...]
    square = jnp.sum(jnp.sum(g * g, axis=0, keepdims=True), axis=1, keepdims=True)
    norm = jnp.sqrt(square) * (1.0 + 1e-5)
    size = square[0, 0]
    limits = step_limits()
    pairs = jnp.int32(0)
    for k in range(7, MOST_STEPS - 2, 2):
        limit = limits[k] * (1.0 - 1e-4)
        pairs = pairs + (size > limit * limit).astype(jnp.int32)
    n_ref[0] = (size > 1.6e7).astype(jnp.int32) + (size > 1e8).astype(jnp.int32)
    eye_ref[...] = diagonal(n, n, 0).astype(F32)
    eye = eye_ref[...]
    first = 2.0 / (2.0 + norm)
    rho = norm * (0.5 * first)
    rho2 = rho * rho
    weight = 2.0 / (2.0 - rho2)
    keep = 0.5 * rho2 * weight
    x = (weight * first * (2.0 - first)) * eye - (weight * first * first) * g
    x_ref[...] = x
    for i, part in enumerate(split(x)):
        wa[i, :, n : 2 * n] = part

    def store(targets, start, left, corner):
        blocks = [(slice(0, n), slice(start, start + head), left)]
        blocks.append((slice(head, n), slice(start + head, start + n), corner))
        blocks.append((slice(0, head), slice(start + head, start + n), jnp.transpose(left[head:n])))
        for rows, columns, block in blocks:
            for target, part in zip(targets, split(block)):
                target[rows, columns] = part

    def corner_of(weight, keep, left, corner):
        left = weight * left - keep * eye_ref[:, 0:head]
        return left, weight * corner - keep * eye_ref[head:n, head:n]

    parts = split(g)
    square_left = dot3(parts, [part[:, 0:head] for part in parts])
    square_corner = dot3([part[head:n] for part in parts], [part[:, head:n] for part in parts])
    two = weight * first * first
    one = -2.0 * weight * first * (1.0 - first)
    none = weight * (1.0 - first) * (1.0 - first) - keep
    left = two * square_left + one * g[:, 0:head] + none * eye[:, 0:head]
    corner = two * square_corner + one * g[head:n, head:n] + none * eye[head:n, head:n]
    store((wa.at[0], wa.at[1]), 0, left, corner)

    def corners_of(source):
        ends = [jnp.concatenate([source[i, :, head:n], source[i, :, n + head : 2 * n]], axis=1) for i in (0, 1)]
        return dot3([source[i, head:n, 0:n] for i in (0, 1)], ends)

    def advance(source, target, rho2):
        weight = 2.0 / (2.0 - rho2)
        keep = 0.5 * rho2 * weight
        parts = (source[0, :, 0:n], source[1, :, 0:n])
        left = dot3(parts, (source[0, :, 0:head], source[1, :, 0:head]))
        corners = corners_of(source)
        both = (target.at[0], target.at[1])
        store(both, 0, *corner_of(weight, keep, left, corners[:, 0:tail]))
        left = dot3(parts, (source[0, :, n : n + head], source[1, :, n : n + head]))
        left = weight * (x_ref[:, 0:head] + left)
        corner = weight * (x_ref[head:n, head:n] + corners[:, tail : 2 * tail])
        x_ref[:, 0:head] = left
        x_ref[head:n, head:n] = corner
        store(both, n, left, corner)
        return keep * keep

    rho2 = keep * keep

    def sides(source, span):
        return [source[i, span[0] : span[1], 0:n] for i in (0, 1)]

    def put(targets, start, span, block):
        for target, part in zip(targets, split(block)):
            target[span[0] : span[1], start : start + head] = part
        low = max(span[0], head)
        if low < span[1]:
            for target, part in zip(targets, split(jnp.transpose(block[low - span[0] :]))):
                target[0:head, start + low : start + span[1]] = part

    def less_diagonal(block, keep, span):
        low, high = span[0], min(span[1], head)
        if low >= high:
            return block
        middle = block[:, low:high] - keep * eye_ref[low : span[1], low:high]
        pieces = [block[:, 0:low], middle, block[:, high:head]]
        return jnp.concatenate([piece for piece in pieces if piece.shape[1]], axis=1)

    def put_corner(targets, start, block):
        for target, part in zip(targets, split(block)):
            target[head:n, start + head : start + n] = part

    def put_x(targets, start, weight, span, product):
        x = weight * (x_ref[span[0] : span[1], 0:head] + product)
        x_ref[span[0] : span[1], 0:head] = x
        put(targets, start, span, x)

    def put_x_corner(targets, start, weight, product):
        x = weight * (x_ref[head:n, head:n] + product)
        x_ref[head:n, head:n] = x
        put_corner(targets, start, x)

    waiting = None
    source, target = wa, wb
    for _ in range(5):
        weight = 2.0 / (2.0 - rho2)
        keep = 0.5 * rho2 * weight
        first = (source[0, :, 0:head], source[1, :, 0:head])
        r = []
        for k, span in enumerate(chunks):
            r.append(dot3(sides(source, span), first))
            if waiting is not None:
                put_x((source.at[0], source.at[1]), n, waiting[0], span, waiting[1][k])
        if waiting is not None:
            put_x_corner((source.at[0], source.at[1]), n, waiting[0], waiting[2])
        corners = corners_of(source)
        first = (source[0, :, n : n + head], source[1, :, n : n + head])
        both = (target.at[0], target.at[1])
        x = []
        for k, span in enumerate(chunks):
            x.append(dot3(sides(source, span), first))
            put(both, 0, span, less_diagonal(weight * r[k], keep, span))
        put_corner(both, 0, weight * corners[:, 0:tail] - keep * eye_ref[head:n, head:n])
        waiting = (weight, x, corners[:, tail : 2 * tail])
        rho2 = keep * keep
        source, target = target, source
    for k, span in enumerate(chunks):
        put_x((source.at[0], source.at[1]), n, waiting[0], span, waiting[1][k])
    put_x_corner((source.at[0], source.at[1]), n, waiting[0], waiting[2])

    def twice(_, rho2):
        return advance(target, source, advance(source, target, rho2))

    rho2 = lax.fori_loop(0, pairs, twice, rho2)
    weight = 2.0 / (2.0 - rho2)
    first = (source[0, :, n : n + head], source[1, :, n : n + head])
    done = (xh_ref, xl_ref)
    ends = [source[i, :, n + head : 2 * n] for i in (0, 1)]
    put_x_corner(done, 0, weight, dot3(sides(source, (head, n)), ends))
    x = [dot3(sides(source, span), first) for span in chunks]
    for k, span in enumerate(chunks):
        put_x(done, 0, weight, span, x[k])


def centred(fields):
    members = sum(field.shape[0] for field in fields)
    mean = sum(jnp.sum(field, axis=0, keepdims=True) for field in fields) * (1.0 / members)
    pairs = [split(field - mean) for field in fields]
    return [jnp.concatenate(parts, axis=0) for parts in zip(*pairs)], mean


def in_chunks(count, product, work):
    waiting = None
    for start in range(0, count, CHUNK):
        span = slice(start, min(start + CHUNK, count))
        result = product(span)
        if waiting is not None:
            work(*waiting)
        waiting = (span, result)
    work(*waiting)


def solve(n_ref, s, g_ref, x, anomaly, z_ref, cross_ref, parts_ref, crossed_already=False, between=()):
    n = z_ref.shape[0]

    def keep(slot, span, value):
        for i, part in enumerate(split(value)):
            parts_ref[slot, i, span] = part

    def kept(slot):
        return parts_ref[slot, 0], parts_ref[slot, 1]

    def some(parts, span):
        return [part[span] for part in parts]

    def crossed(span, value):
        cross_ref[span] = value
        keep(0, span, value)

    def solved(span, value):
        z_ref[span] = value
        keep(1, span, value)

    def left(span, value):
        keep(0, span, cross_ref[span] - z_ref[span] - value)

    def refined(span, value):
        z_ref[span] = z_ref[span] + value

    if crossed_already:
        keep(0, slice(0, n), cross_ref[...])
    else:
        in_chunks(n, lambda span: dot3(some(s, span), [part[...] for part in anomaly]), crossed)
    stages = [
        (lambda span: dot3(some(x, span), kept(0)), solved),
        (lambda span: dot3(split(g_ref[span]), kept(1)), left),
        (lambda span: dot3(some(x, span), kept(0)), refined),
    ]
    for i, (product, work) in enumerate(stages):
        for extra in between[i : i + 1]:
            extra()
        in_chunks(n, product, work)

    def refine(_, carry):
        z = z_ref[...]
        gz = lax.dot_general(g_ref[...], z, NN, precision=HIGHEST, preferred_element_type=F32)
        z_ref[...] = z + dot3([part[...] for part in x], split(cross_ref[...] - z - gz))
        return carry

    lax.fori_loop(0, n_ref[0], refine, 0)


def gain_kernel(batch, parts, own_of, region_ref, column_ref, n_ref, cells_ref, sh_ref, sl_ref, d_ref, g_ref, *refs):
    xh_ref, xl_ref, *refs = refs
    states = refs[:parts]
    z_ref, rows_ref, scratch, anomaly_ref, cross_ref, parts_ref = refs[parts:]
    anomaly, mean = centred([state[...] for state in states])
    for i, part in enumerate(anomaly):
        anomaly_ref[i] = part
    anomaly = (anomaly_ref.at[0], anomaly_ref.at[1])
    picks = cells_ref[pl.ds(own_of(region_ref, column_ref), 1), batch, :]
    hot = selector(picks, mean.shape[1], scratch)
    base = jnp.sum(hot * mean, axis=1, keepdims=True)
    members = anomaly_ref.shape[1]
    count = 3
    size = -(-members // (count * 128)) * 128

    def pick(start, stop):
        picked = select(hot, [part[start:stop] for part in anomaly], NT)
        rows_ref[:, start:stop] = base + picked

    between = [
        functools.partial(pick, i * size, min((i + 1) * size, members)) for i in range(count)
    ]
    x = (xh_ref, xl_ref)
    solve(n_ref, (sh_ref, sl_ref), g_ref, x, anomaly, z_ref, cross_ref, parts_ref, False, between)
    zt = split(select(hot, split(z_ref[...]), NT))
    shift = dot3(zt, split(d_ref[...]))[:, 0:1]
    rows_ref[...] = rows_ref[...] + shift - 0.5 * dot3(zt, (sh_ref[...], sl_ref[...]))


def updated(field, start, s, shift, z):
    size = field.shape[0]
    return field + shift - 0.5 * dot3([h[:, start : start + size] for h in s], z, TN)


def shift_of(z, d_ref):
    return jnp.sum(z * d_ref[:, 0:1], axis=0, keepdims=True)


def update_kernel(starts, sh_ref, sl_ref, d_ref, z_ref, *refs):
    count = len(starts)
    states, outs, parts = refs[:count], refs[count : 2 * count], refs[2 * count :]
    z = z_ref[...]
    shift = shift_of(z, d_ref)
    s, zs = (sh_ref[...], sl_ref[...]), split(z)
    for start, state, out in zip(starts, states, outs):
        out[...] = updated(state[...], start, s, shift, zs)
    if parts:
        anomaly, _ = centred([out[...] for out in outs])
        for ref, part in zip(parts, anomaly):
            ref[...] = part


def last_kernel(given, n_ref, sh_ref, sl_ref, d_ref, g_ref, xh_ref, xl_ref, state_ref, *refs):
    refs, (cross_ref, parts_ref) = refs[:-2], refs[-2:]
    if given:
        cross_ref, *refs = refs
    z_ref, *out_refs = refs
    anomaly = None if given else centred([state_ref[...]])[0]
    x = (xh_ref, xl_ref)
    solve(n_ref, (sh_ref, sl_ref), g_ref, x, anomaly, z_ref, cross_ref, parts_ref, given)
    z = z_ref[...]
    shift, zs = shift_of(z, d_ref), split(z)
    start = sh_ref.shape[1] - state_ref.shape[0]
    s = (sh_ref[...], sl_ref[...])
    first = 0
    for out_ref in out_refs:
        stop = first + out_ref.shape[0]
        out_ref[...] = updated(state_ref[first:stop], start + first, s, shift, zs)
        first = stop


def join_kernel(first, column_ref, mine_ref, theirs_ref, *refs):
    out_ref, both, sems = refs[-3:]
    chunks = sems.shape[0]
    size = both.shape[0] // chunks
    column = column_ref[0]
    copies = []
    for i in range(chunks):
        at = slice(i * size, (i + 1) * size)
        mine, theirs = mine_ref[first + i * size : first + (i + 1) * size, :], theirs_ref[at, :]
        both[at, 0, :] = jnp.where(column == 0, mine, theirs)
        both[at, 1, :] = jnp.where(column == 0, theirs, mine)
        target = out_ref.at[pl.ds(first + i * size, size)]
        copies.append(pltpu.make_async_copy(both.at[pl.ds(i * size, size)], target, sems.at[i]))
        copies[-1].start()
    for copy in copies:
        copy.wait()


def prepare(pieces, batch, members, patches_of, place, near, values, var, anomaly, sources, n):
    width = anomaly[0].shape[1] if anomaly else 0
    outs = [
        ((n, members), BF16, VMEM),
        ((n, members), BF16, VMEM),
        ((n, 128), F32, VMEM),
        ((n, n), F32, VMEM),
    ]
    if anomaly:
        outs.append(((n, width), F32, VMEM))
    outs.append(((values.shape[2], 128), F32, VMEM))
    kernel = functools.partial(
        prepare_kernel, pieces, batch, members, patches_of, len(place), bool(anomaly)
    )
    args = [*place, near, values, var, *anomaly, *sources]
    ins = [SMEM] * (len(place) + 1) + [VMEM] * (len(args) - len(place) - 1)
    return call(kernel, outs, ins, args, [pltpu.VMEM((128, 128), F32)], 6 * n * (width + n // 3) * members)


def factor(pieces, batch, members, chunk, patches_of, place, near, values, var, sources, ready=0, before=()):
    per_patch = values.shape[2]
    n = len(pieces) * per_patch
    outs = [
        ((n, members), BF16, VMEM),
        ((n, members), BF16, VMEM),
        ((n, 128), F32, VMEM),
        ((n, n), F32, VMEM),
        ((n, n), BF16, VMEM),
        ((n, n), BF16, VMEM),
        ((1,), jnp.int32, SMEM),
    ]
    if ready:
        *before, upright = before
        args = [upright, *sources, *before]
        ins = [VMEM] * len(args)
    else:
        args = [*place, near, values, var, *sources]
        ins = [SMEM] * (len(place) + 1) + [VMEM] * (2 + len(sources))
    aliases = {}
    crossing = len(before) > 4
    if crossing:
        outs.append((before[-1].shape, F32, VMEM))
    if ready:
        first = len(args) - 4 - crossing
        aliases = {first: 0, first + 1: 1, first + 2: 2, first + 3: 3}
        if crossing:
            aliases[first + 4] = 7
    scratch = [
        pltpu.VMEM((128, 128), F32),
        pltpu.VMEM((n, n), F32),
        pltpu.VMEM((n, n), F32),
        pltpu.VMEM((2, n, 2 * n), BF16),
        pltpu.VMEM((2, n, 2 * n), BF16),
    ]
    kernel = functools.partial(
        factor_kernel, pieces, batch, members, chunk, patches_of, len(place), ready, crossing
    )
    flops = 6 * n * n * members + (30 if crossing else 20) * n * n * n
    return call(kernel, outs, ins, args, scratch, flops, FACTOR_LIMIT, aliases)


def solver_scratch(n, width):
    return [pltpu.VMEM((n, width), F32), pltpu.VMEM((2, 2, n, width), BF16)]


def gain(batch, own_of, place, cells, factored, states):
    sh, sl, d, g, xh, xl, more = factored[:7]
    n, members = sh.shape
    width = states[0].shape[1]
    kernel = functools.partial(gain_kernel, batch, len(states), own_of)
    outs = [((n, width), F32, VMEM), ((cells.shape[2], members), F32, VMEM)]
    ins = [SMEM] * 3 + [VMEM] * (7 + len(states))
    args = [*place, more, cells, sh, sl, d, g, xh, xl, *states]
    flops = 8 * n * members * width
    scratch = [pltpu.VMEM((8, 128), jnp.int32), pltpu.VMEM((2, members, width), BF16)]
    scratch += solver_scratch(n, width)
    return call(kernel, outs, ins, args, scratch, flops)


def update(factored, z, states, starts, more=False):
    sh, sl, d = factored[:3]
    kernel = functools.partial(update_kernel, starts)
    outs = [(state.shape, F32, VMEM) for state in states]
    if more:
        outs += [((sh.shape[1], z.shape[1]), BF16, VMEM)] * 2
    flops = 6 * sh.shape[0] * sh.shape[1] * z.shape[1]
    return call(kernel, outs, [VMEM] * (4 + len(states)), [sh, sl, d, z, *states], (), flops)


def last(factored, state, counts=None):
    sh, sl, d, g, xh, xl, more, *cross = factored
    n, width = sh.shape[0], state.shape[1]
    outs = [((n, width), F32, VMEM)] + [((count, width), F32, VMEM) for count in counts or state.shape[:1]]
    args = [more, sh, sl, d, g, xh, xl, state, *cross]
    flops = 12 * sh.shape[0] * sh.shape[1] * width
    ins = [SMEM] + [VMEM] * (len(args) - 1)
    kernel = functools.partial(last_kernel, bool(cross))
    return call(kernel, outs, ins, args, solver_scratch(n, width), flops)


def rings(size):
    up = [(i, (i + 1) % size) for i in range(size)]
    return up, [(j, i) for i, j in up]


BOTH = ("region", "member")


def permute(x, moves, regions):
    table = []
    for region in range(regions):
        for column in range(2):
            pair, parity, to = moves(region // 2, region % 2, column)
            pair %= regions // 2
            table.append((region * 2 + column, (pair * 2 + parity) * 2 + to))
    return lax.ppermute(x, BOTH, table)


def paired(state, neighbours, obs_cell, obs_values, obs_var):
    half, _, cells = state.shape
    members = 2 * half
    regions = lax.axis_size("region")
    region, column = lax.axis_index("region"), lax.axis_index("member")
    place = (region.astype(jnp.int32)[None], column.astype(jnp.int32)[None])
    near = neighbours.T

    def own_of(region_ref, column_ref):
        return region_ref[0] * 2 + column_ref[0]

    def around(region):
        side = 2 * lax.rem(region, 2) - 1
        return region, region - side, lax.rem(region + regions + side, regions)

    def patches_first(region_ref, column_ref):
        return [r * 2 + p for r in around(region_ref[0]) for p in (0, 1)], own_of(region_ref, column_ref)

    def patches_next(region_ref, column_ref):
        column = column_ref[0]
        within = (column, 1 - column)
        return [r * 2 + p for p in within for r in around(region_ref[0])], own_of(region_ref, column_ref)

    def across(x):
        return permute(x, lambda c, q, m: (c, q, 1 - m), regions)

    def beside(x):
        return permute(x, lambda c, q, m: (c, 1 - q, m), regions)

    def outside(x):
        return permute(x, lambda c, q, m: (c + 2 * q - 1, 1 - q, m), regions)

    anywhere = pl.BlockSpec(memory_space=pl.ANY)
    shape = ((half, cells), F32, VMEM)
    keep, send = call(sort_kernel, [shape] * 2, [SMEM, VMEM], [place[1], state])
    (rows,) = call(
        pick_kernel,
        [((2, obs_cell.shape[2], half), F32, VMEM)],
        [SMEM, SMEM, VMEM, VMEM, VMEM],
        [*place, obs_cell, keep, send],
        [pltpu.VMEM((8, 128), jnp.int32)],
    )
    other = across(rows)
    sources = [rows, beside(rows), outside(rows), other, beside(other), outside(other)]
    send, values, var = call(
        gate_kernel,
        [((half, cells), F32, anywhere), (obs_values.shape, F32, VMEM), (obs_var.shape, F32, VMEM)],
        [anywhere] * 4,
        [obs_values, obs_var, send, rows],
        [pltpu.SemaphoreType.DMA((2,))],
        aliases={2: 0},
    )
    pieces = [[(i, (p,), 0), (3 + i, (p,), 1)] for i in range(3) for p in range(2)]
    states = [keep, across(send)]
    given = (place, near, values, var)
    n = len(pieces) * obs_cell.shape[2]
    early = [[(0, (p,), 0), (1, (p,), 1)] for p in range(2)]
    done = prepare(early, 0, members, patches_first, *given, (), [rows, other], n)
    factored = factor(pieces, 0, members, CHUNK, patches_first, *given, sources, 2, done)
    everything = slice(None)
    low, high = (everything, slice(0, half)), (everything, slice(half, members))
    pieces = [[(i, low, 0), (i, high, 1)] for i in range(3)]
    pieces += [[(i, high, 0), (i, low, 1)] for i in range(3, 6)]
    early = 4
    for batch in range(1, NBATCH):
        z, rows = gain(batch, own_of, place, obs_cell, factored, states)
        other = across(rows)
        far = permute(rows, lambda c, q, m: (c + 2 * q - 1, 1 - q, 1 - m), regions)
        sources = [rows, beside(rows), outside(rows), other, beside(other), far]
        mine, theirs, *anomaly = update(factored, z, states, (0, half), True)
        states = [mine, theirs]
        done = prepare(pieces[:early], batch, members, patches_next, *given, anomaly, sources[:early], n)
        factored = factor(
            pieces, batch, members, CHUNK, patches_next, *given, sources, early, [*anomaly, *done]
        )
    most = half - half // 4
    z, *theirs = last(factored, states[1], (most, half - most))
    theirs = [across(part) for part in theirs]
    (mine,) = update(factored, z, states[:1], (0,))
    joined = []
    for first, other in zip((0, most), theirs):
        count = other.shape[0]
        (out,) = call(
            functools.partial(join_kernel, first),
            [(state.shape, F32, anywhere)],
            [SMEM, VMEM, VMEM] + [anywhere] * len(joined),
            [place[1], mine, other, *joined],
            [pltpu.VMEM((count, *state.shape[1:]), F32), pltpu.SemaphoreType.DMA((2,))],
            aliases={3: 0} if joined else {},
        )
        joined = [out]
    return out


def listed(table_ref):
    blocks = table_ref.shape[0] - 1
    return [table_ref[i] for i in range(blocks)], table_ref[blocks]


def general(state, neighbours, obs_cell, obs_values, obs_var):
    ensemble = lax.all_to_all(state, "member", split_axis=1, concat_axis=0, tiled=True)
    members, owned, cells = ensemble.shape
    regions = lax.axis_size("region")
    region_patches = owned * lax.axis_size("member")
    region = lax.axis_index("region")
    first = region * region_patches + lax.axis_index("member") * owned
    up, down = rings(regions)
    fields = [ensemble[:, p, :] for p in range(owned)]
    grid = jnp.arange(cells, dtype=jnp.int32)
    for batch in range(NBATCH):
        picks = lax.dynamic_slice_in_dim(obs_cell, first, owned, 0)[:, batch, :]
        hot = (picks[:, :, None] == grid[None, None, :]).astype(F32)
        own_rows = jnp.einsum("poc,pkc->pok", hot, jnp.stack(fields), precision=HIGHEST)
        region_rows = lax.all_gather(own_rows, "member", axis=0, tiled=True)
        before = lax.ppermute(region_rows, "region", up)
        after = lax.ppermute(region_rows, "region", down)
        beside = jnp.concatenate([before, region_rows, after], axis=0)
        new = []
        for p in range(owned):
            own = first + p
            links = lax.dynamic_index_in_dim(neighbours, own, 0, keepdims=False)
            ids = jnp.concatenate([own[None], links]).astype(jnp.int32)
            table = jnp.concatenate([ids, own[None]]).astype(jnp.int32)
            home = (ids // region_patches - region + 1) % regions
            rows = jnp.take(beside, home * region_patches + ids % region_patches, axis=0)
            pieces = [[(0, (i,), 0)] for i in range(ids.shape[0])]
            factored = factor(
                pieces, batch, members, CHUNK, listed, [table], neighbours.T, obs_values, obs_var, [rows]
            )
            new.append(last(factored, fields[p])[1])
        fields = new
    ensemble = jnp.stack(fields, axis=1)
    return lax.all_to_all(ensemble, "member", split_axis=0, concat_axis=1, tiled=True)


def on_device(state, neighbours, obs_cell, obs_values, obs_var):
    patches, links = state.shape[1], neighbours.shape[1]
    even = lax.axis_size("region") % 2 == 0
    if even and patches == 2 and lax.axis_size("member") == 2 and links + 1 == 3 * patches:
        return paired(state, neighbours, obs_cell, obs_values, obs_var)
    return general(state, neighbours, obs_cell, obs_values, obs_var)


def solution(mesh):
    in_specs = (P("member", "region", None), P(), P(), P(), P())
    out_specs = P("member", "region", None)
    return jax.shard_map(
        on_device, mesh=mesh, in_specs=in_specs, out_specs=out_specs, check_vma=False
    )
```

```python
import functools
import math

import jax
import jax.numpy as jnp
from jax import lax
from jax.experimental import pallas as pl
from jax.experimental.pallas import tpu as pltpu
from jax.sharding import PartitionSpec as P

NBATCH = 2
HIGHEST = lax.Precision.HIGHEST
F32 = jnp.float32
BF16 = jnp.bfloat16
VMEM = pl.BlockSpec(memory_space=pltpu.VMEM)
SMEM = pl.BlockSpec(memory_space=pltpu.SMEM)
NN = (((1,), (0,)), ((), ()))
NT = (((1,), (1,)), ((), ()))
TN = (((0,), (0,)), ((), ()))
RESIDUAL = 1e-3
FACTOR_LIMIT = 24
MOST_STEPS = 15
TILE = 256
CHUNK = 128
SOLVE_CHUNK = 192


def call(kernel, outs, ins, args, scratch=(), flops=0, limit=16, aliases=None):
    shapes = [jax.ShapeDtypeStruct(shape, dtype) for shape, dtype, _ in outs]
    moved = sum(math.prod(s.shape) * s.dtype.itemsize for s in shapes)
    moved += sum(a.size * a.dtype.itemsize for a in args)
    return pl.pallas_call(
        kernel,
        out_shape=shapes,
        in_specs=ins,
        out_specs=[space for _, _, space in outs],
        scratch_shapes=list(scratch),
        input_output_aliases=aliases or {},
        compiler_params=pltpu.CompilerParams(vmem_limit_bytes=limit * 1024 * 1024),
        cost_estimate=pl.CostEstimate(flops=flops, bytes_accessed=moved, transcendentals=0),
    )(*args)


def split(x):
    high = x.astype(BF16)
    return high, (x - high.astype(F32)).astype(BF16)


def dot(a, b, dims=NN):
    return lax.dot_general(a, b, dims, preferred_element_type=F32)


def dot3(a, b, dims=NN):
    (left,), (right,) = dims[0]
    lhs = jnp.concatenate([a[0], a[0], a[1]], axis=left)
    rhs = jnp.concatenate([b[0], b[1], b[0]], axis=right)
    return dot(lhs, rhs, dims)


def select(hot, parts, dims):
    (left,), (right,) = dims[0]
    hot = hot.astype(BF16)
    lhs = jnp.concatenate([hot] * len(parts), axis=left)
    return dot(lhs, jnp.concatenate(parts, axis=right), dims)


def split_all(x):
    high, middle = split(x)
    low = x - high.astype(F32) - middle.astype(F32)
    return high, middle, low.astype(BF16)


def step_limits():
    limits = []
    for steps in range(MOST_STEPS):
        rho = RESIDUAL
        for _ in range(steps):
            rho = math.sqrt(2.0 * rho / (1.0 + rho))
        limits.append(2.0 * rho / (1.0 - rho) if rho < 1.0 else math.inf)
    return limits


def diagonal(n, columns, first):
    row = lax.broadcasted_iota(jnp.int32, (n, columns), 0)
    column = lax.broadcasted_iota(jnp.int32, (n, columns), 1)
    return row + first == column


def selector(picks, cells, scratch):
    per_patch = picks.shape[1]
    scratch[...] = jnp.full_like(scratch, -1)
    scratch[0:1, 0:per_patch] = picks
    grid = lax.broadcasted_iota(jnp.int32, (cells, scratch.shape[1]), 0)
    hot = (grid == scratch[0:1, :]).astype(F32)
    return jnp.transpose(hot)[0:per_patch, :]


def sort_kernel(column_ref, state_ref, keep_ref, send_ref):
    column = column_ref[0]
    first, second = state_ref[:, 0, :], state_ref[:, 1, :]
    keep_ref[...] = jnp.where(column == 0, first, second)
    send_ref[...] = jnp.where(column == 0, second, first)


def pick_kernel(region_ref, column_ref, cells_ref, keep_ref, send_ref, rows_ref, scratch):
    column = column_ref[0]
    for patch, field_ref in ((column, keep_ref), (1 - column, send_ref)):
        picks = cells_ref[pl.ds(region_ref[0] * 2 + patch, 1), 0, :]
        hot = selector(picks, field_ref.shape[1], scratch)
        rows_ref[pl.ds(patch, 1)] = select(hot, split_all(field_ref[...]), NT)[None]


def gate_kernel(values_hbm, var_hbm, send_ref, after_ref, out_ref, values_ref, var_ref, sems):
    copies = [
        pltpu.make_async_copy(values_hbm, values_ref, sems.at[0]),
        pltpu.make_async_copy(var_hbm, var_ref, sems.at[1]),
    ]
    for copy in copies:
        copy.start()
    for copy in copies:
        copy.wait()


def table(patches, own, near_ref, values_ref, var_ref, batch, flat):
    per_patch = values_ref.shape[2]
    blocks = len(patches)
    flat[...] = jnp.ones_like(flat)
    for i, patch in enumerate(patches):
        widening = (patch == own).astype(jnp.int32)
        for j in range(near_ref.shape[0]):
            widening = widening + (near_ref[j, own] == patch).astype(jnp.int32) * (j + 2)
        flat[i : i + 1, 0:per_patch] = values_ref[pl.ds(patch, 1), batch, :]
        noise = var_ref[pl.ds(patch, 1), batch, :] * widening.astype(F32)
        flat[blocks + i : blocks + i + 1, 0:per_patch] = noise
    return jnp.transpose(flat[...])[0:per_patch]


def column_of(upright, i, blocks):
    return upright[:, i : i + 1], upright[:, blocks + i : blocks + i + 1]


def scale_block(i, piece, sources, column, members, sh_ref, sl_ref, d_ref):
    value, noise = column
    rows = [sources[which][index] for which, index, _ in piece]
    total = sum(jnp.sum(part, axis=1, keepdims=True) for part in rows)
    mean = total * (1.0 / members)
    scale = lax.rsqrt(noise * (members - 1.0))
    per_patch = value.shape[0]
    at = slice(i * per_patch, (i + 1) * per_patch)
    for part, (_, _, start) in zip(rows, piece):
        size = part.shape[1]
        lanes = slice(start * size, (start + 1) * size)
        sh_ref[at, lanes], sl_ref[at, lanes] = split((part - mean) * scale)
    d_ref[at, :] = jnp.broadcast_to((value - mean) * scale, (per_patch, d_ref.shape[1]))


def prepare_kernel(pieces, batch, members, patches_of, places, crossing, *refs):
    place_refs, refs = refs[:places], refs[places:]
    near_ref, values_ref, var_ref, *refs = refs
    refs, (upright_ref, flat) = refs[:-2], refs[-2:]
    if crossing:
        (ah_ref, al_ref, *refs), cross_ref = refs[:-1], refs[-1]
    sources, (sh_ref, sl_ref, d_ref, g_ref) = refs[:-4], refs[-4:]
    patches, own = patches_of(*place_refs)
    upright = table(patches, own, near_ref, values_ref, var_ref, batch, flat)
    upright_ref[...] = upright
    for i, piece in enumerate(pieces):
        column = column_of(upright, i, len(patches))
        scale_block(i, piece, sources, column, members, sh_ref, sl_ref, d_ref)
    count = len(pieces) * values_ref.shape[2]
    s = (sh_ref[0:count], sl_ref[0:count])
    g_ref[0:count, 0:count] = dot3(s, s, NT)
    if crossing:
        cross_ref[0:count] = dot3(s, (ah_ref[...], al_ref[...]))


def factor_kernel(pieces, batch, members, chunk, patches_of, places, ready, crossing, *refs):
    if ready:
        upright_ref, *refs = refs
    else:
        place_refs, refs = refs[:places], refs[places:]
        near_ref, values_ref, var_ref, *refs = refs
    refs, (flat, eye_ref, x_ref, wa, wb) = refs[:-5], refs[-5:]
    if crossing:
        refs, cross_ref = refs[:-1], refs[-1]
    refs, (sh_ref, sl_ref, d_ref, g_ref, xh_ref, xl_ref, n_ref) = refs[:-7], refs[-7:]
    if crossing:
        refs, (ah_ref, al_ref) = refs[:-7], refs[-7:-5]
    elif ready:
        refs = refs[:-4]
    sources = refs
    blocks = len(pieces)
    if ready:
        upright = upright_ref[...]
    else:
        patches, own = patches_of(*place_refs)
        upright = table(patches, own, near_ref, values_ref, var_ref, batch, flat)
    per_patch = upright.shape[0]
    for i in range(ready, blocks):
        column = column_of(upright, i, blocks)
        scale_block(i, pieces[i], sources, column, members, sh_ref, sl_ref, d_ref)
    n = sh_ref.shape[0]
    head = min(TILE, n)
    tail = n - head
    chunks = [(i, min(i + chunk, n)) for i in range(0, n, chunk)]
    left = (sh_ref[0:head], sl_ref[0:head])
    fresh = ready * per_patch
    g_ref[fresh:n, 0:head] = dot3((sh_ref[fresh:n], sl_ref[fresh:n]), left, NT)
    if 0 < fresh < head:
        g_ref[0:fresh, fresh:head] = jnp.transpose(g_ref[fresh:head, 0:fresh])
    low = (sh_ref[head:n], sl_ref[head:n])
    g_ref[head:n, head:n] = dot3(low, low, NT)
    g_ref[0:head, head:n] = jnp.transpose(g_ref[head:n, 0:head])
    if crossing:
        cross_ref[fresh:n] = dot3((sh_ref[fresh:n], sl_ref[fresh:n]), (ah_ref[...], al_ref[...]))
    g = g_ref[...]
    square = jnp.sum(jnp.sum(g * g, axis=0, keepdims=True), axis=1, keepdims=True)
    norm = jnp.sqrt(square) * (1.0 + 1e-5)
    size = square[0, 0]
    limits = step_limits()
    pairs = jnp.int32(0)
    for k in range(7, MOST_STEPS - 2, 2):
        limit = limits[k] * (1.0 - 1e-4)
        pairs = pairs + (size > limit * limit).astype(jnp.int32)
    n_ref[0] = (size > 1.6e7).astype(jnp.int32) + (size > 1e8).astype(jnp.int32)
    eye_ref[...] = diagonal(n, n, 0).astype(F32)
    eye = eye_ref[...]
    first = 2.0 / (2.0 + norm)
    rho = norm * (0.5 * first)
    rho2 = rho * rho
    weight = 2.0 / (2.0 - rho2)
    keep = 0.5 * rho2 * weight
    x = (weight * first * (2.0 - first)) * eye - (weight * first * first) * g
    x_ref[...] = x
    for i, part in enumerate(split(x)):
        wa[i, :, n : 2 * n] = part

    def store(targets, start, left, corner):
        blocks = [(slice(0, n), slice(start, start + head), left)]
        blocks.append((slice(head, n), slice(start + head, start + n), corner))
        blocks.append((slice(0, head), slice(start + head, start + n), jnp.transpose(left[head:n])))
        for rows, columns, block in blocks:
            for target, part in zip(targets, split(block)):
                target[rows, columns] = part

    def corner_of(weight, keep, left, corner):
        left = weight * left - keep * eye_ref[:, 0:head]
        return left, weight * corner - keep * eye_ref[head:n, head:n]

    parts = split(g)
    square_left = dot3(parts, [part[:, 0:head] for part in parts])
    square_corner = dot3([part[head:n] for part in parts], [part[:, head:n] for part in parts])
    two = weight * first * first
    one = -2.0 * weight * first * (1.0 - first)
    none = weight * (1.0 - first) * (1.0 - first) - keep
    left = two * square_left + one * g[:, 0:head] + none * eye[:, 0:head]
    corner = two * square_corner + one * g[head:n, head:n] + none * eye[head:n, head:n]
    store((wa.at[0], wa.at[1]), 0, left, corner)

    def corners_of(source):
        ends = [jnp.concatenate([source[i, :, head:n], source[i, :, n + head : 2 * n]], axis=1) for i in (0, 1)]
        return dot3([source[i, head:n, 0:n] for i in (0, 1)], ends)

    def advance(source, target, rho2):
        weight = 2.0 / (2.0 - rho2)
        keep = 0.5 * rho2 * weight
        parts = (source[0, :, 0:n], source[1, :, 0:n])
        left = dot3(parts, (source[0, :, 0:head], source[1, :, 0:head]))
        corners = corners_of(source)
        both = (target.at[0], target.at[1])
        store(both, 0, *corner_of(weight, keep, left, corners[:, 0:tail]))
        left = dot3(parts, (source[0, :, n : n + head], source[1, :, n : n + head]))
        left = weight * (x_ref[:, 0:head] + left)
        corner = weight * (x_ref[head:n, head:n] + corners[:, tail : 2 * tail])
        x_ref[:, 0:head] = left
        x_ref[head:n, head:n] = corner
        store(both, n, left, corner)
        return keep * keep

    rho2 = keep * keep

    def sides(source, span):
        return [source[i, span[0] : span[1], 0:n] for i in (0, 1)]

    def put(targets, start, span, block):
        for target, part in zip(targets, split(block)):
            target[span[0] : span[1], start : start + head] = part
        low = max(span[0], head)
        if low < span[1]:
            for target, part in zip(targets, split(jnp.transpose(block[low - span[0] :]))):
                target[0:head, start + low : start + span[1]] = part

    def less_diagonal(block, keep, span):
        low, high = span[0], min(span[1], head)
        if low >= high:
            return block
        middle = block[:, low:high] - keep * eye_ref[low : span[1], low:high]
        pieces = [block[:, 0:low], middle, block[:, high:head]]
        return jnp.concatenate([piece for piece in pieces if piece.shape[1]], axis=1)

    def put_corner(targets, start, block):
        for target, part in zip(targets, split(block)):
            target[head:n, start + head : start + n] = part

    def put_x(targets, start, weight, span, product):
        x = weight * (x_ref[span[0] : span[1], 0:head] + product)
        x_ref[span[0] : span[1], 0:head] = x
        put(targets, start, span, x)

    def put_x_corner(targets, start, weight, product):
        x = weight * (x_ref[head:n, head:n] + product)
        x_ref[head:n, head:n] = x
        put_corner(targets, start, x)

    waiting = None
    source, target = wa, wb
    for _ in range(5):
        weight = 2.0 / (2.0 - rho2)
        keep = 0.5 * rho2 * weight
        first = (source[0, :, 0:head], source[1, :, 0:head])
        r = []
        for k, span in enumerate(chunks):
            r.append(dot3(sides(source, span), first))
            if waiting is not None:
                put_x((source.at[0], source.at[1]), n, waiting[0], span, waiting[1][k])
        if waiting is not None:
            put_x_corner((source.at[0], source.at[1]), n, waiting[0], waiting[2])
        corners = corners_of(source)
        first = (source[0, :, n : n + head], source[1, :, n : n + head])
        both = (target.at[0], target.at[1])
        x = []
        for k, span in enumerate(chunks):
            x.append(dot3(sides(source, span), first))
            put(both, 0, span, less_diagonal(weight * r[k], keep, span))
        put_corner(both, 0, weight * corners[:, 0:tail] - keep * eye_ref[head:n, head:n])
        waiting = (weight, x, corners[:, tail : 2 * tail])
        rho2 = keep * keep
        source, target = target, source
    for k, span in enumerate(chunks):
        put_x((source.at[0], source.at[1]), n, waiting[0], span, waiting[1][k])
    put_x_corner((source.at[0], source.at[1]), n, waiting[0], waiting[2])

    def twice(_, rho2):
        return advance(target, source, advance(source, target, rho2))

    rho2 = lax.fori_loop(0, pairs, twice, rho2)
    weight = 2.0 / (2.0 - rho2)
    first = (source[0, :, n : n + head], source[1, :, n : n + head])
    done = (xh_ref, xl_ref)
    ends = [source[i, :, n + head : 2 * n] for i in (0, 1)]
    put_x_corner(done, 0, weight, dot3(sides(source, (head, n)), ends))
    x = [dot3(sides(source, span), first) for span in chunks]
    for k, span in enumerate(chunks):
        put_x(done, 0, weight, span, x[k])


def centred(fields):
    members = sum(field.shape[0] for field in fields)
    mean = sum(jnp.sum(field, axis=0, keepdims=True) for field in fields) * (1.0 / members)
    pairs = [split(field - mean) for field in fields]
    return [jnp.concatenate(parts, axis=0) for parts in zip(*pairs)], mean


def in_chunks(count, product, work):
    waiting = None
    for start in range(0, count, SOLVE_CHUNK):
        span = slice(start, min(start + SOLVE_CHUNK, count))
        result = product(span)
        if waiting is not None:
            work(*waiting)
        waiting = (span, result)
    work(*waiting)


def solve(n_ref, s, g_ref, x, anomaly, z_ref, cross_ref, parts_ref, crossed_already=False, between=()):
    n = z_ref.shape[0]

    def keep(slot, span, value):
        for i, part in enumerate(split(value)):
            parts_ref[slot, i, span] = part

    def kept(slot):
        return parts_ref[slot, 0], parts_ref[slot, 1]

    def some(parts, span):
        return [part[span] for part in parts]

    def crossed(span, value):
        cross_ref[span] = value
        keep(0, span, value)

    def solved(span, value):
        z_ref[span] = value
        keep(1, span, value)

    def left(span, value):
        keep(0, span, cross_ref[span] - z_ref[span] - value)

    def refined(span, value):
        z_ref[span] = z_ref[span] + value

    if crossed_already:
        keep(0, slice(0, n), cross_ref[...])
    else:
        in_chunks(n, lambda span: dot3(some(s, span), [part[...] for part in anomaly]), crossed)
    stages = [
        (lambda span: dot3(some(x, span), kept(0)), solved),
        (lambda span: dot3(split(g_ref[span]), kept(1)), left),
        (lambda span: dot3(some(x, span), kept(0)), refined),
    ]
    for i, (product, work) in enumerate(stages):
        for extra in between[i : i + 1]:
            extra()
        in_chunks(n, product, work)

    def refine(_, carry):
        z = z_ref[...]
        gz = lax.dot_general(g_ref[...], z, NN, precision=HIGHEST, preferred_element_type=F32)
        z_ref[...] = z + dot3([part[...] for part in x], split(cross_ref[...] - z - gz))
        return carry

    lax.fori_loop(0, n_ref[0], refine, 0)


def gain_kernel(batch, parts, own_of, region_ref, column_ref, n_ref, cells_ref, sh_ref, sl_ref, d_ref, g_ref, *refs):
    xh_ref, xl_ref, *refs = refs
    states = refs[:parts]
    z_ref, rows_ref, scratch, anomaly_ref, cross_ref, parts_ref = refs[parts:]
    anomaly, mean = centred([state[...] for state in states])
    for i, part in enumerate(anomaly):
        anomaly_ref[i] = part
    anomaly = (anomaly_ref.at[0], anomaly_ref.at[1])
    picks = cells_ref[pl.ds(own_of(region_ref, column_ref), 1), batch, :]
    hot = selector(picks, mean.shape[1], scratch)
    base = jnp.sum(hot * mean, axis=1, keepdims=True)
    members = anomaly_ref.shape[1]
    count = 3
    size = -(-members // (count * 128)) * 128

    def pick(start, stop):
        picked = select(hot, [part[start:stop] for part in anomaly], NT)
        rows_ref[:, start:stop] = base + picked

    between = [
        functools.partial(pick, i * size, min((i + 1) * size, members)) for i in range(count)
    ]
    x = (xh_ref, xl_ref)
    solve(n_ref, (sh_ref, sl_ref), g_ref, x, anomaly, z_ref, cross_ref, parts_ref, False, between)
    zt = split(select(hot, split(z_ref[...]), NT))
    shift = dot3(zt, split(d_ref[...]))[:, 0:1]
    rows_ref[...] = rows_ref[...] + shift - 0.5 * dot3(zt, (sh_ref[...], sl_ref[...]))


def updated(field, start, s, shift, z):
    size = field.shape[0]
    return field + shift - 0.5 * dot3([h[:, start : start + size] for h in s], z, TN)


def shift_of(z, d_ref):
    return jnp.sum(z * d_ref[:, 0:1], axis=0, keepdims=True)


def update_kernel(starts, sh_ref, sl_ref, d_ref, z_ref, *refs):
    count = len(starts)
    states, outs, parts = refs[:count], refs[count : 2 * count], refs[2 * count :]
    z = z_ref[...]
    shift = shift_of(z, d_ref)
    s, zs = (sh_ref[...], sl_ref[...]), split(z)
    for start, state, out in zip(starts, states, outs):
        out[...] = updated(state[...], start, s, shift, zs)
    if parts:
        anomaly, _ = centred([out[...] for out in outs])
        for ref, part in zip(parts, anomaly):
            ref[...] = part


def last_kernel(given, n_ref, sh_ref, sl_ref, d_ref, g_ref, xh_ref, xl_ref, state_ref, *refs):
    refs, (cross_ref, parts_ref) = refs[:-2], refs[-2:]
    if given:
        cross_ref, *refs = refs
    z_ref, *out_refs = refs
    anomaly = None if given else centred([state_ref[...]])[0]
    x = (xh_ref, xl_ref)
    solve(n_ref, (sh_ref, sl_ref), g_ref, x, anomaly, z_ref, cross_ref, parts_ref, given)
    z = z_ref[...]
    shift, zs = shift_of(z, d_ref), split(z)
    start = sh_ref.shape[1] - state_ref.shape[0]
    s = (sh_ref[...], sl_ref[...])
    first = 0
    for out_ref in out_refs:
        stop = first + out_ref.shape[0]
        out_ref[...] = updated(state_ref[first:stop], start + first, s, shift, zs)
        first = stop


def join_kernel(first, column_ref, mine_ref, theirs_ref, *refs):
    out_ref, both, sems = refs[-3:]
    chunks = sems.shape[0]
    size = both.shape[0] // chunks
    column = column_ref[0]
    copies = []
    for i in range(chunks):
        at = slice(i * size, (i + 1) * size)
        mine, theirs = mine_ref[first + i * size : first + (i + 1) * size, :], theirs_ref[at, :]
        both[at, 0, :] = jnp.where(column == 0, mine, theirs)
        both[at, 1, :] = jnp.where(column == 0, theirs, mine)
        target = out_ref.at[pl.ds(first + i * size, size)]
        copies.append(pltpu.make_async_copy(both.at[pl.ds(i * size, size)], target, sems.at[i]))
        copies[-1].start()
    for copy in copies:
        copy.wait()


def prepare(pieces, batch, members, patches_of, place, near, values, var, anomaly, sources, n):
    width = anomaly[0].shape[1] if anomaly else 0
    outs = [
        ((n, members), BF16, VMEM),
        ((n, members), BF16, VMEM),
        ((n, 128), F32, VMEM),
        ((n, n), F32, VMEM),
    ]
    if anomaly:
        outs.append(((n, width), F32, VMEM))
    outs.append(((values.shape[2], 128), F32, VMEM))
    kernel = functools.partial(
        prepare_kernel, pieces, batch, members, patches_of, len(place), bool(anomaly)
    )
    args = [*place, near, values, var, *anomaly, *sources]
    ins = [SMEM] * (len(place) + 1) + [VMEM] * (len(args) - len(place) - 1)
    return call(kernel, outs, ins, args, [pltpu.VMEM((128, 128), F32)], 6 * n * (width + n // 3) * members)


def factor(pieces, batch, members, chunk, patches_of, place, near, values, var, sources, ready=0, before=()):
    per_patch = values.shape[2]
    n = len(pieces) * per_patch
    outs = [
        ((n, members), BF16, VMEM),
        ((n, members), BF16, VMEM),
        ((n, 128), F32, VMEM),
        ((n, n), F32, VMEM),
        ((n, n), BF16, VMEM),
        ((n, n), BF16, VMEM),
        ((1,), jnp.int32, SMEM),
    ]
    if ready:
        *before, upright = before
        args = [upright, *sources, *before]
        ins = [VMEM] * len(args)
    else:
        args = [*place, near, values, var, *sources]
        ins = [SMEM] * (len(place) + 1) + [VMEM] * (2 + len(sources))
    aliases = {}
    crossing = len(before) > 4
    if crossing:
        outs.append((before[-1].shape, F32, VMEM))
    if ready:
        first = len(args) - 4 - crossing
        aliases = {first: 0, first + 1: 1, first + 2: 2, first + 3: 3}
        if crossing:
            aliases[first + 4] = 7
    scratch = [
        pltpu.VMEM((128, 128), F32),
        pltpu.VMEM((n, n), F32),
        pltpu.VMEM((n, n), F32),
        pltpu.VMEM((2, n, 2 * n), BF16),
        pltpu.VMEM((2, n, 2 * n), BF16),
    ]
    kernel = functools.partial(
        factor_kernel, pieces, batch, members, chunk, patches_of, len(place), ready, crossing
    )
    flops = 6 * n * n * members + (30 if crossing else 20) * n * n * n
    return call(kernel, outs, ins, args, scratch, flops, FACTOR_LIMIT, aliases)


def solver_scratch(n, width):
    return [pltpu.VMEM((n, width), F32), pltpu.VMEM((2, 2, n, width), BF16)]


def gain(batch, own_of, place, cells, factored, states):
    sh, sl, d, g, xh, xl, more = factored[:7]
    n, members = sh.shape
    width = states[0].shape[1]
    kernel = functools.partial(gain_kernel, batch, len(states), own_of)
    outs = [((n, width), F32, VMEM), ((cells.shape[2], members), F32, VMEM)]
    ins = [SMEM] * 3 + [VMEM] * (7 + len(states))
    args = [*place, more, cells, sh, sl, d, g, xh, xl, *states]
    flops = 8 * n * members * width
    scratch = [pltpu.VMEM((8, 128), jnp.int32), pltpu.VMEM((2, members, width), BF16)]
    scratch += solver_scratch(n, width)
    return call(kernel, outs, ins, args, scratch, flops)


def update(factored, z, states, starts, more=False):
    sh, sl, d = factored[:3]
    kernel = functools.partial(update_kernel, starts)
    outs = [(state.shape, F32, VMEM) for state in states]
    if more:
        outs += [((sh.shape[1], z.shape[1]), BF16, VMEM)] * 2
    flops = 6 * sh.shape[0] * sh.shape[1] * z.shape[1]
    return call(kernel, outs, [VMEM] * (4 + len(states)), [sh, sl, d, z, *states], (), flops)


def last(factored, state, counts=None):
    sh, sl, d, g, xh, xl, more, *cross = factored
    n, width = sh.shape[0], state.shape[1]
    outs = [((n, width), F32, VMEM)] + [((count, width), F32, VMEM) for count in counts or state.shape[:1]]
    args = [more, sh, sl, d, g, xh, xl, state, *cross]
    flops = 12 * sh.shape[0] * sh.shape[1] * width
    ins = [SMEM] + [VMEM] * (len(args) - 1)
    kernel = functools.partial(last_kernel, bool(cross))
    return call(kernel, outs, ins, args, solver_scratch(n, width), flops)


def rings(size):
    up = [(i, (i + 1) % size) for i in range(size)]
    return up, [(j, i) for i, j in up]


BOTH = ("region", "member")


def permute(x, moves, regions):
    table = []
    for region in range(regions):
        for column in range(2):
            pair, parity, to = moves(region // 2, region % 2, column)
            pair %= regions // 2
            table.append((region * 2 + column, (pair * 2 + parity) * 2 + to))
    return lax.ppermute(x, BOTH, table)


def paired(state, neighbours, obs_cell, obs_values, obs_var):
    half, _, cells = state.shape
    members = 2 * half
    regions = lax.axis_size("region")
    region, column = lax.axis_index("region"), lax.axis_index("member")
    place = (region.astype(jnp.int32)[None], column.astype(jnp.int32)[None])
    near = neighbours.T

    def own_of(region_ref, column_ref):
        return region_ref[0] * 2 + column_ref[0]

    def around(region):
        side = 2 * lax.rem(region, 2) - 1
        return region, region - side, lax.rem(region + regions + side, regions)

    def patches_first(region_ref, column_ref):
        return [r * 2 + p for r in around(region_ref[0]) for p in (0, 1)], own_of(region_ref, column_ref)

    def patches_next(region_ref, column_ref):
        column = column_ref[0]
        within = (column, 1 - column)
        return [r * 2 + p for p in within for r in around(region_ref[0])], own_of(region_ref, column_ref)

    def across(x):
        return permute(x, lambda c, q, m: (c, q, 1 - m), regions)

    def beside(x):
        return permute(x, lambda c, q, m: (c, 1 - q, m), regions)

    def outside(x):
        return permute(x, lambda c, q, m: (c + 2 * q - 1, 1 - q, m), regions)

    anywhere = pl.BlockSpec(memory_space=pl.ANY)
    shape = ((half, cells), F32, VMEM)
    keep, send = call(sort_kernel, [shape] * 2, [SMEM, VMEM], [place[1], state])
    (rows,) = call(
        pick_kernel,
        [((2, obs_cell.shape[2], half), F32, VMEM)],
        [SMEM, SMEM, VMEM, VMEM, VMEM],
        [*place, obs_cell, keep, send],
        [pltpu.VMEM((8, 128), jnp.int32)],
    )
    other = across(rows)
    sources = [rows, beside(rows), outside(rows), other, beside(other), outside(other)]
    send, values, var = call(
        gate_kernel,
        [((half, cells), F32, anywhere), (obs_values.shape, F32, VMEM), (obs_var.shape, F32, VMEM)],
        [anywhere] * 4,
        [obs_values, obs_var, send, rows],
        [pltpu.SemaphoreType.DMA((2,))],
        aliases={2: 0},
    )
    pieces = [[(i, (p,), 0), (3 + i, (p,), 1)] for i in range(3) for p in range(2)]
    states = [keep, across(send)]
    given = (place, near, values, var)
    n = len(pieces) * obs_cell.shape[2]
    early = [[(0, (p,), 0), (1, (p,), 1)] for p in range(2)]
    done = prepare(early, 0, members, patches_first, *given, (), [rows, other], n)
    factored = factor(pieces, 0, members, CHUNK, patches_first, *given, sources, 2, done)
    everything = slice(None)
    low, high = (everything, slice(0, half)), (everything, slice(half, members))
    pieces = [[(i, low, 0), (i, high, 1)] for i in range(3)]
    pieces += [[(i, high, 0), (i, low, 1)] for i in range(3, 6)]
    early = 4
    for batch in range(1, NBATCH):
        z, rows = gain(batch, own_of, place, obs_cell, factored, states)
        other = across(rows)
        far = permute(rows, lambda c, q, m: (c + 2 * q - 1, 1 - q, 1 - m), regions)
        sources = [rows, beside(rows), outside(rows), other, beside(other), far]
        mine, theirs, *anomaly = update(factored, z, states, (0, half), True)
        states = [mine, theirs]
        done = prepare(pieces[:early], batch, members, patches_next, *given, anomaly, sources[:early], n)
        factored = factor(
            pieces, batch, members, CHUNK, patches_next, *given, sources, early, [*anomaly, *done]
        )
    most = half - half // 4
    z, *theirs = last(factored, states[1], (most, half - most))
    theirs = [across(part) for part in theirs]
    (mine,) = update(factored, z, states[:1], (0,))
    joined = []
    for first, other in zip((0, most), theirs):
        count = other.shape[0]
        (out,) = call(
            functools.partial(join_kernel, first),
            [(state.shape, F32, anywhere)],
            [SMEM, VMEM, VMEM] + [anywhere] * len(joined),
            [place[1], mine, other, *joined],
            [pltpu.VMEM((count, *state.shape[1:]), F32), pltpu.SemaphoreType.DMA((2,))],
            aliases={3: 0} if joined else {},
        )
        joined = [out]
    return out


def listed(table_ref):
    blocks = table_ref.shape[0] - 1
    return [table_ref[i] for i in range(blocks)], table_ref[blocks]


def general(state, neighbours, obs_cell, obs_values, obs_var):
    ensemble = lax.all_to_all(state, "member", split_axis=1, concat_axis=0, tiled=True)
    members, owned, cells = ensemble.shape
    regions = lax.axis_size("region")
    region_patches = owned * lax.axis_size("member")
    region = lax.axis_index("region")
    first = region * region_patches + lax.axis_index("member") * owned
    up, down = rings(regions)
    fields = [ensemble[:, p, :] for p in range(owned)]
    grid = jnp.arange(cells, dtype=jnp.int32)
    for batch in range(NBATCH):
        picks = lax.dynamic_slice_in_dim(obs_cell, first, owned, 0)[:, batch, :]
        hot = (picks[:, :, None] == grid[None, None, :]).astype(F32)
        own_rows = jnp.einsum("poc,pkc->pok", hot, jnp.stack(fields), precision=HIGHEST)
        region_rows = lax.all_gather(own_rows, "member", axis=0, tiled=True)
        before = lax.ppermute(region_rows, "region", up)
        after = lax.ppermute(region_rows, "region", down)
        beside = jnp.concatenate([before, region_rows, after], axis=0)
        new = []
        for p in range(owned):
            own = first + p
            links = lax.dynamic_index_in_dim(neighbours, own, 0, keepdims=False)
            ids = jnp.concatenate([own[None], links]).astype(jnp.int32)
            table = jnp.concatenate([ids, own[None]]).astype(jnp.int32)
            home = (ids // region_patches - region + 1) % regions
            rows = jnp.take(beside, home * region_patches + ids % region_patches, axis=0)
            pieces = [[(0, (i,), 0)] for i in range(ids.shape[0])]
            factored = factor(
                pieces, batch, members, CHUNK, listed, [table], neighbours.T, obs_values, obs_var, [rows]
            )
            new.append(last(factored, fields[p])[1])
        fields = new
    ensemble = jnp.stack(fields, axis=1)
    return lax.all_to_all(ensemble, "member", split_axis=0, concat_axis=1, tiled=True)


def on_device(state, neighbours, obs_cell, obs_values, obs_var):
    patches, links = state.shape[1], neighbours.shape[1]
    even = lax.axis_size("region") % 2 == 0
    if even and patches == 2 and lax.axis_size("member") == 2 and links + 1 == 3 * patches:
        return paired(state, neighbours, obs_cell, obs_values, obs_var)
    return general(state, neighbours, obs_cell, obs_values, obs_var)


def solution(mesh):
    in_specs = (P("member", "region", None), P(), P(), P(), P())
    out_specs = P("member", "region", None)
    return jax.shard_map(
        on_device, mesh=mesh, in_specs=in_specs, out_specs=out_specs, check_vma=False
    )
```

```python
import functools
import math

import jax
import jax.numpy as jnp
from jax import lax
from jax.experimental import pallas as pl
from jax.experimental.pallas import tpu as pltpu
from jax.sharding import PartitionSpec as P

NBATCH = 2
HIGHEST = lax.Precision.HIGHEST
F32 = jnp.float32
BF16 = jnp.bfloat16
VMEM = pl.BlockSpec(memory_space=pltpu.VMEM)
SMEM = pl.BlockSpec(memory_space=pltpu.SMEM)
NN = (((1,), (0,)), ((), ()))
NT = (((1,), (1,)), ((), ()))
TN = (((0,), (0,)), ((), ()))
RESIDUAL = 1e-3
FACTOR_LIMIT = 24
MOST_STEPS = 15
TILE = 256
CHUNK = 128
SOLVE_CHUNK = 192


def call(kernel, outs, ins, args, scratch=(), flops=0, limit=16, aliases=None):
    shapes = [jax.ShapeDtypeStruct(shape, dtype) for shape, dtype, _ in outs]
    moved = sum(math.prod(s.shape) * s.dtype.itemsize for s in shapes)
    moved += sum(a.size * a.dtype.itemsize for a in args)
    return pl.pallas_call(
        kernel,
        out_shape=shapes,
        in_specs=ins,
        out_specs=[space for _, _, space in outs],
        scratch_shapes=list(scratch),
        input_output_aliases=aliases or {},
        compiler_params=pltpu.CompilerParams(vmem_limit_bytes=limit * 1024 * 1024),
        cost_estimate=pl.CostEstimate(flops=flops, bytes_accessed=moved, transcendentals=0),
    )(*args)


def split(x):
    high = x.astype(BF16)
    return high, (x - high.astype(F32)).astype(BF16)


def dot(a, b, dims=NN):
    return lax.dot_general(a, b, dims, preferred_element_type=F32)


def dot3(a, b, dims=NN):
    (left,), (right,) = dims[0]
    lhs = jnp.concatenate([a[0], a[0], a[1]], axis=left)
    rhs = jnp.concatenate([b[0], b[1], b[0]], axis=right)
    return dot(lhs, rhs, dims)


def select(hot, parts, dims):
    (left,), (right,) = dims[0]
    hot = hot.astype(BF16)
    lhs = jnp.concatenate([hot] * len(parts), axis=left)
    return dot(lhs, jnp.concatenate(parts, axis=right), dims)


def split_all(x):
    high, middle = split(x)
    low = x - high.astype(F32) - middle.astype(F32)
    return high, middle, low.astype(BF16)


def step_limits():
    limits = []
    for steps in range(MOST_STEPS):
        rho = RESIDUAL
        for _ in range(steps):
            rho = math.sqrt(2.0 * rho / (1.0 + rho))
        limits.append(2.0 * rho / (1.0 - rho) if rho < 1.0 else math.inf)
    return limits


def diagonal(n, columns, first):
    row = lax.broadcasted_iota(jnp.int32, (n, columns), 0)
    column = lax.broadcasted_iota(jnp.int32, (n, columns), 1)
    return row + first == column


def selector(picks, cells, scratch):
    per_patch = picks.shape[1]
    scratch[...] = jnp.full_like(scratch, -1)
    scratch[0:1, 0:per_patch] = picks
    grid = lax.broadcasted_iota(jnp.int32, (cells, scratch.shape[1]), 0)
    hot = (grid == scratch[0:1, :]).astype(F32)
    return jnp.transpose(hot)[0:per_patch, :]


def sort_kernel(column_ref, state_ref, keep_ref, send_ref):
    column = column_ref[0]
    first, second = state_ref[:, 0, :], state_ref[:, 1, :]
    keep_ref[...] = jnp.where(column == 0, first, second)
    send_ref[...] = jnp.where(column == 0, second, first)


def pick_kernel(region_ref, column_ref, cells_ref, keep_ref, send_ref, rows_ref, scratch):
    column = column_ref[0]
    for patch, field_ref in ((column, keep_ref), (1 - column, send_ref)):
        picks = cells_ref[pl.ds(region_ref[0] * 2 + patch, 1), 0, :]
        hot = selector(picks, field_ref.shape[1], scratch)
        rows_ref[pl.ds(patch, 1)] = select(hot, split_all(field_ref[...]), NT)[None]


def gate_kernel(values_hbm, var_hbm, send_ref, after_ref, out_ref, values_ref, var_ref, sems):
    copies = [
        pltpu.make_async_copy(values_hbm, values_ref, sems.at[0]),
        pltpu.make_async_copy(var_hbm, var_ref, sems.at[1]),
    ]
    for copy in copies:
        copy.start()
    for copy in copies:
        copy.wait()


def table(patches, own, near_ref, values_ref, var_ref, batch, flat):
    per_patch = values_ref.shape[2]
    blocks = len(patches)
    flat[...] = jnp.ones_like(flat)
    for i, patch in enumerate(patches):
        widening = (patch == own).astype(jnp.int32)
        for j in range(near_ref.shape[0]):
            widening = widening + (near_ref[j, own] == patch).astype(jnp.int32) * (j + 2)
        flat[i : i + 1, 0:per_patch] = values_ref[pl.ds(patch, 1), batch, :]
        noise = var_ref[pl.ds(patch, 1), batch, :] * widening.astype(F32)
        flat[blocks + i : blocks + i + 1, 0:per_patch] = noise
    return jnp.transpose(flat[...])[0:per_patch]


def column_of(upright, i, blocks):
    return upright[:, i : i + 1], upright[:, blocks + i : blocks + i + 1]


def scale_block(i, piece, sources, column, members, sh_ref, sl_ref, d_ref):
    value, noise = column
    rows = [sources[which][index] for which, index, _ in piece]
    total = sum(jnp.sum(part, axis=1, keepdims=True) for part in rows)
    mean = total * (1.0 / members)
    scale = lax.rsqrt(noise * (members - 1.0))
    per_patch = value.shape[0]
    at = slice(i * per_patch, (i + 1) * per_patch)
    for part, (_, _, start) in zip(rows, piece):
        size = part.shape[1]
        lanes = slice(start * size, (start + 1) * size)
        sh_ref[at, lanes], sl_ref[at, lanes] = split((part - mean) * scale)
    d_ref[at, :] = jnp.broadcast_to((value - mean) * scale, (per_patch, d_ref.shape[1]))


def prepare_kernel(pieces, batch, members, patches_of, places, crossing, *refs):
    place_refs, refs = refs[:places], refs[places:]
    near_ref, values_ref, var_ref, *refs = refs
    refs, (upright_ref, flat) = refs[:-2], refs[-2:]
    if crossing:
        (ah_ref, al_ref, *refs), cross_ref = refs[:-1], refs[-1]
    sources, (sh_ref, sl_ref, d_ref, g_ref) = refs[:-4], refs[-4:]
    patches, own = patches_of(*place_refs)
    upright = table(patches, own, near_ref, values_ref, var_ref, batch, flat)
    upright_ref[...] = upright
    for i, piece in enumerate(pieces):
        column = column_of(upright, i, len(patches))
        scale_block(i, piece, sources, column, members, sh_ref, sl_ref, d_ref)
    count = len(pieces) * values_ref.shape[2]
    s = (sh_ref[0:count], sl_ref[0:count])
    g_ref[0:count, 0:count] = dot3(s, s, NT)
    if crossing:
        cross_ref[0:count] = dot3(s, (ah_ref[...], al_ref[...]))


def factor_kernel(pieces, batch, members, chunk, patches_of, places, ready, crossing, *refs):
    if ready:
        upright_ref, *refs = refs
    else:
        place_refs, refs = refs[:places], refs[places:]
        near_ref, values_ref, var_ref, *refs = refs
    refs, (flat, eye_ref, x_ref, wa, wb) = refs[:-5], refs[-5:]
    if crossing:
        refs, cross_ref = refs[:-1], refs[-1]
    refs, (sh_ref, sl_ref, d_ref, g_ref, xh_ref, xl_ref, n_ref) = refs[:-7], refs[-7:]
    if crossing:
        refs, (ah_ref, al_ref) = refs[:-7], refs[-7:-5]
    elif ready:
        refs = refs[:-4]
    sources = refs
    blocks = len(pieces)
    if ready:
        upright = upright_ref[...]
    else:
        patches, own = patches_of(*place_refs)
        upright = table(patches, own, near_ref, values_ref, var_ref, batch, flat)
    per_patch = upright.shape[0]
    for i in range(ready, blocks):
        column = column_of(upright, i, blocks)
        scale_block(i, pieces[i], sources, column, members, sh_ref, sl_ref, d_ref)
    n = sh_ref.shape[0]
    head = min(TILE, n)
    tail = n - head
    chunks = [(i, min(i + chunk, n)) for i in range(0, n, chunk)]
    left = (sh_ref[0:head], sl_ref[0:head])
    fresh = ready * per_patch
    g_ref[fresh:n, 0:head] = dot3((sh_ref[fresh:n], sl_ref[fresh:n]), left, NT)
    if 0 < fresh < head:
        g_ref[0:fresh, fresh:head] = jnp.transpose(g_ref[fresh:head, 0:fresh])
    low = (sh_ref[head:n], sl_ref[head:n])
    g_ref[head:n, head:n] = dot3(low, low, NT)
    g_ref[0:head, head:n] = jnp.transpose(g_ref[head:n, 0:head])
    if crossing:
        cross_ref[fresh:n] = dot3((sh_ref[fresh:n], sl_ref[fresh:n]), (ah_ref[...], al_ref[...]))
    g = g_ref[...]
    square = jnp.sum(jnp.sum(g * g, axis=0, keepdims=True), axis=1, keepdims=True)
    norm = jnp.sqrt(square) * (1.0 + 1e-5)
    size = square[0, 0]
    limits = step_limits()
    pairs = jnp.int32(0)
    for k in range(7, MOST_STEPS - 2, 2):
        limit = limits[k] * (1.0 - 1e-4)
        pairs = pairs + (size > limit * limit).astype(jnp.int32)
    n_ref[0] = (size > 1.6e7).astype(jnp.int32) + (size > 1e8).astype(jnp.int32)
    eye_ref[...] = diagonal(n, n, 0).astype(F32)
    eye = eye_ref[...]
    first = 2.0 / (2.0 + norm)
    rho = norm * (0.5 * first)
    rho2 = rho * rho
    weight = 2.0 / (2.0 - rho2)
    keep = 0.5 * rho2 * weight
    x = (weight * first * (2.0 - first)) * eye - (weight * first * first) * g
    x_ref[...] = x
    for i, part in enumerate(split(x)):
        wa[i, :, n : 2 * n] = part

    def store(targets, start, left, corner):
        blocks = [(slice(0, n), slice(start, start + head), left)]
        blocks.append((slice(head, n), slice(start + head, start + n), corner))
        blocks.append((slice(0, head), slice(start + head, start + n), jnp.transpose(left[head:n])))
        for rows, columns, block in blocks:
            for target, part in zip(targets, split(block)):
                target[rows, columns] = part

    def corner_of(weight, keep, left, corner):
        left = weight * left - keep * eye_ref[:, 0:head]
        return left, weight * corner - keep * eye_ref[head:n, head:n]

    parts = split(g)
    square_left = dot3(parts, [part[:, 0:head] for part in parts])
    square_corner = dot3([part[head:n] for part in parts], [part[:, head:n] for part in parts])
    two = weight * first * first
    one = -2.0 * weight * first * (1.0 - first)
    none = weight * (1.0 - first) * (1.0 - first) - keep
    left = two * square_left + one * g[:, 0:head] + none * eye[:, 0:head]
    corner = two * square_corner + one * g[head:n, head:n] + none * eye[head:n, head:n]
    store((wa.at[0], wa.at[1]), 0, left, corner)

    def corners_of(source):
        ends = [jnp.concatenate([source[i, :, head:n], source[i, :, n + head : 2 * n]], axis=1) for i in (0, 1)]
        return dot3([source[i, head:n, 0:n] for i in (0, 1)], ends)

    def advance(source, target, rho2):
        weight = 2.0 / (2.0 - rho2)
        keep = 0.5 * rho2 * weight
        parts = (source[0, :, 0:n], source[1, :, 0:n])
        left = dot3(parts, (source[0, :, 0:head], source[1, :, 0:head]))
        corners = corners_of(source)
        both = (target.at[0], target.at[1])
        store(both, 0, *corner_of(weight, keep, left, corners[:, 0:tail]))
        left = dot3(parts, (source[0, :, n : n + head], source[1, :, n : n + head]))
        left = weight * (x_ref[:, 0:head] + left)
        corner = weight * (x_ref[head:n, head:n] + corners[:, tail : 2 * tail])
        x_ref[:, 0:head] = left
        x_ref[head:n, head:n] = corner
        store(both, n, left, corner)
        return keep * keep

    rho2 = keep * keep

    def sides(source, span):
        return [source[i, span[0] : span[1], 0:n] for i in (0, 1)]

    def put(targets, start, span, block):
        for target, part in zip(targets, split(block)):
            target[span[0] : span[1], start : start + head] = part
        low = max(span[0], head)
        if low < span[1]:
            for target, part in zip(targets, split(jnp.transpose(block[low - span[0] :]))):
                target[0:head, start + low : start + span[1]] = part

    def less_diagonal(block, keep, span):
        low, high = span[0], min(span[1], head)
        if low >= high:
            return block
        middle = block[:, low:high] - keep * eye_ref[low : span[1], low:high]
        pieces = [block[:, 0:low], middle, block[:, high:head]]
        return jnp.concatenate([piece for piece in pieces if piece.shape[1]], axis=1)

    def put_corner(targets, start, block):
        for target, part in zip(targets, split(block)):
            target[head:n, start + head : start + n] = part

    def put_x(targets, start, weight, span, product):
        x = weight * (x_ref[span[0] : span[1], 0:head] + product)
        x_ref[span[0] : span[1], 0:head] = x
        put(targets, start, span, x)

    def put_x_corner(targets, start, weight, product):
        x = weight * (x_ref[head:n, head:n] + product)
        x_ref[head:n, head:n] = x
        put_corner(targets, start, x)

    waiting = None
    source, target = wa, wb
    for _ in range(5):
        weight = 2.0 / (2.0 - rho2)
        keep = 0.5 * rho2 * weight
        first = (source[0, :, 0:head], source[1, :, 0:head])
        r = []
        for k, span in enumerate(chunks):
            r.append(dot3(sides(source, span), first))
            if waiting is not None:
                put_x((source.at[0], source.at[1]), n, waiting[0], span, waiting[1][k])
        if waiting is not None:
            put_x_corner((source.at[0], source.at[1]), n, waiting[0], waiting[2])
        corners = corners_of(source)
        first = (source[0, :, n : n + head], source[1, :, n : n + head])
        both = (target.at[0], target.at[1])
        x = []
        for k, span in enumerate(chunks):
            x.append(dot3(sides(source, span), first))
            put(both, 0, span, less_diagonal(weight * r[k], keep, span))
        put_corner(both, 0, weight * corners[:, 0:tail] - keep * eye_ref[head:n, head:n])
        waiting = (weight, x, corners[:, tail : 2 * tail])
        rho2 = keep * keep
        source, target = target, source
    for k, span in enumerate(chunks):
        put_x((source.at[0], source.at[1]), n, waiting[0], span, waiting[1][k])
    put_x_corner((source.at[0], source.at[1]), n, waiting[0], waiting[2])

    def twice(_, rho2):
        return advance(target, source, advance(source, target, rho2))

    rho2 = lax.fori_loop(0, pairs, twice, rho2)
    weight = 2.0 / (2.0 - rho2)
    first = (source[0, :, n : n + head], source[1, :, n : n + head])
    done = (xh_ref, xl_ref)
    ends = [source[i, :, n + head : 2 * n] for i in (0, 1)]
    put_x_corner(done, 0, weight, dot3(sides(source, (head, n)), ends))
    x = [dot3(sides(source, span), first) for span in chunks]
    for k, span in enumerate(chunks):
        put_x(done, 0, weight, span, x[k])


def centred(fields):
    members = sum(field.shape[0] for field in fields)
    mean = sum(jnp.sum(field, axis=0, keepdims=True) for field in fields) * (1.0 / members)
    pairs = [split(field - mean) for field in fields]
    return [jnp.concatenate(parts, axis=0) for parts in zip(*pairs)], mean


def in_chunks(count, product, work):
    waiting = None
    for start in range(0, count, SOLVE_CHUNK):
        span = slice(start, min(start + SOLVE_CHUNK, count))
        result = product(span)
        if waiting is not None:
            work(*waiting)
        waiting = (span, result)
    work(*waiting)


def solve(n_ref, s, g_ref, x, anomaly, z_ref, cross_ref, parts_ref, crossed_already=False, between=()):
    n = z_ref.shape[0]

    def keep(slot, span, value):
        for i, part in enumerate(split(value)):
            parts_ref[slot, i, span] = part

    def kept(slot):
        return parts_ref[slot, 0], parts_ref[slot, 1]

    def some(parts, span):
        return [part[span] for part in parts]

    def crossed(span, value):
        cross_ref[span] = value
        keep(0, span, value)

    def solved(span, value):
        z_ref[span] = value
        keep(1, span, value)

    def left(span, value):
        keep(0, span, cross_ref[span] - z_ref[span] - value)

    def refined(span, value):
        z_ref[span] = z_ref[span] + value

    if crossed_already:
        keep(0, slice(0, n), cross_ref[...])
    else:
        in_chunks(n, lambda span: dot3(some(s, span), [part[...] for part in anomaly]), crossed)
    stages = [
        (lambda span: dot3(some(x, span), kept(0)), solved),
        (lambda span: dot3(split(g_ref[span]), kept(1)), left),
        (lambda span: dot3(some(x, span), kept(0)), refined),
    ]
    for i, (product, work) in enumerate(stages):
        for extra in between[i : i + 1]:
            extra()
        in_chunks(n, product, work)

    def refine(_, carry):
        z = z_ref[...]
        gz = lax.dot_general(g_ref[...], z, NN, precision=HIGHEST, preferred_element_type=F32)
        z_ref[...] = z + dot3([part[...] for part in x], split(cross_ref[...] - z - gz))
        return carry

    lax.fori_loop(0, n_ref[0], refine, 0)


def gain_kernel(batch, parts, own_of, region_ref, column_ref, n_ref, cells_ref, sh_ref, sl_ref, d_ref, g_ref, *refs):
    xh_ref, xl_ref, *refs = refs
    states = refs[:parts]
    z_ref, rows_ref, scratch, anomaly_ref, cross_ref, parts_ref = refs[parts:]
    anomaly, mean = centred([state[...] for state in states])
    for i, part in enumerate(anomaly):
        anomaly_ref[i] = part
    anomaly = (anomaly_ref.at[0], anomaly_ref.at[1])
    picks = cells_ref[pl.ds(own_of(region_ref, column_ref), 1), batch, :]
    hot = selector(picks, mean.shape[1], scratch)
    base = jnp.sum(hot * mean, axis=1, keepdims=True)
    members = anomaly_ref.shape[1]
    count = 3
    size = -(-members // (count * 128)) * 128

    def pick(start, stop):
        picked = select(hot, [part[start:stop] for part in anomaly], NT)
        rows_ref[:, start:stop] = base + picked

    between = [
        functools.partial(pick, i * size, min((i + 1) * size, members)) for i in range(count)
    ]
    x = (xh_ref, xl_ref)
    solve(n_ref, (sh_ref, sl_ref), g_ref, x, anomaly, z_ref, cross_ref, parts_ref, False, between)
    zt = split(select(hot, split(z_ref[...]), NT))
    shift = dot3(zt, split(d_ref[...]))[:, 0:1]
    rows_ref[...] = rows_ref[...] + shift - 0.5 * dot3(zt, (sh_ref[...], sl_ref[...]))


def updated(field, start, s, shift, z):
    size = field.shape[0]
    return field + shift - 0.5 * dot3([h[:, start : start + size] for h in s], z, TN)


def shift_of(z, d_ref):
    return jnp.sum(z * d_ref[:, 0:1], axis=0, keepdims=True)


def update_kernel(starts, sh_ref, sl_ref, d_ref, z_ref, *refs):
    count = len(starts)
    states, outs, parts = refs[:count], refs[count : 2 * count], refs[2 * count :]
    z = z_ref[...]
    shift = shift_of(z, d_ref)
    s, zs = (sh_ref[...], sl_ref[...]), split(z)
    for start, state, out in zip(starts, states, outs):
        out[...] = updated(state[...], start, s, shift, zs)
    if parts:
        anomaly, _ = centred([out[...] for out in outs])
        for ref, part in zip(parts, anomaly):
            ref[...] = part


def last_kernel(given, n_ref, sh_ref, sl_ref, d_ref, g_ref, xh_ref, xl_ref, state_ref, *refs):
    refs, (cross_ref, parts_ref) = refs[:-2], refs[-2:]
    if given:
        cross_ref, *refs = refs
    z_ref, *out_refs = refs
    anomaly = None if given else centred([state_ref[...]])[0]
    x = (xh_ref, xl_ref)
    solve(n_ref, (sh_ref, sl_ref), g_ref, x, anomaly, z_ref, cross_ref, parts_ref, given)
    z = z_ref[...]
    shift, zs = shift_of(z, d_ref), split(z)
    start = sh_ref.shape[1] - state_ref.shape[0]
    s = (sh_ref[...], sl_ref[...])
    first = 0
    for out_ref in out_refs:
        stop = first + out_ref.shape[0]
        out_ref[...] = updated(state_ref[first:stop], start + first, s, shift, zs)
        first = stop


def join_kernel(first, column_ref, mine_ref, theirs_ref, *refs):
    out_ref, both, sems = refs[-3:]
    chunks = sems.shape[0]
    size = both.shape[0] // chunks
    column = column_ref[0]
    copies = []
    for i in range(chunks):
        at = slice(i * size, (i + 1) * size)
        mine, theirs = mine_ref[first + i * size : first + (i + 1) * size, :], theirs_ref[at, :]
        both[at, 0, :] = jnp.where(column == 0, mine, theirs)
        both[at, 1, :] = jnp.where(column == 0, theirs, mine)
        target = out_ref.at[pl.ds(first + i * size, size)]
        copies.append(pltpu.make_async_copy(both.at[pl.ds(i * size, size)], target, sems.at[i]))
        copies[-1].start()
    for copy in copies:
        copy.wait()


def prepare(pieces, batch, members, patches_of, place, near, values, var, anomaly, sources, n):
    width = anomaly[0].shape[1] if anomaly else 0
    outs = [
        ((n, members), BF16, VMEM),
        ((n, members), BF16, VMEM),
        ((n, 128), F32, VMEM),
        ((n, n), F32, VMEM),
    ]
    if anomaly:
        outs.append(((n, width), F32, VMEM))
    outs.append(((values.shape[2], 128), F32, VMEM))
    kernel = functools.partial(
        prepare_kernel, pieces, batch, members, patches_of, len(place), bool(anomaly)
    )
    args = [*place, near, values, var, *anomaly, *sources]
    ins = [SMEM] * (len(place) + 1) + [VMEM] * (len(args) - len(place) - 1)
    return call(kernel, outs, ins, args, [pltpu.VMEM((128, 128), F32)], 6 * n * (width + n // 3) * members)


def factor(pieces, batch, members, chunk, patches_of, place, near, values, var, sources, ready=0, before=()):
    per_patch = values.shape[2]
    n = len(pieces) * per_patch
    outs = [
        ((n, members), BF16, VMEM),
        ((n, members), BF16, VMEM),
        ((n, 128), F32, VMEM),
        ((n, n), F32, VMEM),
        ((n, n), BF16, VMEM),
        ((n, n), BF16, VMEM),
        ((1,), jnp.int32, SMEM),
    ]
    if ready:
        *before, upright = before
        args = [upright, *sources, *before]
        ins = [VMEM] * len(args)
    else:
        args = [*place, near, values, var, *sources]
        ins = [SMEM] * (len(place) + 1) + [VMEM] * (2 + len(sources))
    aliases = {}
    crossing = len(before) > 4
    if crossing:
        outs.append((before[-1].shape, F32, VMEM))
    if ready:
        first = len(args) - 4 - crossing
        aliases = {first: 0, first + 1: 1, first + 2: 2, first + 3: 3}
        if crossing:
            aliases[first + 4] = 7
    scratch = [
        pltpu.VMEM((128, 128), F32),
        pltpu.VMEM((n, n), F32),
        pltpu.VMEM((n, n), F32),
        pltpu.VMEM((2, n, 2 * n), BF16),
        pltpu.VMEM((2, n, 2 * n), BF16),
    ]
    kernel = functools.partial(
        factor_kernel, pieces, batch, members, chunk, patches_of, len(place), ready, crossing
    )
    flops = 6 * n * n * members + (30 if crossing else 20) * n * n * n
    return call(kernel, outs, ins, args, scratch, flops, FACTOR_LIMIT, aliases)


def solver_scratch(n, width):
    return [pltpu.VMEM((n, width), F32), pltpu.VMEM((2, 2, n, width), BF16)]


def gain(batch, own_of, place, cells, factored, states):
    sh, sl, d, g, xh, xl, more = factored[:7]
    n, members = sh.shape
    width = states[0].shape[1]
    kernel = functools.partial(gain_kernel, batch, len(states), own_of)
    outs = [((n, width), F32, VMEM), ((cells.shape[2], members), F32, VMEM)]
    ins = [SMEM] * 3 + [VMEM] * (7 + len(states))
    args = [*place, more, cells, sh, sl, d, g, xh, xl, *states]
    flops = 8 * n * members * width
    scratch = [pltpu.VMEM((8, 128), jnp.int32), pltpu.VMEM((2, members, width), BF16)]
    scratch += solver_scratch(n, width)
    return call(kernel, outs, ins, args, scratch, flops)


def update(factored, z, states, starts, more=False):
    sh, sl, d = factored[:3]
    kernel = functools.partial(update_kernel, starts)
    outs = [(state.shape, F32, VMEM) for state in states]
    if more:
        outs += [((sh.shape[1], z.shape[1]), BF16, VMEM)] * 2
    flops = 6 * sh.shape[0] * sh.shape[1] * z.shape[1]
    return call(kernel, outs, [VMEM] * (4 + len(states)), [sh, sl, d, z, *states], (), flops)


def last(factored, state, counts=None):
    sh, sl, d, g, xh, xl, more, *cross = factored
    n, width = sh.shape[0], state.shape[1]
    outs = [((n, width), F32, VMEM)] + [((count, width), F32, VMEM) for count in counts or state.shape[:1]]
    args = [more, sh, sl, d, g, xh, xl, state, *cross]
    flops = 12 * sh.shape[0] * sh.shape[1] * width
    ins = [SMEM] + [VMEM] * (len(args) - 1)
    kernel = functools.partial(last_kernel, bool(cross))
    return call(kernel, outs, ins, args, solver_scratch(n, width), flops)


def rings(size):
    up = [(i, (i + 1) % size) for i in range(size)]
    return up, [(j, i) for i, j in up]


BOTH = ("region", "member")


def permute(x, moves, regions):
    table = []
    for region in range(regions):
        for column in range(2):
            pair, parity, to = moves(region // 2, region % 2, column)
            pair %= regions // 2
            table.append((region * 2 + column, (pair * 2 + parity) * 2 + to))
    return lax.ppermute(x, BOTH, table)


def paired(state, neighbours, obs_cell, obs_values, obs_var):
    half, _, cells = state.shape
    members = 2 * half
    regions = lax.axis_size("region")
    region, column = lax.axis_index("region"), lax.axis_index("member")
    place = (region.astype(jnp.int32)[None], column.astype(jnp.int32)[None])
    near = neighbours.T

    def own_of(region_ref, column_ref):
        return region_ref[0] * 2 + column_ref[0]

    def around(region):
        side = 2 * lax.rem(region, 2) - 1
        return region, region - side, lax.rem(region + regions + side, regions)

    def patches_first(region_ref, column_ref):
        return [r * 2 + p for r in around(region_ref[0]) for p in (0, 1)], own_of(region_ref, column_ref)

    def patches_next(region_ref, column_ref):
        column = column_ref[0]
        within = (column, 1 - column)
        return [r * 2 + p for p in within for r in around(region_ref[0])], own_of(region_ref, column_ref)

    def across(x):
        return permute(x, lambda c, q, m: (c, q, 1 - m), regions)

    def beside(x):
        return permute(x, lambda c, q, m: (c, 1 - q, m), regions)

    def outside(x):
        return permute(x, lambda c, q, m: (c + 2 * q - 1, 1 - q, m), regions)

    anywhere = pl.BlockSpec(memory_space=pl.ANY)
    shape = ((half, cells), F32, VMEM)
    keep, send = call(sort_kernel, [shape] * 2, [SMEM, VMEM], [place[1], state])
    (rows,) = call(
        pick_kernel,
        [((2, obs_cell.shape[2], half), F32, VMEM)],
        [SMEM, SMEM, VMEM, VMEM, VMEM],
        [*place, obs_cell, keep, send],
        [pltpu.VMEM((8, 128), jnp.int32)],
    )
    other = across(rows)
    sources = [rows, beside(rows), outside(rows), other, beside(other), outside(other)]
    send, values, var = call(
        gate_kernel,
        [((half, cells), F32, anywhere), (obs_values.shape, F32, VMEM), (obs_var.shape, F32, VMEM)],
        [anywhere] * 4,
        [obs_values, obs_var, send, rows],
        [pltpu.SemaphoreType.DMA((2,))],
        aliases={2: 0},
    )
    pieces = [[(i, (p,), 0), (3 + i, (p,), 1)] for i in range(3) for p in range(2)]
    states = [keep, across(send)]
    given = (place, near, values, var)
    n = len(pieces) * obs_cell.shape[2]
    early = [[(0, (p,), 0), (1, (p,), 1)] for p in range(2)]
    done = prepare(early, 0, members, patches_first, *given, (), [rows, other], n)
    factored = factor(pieces, 0, members, CHUNK, patches_first, *given, sources, 2, done)
    everything = slice(None)
    low, high = (everything, slice(0, half)), (everything, slice(half, members))
    pieces = [[(i, low, 0), (i, high, 1)] for i in range(3)]
    pieces += [[(i, high, 0), (i, low, 1)] for i in range(3, 6)]
    early = 4
    for batch in range(1, NBATCH):
        z, rows = gain(batch, own_of, place, obs_cell, factored, states)
        other = across(rows)
        far = permute(rows, lambda c, q, m: (c + 2 * q - 1, 1 - q, 1 - m), regions)
        sources = [rows, beside(rows), outside(rows), other, beside(other), far]
        mine, theirs, *anomaly = update(factored, z, states, (0, half), True)
        states = [mine, theirs]
        done = prepare(pieces[:early], batch, members, patches_next, *given, anomaly, sources[:early], n)
        factored = factor(
            pieces, batch, members, SOLVE_CHUNK, patches_next, *given, sources, early, [*anomaly, *done]
        )
    most = half - half // 4
    z, *theirs = last(factored, states[1], (most, half - most))
    theirs = [across(part) for part in theirs]
    (mine,) = update(factored, z, states[:1], (0,))
    joined = []
    for first, other in zip((0, most), theirs):
        count = other.shape[0]
        (out,) = call(
            functools.partial(join_kernel, first),
            [(state.shape, F32, anywhere)],
            [SMEM, VMEM, VMEM] + [anywhere] * len(joined),
            [place[1], mine, other, *joined],
            [pltpu.VMEM((count, *state.shape[1:]), F32), pltpu.SemaphoreType.DMA((2,))],
            aliases={3: 0} if joined else {},
        )
        joined = [out]
    return out


def listed(table_ref):
    blocks = table_ref.shape[0] - 1
    return [table_ref[i] for i in range(blocks)], table_ref[blocks]


def general(state, neighbours, obs_cell, obs_values, obs_var):
    ensemble = lax.all_to_all(state, "member", split_axis=1, concat_axis=0, tiled=True)
    members, owned, cells = ensemble.shape
    regions = lax.axis_size("region")
    region_patches = owned * lax.axis_size("member")
    region = lax.axis_index("region")
    first = region * region_patches + lax.axis_index("member") * owned
    up, down = rings(regions)
    fields = [ensemble[:, p, :] for p in range(owned)]
    grid = jnp.arange(cells, dtype=jnp.int32)
    for batch in range(NBATCH):
        picks = lax.dynamic_slice_in_dim(obs_cell, first, owned, 0)[:, batch, :]
        hot = (picks[:, :, None] == grid[None, None, :]).astype(F32)
        own_rows = jnp.einsum("poc,pkc->pok", hot, jnp.stack(fields), precision=HIGHEST)
        region_rows = lax.all_gather(own_rows, "member", axis=0, tiled=True)
        before = lax.ppermute(region_rows, "region", up)
        after = lax.ppermute(region_rows, "region", down)
        beside = jnp.concatenate([before, region_rows, after], axis=0)
        new = []
        for p in range(owned):
            own = first + p
            links = lax.dynamic_index_in_dim(neighbours, own, 0, keepdims=False)
            ids = jnp.concatenate([own[None], links]).astype(jnp.int32)
            table = jnp.concatenate([ids, own[None]]).astype(jnp.int32)
            home = (ids // region_patches - region + 1) % regions
            rows = jnp.take(beside, home * region_patches + ids % region_patches, axis=0)
            pieces = [[(0, (i,), 0)] for i in range(ids.shape[0])]
            factored = factor(
                pieces, batch, members, CHUNK, listed, [table], neighbours.T, obs_values, obs_var, [rows]
            )
            new.append(last(factored, fields[p])[1])
        fields = new
    ensemble = jnp.stack(fields, axis=1)
    return lax.all_to_all(ensemble, "member", split_axis=0, concat_axis=1, tiled=True)


def on_device(state, neighbours, obs_cell, obs_values, obs_var):
    patches, links = state.shape[1], neighbours.shape[1]
    even = lax.axis_size("region") % 2 == 0
    if even and patches == 2 and lax.axis_size("member") == 2 and links + 1 == 3 * patches:
        return paired(state, neighbours, obs_cell, obs_values, obs_var)
    return general(state, neighbours, obs_cell, obs_values, obs_var)


def solution(mesh):
    in_specs = (P("member", "region", None), P(), P(), P(), P())
    out_specs = P("member", "region", None)
    return jax.shard_map(
        on_device, mesh=mesh, in_specs=in_specs, out_specs=out_specs, check_vma=False
    )
```
